32 devices in a mesh: lat: 4 (over x, core), lon: 8 (over z, y).
Axes of the slice: x: 2, y: 2, z: 4, core: 2. Of those that a mesh axis runs over, the one named last changes fastest.
Arguments:
- inputs_below: bfloat16 [64, 32, 1024], P(None, 'lat', 'lon'), may hold values from -6 to 6
- hidden_prev: bfloat16 [64, 32, 1024], P(None, 'lat', 'lon'), may hold values from -0.8984375 to 0.8984375
- cell_prev: float32 [64, 32, 1024], P(None, 'lat', 'lon'), may hold values from -5 to 5
- kernel_weights: bfloat16 [9, 256, 128], replicated, may hold values from -0.1875 to 0.1875
- gate_bias: float32 [256], replicated, may hold values from -4 to 4
- readout: float32 [64], replicated, may hold values from -0.75 to 0.75
- target_field: float32 [32, 1024], P('lat', 'lon'), may hold values from -6 to 6
- land_mask: int32 [32, 1024], P('lat', 'lon'), may hold values 0 or 1
- fire_mask: int32 [32, 1024], P('lat', 'lon'), may hold values 0 or 1
- hidden_grad: bfloat16 [64, 32, 1024], P(None, 'lat', 'lon'), may hold values from -10 to 10
Outputs:
- hidden_next: bfloat16 [64, 32, 1024], P(None, 'lat', 'lon')
- cell_next: float32 [64, 32, 1024], P(None, 'lat', 'lon')
- grad_inputs: bfloat16 [64, 32, 1024], P(None, 'lat', 'lon')
- grad_hidden: bfloat16 [64, 32, 1024], P(None, 'lat', 'lon')
- grad_cell: float32 [64, 32, 1024], P(None, 'lat', 'lon')
- grad_kernel: float32 [9, 256, 128], replicated
- grad_bias: float32 [256], replicated
The draws below stay inside these ranges and needn't reach their ends.
Inputs may be any that keep to these rules, and one draw needn't show every extreme that they name: `land_mask`: 1 marks land cells, 0 sea cells. `fire_mask`: 1 marks cells where fire danger is observed.
All inputs are finite; a program needn't handle non-finite values. No bound on the sum of `land_mask` or of `fire_mask` on one device may be relied on, other than what follows from the above.
Results may differ from the reference program's by a relative error of at most 0.0049.
Values may be sent and summed in bfloat16 or wider, within the bound.
No kernel may reach another device: no remote copies, remote signals or barrier semaphores. Data moves between devices by JAX's collectives and lax.ppermute only.
A program may use at most 64 MiB of HBM per device.

```python
import math
import jax
import jax.numpy as jnp
from jax import lax

CIN = 64
HID = 64
GATES = 256
NLAT = 32
NLON = 1024


def plant(entries, stream_key, low, top_value):
    extent = entries.shape
    index_at = [jax.random.randint(jax.random.fold_in(stream_key, axis), (), 0, extent[axis]) for axis in range(len(extent))]
    entries = entries.at[tuple(index_at)].set(low)
    longest = extent.index(max(extent))
    index_at[longest] = (index_at[longest] + 1) % extent[longest]
    return entries.at[tuple(index_at)].set(top_value)


def steps_of(key, dims, split, least, high):
    factor_of, own = 1.0, jax.random.fold_in(key, 6)
    for axis_at, parts in split:
        draws = jnp.exp(jax.random.uniform(jax.random.fold_in(own, axis_at), (parts,), jnp.float32, least / len(split), high / len(split)))
        factor_of = factor_of * jnp.repeat(draws, dims[axis_at] // parts).reshape([-1 if axis == axis_at else 1 for axis in range(len(dims))])
    return factor_of


def noise(stream_key, shape, scale, bound, pieces=(), kind=jnp.bfloat16):
    array = scale * jax.random.normal(stream_key, shape, jnp.float32)
    if pieces:
        array = array * steps_of(stream_key, shape, pieces, -0.22, 0.18)
    return jnp.clip(array, -bound, bound).astype(kind)


def setup_inputs(seed: int = 0) -> dict:
    key_list = jax.random.split(jax.random.key(seed), 11)
    inputs_below = noise(key_list[0], (CIN, NLAT, NLON), 1.0, 6.0, ((1, 4), (2, 8)))
    hidden_prev = jnp.clip(jax.random.uniform(key_list[1], (HID, NLAT, NLON), jnp.float32, -0.8984375, 0.8984375) * steps_of(key_list[1], (HID, NLAT, NLON), ((1, 4), (2, 8)), -0.4, 0.0), -0.8984375, 0.8984375).astype(jnp.bfloat16)
    cell_prev = noise(key_list[2], (HID, NLAT, NLON), 1.0, 5.0, ((1, 4), (2, 8)), jnp.float32)
    kernel_weights = noise(key_list[3], (9, GATES, CIN + HID), (9 * (CIN + HID)) ** -0.5, 0.1875)
    gate_bias = noise(key_list[4], (GATES,), 1.0, 4.0, (), jnp.float32)
    readout = noise(key_list[5], (HID,), HID ** -0.5, 0.75, (), jnp.float32)
    target_field = noise(key_list[6], (NLAT, NLON), 1.0, 6.0, ((0, 4), (1, 8)), jnp.float32)
    land_mask = plant((jax.random.randint(key_list[7], (NLAT, NLON), 0, 4) < 3).astype(jnp.int32), jax.random.fold_in(key_list[7], 1), 0, 1)
    fire_mask = plant((jax.random.randint(key_list[8], (NLAT, NLON), 0, 2) < 1).astype(jnp.int32), jax.random.fold_in(key_list[8], 1), 0, 1)
    hidden_grad = noise(key_list[9], (HID, NLAT, NLON), 2.0, 10.0, ((1, 4), (2, 8)))
    return {"inputs_below": inputs_below, "hidden_prev": hidden_prev, "cell_prev": cell_prev, "kernel_weights": kernel_weights, "gate_bias": gate_bias, "readout": readout, "target_field": target_field, "land_mask": land_mask, "fire_mask": fire_mask, "hidden_grad": hidden_grad}


def fold_pad(field):
    halfway = field.shape[2] // 2
    north_row = jnp.roll(field[:, :1], -halfway, axis=2)
    south_row = jnp.roll(field[:, -1:], -halfway, axis=2)
    banded = jnp.concatenate([north_row, field, south_row], axis=1)
    return jnp.concatenate([banded[:, :, -1:], banded, banded[:, :, :1]], axis=2)

def convolve(padded, kernel):
    channels = padded.shape[0]
    row_count = padded.shape[1] - 2
    col_count = padded.shape[2] - 2
    running = jnp.zeros((kernel.shape[1], row_count * col_count), jnp.float32)
    for position in range(9):
        lat_start = position // 3
        lon_start = position % 3
        window = padded[:, lat_start:lat_start + row_count, lon_start:lon_start + col_count].reshape(channels, row_count * col_count)
        running = running + jnp.dot(kernel[position], window, preferred_element_type=jnp.float32, precision=lax.Precision.HIGHEST)
    return running.reshape(kernel.shape[1], row_count, col_count)

def reference(inputs_below, hidden_prev, cell_prev, kernel_weights, gate_bias, readout, target_field, land_mask, fire_mask, hidden_grad):
    stacked = jnp.concatenate([inputs_below, hidden_prev], axis=0)
    padded = fold_pad(stacked)
    preact = convolve(padded, kernel_weights) + gate_bias[:, None, None]
    input_gate = jax.nn.sigmoid(preact[0:HID])
    forget_gate = jax.nn.sigmoid(preact[HID:2 * HID])
    output_gate = jax.nn.sigmoid(preact[2 * HID:3 * HID])
    candidate = jnp.tanh(preact[3 * HID:4 * HID])
    land_float = land_mask.astype(jnp.float32)[None]
    fire_float = fire_mask.astype(jnp.float32)
    cell_next = land_float * (forget_gate * cell_prev + input_gate * candidate)
    squashed = jnp.tanh(cell_next)
    hidden_next = (output_gate * squashed).astype(jnp.bfloat16)
    predicted = lax.optimization_barrier(jnp.sum(readout[:, None, None] * hidden_next.astype(jnp.float32), axis=0))
    total_grad = hidden_grad.astype(jnp.float32) + 2.0 * (fire_float * (predicted - target_field))[None] * readout[:, None, None]
    cell_grad = land_float * total_grad * output_gate * (1.0 - squashed * squashed)
    grad_cell = cell_grad * forget_gate
    pre_grad = jnp.concatenate([cell_grad * candidate * input_gate * (1.0 - input_gate), cell_grad * cell_prev * forget_gate * (1.0 - forget_gate), total_grad * squashed * output_gate * (1.0 - output_gate), cell_grad * input_gate * (1.0 - candidate * candidate)], axis=0)
    pre_low = pre_grad.astype(jnp.bfloat16)
    scaling = 1.0 / math.sqrt(NLAT * NLON)
    grad_bias = lax.optimization_barrier(jnp.sum(pre_grad, axis=(1, 2))) * scaling
    low_flat = pre_low.reshape(4 * HID, NLAT * NLON)
    kernel_grads = []
    for position in range(9):
        lat_start = position // 3
        lon_start = position % 3
        window = padded[:, lat_start:lat_start + NLAT, lon_start:lon_start + NLON].reshape(CIN + HID, NLAT * NLON)
        kernel_grads.append(jnp.dot(low_flat, window.T, preferred_element_type=jnp.float32))
    grad_kernel = jnp.stack(kernel_grads, axis=0) * scaling
    kernel_float = kernel_weights.astype(jnp.float32)

    def linear(values):
        return convolve(fold_pad(values), kernel_float)
    unused_out, pullback = jax.vjp(linear, stacked.astype(jnp.float32))
    field_grad = pullback(pre_low.astype(jnp.float32))[0]
    grad_inputs = field_grad[:CIN].astype(jnp.bfloat16)
    grad_hidden = field_grad[CIN:].astype(jnp.bfloat16)
    return (hidden_next, cell_next, grad_inputs, grad_hidden, grad_cell, grad_kernel, grad_bias)
```

```python
import functools
import math

import jax
import jax.numpy as jnp
from jax import lax
from jax.experimental import pallas as pl
from jax.experimental.pallas import tpu as pltpu
from jax.sharding import PartitionSpec as P

F32 = jnp.float32
BF16 = jnp.bfloat16
AXES = ("lat", "lon")
BIAS_ROWS = 16
VMEM = pl.BlockSpec(memory_space=pltpu.VMEM)


def sds(shape, dtype):
    return jax.ShapeDtypeStruct(shape, dtype)


def call(kernel, out_shape, scratch=(), flops=0, moved=0, transcendentals=0, vmem=24):
    def run(*args):
        return pl.pallas_call(
            kernel,
            out_shape=out_shape,
            in_specs=[VMEM] * len(args),
            out_specs=jax.tree.map(lambda _: VMEM, out_shape),
            scratch_shapes=list(scratch),
            cost_estimate=pl.CostEstimate(
                flops=flops, bytes_accessed=moved, transcendentals=transcendentals
            ),
            compiler_params=pltpu.CompilerParams(vmem_limit_bytes=vmem * 1024 * 1024),
        )(*args)

    return run


class Layout:
    def __init__(self, lat_count, lon_count, kernel_rows):
        self.lat, self.lon = lat_count, lon_count
        self.half = lon_count // 2
        self.groups = (2, (lat_count // 2) * 2, lon_count // 2)
        devices = lat_count * lon_count
        self.rows = -(-kernel_rows // (devices * 8)) * devices * 8
        sizes = []
        rows = self.rows
        for group in self.groups:
            rows //= group
            sizes.append(rows)
        self.chunks = tuple(sizes)

    def ranks(self):
        lat, lon = lax.axis_index("lat"), lax.axis_index("lon")
        return (lat % 2, (lat // 2) * 2 + lon % 2, lon // 2)

    def device(self, ranks):
        lat = (ranks[1] // 2) * 2 + ranks[0]
        lon = ranks[2] * 2 + ranks[1] % 2
        return lat * self.lon + lon

    def exchange(self, level, step):
        pairs = []
        for first in range(self.groups[0]):
            for second in range(self.groups[1]):
                for third in range(self.groups[2]):
                    here = [first, second, third]
                    there = list(here)
                    there[level] ^= step
                    pairs.append((self.device(here), self.device(there)))
        return pairs

    def source(self, lat, lon, forward, steps):
        north = (lon < self.half) == forward
        beside = lat - 1 if north else lat + 1
        if 0 <= beside < self.lat:
            return beside, (lon + steps) % self.lon
        return lat, (lon + steps + self.half) % self.lon

    def meridian(self, forward, steps):
        pairs = []
        for lat in range(self.lat):
            for lon in range(self.lon):
                from_lat, from_lon = self.source(lat, lon, forward, steps)
                pairs.append((from_lat * self.lon + from_lon, lat * self.lon + lon))
        return pairs

    def zonal(self, steps):
        return [
            (lat * self.lon + (lon + steps) % self.lon, lat * self.lon + lon)
            for lat in range(self.lat)
            for lon in range(self.lon)
        ]


def halo_exchange(place, row_forward, row_backward, columns):
    def send(value, pairs):
        return lax.ppermute(value, AXES, pairs)

    return (
        send(row_forward, place.meridian(True, 0)),
        send(row_backward, place.meridian(False, 0)),
        send(columns, place.zonal(-1)),
        send(columns, place.zonal(1)),
        send(columns, place.meridian(True, -1)),
        send(columns, place.meridian(True, 1)),
        send(columns, place.meridian(False, -1)),
        send(columns, place.meridian(False, 1)),
    )


def lanes(shape):
    return lax.broadcasted_iota(jnp.int32, shape, len(shape) - 1)


def edge_columns(row, index, count, columns):
    width = row.shape[1]
    lane = lanes(row.shape)
    first = pltpu.roll(row, index, 1) if index else row
    last = pltpu.roll(row, (count + index + 1) % width, 1)
    columns = jnp.where(lane == index, first, columns)
    return jnp.where(lane == count + index, last, columns)


def pick(flag, yes, no):
    return jnp.where(flag, yes, no)


def widened(place, row_count, rows, halo, emit):
    forward_row, backward_row, west, east, fw_west, fw_east, bw_west, bw_east = halo
    lat, lon = lax.axis_index("lat"), lax.axis_index("lon")
    near = lon < place.half
    northern = lat == 0
    southern = lat == place.lat - 1

    def load(ref):
        return ref[...].astype(F32)

    west_value, east_value = load(west), load(east)
    width = west_value.shape[1]
    lane = lanes(west_value.shape)
    forward_west, backward_west = load(fw_west), load(bw_west)
    forward_east, backward_east = load(fw_east), load(bw_east)

    def corner(value, is_last, offset, target):
        at_last = pltpu.roll(value, (target - offset - row_count + 1) % width, 1)
        at_first = pltpu.roll(value, (target - offset) % width, 1)
        return pick(is_last, at_last, at_first)

    for position in range(row_count + 2):
        index = position - 1
        if index == -1:
            row = pick(near, load(forward_row), load(backward_row))
            left = corner(
                pick(near, forward_west, backward_west), jnp.logical_not(northern), row_count, 0
            )
            right = corner(
                pick(near, forward_east, backward_east), jnp.logical_not(northern), 0, width - 1
            )
        elif index == row_count:
            row = pick(near, load(backward_row), load(forward_row))
            left = corner(pick(near, backward_west, forward_west), southern, row_count, 0)
            right = corner(pick(near, backward_east, forward_east), southern, 0, width - 1)
        else:
            row = rows(index)
            left = pltpu.roll(west_value, (-row_count - index) % width, 1)
            right = pltpu.roll(east_value, (width - 1 - index) % width, 1)
        emit(
            position,
            jnp.where(lane == 0, left, pltpu.roll(row, 1, 1)),
            row,
            jnp.where(lane == width - 1, right, pltpu.roll(row, width - 1, 1)),
        )


def pack_kernel(place, below, hidden, rows_out, forward_out, backward_out, columns_out, wide):
    channels, row_count, width = below.shape
    size = channels * row_count
    wide[0:size, :] = below[...].astype(F32).reshape(size, width)
    wide[size : 2 * size, :] = hidden[...].astype(F32).reshape(size, width)
    columns = jnp.zeros((2 * channels, width), F32)
    edges = []
    for index in range(row_count):
        row = jnp.concatenate(
            [
                wide[pl.ds(index, channels, stride=row_count), :],
                wide[pl.ds(size + index, channels, stride=row_count), :],
            ],
            axis=0,
        )
        rows_out[index] = row.astype(BF16)
        columns = edge_columns(row, index, row_count, columns)
        if index in (0, row_count - 1):
            edges.append(row)
    near = lax.axis_index("lon") < place.half
    forward_out[...] = pick(near, edges[-1], edges[0]).astype(BF16)
    backward_out[...] = pick(near, edges[0], edges[-1]).astype(BF16)
    columns_out[...] = columns.astype(BF16)


def encode(bias):
    high = bias.astype(BF16).astype(F32)
    return jnp.concatenate([high, bias - high], axis=0).astype(BF16)


def decode(block):
    value = block.astype(F32)
    return value[0:8] + value[8:16]


def gates_kernel(
    place,
    rows_in,
    forward_row,
    backward_row,
    west,
    east,
    fw_west,
    fw_east,
    bw_west,
    bw_east,
    cell_prev,
    weights,
    bias_wide,
    readout_wide,
    target,
    land,
    fire,
    hidden_grad,
    hidden_out,
    cell_out,
    grad_cell_out,
    pre_out,
    forward_out,
    backward_out,
    columns_out,
    send_out,
    keep_out,
    bias_out,
    shifted,
    hidden_wide,
    grad_wide,
    sums,
):
    row_count, channels, width = rows_in.shape
    gate_count = weights.shape[1]
    hid = gate_count // 4
    halo = (forward_row, backward_row, west, east, fw_west, fw_east, bw_west, bw_east)

    def emit(position, left, row, right):
        at = pl.ds(position * width, width)
        shifted[0:channels, at] = left.astype(BF16)
        shifted[channels : 2 * channels, at] = row.astype(BF16)
        shifted[2 * channels : 3 * channels, at] = right.astype(BF16)

    widened(place, row_count, lambda index: rows_in[index].astype(F32), halo, emit)
    grad_wide[...] = hidden_grad[...].astype(F32).reshape(hid * row_count, width)

    taps = [
        jnp.concatenate([weights[3 * a], weights[3 * a + 1], weights[3 * a + 2]], axis=1)
        for a in range(3)
    ]
    bias_total = jnp.zeros((gate_count, width), F32)
    columns = jnp.zeros((gate_count, width), F32)
    edges = []
    readout = readout_wide[...]
    pair = 2 if row_count % 2 == 0 else 1
    for base in range(0, row_count, pair):
        preact = jnp.zeros((gate_count, pair * width), F32)
        for a in range(3):
            preact += jnp.dot(
                taps[a],
                shifted[:, pl.ds((base + a) * width, pair * width)],
                preferred_element_type=F32,
            )
        for offset in range(pair):
            index = base + offset
            strided = pl.ds(index, hid, stride=row_count)
            part = preact[:, offset * width : (offset + 1) * width] + bias_wide[...]
            input_gate = 0.5 + 0.5 * jnp.tanh(0.5 * part[0:hid])
            forget_gate = 0.5 + 0.5 * jnp.tanh(0.5 * part[hid : 2 * hid])
            output_gate = 0.5 + 0.5 * jnp.tanh(0.5 * part[2 * hid : 3 * hid])
            candidate = jnp.tanh(part[3 * hid : 4 * hid])
            cell_before = cell_prev[strided, :]
            land_row = land[index : index + 1, :].astype(F32)
            fire_row = fire[index : index + 1, :].astype(F32)
            cell_next = land_row * (forget_gate * cell_before + input_gate * candidate)
            squashed = jnp.tanh(cell_next)
            hidden_next = (output_gate * squashed).astype(BF16).astype(F32)
            predicted = jnp.sum(readout * hidden_next, axis=0, keepdims=True)
            miss = 2.0 * (fire_row * (predicted - target[index : index + 1, :]))
            total_grad = grad_wide[strided, :] + miss * readout
            cell_grad = land_row * total_grad * output_gate * (1.0 - squashed * squashed)
            cell_out[strided, :] = cell_next
            hidden_wide[strided, :] = hidden_next
            grad_cell_out[strided, :] = cell_grad * forget_gate
            pre_grad = jnp.concatenate(
                [
                    cell_grad * candidate * input_gate * (1.0 - input_gate),
                    cell_grad * cell_before * forget_gate * (1.0 - forget_gate),
                    total_grad * squashed * output_gate * (1.0 - output_gate),
                    cell_grad * input_gate * (1.0 - candidate * candidate),
                ],
                axis=0,
            )
            bias_total += pre_grad
            columns = edge_columns(pre_grad, index, row_count, columns)
            pre_out[:, pl.ds(index * width, width)] = pre_grad.astype(BF16)
            if index in (0, row_count - 1):
                edges.append(pre_grad)
    hidden_out[...] = hidden_wide[...].reshape(hidden_out.shape).astype(BF16)
    near = lax.axis_index("lon") < place.half
    forward_out[...] = pick(near, edges[-1], edges[0]).astype(BF16)
    backward_out[...] = pick(near, edges[0], edges[-1]).astype(BF16)
    columns_out[...] = columns.astype(BF16)

    across = (((1,), (1,)), ((), ()))
    for a in range(3):
        product = lax.dot_general(
            pre_out[...],
            shifted[:, pl.ds(a * width, row_count * width)],
            across,
            preferred_element_type=F32,
        )
        for b in range(3):
            at = (3 * a + b) * gate_count
            sums[at : at + gate_count, :] = product[:, b * channels : (b + 1) * channels]
    used = 9 * gate_count
    if place.rows > used:
        sums[used:, :] = jnp.zeros((place.rows - used, channels), F32)

    ones = jnp.ones((8, width), BF16)
    high = bias_total.astype(BF16)
    low = (bias_total - high.astype(F32)).astype(BF16)
    flat = lax.dot_general(ones, high, across, preferred_element_type=F32)
    flat += lax.dot_general(ones, low, across, preferred_element_type=F32)
    odd = lax.broadcasted_iota(jnp.int32, (8, channels), 0) % 2 == 1
    bias_rows = jnp.where(odd, flat[:, channels : 2 * channels], flat[:, 0:channels])
    bias_out[...] = bias_rows

    rank = place.ranks()[0]
    chunk = place.chunks[0]
    send_out[0:BIAS_ROWS, :] = encode(bias_rows)
    send_out[BIAS_ROWS:, :] = sums[pl.ds(pl.multiple_of((1 - rank) * chunk, 8), chunk), :].astype(
        BF16
    )
    keep_out[...] = sums[pl.ds(pl.multiple_of(rank * chunk, 8), chunk), :]


def reduce_kernel(place, level, scaling, *refs):
    arrived = place.groups[level] - 1
    keep, bias = refs[0], refs[1]
    received = refs[2 : 2 + arrived]
    outs = refs[2 + arrived :]
    total = keep[...]
    bias_total = bias[...]
    for ref in received:
        total += ref[BIAS_ROWS:, :].astype(F32)
        bias_total += decode(ref[0:BIAS_ROWS, :])
    if level == len(place.groups) - 1:
        outs[0][0:BIAS_ROWS, :] = encode(bias_total * scaling)
        outs[0][BIAS_ROWS:, :] = (total * scaling).astype(BF16)
        return
    group, chunk = place.groups[level + 1], place.chunks[level + 1]
    sends = outs[: group - 1]
    keep_out, bias_out, scratch = outs[group - 1 :]
    scratch[...] = total
    rank = place.ranks()[level + 1]
    block = encode(bias_total)
    for step, send in enumerate(sends, 1):
        at = pl.ds(pl.multiple_of((rank ^ step) * chunk, 8), chunk)
        send[0:BIAS_ROWS, :] = block
        send[BIAS_ROWS:, :] = scratch[at, :].astype(BF16)
    keep_out[...] = scratch[pl.ds(pl.multiple_of(rank * chunk, 8), chunk), :]
    bias_out[...] = bias_total


def choose(rank, blocks):
    chosen = blocks[0]
    for step in range(1, len(blocks)):
        chosen = pick(rank == step, blocks[step], chosen)
    return chosen


def gather_kernel(place, level, *refs):
    blocks, out, scratch = refs[:-2], refs[-2], refs[-1]
    rank = place.ranks()[level]
    chunk = blocks[0].shape[0] - BIAS_ROWS
    bias = choose(rank, [block[0:BIAS_ROWS, :].astype(F32) for block in blocks])
    for step, block in enumerate(blocks):
        scratch[step * chunk : (step + 1) * chunk, :] = block[BIAS_ROWS:, :].astype(F32)
    out[0:BIAS_ROWS, :] = bias.astype(BF16)
    out[BIAS_ROWS:, :] = scratch[...].astype(BF16)


def place_kernel(place, *refs):
    blocks, out, bias_out, scratch = refs[:-3], refs[-3], refs[-2], refs[-1]
    ranks = place.ranks()
    middle, last = place.groups[1], place.groups[2]
    chunk = place.chunks[2]
    biases = []
    for first in range(2):
        part = blocks[first * middle : (first + 1) * middle]
        biases.append(
            choose(ranks[1], [block[0:BIAS_ROWS, :].astype(F32) for block in part])
        )
        for second in range(middle):
            scratch[...] = part[second][BIAS_ROWS:, :].astype(F32)
            base = (ranks[0] ^ first) * place.chunks[0] + (ranks[1] ^ second) * place.chunks[1]
            for third in range(last):
                at = pl.multiple_of(base + (ranks[2] ^ third) * chunk, 8)
                out[pl.ds(at, chunk), :] = scratch[third * chunk : (third + 1) * chunk, :]
    bias_out[...] = decode(choose(ranks[0], biases))


def field_kernel(
    place,
    pre,
    forward_row,
    backward_row,
    west,
    east,
    fw_west,
    fw_east,
    bw_west,
    bw_east,
    weights,
    inputs_out,
    hidden_out,
    shifted,
    turned,
    wide,
):
    gate_count, cells = pre.shape
    channels = weights.shape[2]
    hid, row_count, width = hidden_out.shape
    halo = (forward_row, backward_row, west, east, fw_west, fw_east, bw_west, bw_east)

    def emit(position, left, row, right):
        at = pl.ds(position * width, width)
        shifted[0:gate_count, at] = right.astype(BF16)
        shifted[gate_count : 2 * gate_count, at] = row.astype(BF16)
        shifted[2 * gate_count : 3 * gate_count, at] = left.astype(BF16)

    widened(
        place,
        row_count,
        lambda index: pre[:, pl.ds(index * width, width)].astype(F32),
        halo,
        emit,
    )
    for a in range(3):
        for b in range(3):
            turned[a, :, b * gate_count : (b + 1) * gate_count] = weights[3 * a + b].T
    northern = lax.axis_index("lat") == 0
    southern = lax.axis_index("lat") == place.lat - 1
    top = turned[jnp.where(northern, 0, 2)]
    bottom = turned[jnp.where(southern, 2, 0)]

    def product(matrix, position, count):
        return jnp.dot(
            matrix, shifted[:, pl.ds(position * width, count * width)], preferred_element_type=F32
        )

    pair = 2 if row_count % 2 == 0 else 1
    for base in range(0, row_count, pair):
        total = product(turned[1], base + 1, pair)
        if base == 0:
            above = product(top, 0, 1)
            if pair == 2:
                above = jnp.concatenate([above, product(turned[2], 1, 1)], axis=1)
        else:
            above = product(turned[2], base, pair)
        if base + pair == row_count:
            below = product(bottom, row_count + 1, 1)
            if pair == 2:
                below = jnp.concatenate([product(turned[0], row_count, 1), below], axis=1)
        else:
            below = product(turned[0], base + 2, pair)
        total = total + above + below
        for offset in range(pair):
            value = total[:, offset * width : (offset + 1) * width]
            index = base + offset
            wide[pl.ds(index, channels, stride=row_count), :] = value
    size = (channels - hid) * row_count
    inputs_out[...] = wide[0:size, :].reshape(inputs_out.shape).astype(BF16)
    hidden_out[...] = wide[size:, :].reshape(hidden_out.shape).astype(BF16)


def body(
    place,
    inputs_below,
    hidden_prev,
    cell_prev,
    kernel_weights,
    gate_bias,
    readout,
    target_field,
    land_mask,
    fire_mask,
    hidden_grad,
):
    hid, row_count, width = hidden_prev.shape
    gate_count, channels = kernel_weights.shape[1:]
    cells = row_count * width
    halo_cells = (row_count + 2) * width
    scaling = 1.0 / math.sqrt(cells * place.lat * place.lon)
    bind = functools.partial

    packed, forward, backward, columns = call(
        bind(pack_kernel, place),
        (
            sds((row_count, channels, width), BF16),
            sds((channels, width), BF16),
            sds((channels, width), BF16),
            sds((channels, width), BF16),
        ),
        [pltpu.VMEM((channels * row_count, width), F32)],
        moved=4 * channels * cells,
    )(inputs_below, hidden_prev)
    halo = halo_exchange(place, forward, backward, columns)

    chunks, groups = place.chunks, place.groups
    (
        hidden_next,
        cell_next,
        grad_cell,
        pre,
        pre_forward,
        pre_backward,
        pre_columns,
        send,
        keep,
        bias,
    ) = call(
        bind(gates_kernel, place),
        (
            sds((hid, row_count, width), BF16),
            sds((hid * row_count, width), F32),
            sds((hid * row_count, width), F32),
            sds((gate_count, cells), BF16),
            sds((gate_count, width), BF16),
            sds((gate_count, width), BF16),
            sds((gate_count, width), BF16),
            sds((BIAS_ROWS + chunks[0], channels), BF16),
            sds((chunks[0], channels), F32),
            sds((8, channels), F32),
        ),
        [
            pltpu.VMEM((3 * channels, halo_cells), BF16),
            pltpu.VMEM((hid * row_count, width), F32),
            pltpu.VMEM((hid * row_count, width), F32),
            pltpu.VMEM((place.rows, channels), F32),
        ],
        flops=4 * 9 * gate_count * channels * cells,
        moved=4_000_000,
        transcendentals=5 * hid * cells,
    )(
        packed,
        *halo,
        cell_prev.reshape(hid * row_count, width),
        kernel_weights,
        jnp.broadcast_to(gate_bias[:, None], (gate_count, width)),
        jnp.broadcast_to(readout[:, None], (hid, width)),
        target_field,
        land_mask,
        fire_mask,
        hidden_grad,
    )

    def swap(value, level, step):
        return lax.ppermute(value, AXES, place.exchange(level, step))

    sends = [send]
    pre_halo = None
    for level in range(3):
        received = [swap(block, level, step) for step, block in enumerate(sends, 1)]
        if level == 0:
            pre_halo = halo_exchange(place, pre_forward, pre_backward, pre_columns)
        if level < 2:
            outs = [sds((BIAS_ROWS + chunks[level + 1], channels), BF16)] * (groups[level + 1] - 1)
            outs += [sds((chunks[level + 1], channels), F32), sds((8, channels), F32)]
            scratch = [pltpu.VMEM((chunks[level], channels), F32)]
        else:
            outs = [sds((BIAS_ROWS + chunks[2], channels), BF16)]
            scratch = []
        results = call(
            bind(reduce_kernel, place, level, scaling),
            tuple(outs),
            scratch,
            moved=8 * chunks[level] * channels,
        )(keep, bias, *received)
        if level < 2:
            sends, keep, bias = results[:-2], results[-2], results[-1]
    block = results[0]

    grad_inputs, grad_hidden = call(
        bind(field_kernel, place),
        (sds((channels - hid, row_count, width), BF16), sds((hid, row_count, width), BF16)),
        [
            pltpu.VMEM((3 * gate_count, halo_cells), BF16),
            pltpu.VMEM((3, channels, 3 * gate_count), BF16),
            pltpu.VMEM((channels * row_count, width), F32),
        ],
        flops=2 * 9 * gate_count * channels * cells,
        moved=2_000_000,
    )(pre, *pre_halo, kernel_weights)

    blocks = [block] + [swap(block, 2, step) for step in range(1, groups[2])]
    joined = call(
        bind(gather_kernel, place, 2),
        sds((BIAS_ROWS + chunks[1], channels), BF16),
        [pltpu.VMEM((chunks[1], channels), F32)],
        moved=4 * chunks[1] * channels,
    )(*blocks)
    parts = [joined] + [swap(joined, 1, step) for step in range(1, groups[1])]
    parts += [swap(part, 0, 1) for part in parts]
    grad_kernel, grad_bias = call(
        bind(place_kernel, place),
        (sds((place.rows, channels), F32), sds((8, channels), F32)),
        [pltpu.VMEM((chunks[1], channels), F32)],
        moved=6 * place.rows * channels,
    )(*parts)
    shape = hidden_prev.shape
    return (
        hidden_next,
        cell_next.reshape(shape),
        grad_inputs,
        grad_hidden,
        grad_cell.reshape(shape),
        grad_kernel[: 9 * gate_count].reshape(kernel_weights.shape),
        grad_bias[: gate_count // channels].reshape(gate_count),
    )


def solution(mesh):
    field = P(None, "lat", "lon")
    flat = P("lat", "lon")

    def run(*args):
        place = Layout(
            mesh.shape["lat"], mesh.shape["lon"], args[3].shape[0] * args[3].shape[1]
        )
        return jax.shard_map(
            functools.partial(body, place),
            mesh=mesh,
            in_specs=(field, field, field, P(), P(), P(), flat, flat, flat, field),
            out_specs=(field, field, field, field, field, P(), P()),
            check_vma=False,
        )(*args)

    return run
```

```python
import functools
import math

import jax
import jax.numpy as jnp
from jax import lax
from jax.experimental import pallas as pl
from jax.experimental.pallas import tpu as pltpu
from jax.sharding import Mesh, PartitionSpec as P

F32 = jnp.float32
BF16 = jnp.bfloat16
AXES = ("band", "core", "lon")
RING = ("band", "lon")
BIAS_ROWS = 16
VMEM = pl.BlockSpec(memory_space=pltpu.VMEM)


def sds(shape, dtype):
    return jax.ShapeDtypeStruct(shape, dtype)


def call(kernel, out_shape, scratch=(), flops=0, moved=0, transcendentals=0, vmem=24):
    def run(*args):
        return pl.pallas_call(
            kernel,
            out_shape=out_shape,
            in_specs=[VMEM] * len(args),
            out_specs=jax.tree.map(lambda _: VMEM, out_shape),
            scratch_shapes=list(scratch),
            cost_estimate=pl.CostEstimate(
                flops=flops, bytes_accessed=moved, transcendentals=transcendentals
            ),
            compiler_params=pltpu.CompilerParams(vmem_limit_bytes=vmem * 1024 * 1024),
        )(*args)

    return run


class Layout:
    def __init__(self, lat_count, lon_count, kernel_rows):
        self.lat, self.lon = lat_count, lon_count
        self.half = lon_count // 2
        self.groups = (2, (lat_count // 2) * lon_count)
        devices = lat_count * lon_count
        self.rows = -(-kernel_rows // (devices * 8)) * devices * 8
        self.chunks = (self.rows // 2, self.rows // devices)

    def position(self):
        return 2 * lax.axis_index("band") + lax.axis_index("core"), lax.axis_index("lon")

    def swapped(self):
        return [
            (lat * self.lon + lon, (lat ^ 1) * self.lon + lon)
            for lat in range(self.lat)
            for lon in range(self.lon)
        ]

    def source(self, lat, lon, forward, steps):
        north = (lon < self.half) == forward
        beside = lat - 1 if north else lat + 1
        if 0 <= beside < self.lat:
            return beside, (lon + steps) % self.lon
        return lat, (lon + steps + self.half) % self.lon

    def meridian(self, forward, steps):
        pairs = []
        for lat in range(self.lat):
            for lon in range(self.lon):
                from_lat, from_lon = self.source(lat, lon, forward, steps)
                pairs.append((from_lat * self.lon + from_lon, lat * self.lon + lon))
        return pairs

    def zonal(self, steps):
        return [
            (lat * self.lon + (lon + steps) % self.lon, lat * self.lon + lon)
            for lat in range(self.lat)
            for lon in range(self.lon)
        ]


def halo_exchange(place, row_forward, row_backward, columns):
    def send(value, pairs):
        return lax.ppermute(value, AXES, pairs)

    return (
        send(row_forward, place.meridian(True, 0)),
        send(row_backward, place.meridian(False, 0)),
        send(columns, place.zonal(-1)),
        send(columns, place.zonal(1)),
        send(columns, place.meridian(True, -1)),
        send(columns, place.meridian(True, 1)),
        send(columns, place.meridian(False, -1)),
        send(columns, place.meridian(False, 1)),
    )


def lanes(shape):
    return lax.broadcasted_iota(jnp.int32, shape, len(shape) - 1)


def edge_columns(row, index, count, columns):
    width = row.shape[1]
    lane = lanes(row.shape)
    first = pltpu.roll(row, index, 1) if index else row
    last = pltpu.roll(row, (count + index + 1) % width, 1)
    columns = jnp.where(lane == index, first, columns)
    return jnp.where(lane == count + index, last, columns)


def pick(flag, yes, no):
    return jnp.where(flag, yes, no)


def widened(place, row_count, rows, halo, emit):
    forward_row, backward_row, west, east, fw_west, fw_east, bw_west, bw_east = halo
    lat, lon = place.position()
    near = lon < place.half
    northern = lat == 0
    southern = lat == place.lat - 1

    def load(ref):
        return ref[...].astype(F32)

    west_value, east_value = load(west), load(east)
    width = west_value.shape[1]
    lane = lanes(west_value.shape)
    forward_west, backward_west = load(fw_west), load(bw_west)
    forward_east, backward_east = load(fw_east), load(bw_east)

    def corner(value, is_last, offset, target):
        at_last = pltpu.roll(value, (target - offset - row_count + 1) % width, 1)
        at_first = pltpu.roll(value, (target - offset) % width, 1)
        return pick(is_last, at_last, at_first)

    for position in range(row_count + 2):
        index = position - 1
        if index == -1:
            row = pick(near, load(forward_row), load(backward_row))
            left = corner(
                pick(near, forward_west, backward_west), jnp.logical_not(northern), row_count, 0
            )
            right = corner(
                pick(near, forward_east, backward_east), jnp.logical_not(northern), 0, width - 1
            )
        elif index == row_count:
            row = pick(near, load(backward_row), load(forward_row))
            left = corner(pick(near, backward_west, forward_west), southern, row_count, 0)
            right = corner(pick(near, backward_east, forward_east), southern, 0, width - 1)
        else:
            row = rows(index)
            left = pltpu.roll(west_value, (-row_count - index) % width, 1)
            right = pltpu.roll(east_value, (width - 1 - index) % width, 1)
        emit(
            position,
            jnp.where(lane == 0, left, pltpu.roll(row, 1, 1)),
            row,
            jnp.where(lane == width - 1, right, pltpu.roll(row, width - 1, 1)),
        )


def pack_kernel(place, below, hidden, rows_out, forward_out, backward_out, columns_out, wide):
    channels, row_count, width = below.shape
    size = channels * row_count
    wide[0:size, :] = below[...].astype(F32).reshape(size, width)
    wide[size : 2 * size, :] = hidden[...].astype(F32).reshape(size, width)
    columns = jnp.zeros((2 * channels, width), F32)
    edges = []
    for index in range(row_count):
        row = jnp.concatenate(
            [
                wide[pl.ds(index, channels, stride=row_count), :],
                wide[pl.ds(size + index, channels, stride=row_count), :],
            ],
            axis=0,
        )
        rows_out[index] = row.astype(BF16)
        columns = edge_columns(row, index, row_count, columns)
        if index in (0, row_count - 1):
            edges.append(row)
    near = lax.axis_index("lon") < place.half
    forward_out[...] = pick(near, edges[-1], edges[0]).astype(BF16)
    backward_out[...] = pick(near, edges[0], edges[-1]).astype(BF16)
    columns_out[...] = columns.astype(BF16)


def encode(bias):
    high = bias.astype(BF16).astype(F32)
    return jnp.concatenate([high, bias - high], axis=0).astype(BF16)


def decode(block):
    value = block.astype(F32)
    return value[0:8] + value[8:16]


def gates_kernel(
    place,
    rows_in,
    forward_row,
    backward_row,
    west,
    east,
    fw_west,
    fw_east,
    bw_west,
    bw_east,
    cell_prev,
    weights,
    bias_wide,
    readout_wide,
    target,
    land,
    fire,
    hidden_grad,
    hidden_out,
    cell_out,
    grad_cell_out,
    pre_out,
    forward_out,
    backward_out,
    columns_out,
    send_out,
    keep_out,
    bias_out,
    shifted,
    hidden_wide,
    grad_wide,
    sums,
):
    row_count, channels, width = rows_in.shape
    gate_count = weights.shape[1]
    hid = gate_count // 4
    halo = (forward_row, backward_row, west, east, fw_west, fw_east, bw_west, bw_east)

    def emit(position, left, row, right):
        at = pl.ds(position * width, width)
        shifted[0:channels, at] = left.astype(BF16)
        shifted[channels : 2 * channels, at] = row.astype(BF16)
        shifted[2 * channels : 3 * channels, at] = right.astype(BF16)

    widened(place, row_count, lambda index: rows_in[index].astype(F32), halo, emit)
    grad_wide[...] = hidden_grad[...].astype(F32).reshape(hid * row_count, width)

    taps = [
        jnp.concatenate([weights[3 * a], weights[3 * a + 1], weights[3 * a + 2]], axis=1)
        for a in range(3)
    ]
    bias_total = jnp.zeros((gate_count, width), F32)
    columns = jnp.zeros((gate_count, width), F32)
    edges = []
    readout = readout_wide[...]
    pair = 2 if row_count % 2 == 0 else 1
    for base in range(0, row_count, pair):
        preact = jnp.zeros((gate_count, pair * width), F32)
        for a in range(3):
            preact += jnp.dot(
                taps[a],
                shifted[:, pl.ds((base + a) * width, pair * width)],
                preferred_element_type=F32,
            )
        for offset in range(pair):
            index = base + offset
            strided = pl.ds(index, hid, stride=row_count)
            part = preact[:, offset * width : (offset + 1) * width] + bias_wide[...]
            input_gate = 0.5 + 0.5 * jnp.tanh(0.5 * part[0:hid])
            forget_gate = 0.5 + 0.5 * jnp.tanh(0.5 * part[hid : 2 * hid])
            output_gate = 0.5 + 0.5 * jnp.tanh(0.5 * part[2 * hid : 3 * hid])
            candidate = jnp.tanh(part[3 * hid : 4 * hid])
            cell_before = cell_prev[strided, :]
            land_row = land[index : index + 1, :].astype(F32)
            fire_row = fire[index : index + 1, :].astype(F32)
            cell_next = land_row * (forget_gate * cell_before + input_gate * candidate)
            squashed = jnp.tanh(cell_next)
            hidden_next = (output_gate * squashed).astype(BF16).astype(F32)
            predicted = jnp.sum(readout * hidden_next, axis=0, keepdims=True)
            miss = 2.0 * (fire_row * (predicted - target[index : index + 1, :]))
            total_grad = grad_wide[strided, :] + miss * readout
            cell_grad = land_row * total_grad * output_gate * (1.0 - squashed * squashed)
            cell_out[strided, :] = cell_next
            hidden_wide[strided, :] = hidden_next
            grad_cell_out[strided, :] = cell_grad * forget_gate
            pre_grad = jnp.concatenate(
                [
                    cell_grad * candidate * input_gate * (1.0 - input_gate),
                    cell_grad * cell_before * forget_gate * (1.0 - forget_gate),
                    total_grad * squashed * output_gate * (1.0 - output_gate),
                    cell_grad * input_gate * (1.0 - candidate * candidate),
                ],
                axis=0,
            )
            bias_total += pre_grad
            columns = edge_columns(pre_grad, index, row_count, columns)
            pre_out[:, pl.ds(index * width, width)] = pre_grad.astype(BF16)
            if index in (0, row_count - 1):
                edges.append(pre_grad)
    hidden_out[...] = hidden_wide[...].reshape(hidden_out.shape).astype(BF16)
    near = lax.axis_index("lon") < place.half
    forward_out[...] = pick(near, edges[-1], edges[0]).astype(BF16)
    backward_out[...] = pick(near, edges[0], edges[-1]).astype(BF16)
    columns_out[...] = columns.astype(BF16)

    across = (((1,), (1,)), ((), ()))
    for a in range(3):
        product = lax.dot_general(
            pre_out[...],
            shifted[:, pl.ds(a * width, row_count * width)],
            across,
            preferred_element_type=F32,
        )
        for b in range(3):
            at = (3 * a + b) * gate_count
            sums[at : at + gate_count, :] = product[:, b * channels : (b + 1) * channels]
    used = 9 * gate_count
    if place.rows > used:
        sums[used:, :] = jnp.zeros((place.rows - used, channels), F32)

    ones = jnp.ones((8, width), BF16)
    high = bias_total.astype(BF16)
    low = (bias_total - high.astype(F32)).astype(BF16)
    flat = lax.dot_general(ones, high, across, preferred_element_type=F32)
    flat += lax.dot_general(ones, low, across, preferred_element_type=F32)
    odd = lax.broadcasted_iota(jnp.int32, (8, channels), 0) % 2 == 1
    bias_rows = jnp.where(odd, flat[:, channels : 2 * channels], flat[:, 0:channels])
    bias_out[...] = bias_rows

    rank = lax.axis_index("core")
    chunk = place.chunks[0]
    send_out[0:BIAS_ROWS, :] = encode(bias_rows)
    send_out[BIAS_ROWS:, :] = sums[pl.ds(pl.multiple_of((1 - rank) * chunk, 8), chunk), :].astype(
        BF16
    )
    keep_out[...] = sums[pl.ds(pl.multiple_of(rank * chunk, 8), chunk), :]


def pair_kernel(place, keep, bias, received, send_out, scratch):
    count, chunk = place.groups[1], place.chunks[1]
    scratch[...] = keep[...] + received[BIAS_ROWS:, :].astype(F32)
    block = encode(bias[...] + decode(received[0:BIAS_ROWS, :]))
    for index in range(count):
        send_out[index, 0:BIAS_ROWS, :] = block
        send_out[index, BIAS_ROWS:, :] = scratch[index * chunk : (index + 1) * chunk, :].astype(
            BF16
        )


def total_kernel(place, scaling, received, send_out):
    count = place.groups[1]
    total = received[0, BIAS_ROWS:, :].astype(F32)
    bias = decode(received[0, 0:BIAS_ROWS, :])
    for index in range(1, count):
        total += received[index, BIAS_ROWS:, :].astype(F32)
        bias += decode(received[index, 0:BIAS_ROWS, :])
    block = encode(bias * scaling)
    result = (total * scaling).astype(BF16)
    for index in range(count):
        send_out[index, 0:BIAS_ROWS, :] = block
        send_out[index, BIAS_ROWS:, :] = result


def place_kernel(place, own, other, out, bias_out):
    core = lax.axis_index("core")
    chunk = place.chunks[1]
    for first, blocks in enumerate((own, other)):
        base = (core ^ first) * place.chunks[0]
        for index in range(place.groups[1]):
            at = pl.multiple_of(base + index * chunk, 8)
            out[pl.ds(at, chunk), :] = blocks[index, BIAS_ROWS:, :].astype(F32)
    bias_out[...] = pick(
        core == 0, decode(own[0, 0:BIAS_ROWS, :]), decode(other[0, 0:BIAS_ROWS, :])
    )


def field_kernel(
    place,
    pre,
    forward_row,
    backward_row,
    west,
    east,
    fw_west,
    fw_east,
    bw_west,
    bw_east,
    weights,
    inputs_out,
    hidden_out,
    shifted,
    turned,
    wide,
):
    gate_count, cells = pre.shape
    channels = weights.shape[2]
    hid, row_count, width = hidden_out.shape
    halo = (forward_row, backward_row, west, east, fw_west, fw_east, bw_west, bw_east)

    def emit(position, left, row, right):
        at = pl.ds(position * width, width)
        shifted[0:gate_count, at] = right.astype(BF16)
        shifted[gate_count : 2 * gate_count, at] = row.astype(BF16)
        shifted[2 * gate_count : 3 * gate_count, at] = left.astype(BF16)

    widened(
        place,
        row_count,
        lambda index: pre[:, pl.ds(index * width, width)].astype(F32),
        halo,
        emit,
    )
    for a in range(3):
        for b in range(3):
            turned[a, :, b * gate_count : (b + 1) * gate_count] = weights[3 * a + b].T
    northern = place.position()[0] == 0
    southern = place.position()[0] == place.lat - 1
    top = turned[jnp.where(northern, 0, 2)]
    bottom = turned[jnp.where(southern, 2, 0)]

    def product(matrix, position, count):
        return jnp.dot(
            matrix, shifted[:, pl.ds(position * width, count * width)], preferred_element_type=F32
        )

    pair = 2 if row_count % 2 == 0 else 1
    for base in range(0, row_count, pair):
        total = product(turned[1], base + 1, pair)
        if base == 0:
            above = product(top, 0, 1)
            if pair == 2:
                above = jnp.concatenate([above, product(turned[2], 1, 1)], axis=1)
        else:
            above = product(turned[2], base, pair)
        if base + pair == row_count:
            below = product(bottom, row_count + 1, 1)
            if pair == 2:
                below = jnp.concatenate([product(turned[0], row_count, 1), below], axis=1)
        else:
            below = product(turned[0], base + 2, pair)
        total = total + above + below
        for offset in range(pair):
            value = total[:, offset * width : (offset + 1) * width]
            index = base + offset
            wide[pl.ds(index, channels, stride=row_count), :] = value
    size = (channels - hid) * row_count
    inputs_out[...] = wide[0:size, :].reshape(inputs_out.shape).astype(BF16)
    hidden_out[...] = wide[size:, :].reshape(hidden_out.shape).astype(BF16)


def body(
    place,
    inputs_below,
    hidden_prev,
    cell_prev,
    kernel_weights,
    gate_bias,
    readout,
    target_field,
    land_mask,
    fire_mask,
    hidden_grad,
):
    hid, row_count, width = hidden_prev.shape
    gate_count, channels = kernel_weights.shape[1:]
    cells = row_count * width
    halo_cells = (row_count + 2) * width
    scaling = 1.0 / math.sqrt(cells * place.lat * place.lon)
    bind = functools.partial

    packed, forward, backward, columns = call(
        bind(pack_kernel, place),
        (
            sds((row_count, channels, width), BF16),
            sds((channels, width), BF16),
            sds((channels, width), BF16),
            sds((channels, width), BF16),
        ),
        [pltpu.VMEM((channels * row_count, width), F32)],
        moved=4 * channels * cells,
    )(inputs_below, hidden_prev)
    halo = halo_exchange(place, forward, backward, columns)

    chunks = place.chunks
    (
        hidden_next,
        cell_next,
        grad_cell,
        pre,
        pre_forward,
        pre_backward,
        pre_columns,
        send,
        keep,
        bias,
    ) = call(
        bind(gates_kernel, place),
        (
            sds((hid, row_count, width), BF16),
            sds((hid * row_count, width), F32),
            sds((hid * row_count, width), F32),
            sds((gate_count, cells), BF16),
            sds((gate_count, width), BF16),
            sds((gate_count, width), BF16),
            sds((gate_count, width), BF16),
            sds((BIAS_ROWS + chunks[0], channels), BF16),
            sds((chunks[0], channels), F32),
            sds((8, channels), F32),
        ),
        [
            pltpu.VMEM((3 * channels, halo_cells), BF16),
            pltpu.VMEM((hid * row_count, width), F32),
            pltpu.VMEM((hid * row_count, width), F32),
            pltpu.VMEM((place.rows, channels), F32),
        ],
        flops=4 * 9 * gate_count * channels * cells,
        moved=4_000_000,
        transcendentals=5 * hid * cells,
    )(
        packed,
        *halo,
        cell_prev.reshape(hid * row_count, width),
        kernel_weights,
        jnp.broadcast_to(gate_bias[:, None], (gate_count, width)),
        jnp.broadcast_to(readout[:, None], (hid, width)),
        target_field,
        land_mask,
        fire_mask,
        hidden_grad,
    )

    def swap(value):
        return lax.ppermute(value, AXES, place.swapped())

    def scatter(value):
        return lax.all_to_all(value, RING, 0, 0, tiled=True)

    blocks = sds((place.groups[1], BIAS_ROWS + chunks[1], channels), BF16)
    received = swap(send)
    pre_halo = halo_exchange(place, pre_forward, pre_backward, pre_columns)
    parts = call(
        bind(pair_kernel, place),
        blocks,
        [pltpu.VMEM((chunks[0], channels), F32)],
        moved=8 * chunks[0] * channels,
    )(keep, bias, received)
    totals = call(bind(total_kernel, place, scaling), blocks, moved=4 * chunks[0] * channels)(
        scatter(parts)
    )
    gathered = scatter(totals)

    grad_inputs, grad_hidden = call(
        bind(field_kernel, place),
        (sds((channels - hid, row_count, width), BF16), sds((hid, row_count, width), BF16)),
        [
            pltpu.VMEM((3 * gate_count, halo_cells), BF16),
            pltpu.VMEM((3, channels, 3 * gate_count), BF16),
            pltpu.VMEM((channels * row_count, width), F32),
        ],
        flops=2 * 9 * gate_count * channels * cells,
        moved=2_000_000,
    )(pre, *pre_halo, kernel_weights)

    grad_kernel, grad_bias = call(
        bind(place_kernel, place),
        (sds((place.rows, channels), F32), sds((8, channels), F32)),
        moved=6 * place.rows * channels,
    )(gathered, swap(gathered))
    shape = hidden_prev.shape
    return (
        hidden_next,
        cell_next.reshape(shape),
        grad_inputs,
        grad_hidden,
        grad_cell.reshape(shape),
        grad_kernel[: 9 * gate_count].reshape(kernel_weights.shape),
        grad_bias[: gate_count // channels].reshape(gate_count),
    )


def solution(mesh):
    lat_count, lon_count = mesh.shape["lat"], mesh.shape["lon"]
    split = Mesh(mesh.devices.reshape(lat_count // 2, 2, lon_count), AXES)
    field = P(None, ("band", "core"), "lon")
    flat = P(("band", "core"), "lon")

    def run(*args):
        place = Layout(lat_count, lon_count, args[3].shape[0] * args[3].shape[1])
        return jax.shard_map(
            functools.partial(body, place),
            mesh=split,
            in_specs=(field, field, field, P(), P(), P(), flat, flat, flat, field),
            out_specs=(field, field, field, field, field, P(), P()),
            check_vma=False,
        )(*args)

    return run
```

```python
import functools
import math

import jax
import jax.numpy as jnp
from jax import lax
from jax.experimental import pallas as pl
from jax.experimental.pallas import tpu as pltpu
from jax.sharding import Mesh, PartitionSpec as P

F32 = jnp.float32
BF16 = jnp.bfloat16
AXES = ("band", "core", "lon")
BIAS_ROWS = 16
LAST = 16
VMEM = pl.BlockSpec(memory_space=pltpu.VMEM)
HBM = pl.BlockSpec(memory_space=pltpu.HBM)
ACROSS = (((1,), (1,)), ((), ()))


def sds(shape, dtype):
    return jax.ShapeDtypeStruct(shape, dtype)


def call(kernel, out_shape, scratch=(), remote=0, flops=0, moved=0, transcendentals=0):
    def run(*args):
        near = len(args) - remote
        far = [pltpu.with_memory_space_constraint(arg, pltpu.HBM) for arg in args[near:]]
        return pl.pallas_call(
            kernel,
            out_shape=out_shape,
            in_specs=[VMEM] * near + [HBM] * remote,
            out_specs=jax.tree.map(lambda _: VMEM, out_shape),
            scratch_shapes=list(scratch),
            cost_estimate=pl.CostEstimate(
                flops=flops, bytes_accessed=moved, transcendentals=transcendentals
            ),
            compiler_params=pltpu.CompilerParams(vmem_limit_bytes=24 * 1024 * 1024),
        )(*args[:near], *far)

    return run


class Layout:
    def __init__(self, lat_count, lon_count, kernel_rows):
        self.lat, self.lon = lat_count, lon_count
        self.half = lon_count // 2
        devices = lat_count * lon_count
        self.rows = -(-kernel_rows // (devices * 8)) * devices * 8
        self.bits = [("lat", 1 << k) for k in range(lat_count.bit_length() - 1)]
        self.bits += [("lon", 1 << k) for k in range(lon_count.bit_length() - 1)]

    def position(self):
        return 2 * lax.axis_index("band") + lax.axis_index("core"), lax.axis_index("lon")

    def rank(self, phase):
        axis, bit = self.bits[phase]
        lat, lon = self.position()
        return ((lat if axis == "lat" else lon) // bit) % 2

    def pairs(self, partner):
        result = []
        for lat in range(self.lat):
            for lon in range(self.lon):
                there = partner(lat, lon)
                result.append((lat * self.lon + lon, there[0] * self.lon + there[1]))
        return result

    def phase_pairs(self, phase):
        axis, bit = self.bits[phase]
        if axis == "lat":
            return self.pairs(lambda lat, lon: (lat ^ bit, lon))
        return self.pairs(lambda lat, lon: (lat, lon ^ bit))

    def inner_rows(self, lat, lon):
        return lat ^ 1, lon

    def outer_rows(self, lat, lon):
        there = lat + 1 if lat % 2 else lat - 1
        if 0 <= there < self.lat:
            return there, lon
        return lat, (lon + self.half) % self.lon

    def inner_columns(self, lat, lon):
        return lat, lon ^ 1

    def outer_columns(self, lat, lon):
        return lat, (lon + (1 if lon % 2 else -1)) % self.lon


def permuted(value, pairs):
    return lax.ppermute(value, AXES, pairs)


def lanes(shape):
    return lax.broadcasted_iota(jnp.int32, shape, len(shape) - 1)


def rolled(value, shift):
    shift %= value.shape[1]
    return pltpu.roll(value, shift, 1) if shift else value


def edge_columns(row, position, columns):
    lane = lanes(row.shape)
    columns = jnp.where(lane == position, rolled(row, position), columns)
    return jnp.where(lane == LAST + position, rolled(row, LAST + position + 1), columns)


def pick(flag, yes, no):
    return jnp.where(flag, yes, no)


def is_odd(axis):
    return lax.axis_index(axis) % 2 == 1


def row_sends(first, last, inner_out, outer_out):
    odd = is_odd("core")
    inner_out[...] = pick(odd, first, last).astype(BF16)
    outer_out[...] = pick(odd, last, first).astype(BF16)


def row_halo(inner, outer):
    odd = is_odd("core")
    inner, outer = inner[...].astype(F32), outer[...].astype(F32)
    return pick(odd, inner, outer), pick(odd, outer, inner)


def column_halo(inner, outer):
    odd = is_odd("lon")
    inner, outer = inner[...].astype(F32), outer[...].astype(F32)
    return pick(odd, inner, outer), pick(odd, outer, inner)


def widened(row_count, rows, row_blocks, column_blocks, emit):
    north, south = row_halo(*row_blocks)
    west, east = column_halo(*column_blocks)
    width = west.shape[1]
    lane = lanes(west.shape)
    for position in range(row_count + 2):
        if position == 0:
            row = north
        elif position == row_count + 1:
            row = south
        else:
            row = rows(position - 1)
        left = rolled(west, -LAST - position)
        right = rolled(east, width - 1 - position)
        emit(
            position,
            jnp.where(lane == 0, left, rolled(row, 1)),
            row,
            jnp.where(lane == width - 1, right, rolled(row, -1)),
        )


def pack_kernel(below, hidden, inner_out, outer_out, wide_out, below_here, hidden_here, arrived):
    first = pltpu.make_async_copy(below, below_here, arrived.at[0])
    second = pltpu.make_async_copy(hidden, hidden_here, arrived.at[1])
    first.start()
    second.start()
    channels, row_count, width = below.shape
    size = channels * row_count
    first.wait()
    wide_out[0:size, :] = below_here[...].astype(F32).reshape(size, width)
    second.wait()
    wide_out[size : 2 * size, :] = hidden_here[...].astype(F32).reshape(size, width)
    edges = [
        wide_out[pl.ds(index, 2 * channels, stride=row_count), :] for index in (0, row_count - 1)
    ]
    row_sends(edges[0], edges[1], inner_out, outer_out)


def down_rows(values, width):
    count = values.shape[0]
    return jnp.broadcast_to(values[None, :], (width, count)).T


def prepare_kernel(
    wide,
    cell_hbm,
    weights_hbm,
    hidden_grad_hbm,
    target_hbm,
    land_hbm,
    fire_hbm,
    gate_bias_hbm,
    readout_hbm,
    rows_out,
    columns_out,
    cell_out,
    weights_out,
    hidden_grad_out,
    target_out,
    land_out,
    fire_out,
    bias_wide_out,
    readout_wide_out,
    hidden_grad_here,
    gate_bias_here,
    readout_here,
    arrived,
):
    copies = [
        pltpu.make_async_copy(source, target, arrived.at[index])
        for index, (source, target) in enumerate(
            (
                (cell_hbm, cell_out),
                (weights_hbm, weights_out),
                (hidden_grad_hbm, hidden_grad_here),
                (target_hbm, target_out),
                (land_hbm, land_out),
                (fire_hbm, fire_out),
                (gate_bias_hbm, gate_bias_here),
                (readout_hbm, readout_here),
            )
        )
    ]
    for copy in copies:
        copy.start()
    row_count, channels, width = rows_out.shape
    columns = jnp.zeros((channels, width), F32)
    for index in range(row_count):
        row = wide[pl.ds(index, channels, stride=row_count), :]
        rows_out[index] = row.astype(BF16)
        columns = edge_columns(row, index + 1, columns)
    columns_out[...] = columns
    for copy in copies:
        copy.wait()
    hidden_grad_out[...] = hidden_grad_here[...].astype(F32).reshape(hidden_grad_out.shape)
    bias_wide_out[...] = down_rows(gate_bias_here[...], width)
    readout_wide_out[...] = down_rows(readout_here[...], width)


def columns_kernel(row_count, columns, inner, outer, out):
    north, south = row_halo(inner, outer)
    value = edge_columns(north, 0, columns[...].astype(F32))
    out[...] = edge_columns(south, row_count + 1, value).astype(BF16)


def encode(bias):
    high = bias.astype(BF16).astype(F32)
    return jnp.concatenate([high, bias - high], axis=0)


def decode(block):
    return block[0:8] + block[8:16]


def split_sum(place, phase, bias, sums, rows, send_out, keep_out):
    half = rows // 2
    rank = place.rank(phase)
    send_out[0:BIAS_ROWS, :] = encode(bias).astype(BF16)
    away = pl.ds(pl.multiple_of((1 - rank) * half, 8), half)
    send_out[BIAS_ROWS:, :] = sums[away, :].astype(BF16)
    keep_out[...] = sums[pl.ds(pl.multiple_of(rank * half, 8), half), :]


def gates_kernel(
    place,
    rows_in,
    inner_row,
    outer_row,
    inner_column,
    outer_column,
    cell_prev,
    weights,
    hidden_grad,
    target,
    land,
    fire,
    bias_wide,
    readout_wide,
    hidden_out,
    cell_out,
    grad_cell_out,
    pre_out,
    inner_out,
    outer_out,
    columns_out,
    send_out,
    keep_out,
    bias_out,
    shifted,
    hidden_wide,
    sums,
):
    row_count, channels, width = rows_in.shape
    gate_count = weights.shape[1]
    hid = gate_count // 4

    def emit(position, left, row, right):
        at = pl.ds(position * width, width)
        shifted[0:channels, at] = left.astype(BF16)
        shifted[channels : 2 * channels, at] = row.astype(BF16)
        shifted[2 * channels : 3 * channels, at] = right.astype(BF16)

    widened(
        row_count,
        lambda index: rows_in[index].astype(F32),
        (inner_row, outer_row),
        (inner_column, outer_column),
        emit,
    )

    taps = [
        jnp.concatenate([weights[3 * a], weights[3 * a + 1], weights[3 * a + 2]], axis=1)
        for a in range(3)
    ]
    bias_total = jnp.zeros((gate_count, width), F32)
    columns = jnp.zeros((gate_count, width), F32)
    edges = []
    readout = readout_wide[...]
    pair = 2 if row_count % 2 == 0 else 1
    for base in range(0, row_count, pair):
        preact = jnp.zeros((gate_count, pair * width), F32)
        for a in range(3):
            preact += jnp.dot(
                taps[a],
                shifted[:, pl.ds((base + a) * width, pair * width)],
                preferred_element_type=F32,
            )
        for offset in range(pair):
            index = base + offset
            strided = pl.ds(index, hid, stride=row_count)
            part = preact[:, offset * width : (offset + 1) * width] + bias_wide[...]
            input_gate = 0.5 + 0.5 * jnp.tanh(0.5 * part[0:hid])
            forget_gate = 0.5 + 0.5 * jnp.tanh(0.5 * part[hid : 2 * hid])
            output_gate = 0.5 + 0.5 * jnp.tanh(0.5 * part[2 * hid : 3 * hid])
            candidate = jnp.tanh(part[3 * hid : 4 * hid])
            cell_before = cell_prev[strided, :]
            land_row = land[index : index + 1, :].astype(F32)
            fire_row = fire[index : index + 1, :].astype(F32)
            cell_next = land_row * (forget_gate * cell_before + input_gate * candidate)
            squashed = jnp.tanh(cell_next)
            hidden_next = (output_gate * squashed).astype(BF16).astype(F32)
            predicted = jnp.sum(readout * hidden_next, axis=0, keepdims=True)
            miss = 2.0 * (fire_row * (predicted - target[index : index + 1, :]))
            total_grad = hidden_grad[strided, :] + miss * readout
            cell_grad = land_row * total_grad * output_gate * (1.0 - squashed * squashed)
            cell_out[strided, :] = cell_next
            hidden_wide[strided, :] = hidden_next
            grad_cell_out[strided, :] = cell_grad * forget_gate
            pre_grad = jnp.concatenate(
                [
                    cell_grad * candidate * input_gate * (1.0 - input_gate),
                    cell_grad * cell_before * forget_gate * (1.0 - forget_gate),
                    total_grad * squashed * output_gate * (1.0 - output_gate),
                    cell_grad * input_gate * (1.0 - candidate * candidate),
                ],
                axis=0,
            )
            bias_total += pre_grad
            columns = edge_columns(pre_grad, index + 1, columns)
            pre_out[:, pl.ds(index * width, width)] = pre_grad.astype(BF16)
            if index in (0, row_count - 1):
                edges.append(pre_grad)
    hidden_out[...] = hidden_wide[...].reshape(hidden_out.shape).astype(BF16)
    row_sends(edges[0], edges[-1], inner_out, outer_out)
    columns_out[...] = columns.astype(BF16)

    for a in range(3):
        product = lax.dot_general(
            pre_out[...],
            shifted[:, pl.ds(a * width, row_count * width)],
            ACROSS,
            preferred_element_type=F32,
        )
        for b in range(3):
            at = (3 * a + b) * gate_count
            sums[at : at + gate_count, :] = product[:, b * channels : (b + 1) * channels]
    used = 9 * gate_count
    if place.rows > used:
        sums[used:, :] = jnp.zeros((place.rows - used, channels), F32)

    ones = jnp.ones((8, width), BF16)
    high = bias_total.astype(BF16)
    low = (bias_total - high.astype(F32)).astype(BF16)
    flat = lax.dot_general(ones, high, ACROSS, preferred_element_type=F32)
    flat += lax.dot_general(ones, low, ACROSS, preferred_element_type=F32)
    odd = lax.broadcasted_iota(jnp.int32, (8, channels), 0) % 2 == 1
    bias_rows = jnp.where(odd, flat[:, channels : 2 * channels], flat[:, 0:channels])
    bias_out[...] = bias_rows
    split_sum(place, 0, bias_rows, sums, place.rows, send_out, keep_out)


def halve_kernel(place, phase, scaling, keep, bias, received, after, *outs):
    del after
    total = keep[...] + received[BIAS_ROWS:, :].astype(F32)
    bias_total = bias[...] + decode(received[0:BIAS_ROWS, :].astype(F32))
    if phase == len(place.bits) - 1:
        (out,) = outs
        out[0:BIAS_ROWS, :] = encode(bias_total * scaling).astype(BF16)
        out[BIAS_ROWS:, :] = (total * scaling).astype(BF16)
        return
    send_out, keep_out, bias_out, scratch = outs
    scratch[...] = total
    bias_out[...] = bias_total
    split_sum(place, phase + 1, bias_total, scratch, total.shape[0], send_out, keep_out)


def double_kernel(place, phase, own, received, out):
    odd = place.rank(phase) == 1
    here, there = own[...].astype(F32), received[...].astype(F32)
    first, second = pick(odd, there, here), pick(odd, here, there)
    out[...] = jnp.concatenate([first, second[BIAS_ROWS:]], axis=0).astype(BF16)


def finish_kernel(place, own, received, out, bias_out):
    odd = place.rank(0) == 1
    rows = own.shape[0] - BIAS_ROWS
    here, there = own[...].astype(F32), received[...].astype(F32)
    rank = place.rank(0)
    out[pl.ds(pl.multiple_of(rank * rows, 8), rows), :] = here[BIAS_ROWS:]
    out[pl.ds(pl.multiple_of((1 - rank) * rows, 8), rows), :] = there[BIAS_ROWS:]
    bias_out[...] = decode(pick(odd, there[0:BIAS_ROWS], here[0:BIAS_ROWS]))


def field_kernel(
    place,
    pre,
    inner_row,
    outer_row,
    inner_column,
    outer_column,
    weights,
    inputs_out,
    hidden_out,
    done_out,
    shifted,
    turned,
    wide,
):
    gate_count = pre.shape[0]
    channels = weights.shape[2]
    done_out[...] = jnp.zeros(done_out.shape, F32)
    hid, row_count, width = hidden_out.shape

    def emit(position, left, row, right):
        at = pl.ds(position * width, width)
        shifted[0:gate_count, at] = right.astype(BF16)
        shifted[gate_count : 2 * gate_count, at] = row.astype(BF16)
        shifted[2 * gate_count : 3 * gate_count, at] = left.astype(BF16)

    widened(
        row_count,
        lambda index: pre[:, pl.ds(index * width, width)].astype(F32),
        (inner_row, outer_row),
        (inner_column, outer_column),
        emit,
    )
    for a in range(3):
        for b in range(3):
            turned[a, :, b * gate_count : (b + 1) * gate_count] = weights[3 * a + b].T
    lat = place.position()[0]
    top = turned[jnp.where(lat == 0, 0, 2)]
    bottom = turned[jnp.where(lat == place.lat - 1, 2, 0)]

    def product(matrix, position, count):
        return jnp.dot(
            matrix, shifted[:, pl.ds(position * width, count * width)], preferred_element_type=F32
        )

    pair = 2 if row_count % 2 == 0 else 1
    for base in range(0, row_count, pair):
        total = product(turned[1], base + 1, pair)
        if base == 0:
            above = product(top, 0, 1)
            if pair == 2:
                above = jnp.concatenate([above, product(turned[2], 1, 1)], axis=1)
        else:
            above = product(turned[2], base, pair)
        if base + pair == row_count:
            below = product(bottom, row_count + 1, 1)
            if pair == 2:
                below = jnp.concatenate([product(turned[0], row_count, 1), below], axis=1)
        else:
            below = product(turned[0], base + 2, pair)
        total = total + above + below
        for offset in range(pair):
            value = total[:, offset * width : (offset + 1) * width]
            wide[pl.ds(base + offset, channels, stride=row_count), :] = value
    size = (channels - hid) * row_count
    inputs_out[...] = wide[0:size, :].reshape(inputs_out.shape).astype(BF16)
    hidden_out[...] = wide[size:, :].reshape(hidden_out.shape).astype(BF16)


def body(
    place,
    inputs_below,
    hidden_prev,
    cell_prev,
    kernel_weights,
    gate_bias,
    readout,
    target_field,
    land_mask,
    fire_mask,
    hidden_grad,
):
    hid, row_count, width = hidden_prev.shape
    gate_count, channels = kernel_weights.shape[1:]
    cells = row_count * width
    halo_cells = (row_count + 2) * width
    scaling = 1.0 / math.sqrt(cells * place.lat * place.lon)
    bind = functools.partial
    inner_rows, outer_rows = place.pairs(place.inner_rows), place.pairs(place.outer_rows)
    inner_columns = place.pairs(place.inner_columns)
    outer_columns = place.pairs(place.outer_columns)
    flat = sds((hid * row_count, width), F32)

    inner, outer, wide = call(
        pack_kernel,
        (
            sds((channels, width), BF16),
            sds((channels, width), BF16),
            sds((channels * row_count, width), F32),
        ),
        [
            pltpu.VMEM(inputs_below.shape, BF16),
            pltpu.VMEM(hidden_prev.shape, BF16),
            pltpu.SemaphoreType.DMA((2,)),
        ],
        remote=2,
        moved=4 * channels * cells,
    )(inputs_below, hidden_prev)
    inner, outer = permuted(inner, inner_rows), permuted(outer, outer_rows)
    (
        rows,
        columns,
        cell_here,
        weights_here,
        hidden_grad_here,
        target_here,
        land_here,
        fire_here,
        bias_wide,
        readout_wide,
    ) = call(
        prepare_kernel,
        (
            sds((row_count, channels, width), BF16),
            sds((channels, width), F32),
            flat,
            sds(kernel_weights.shape, BF16),
            flat,
            sds(target_field.shape, F32),
            sds(land_mask.shape, jnp.int32),
            sds(fire_mask.shape, jnp.int32),
            sds((gate_count, width), F32),
            sds((hid, width), F32),
        ),
        [
            pltpu.VMEM(hidden_grad.shape, BF16),
            pltpu.VMEM(gate_bias.shape, F32),
            pltpu.VMEM(readout.shape, F32),
            pltpu.SemaphoreType.DMA((8,)),
        ],
        remote=8,
        moved=6_000_000,
    )(
        wide,
        cell_prev.reshape(hid * row_count, width),
        kernel_weights,
        hidden_grad,
        target_field,
        land_mask,
        fire_mask,
        gate_bias,
        readout,
    )
    columns = call(bind(columns_kernel, row_count), sds((channels, width), BF16))(
        columns, inner, outer
    )

    sizes = [place.rows >> (phase + 1) for phase in range(len(place.bits))]
    (
        hidden_next,
        cell_next,
        grad_cell,
        pre,
        pre_inner,
        pre_outer,
        pre_columns,
        send,
        keep,
        bias,
    ) = call(
        bind(gates_kernel, place),
        (
            sds((hid, row_count, width), BF16),
            flat,
            flat,
            sds((gate_count, cells), BF16),
            sds((gate_count, width), BF16),
            sds((gate_count, width), BF16),
            sds((gate_count, width), BF16),
            sds((BIAS_ROWS + sizes[0], channels), BF16),
            sds((sizes[0], channels), F32),
            sds((8, channels), F32),
        ),
        [
            pltpu.VMEM((3 * channels, halo_cells), BF16),
            pltpu.VMEM((hid * row_count, width), F32),
            pltpu.VMEM((place.rows, channels), F32),
        ],
        flops=4 * 9 * gate_count * channels * cells,
        moved=4_000_000,
        transcendentals=5 * hid * cells,
    )(
        rows,
        inner,
        outer,
        permuted(columns, inner_columns),
        permuted(columns, outer_columns),
        cell_here,
        weights_here,
        hidden_grad_here,
        target_here,
        land_here,
        fire_here,
        bias_wide,
        readout_wide,
    )

    pre_inner, pre_outer = permuted(pre_inner, inner_rows), permuted(pre_outer, outer_rows)
    pre_columns = call(bind(columns_kernel, row_count), sds((gate_count, width), BF16))(
        pre_columns, pre_inner, pre_outer
    )
    grad_inputs, grad_hidden, field_done = call(
        bind(field_kernel, place),
        (
            sds((channels - hid, row_count, width), BF16),
            sds((hid, row_count, width), BF16),
            sds((8, width), F32),
        ),
        [
            pltpu.VMEM((3 * gate_count, halo_cells), BF16),
            pltpu.VMEM((3, channels, 3 * gate_count), BF16),
            pltpu.VMEM((channels * row_count, width), F32),
        ],
        flops=2 * 9 * gate_count * channels * cells,
        moved=2_000_000,
    )(
        pre,
        pre_inner,
        pre_outer,
        permuted(pre_columns, inner_columns),
        permuted(pre_columns, outer_columns),
        weights_here,
    )

    last = len(place.bits) - 1
    after = [target_here, pre_columns, target_here, field_done]
    after += [target_here] * last
    for phase in range(last + 1):
        received = permuted(send, place.phase_pairs(phase))
        kernel = bind(halve_kernel, place, phase, scaling)
        if phase < last:
            size = sizes[phase + 1]
            send, keep, bias = call(
                kernel,
                (
                    sds((BIAS_ROWS + size, channels), BF16),
                    sds((size, channels), F32),
                    sds((8, channels), F32),
                ),
                [pltpu.VMEM((2 * size, channels), F32)],
            )(keep, bias, received, after[phase])
        else:
            block = call(kernel, (sds((BIAS_ROWS + sizes[last], channels), BF16),))(
                keep, bias, received, after[phase]
            )[0]
    for phase in range(last, 0, -1):
        received = permuted(block, place.phase_pairs(phase))
        block = call(
            bind(double_kernel, place, phase),
            sds((BIAS_ROWS + sizes[phase - 1], channels), BF16),
        )(block, received)
    grad_kernel, grad_bias = call(
        bind(finish_kernel, place),
        (sds((place.rows, channels), F32), sds((8, channels), F32)),
    )(block, permuted(block, place.phase_pairs(0)))
    shape = hidden_prev.shape
    return (
        hidden_next,
        cell_next.reshape(shape),
        grad_inputs,
        grad_hidden,
        grad_cell.reshape(shape),
        grad_kernel[: 9 * gate_count].reshape(kernel_weights.shape),
        grad_bias[: gate_count // channels].reshape(gate_count),
    )


def solution(mesh):
    lat_count, lon_count = mesh.shape["lat"], mesh.shape["lon"]
    split = Mesh(mesh.devices.reshape(lat_count // 2, 2, lon_count), AXES)
    field = P(None, ("band", "core"), "lon")
    flat = P(("band", "core"), "lon")

    def run(*args):
        place = Layout(lat_count, lon_count, args[3].shape[0] * args[3].shape[1])
        return jax.shard_map(
            functools.partial(body, place),
            mesh=split,
            in_specs=(field, field, field, P(), P(), P(), flat, flat, flat, field),
            out_specs=(field, field, field, field, field, P(), P()),
            check_vma=False,
        )(*args)

    return run
```

```python
import functools
import math

import jax
import jax.numpy as jnp
from jax import lax
from jax.experimental import pallas as pl
from jax.experimental.pallas import tpu as pltpu
from jax.sharding import Mesh, PartitionSpec as P

F32 = jnp.float32
BF16 = jnp.bfloat16
AXES = ("band", "core", "lon")
BIAS_ROWS = 16
LAST = 16
VMEM = pl.BlockSpec(memory_space=pltpu.VMEM)
HBM = pl.BlockSpec(memory_space=pltpu.HBM)
ACROSS = (((1,), (1,)), ((), ()))


def sds(shape, dtype):
    return jax.ShapeDtypeStruct(shape, dtype)


def call(
    kernel,
    out_shape,
    scratch=(),
    remote=0,
    leaving=0,
    aliases=None,
    flops=0,
    moved=0,
    transcendentals=0,
):
    several = isinstance(out_shape, tuple)
    shapes = out_shape if several else (out_shape,)
    out_specs = tuple([HBM] * leaving + [VMEM] * (len(shapes) - leaving))

    def run(*args):
        near = len(args) - remote
        far = [pltpu.with_memory_space_constraint(arg, pltpu.HBM) for arg in args[near:]]
        return pl.pallas_call(
            kernel,
            out_shape=out_shape,
            in_specs=[VMEM] * near + [HBM] * remote,
            out_specs=out_specs if several else out_specs[0],
            input_output_aliases=aliases or {},
            scratch_shapes=list(scratch),
            cost_estimate=pl.CostEstimate(
                flops=flops, bytes_accessed=moved, transcendentals=transcendentals
            ),
            compiler_params=pltpu.CompilerParams(vmem_limit_bytes=24 * 1024 * 1024),
        )(*args[:near], *far)

    return run


class Layout:
    def __init__(self, lat_count, lon_count, kernel_rows):
        self.lat, self.lon = lat_count, lon_count
        self.half = lon_count // 2
        scatter = [("lat", 1 << k) for k in range(1, lat_count.bit_length() - 1)]
        lon_bits = [("lon", 1 << k) for k in range(lon_count.bit_length() - 1)]
        scatter += lon_bits[:-2]
        whole = lon_bits[-2:]
        self.scatter_phases = 1 + len(scatter)
        self.orders = (
            [("lat", 1)] + scatter + whole,
            [("lat", 1)] + scatter[::-1] + whole[::-1],
        )
        step = 8 << self.scatter_phases
        self.rows = -(-kernel_rows // step) * step
        self.sizes = [self.rows >> (phase + 1) for phase in range(self.scatter_phases)]

    def position(self):
        return 2 * lax.axis_index("band") + lax.axis_index("core"), lax.axis_index("lon")

    def rank(self, phase):
        lat, lon = self.position()

        def digit(order):
            axis, bit = order[phase]
            return ((lat if axis == "lat" else lon) // bit) % 2

        return jnp.where(lat % 2 == 0, digit(self.orders[0]), digit(self.orders[1]))

    def pairs(self, partner):
        result = []
        for lat in range(self.lat):
            for lon in range(self.lon):
                there = partner(lat, lon)
                result.append((lat * self.lon + lon, there[0] * self.lon + there[1]))
        return result

    def phase_pairs(self, phase):
        def partner(lat, lon):
            axis, bit = self.orders[lat % 2][phase]
            return (lat ^ bit, lon) if axis == "lat" else (lat, lon ^ bit)

        return self.pairs(partner)

    def inner_rows(self, lat, lon):
        return lat ^ 1, lon

    def outer_rows(self, lat, lon):
        there = lat + 1 if lat % 2 else lat - 1
        if 0 <= there < self.lat:
            return there, lon
        return lat, (lon + self.half) % self.lon

    def inner_columns(self, lat, lon):
        return lat, lon ^ 1

    def outer_columns(self, lat, lon):
        return lat, (lon + (1 if lon % 2 else -1)) % self.lon


def permuted(value, pairs):
    return lax.ppermute(value, AXES, pairs)


def lanes(shape):
    return lax.broadcasted_iota(jnp.int32, shape, len(shape) - 1)


def rolled(value, shift):
    shift %= value.shape[1]
    return pltpu.roll(value, shift, 1) if shift else value


def edge_columns(row, position, columns):
    lane = lanes(row.shape)
    columns = jnp.where(lane == position, rolled(row, position), columns)
    return jnp.where(lane == LAST + position, rolled(row, LAST + position + 1), columns)


def pick(flag, yes, no):
    return jnp.where(flag, yes, no)


def is_odd(axis):
    return lax.axis_index(axis) % 2 == 1


def row_sends(first, last, inner_out, outer_out):
    odd = is_odd("core")
    inner_out[...] = pick(odd, first, last).astype(BF16)
    outer_out[...] = pick(odd, last, first).astype(BF16)


def row_halo(inner, outer):
    odd = is_odd("core")
    inner, outer = inner[...].astype(F32), outer[...].astype(F32)
    return pick(odd, inner, outer), pick(odd, outer, inner)


def column_halo(inner, outer):
    odd = is_odd("lon")
    inner, outer = inner[...].astype(F32), outer[...].astype(F32)
    return pick(odd, inner, outer), pick(odd, outer, inner)


def widened(row_count, rows, row_blocks, column_blocks, emit):
    north, south = row_halo(*row_blocks)
    west, east = column_halo(*column_blocks)
    width = west.shape[1]
    lane = lanes(west.shape)
    for position in range(row_count + 2):
        if position == 0:
            row = north
        elif position == row_count + 1:
            row = south
        else:
            row = rows(position - 1)
        left = rolled(west, -LAST - position)
        right = rolled(east, width - 1 - position)
        emit(
            position,
            jnp.where(lane == 0, left, rolled(row, 1)),
            row,
            jnp.where(lane == width - 1, right, rolled(row, -1)),
        )


def pack_kernel(below, hidden, inner_out, outer_out, wide_out, below_here, hidden_here, arrived):
    first = pltpu.make_async_copy(below, below_here, arrived.at[0])
    second = pltpu.make_async_copy(hidden, hidden_here, arrived.at[1])
    first.start()
    second.start()
    channels, row_count, width = below.shape
    size = channels * row_count
    first.wait()
    wide_out[0:size, :] = below_here[...].astype(F32).reshape(size, width)
    second.wait()
    wide_out[size : 2 * size, :] = hidden_here[...].astype(F32).reshape(size, width)
    edges = [
        wide_out[pl.ds(index, 2 * channels, stride=row_count), :] for index in (0, row_count - 1)
    ]
    row_sends(edges[0], edges[1], inner_out, outer_out)


def down_rows(values, width):
    count = values.shape[0]
    return jnp.broadcast_to(values[None, :], (width, count)).T


def prepare_kernel(
    wide,
    cell_hbm,
    weights_hbm,
    hidden_grad_hbm,
    target_hbm,
    land_hbm,
    fire_hbm,
    gate_bias_hbm,
    readout_hbm,
    rows_out,
    columns_out,
    cell_out,
    weights_out,
    hidden_grad_out,
    target_out,
    land_out,
    fire_out,
    bias_wide_out,
    readout_wide_out,
    hidden_grad_here,
    gate_bias_here,
    readout_here,
    arrived,
):
    copies = [
        pltpu.make_async_copy(source, target, arrived.at[index])
        for index, (source, target) in enumerate(
            (
                (cell_hbm, cell_out),
                (weights_hbm, weights_out),
                (hidden_grad_hbm, hidden_grad_here),
                (target_hbm, target_out),
                (land_hbm, land_out),
                (fire_hbm, fire_out),
                (gate_bias_hbm, gate_bias_here),
                (readout_hbm, readout_here),
            )
        )
    ]
    for copy in copies:
        copy.start()
    row_count, channels, width = rows_out.shape
    columns = jnp.zeros((channels, width), F32)
    for index in range(row_count):
        row = wide[pl.ds(index, channels, stride=row_count), :]
        rows_out[index] = row.astype(BF16)
        columns = edge_columns(row, index + 1, columns)
    columns_out[...] = columns
    for copy in copies:
        copy.wait()
    hidden_grad_out[...] = hidden_grad_here[...].astype(F32).reshape(hidden_grad_out.shape)
    bias_wide_out[...] = down_rows(gate_bias_here[...], width)
    readout_wide_out[...] = down_rows(readout_here[...], width)


def columns_kernel(row_count, columns, inner, outer, out):
    north, south = row_halo(inner, outer)
    value = edge_columns(north, 0, columns[...])
    out[...] = edge_columns(south, row_count + 1, value).astype(BF16)


def pre_columns_kernel(row_count, pre, inner, outer, out):
    width = out.shape[1]
    north, south = row_halo(inner, outer)
    value = edge_columns(north, 0, jnp.zeros(north.shape, F32))
    for index in range(row_count):
        row = pre[:, pl.ds(index * width, width)].astype(F32)
        value = edge_columns(row, index + 1, value)
    out[...] = edge_columns(south, row_count + 1, value).astype(BF16)


def encode(bias):
    high = bias.astype(BF16).astype(F32)
    return jnp.concatenate([high, bias - high], axis=0)


def decode(block):
    return block[0:8] + block[8:16]


def split_sum(place, phase, bias, sums, rows, send_out, keep_out):
    half = rows // 2
    rank = place.rank(phase)
    send_out[0:BIAS_ROWS, :] = encode(bias).astype(BF16)
    away = pl.ds(pl.multiple_of((1 - rank) * half, 8), half)
    send_out[BIAS_ROWS:, :] = sums[away, :].astype(BF16)
    keep_out[...] = sums[pl.ds(pl.multiple_of(rank * half, 8), half), :]


def gates_kernel(
    place,
    rows_in,
    inner_row,
    outer_row,
    inner_column,
    outer_column,
    cell_prev,
    weights,
    hidden_grad,
    target,
    land,
    fire,
    bias_wide,
    readout_wide,
    hidden_hbm,
    cell_hbm,
    grad_cell_hbm,
    pre_out,
    inner_out,
    outer_out,
    send_out,
    keep_out,
    bias_out,
    shifted,
    hidden_wide,
    hidden_low,
    cell_out,
    grad_cell_out,
    sums,
    left,
):
    row_count, channels, width = rows_in.shape
    gate_count = weights.shape[1]
    hid = gate_count // 4

    def emit(position, left, row, right):
        at = pl.ds(position * width, width)
        shifted[0:channels, at] = left.astype(BF16)
        shifted[channels : 2 * channels, at] = row.astype(BF16)
        shifted[2 * channels : 3 * channels, at] = right.astype(BF16)

    widened(
        row_count,
        lambda index: rows_in[index].astype(F32),
        (inner_row, outer_row),
        (inner_column, outer_column),
        emit,
    )

    taps = [
        jnp.concatenate([weights[3 * a], weights[3 * a + 1], weights[3 * a + 2]], axis=1)
        for a in range(3)
    ]
    bias_total = jnp.zeros((gate_count, width), F32)
    edges = []
    readout = readout_wide[...]
    pair = 2 if row_count % 2 == 0 else 1
    for base in range(0, row_count, pair):
        preact = jnp.zeros((gate_count, pair * width), F32)
        for a in range(3):
            preact += jnp.dot(
                taps[a],
                shifted[:, pl.ds((base + a) * width, pair * width)],
                preferred_element_type=F32,
            )
        for offset in range(pair):
            index = base + offset
            strided = pl.ds(index, hid, stride=row_count)
            part = preact[:, offset * width : (offset + 1) * width] + bias_wide[...]
            input_gate = 0.5 + 0.5 * jnp.tanh(0.5 * part[0:hid])
            forget_gate = 0.5 + 0.5 * jnp.tanh(0.5 * part[hid : 2 * hid])
            output_gate = 0.5 + 0.5 * jnp.tanh(0.5 * part[2 * hid : 3 * hid])
            candidate = jnp.tanh(part[3 * hid : 4 * hid])
            cell_before = cell_prev[strided, :]
            land_row = land[index : index + 1, :].astype(F32)
            fire_row = fire[index : index + 1, :].astype(F32)
            cell_next = land_row * (forget_gate * cell_before + input_gate * candidate)
            squashed = jnp.tanh(cell_next)
            hidden_next = (output_gate * squashed).astype(BF16).astype(F32)
            predicted = jnp.sum(readout * hidden_next, axis=0, keepdims=True)
            miss = 2.0 * (fire_row * (predicted - target[index : index + 1, :]))
            total_grad = hidden_grad[strided, :] + miss * readout
            cell_grad = land_row * total_grad * output_gate * (1.0 - squashed * squashed)
            cell_out[strided, :] = cell_next
            hidden_wide[strided, :] = hidden_next
            grad_cell_out[strided, :] = cell_grad * forget_gate
            pre_grad = jnp.concatenate(
                [
                    cell_grad * candidate * input_gate * (1.0 - input_gate),
                    cell_grad * cell_before * forget_gate * (1.0 - forget_gate),
                    total_grad * squashed * output_gate * (1.0 - output_gate),
                    cell_grad * input_gate * (1.0 - candidate * candidate),
                ],
                axis=0,
            )
            bias_total += pre_grad
            pre_out[:, pl.ds(index * width, width)] = pre_grad.astype(BF16)
            if index in (0, row_count - 1):
                edges.append(pre_grad)
    hidden_low[...] = hidden_wide[...].reshape(hidden_low.shape).astype(BF16)
    leaving = [
        pltpu.make_async_copy(source, target, left.at[index])
        for index, (source, target) in enumerate(
            ((hidden_low, hidden_hbm), (cell_out, cell_hbm), (grad_cell_out, grad_cell_hbm))
        )
    ]
    for copy in leaving:
        copy.start()
    row_sends(edges[0], edges[-1], inner_out, outer_out)

    for a in range(3):
        product = lax.dot_general(
            pre_out[...],
            shifted[:, pl.ds(a * width, row_count * width)],
            ACROSS,
            preferred_element_type=F32,
        )
        for b in range(3):
            at = (3 * a + b) * gate_count
            sums[at : at + gate_count, :] = product[:, b * channels : (b + 1) * channels]
    used = 9 * gate_count
    if place.rows > used:
        sums[used:, :] = jnp.zeros((place.rows - used, channels), F32)

    ones = jnp.ones((8, width), BF16)
    high = bias_total.astype(BF16)
    low = (bias_total - high.astype(F32)).astype(BF16)
    flat = lax.dot_general(ones, high, ACROSS, preferred_element_type=F32)
    flat += lax.dot_general(ones, low, ACROSS, preferred_element_type=F32)
    odd = lax.broadcasted_iota(jnp.int32, (8, channels), 0) % 2 == 1
    bias_rows = jnp.where(odd, flat[:, channels : 2 * channels], flat[:, 0:channels])
    bias_out[...] = bias_rows
    split_sum(place, 0, bias_rows, sums, place.rows, send_out, keep_out)
    for copy in leaving:
        copy.wait()


def halve_kernel(place, phase, keep, bias, received, after, *outs):
    del after
    total = keep[...] + received[BIAS_ROWS:, :].astype(F32)
    bias_total = bias[...] + decode(received[0:BIAS_ROWS, :].astype(F32))
    if phase == place.scatter_phases - 1:
        (out,) = outs
        out[0:BIAS_ROWS, :] = encode(bias_total).astype(BF16)
        out[BIAS_ROWS:, :] = total.astype(BF16)
        return
    send_out, keep_out, bias_out, scratch = outs
    scratch[...] = total
    bias_out[...] = bias_total
    split_sum(place, phase + 1, bias_total, scratch, total.shape[0], send_out, keep_out)


def add_kernel(scale, own, received, after, out):
    del after
    here, there = own[...].astype(F32), received[...].astype(F32)
    bias = (decode(here[0:BIAS_ROWS]) + decode(there[0:BIAS_ROWS])) * scale
    out[0:BIAS_ROWS, :] = encode(bias).astype(BF16)
    out[BIAS_ROWS:, :] = ((here[BIAS_ROWS:] + there[BIAS_ROWS:]) * scale).astype(BF16)


def double_kernel(place, phase, own, received, out):
    odd = place.rank(phase) == 1
    here, there = own[...].astype(F32), received[...].astype(F32)
    first, second = pick(odd, there, here), pick(odd, here, there)
    out[...] = jnp.concatenate([first, second[BIAS_ROWS:]], axis=0).astype(BF16)


def own_half_kernel(place, own, out, wide, left):
    rows = own.shape[0] - BIAS_ROWS
    wide[...] = own[BIAS_ROWS:, :].astype(F32)
    at = pl.ds(pl.multiple_of(place.rank(0) * rows, 8), rows)
    copy = pltpu.make_async_copy(wide, out.at[at, :], left.at[0])
    copy.start()
    copy.wait()


def other_half_kernel(place, own, received, out_before, out, bias_out, wide, left):
    del out_before
    rows = received.shape[0] - BIAS_ROWS
    wide[...] = received[BIAS_ROWS:, :].astype(F32)
    rank = place.rank(0)
    at = pl.ds(pl.multiple_of((1 - rank) * rows, 8), rows)
    copy = pltpu.make_async_copy(wide, out.at[at, :], left.at[0])
    copy.start()
    here, there = own[0:BIAS_ROWS, :].astype(F32), received[0:BIAS_ROWS, :].astype(F32)
    bias = decode(pick(rank == 1, there, here))
    width = bias.shape[1]
    for index in range(bias_out.shape[0] // width):
        bias_out[pl.ds(index * width, width)] = bias[index]
    copy.wait()


def field_kernel(
    place,
    pre,
    inner_row,
    outer_row,
    inner_column,
    outer_column,
    weights,
    inputs_out,
    hidden_out,
    done_out,
    shifted,
    turned,
    wide,
):
    gate_count = pre.shape[0]
    channels = weights.shape[2]
    done_out[...] = jnp.zeros(done_out.shape, F32)
    hid, row_count, width = hidden_out.shape

    def emit(position, left, row, right):
        at = pl.ds(position * width, width)
        shifted[0:gate_count, at] = right.astype(BF16)
        shifted[gate_count : 2 * gate_count, at] = row.astype(BF16)
        shifted[2 * gate_count : 3 * gate_count, at] = left.astype(BF16)

    widened(
        row_count,
        lambda index: pre[:, pl.ds(index * width, width)].astype(F32),
        (inner_row, outer_row),
        (inner_column, outer_column),
        emit,
    )
    for a in range(3):
        for b in range(3):
            turned[a, :, b * gate_count : (b + 1) * gate_count] = weights[3 * a + b].T
    lat = place.position()[0]
    top = turned[jnp.where(lat == 0, 0, 2)]
    bottom = turned[jnp.where(lat == place.lat - 1, 2, 0)]

    def product(matrix, position, count):
        return jnp.dot(
            matrix, shifted[:, pl.ds(position * width, count * width)], preferred_element_type=F32
        )

    pair = 2 if row_count % 2 == 0 else 1
    for base in range(0, row_count, pair):
        total = product(turned[1], base + 1, pair)
        if base == 0:
            above = product(top, 0, 1)
            if pair == 2:
                above = jnp.concatenate([above, product(turned[2], 1, 1)], axis=1)
        else:
            above = product(turned[2], base, pair)
        if base + pair == row_count:
            below = product(bottom, row_count + 1, 1)
            if pair == 2:
                below = jnp.concatenate([product(turned[0], row_count, 1), below], axis=1)
        else:
            below = product(turned[0], base + 2, pair)
        total = total + above + below
        for offset in range(pair):
            value = total[:, offset * width : (offset + 1) * width]
            wide[pl.ds(base + offset, channels, stride=row_count), :] = value
    size = (channels - hid) * row_count
    inputs_out[...] = wide[0:size, :].reshape(inputs_out.shape).astype(BF16)
    hidden_out[...] = wide[size:, :].reshape(hidden_out.shape).astype(BF16)


def body(
    place,
    inputs_below,
    hidden_prev,
    cell_prev,
    kernel_weights,
    gate_bias,
    readout,
    target_field,
    land_mask,
    fire_mask,
    hidden_grad,
):
    hid, row_count, width = hidden_prev.shape
    gate_count, channels = kernel_weights.shape[1:]
    cells = row_count * width
    halo_cells = (row_count + 2) * width
    scaling = 1.0 / math.sqrt(cells * place.lat * place.lon)
    bind = functools.partial
    inner_rows, outer_rows = place.pairs(place.inner_rows), place.pairs(place.outer_rows)
    inner_columns = place.pairs(place.inner_columns)
    outer_columns = place.pairs(place.outer_columns)
    flat = sds((hid * row_count, width), F32)

    inner, outer, wide = call(
        pack_kernel,
        (
            sds((channels, width), BF16),
            sds((channels, width), BF16),
            sds((channels * row_count, width), F32),
        ),
        [
            pltpu.VMEM(inputs_below.shape, BF16),
            pltpu.VMEM(hidden_prev.shape, BF16),
            pltpu.SemaphoreType.DMA((2,)),
        ],
        remote=2,
        moved=4 * channels * cells,
    )(inputs_below, hidden_prev)
    inner, outer = permuted(inner, inner_rows), permuted(outer, outer_rows)
    (
        rows,
        columns,
        cell_here,
        weights_here,
        hidden_grad_here,
        target_here,
        land_here,
        fire_here,
        bias_wide,
        readout_wide,
    ) = call(
        prepare_kernel,
        (
            sds((row_count, channels, width), BF16),
            sds((channels, width), F32),
            flat,
            sds(kernel_weights.shape, BF16),
            flat,
            sds(target_field.shape, F32),
            sds(land_mask.shape, jnp.int32),
            sds(fire_mask.shape, jnp.int32),
            sds((gate_count, width), F32),
            sds((hid, width), F32),
        ),
        [
            pltpu.VMEM(hidden_grad.shape, BF16),
            pltpu.VMEM(gate_bias.shape, F32),
            pltpu.VMEM(readout.shape, F32),
            pltpu.SemaphoreType.DMA((8,)),
        ],
        remote=8,
        moved=6_000_000,
    )(
        wide,
        cell_prev.reshape(hid * row_count, width),
        kernel_weights,
        hidden_grad,
        target_field,
        land_mask,
        fire_mask,
        gate_bias,
        readout,
    )
    columns = call(bind(columns_kernel, row_count), sds((channels, width), BF16))(
        columns, inner, outer
    )

    sizes = place.sizes
    (
        hidden_next,
        cell_next,
        grad_cell,
        pre,
        pre_inner,
        pre_outer,
        send,
        keep,
        bias,
    ) = call(
        bind(gates_kernel, place),
        (
            sds((hid, row_count, width), BF16),
            flat,
            flat,
            sds((gate_count, cells), BF16),
            sds((gate_count, width), BF16),
            sds((gate_count, width), BF16),
            sds((BIAS_ROWS + sizes[0], channels), BF16),
            sds((sizes[0], channels), F32),
            sds((8, channels), F32),
        ),
        [
            pltpu.VMEM((3 * channels, halo_cells), BF16),
            pltpu.VMEM((hid * row_count, width), F32),
            pltpu.VMEM((hid, row_count, width), BF16),
            pltpu.VMEM((hid * row_count, width), F32),
            pltpu.VMEM((hid * row_count, width), F32),
            pltpu.VMEM((place.rows, channels), F32),
            pltpu.SemaphoreType.DMA((3,)),
        ],
        leaving=3,
        flops=4 * 9 * gate_count * channels * cells,
        moved=4_000_000,
        transcendentals=5 * hid * cells,
    )(
        rows,
        inner,
        outer,
        permuted(columns, inner_columns),
        permuted(columns, outer_columns),
        cell_here,
        weights_here,
        hidden_grad_here,
        target_here,
        land_here,
        fire_here,
        bias_wide,
        readout_wide,
    )

    pre_inner, pre_outer = permuted(pre_inner, inner_rows), permuted(pre_outer, outer_rows)
    pre_columns = call(bind(pre_columns_kernel, row_count), sds((gate_count, width), BF16))(
        pre, pre_inner, pre_outer
    )
    grad_inputs, grad_hidden, field_done = call(
        bind(field_kernel, place),
        (
            sds((channels - hid, row_count, width), BF16),
            sds((hid, row_count, width), BF16),
            sds((8, width), F32),
        ),
        [
            pltpu.VMEM((3 * gate_count, halo_cells), BF16),
            pltpu.VMEM((3, channels, 3 * gate_count), BF16),
            pltpu.VMEM((channels * row_count, width), F32),
        ],
        flops=2 * 9 * gate_count * channels * cells,
        moved=2_000_000,
    )(
        pre,
        pre_inner,
        pre_outer,
        permuted(pre_columns, inner_columns),
        permuted(pre_columns, outer_columns),
        weights_here,
    )

    last = place.scatter_phases - 1
    phases = len(place.orders[0])
    after = [target_here] * phases
    after[1] = pre_columns
    after[3] = field_done
    for phase in range(last + 1):
        received = permuted(send, place.phase_pairs(phase))
        kernel = bind(halve_kernel, place, phase)
        if phase < last:
            size = sizes[phase + 1]
            send, keep, bias = call(
                kernel,
                (
                    sds((BIAS_ROWS + size, channels), BF16),
                    sds((size, channels), F32),
                    sds((8, channels), F32),
                ),
                [pltpu.VMEM((2 * size, channels), F32)],
            )(keep, bias, received, after[phase])
        else:
            block = call(kernel, (sds((BIAS_ROWS + sizes[last], channels), BF16),))(
                keep, bias, received, after[phase]
            )[0]
    for phase in range(last + 1, phases):
        received = permuted(block, place.phase_pairs(phase))
        scale = scaling if phase == phases - 1 else 1.0
        block = call(bind(add_kernel, scale), sds(block.shape, BF16))(
            block, received, after[phase]
        )
    for phase in range(last, 0, -1):
        received = permuted(block, place.phase_pairs(phase))
        block = call(
            bind(double_kernel, place, phase),
            sds((BIAS_ROWS + sizes[phase - 1], channels), BF16),
        )(block, received)
    received = permuted(block, place.phase_pairs(0))
    half = [pltpu.VMEM((sizes[0], channels), F32), pltpu.SemaphoreType.DMA((1,))]
    grad_kernel = call(
        bind(own_half_kernel, place),
        (sds((place.rows, channels), F32),),
        half,
        leaving=1,
        moved=6 * sizes[0] * channels,
    )(block)[0]
    grad_kernel, grad_bias = call(
        bind(other_half_kernel, place),
        (sds((place.rows, channels), F32), sds((gate_count,), F32)),
        half,
        remote=1,
        leaving=1,
        aliases={2: 0},
        moved=6 * sizes[0] * channels,
    )(block, received, grad_kernel)
    shape = hidden_prev.shape
    return (
        hidden_next,
        cell_next.reshape(shape),
        grad_inputs,
        grad_hidden,
        grad_cell.reshape(shape),
        grad_kernel[: 9 * gate_count].reshape(kernel_weights.shape),
        grad_bias,
    )


def solution(mesh):
    lat_count, lon_count = mesh.shape["lat"], mesh.shape["lon"]
    split = Mesh(mesh.devices.reshape(lat_count // 2, 2, lon_count), AXES)
    field = P(None, ("band", "core"), "lon")
    flat = P(("band", "core"), "lon")

    def run(*args):
        place = Layout(lat_count, lon_count, args[3].shape[0] * args[3].shape[1])
        return jax.shard_map(
            functools.partial(body, place),
            mesh=split,
            in_specs=(field, field, field, P(), P(), P(), flat, flat, flat, field),
            out_specs=(field, field, field, field, field, P(), P()),
            check_vma=False,
        )(*args)

    return run
```

```python
import functools
import math

import jax
import jax.numpy as jnp
from jax import lax
from jax.experimental import pallas as pl
from jax.experimental.pallas import tpu as pltpu
from jax.sharding import Mesh, PartitionSpec as P

F32 = jnp.float32
BF16 = jnp.bfloat16
AXES = ("band", "core", "reach", "near")
PLANE = ("band", "near")
BIAS_ROWS = 16
LAST = 16
VMEM = pl.BlockSpec(memory_space=pltpu.VMEM)
HBM = pl.BlockSpec(memory_space=pltpu.HBM)
ACROSS = (((1,), (1,)), ((), ()))


def sds(shape, dtype):
    return jax.ShapeDtypeStruct(shape, dtype)


def call(
    kernel,
    out_shape,
    scratch=(),
    remote=0,
    leaving=0,
    aliases=None,
    flops=0,
    moved=0,
    transcendentals=0,
):
    several = isinstance(out_shape, tuple)
    shapes = out_shape if several else (out_shape,)
    out_specs = tuple([HBM] * leaving + [VMEM] * (len(shapes) - leaving))

    def run(*args):
        near = len(args) - remote
        far = [pltpu.with_memory_space_constraint(arg, pltpu.HBM) for arg in args[near:]]
        return pl.pallas_call(
            kernel,
            out_shape=out_shape,
            in_specs=[VMEM] * near + [HBM] * remote,
            out_specs=out_specs if several else out_specs[0],
            input_output_aliases=aliases or {},
            scratch_shapes=list(scratch),
            cost_estimate=pl.CostEstimate(
                flops=flops, bytes_accessed=moved, transcendentals=transcendentals
            ),
            compiler_params=pltpu.CompilerParams(vmem_limit_bytes=24 * 1024 * 1024),
        )(*args[:near], *far)

    return run


class Layout:
    def __init__(self, lat_count, lon_count, kernel_rows):
        self.lat, self.lon = lat_count, lon_count
        self.half = lon_count // 2
        self.plane = lat_count
        whole = [("lon", 1 << k) for k in range(1, lon_count.bit_length() - 1)]
        self.orders = ([("lat", 1)] + whole, [("lat", 1)] + whole[::-1])
        step = 16 * self.plane
        self.rows = -(-kernel_rows // step) * step
        self.half_rows = self.rows // 2
        self.chunk = self.half_rows // self.plane

    def position(self):
        lat = 2 * lax.axis_index("band") + lax.axis_index("core")
        return lat, 2 * lax.axis_index("reach") + lax.axis_index("near")

    def rank(self, phase):
        lat, lon = self.position()

        def digit(order):
            axis, bit = order[phase]
            return ((lat if axis == "lat" else lon) // bit) % 2

        return jnp.where(lat % 2 == 0, digit(self.orders[0]), digit(self.orders[1]))

    def pairs(self, partner):
        result = []
        for lat in range(self.lat):
            for lon in range(self.lon):
                there = partner(lat, lon)
                result.append((lat * self.lon + lon, there[0] * self.lon + there[1]))
        return result

    def phase_pairs(self, phase):
        def partner(lat, lon):
            axis, bit = self.orders[lat % 2][phase]
            return (lat ^ bit, lon) if axis == "lat" else (lat, lon ^ bit)

        return self.pairs(partner)

    def inner_rows(self, lat, lon):
        return lat ^ 1, lon

    def outer_rows(self, lat, lon):
        there = lat + 1 if lat % 2 else lat - 1
        if 0 <= there < self.lat:
            return there, lon
        return lat, (lon + self.half) % self.lon

    def inner_columns(self, lat, lon):
        return lat, lon ^ 1

    def outer_columns(self, lat, lon):
        return lat, (lon + (1 if lon % 2 else -1)) % self.lon


def permuted(value, pairs):
    return lax.ppermute(value, AXES, pairs)


def lanes(shape):
    return lax.broadcasted_iota(jnp.int32, shape, len(shape) - 1)


def rolled(value, shift):
    shift %= value.shape[1]
    return pltpu.roll(value, shift, 1) if shift else value


def edge_columns(row, position, columns):
    lane = lanes(row.shape)
    columns = jnp.where(lane == position, rolled(row, position), columns)
    return jnp.where(lane == LAST + position, rolled(row, LAST + position + 1), columns)


def pick(flag, yes, no):
    return jnp.where(flag, yes, no)


def is_odd(axis):
    return lax.axis_index(axis) % 2 == 1


def row_sends(first, last, inner_out, outer_out):
    odd = is_odd("core")
    inner_out[...] = pick(odd, first, last).astype(BF16)
    outer_out[...] = pick(odd, last, first).astype(BF16)


def row_halo(inner, outer):
    odd = is_odd("core")
    inner, outer = inner[...].astype(F32), outer[...].astype(F32)
    return pick(odd, inner, outer), pick(odd, outer, inner)


def column_halo(inner, outer):
    odd = is_odd("near")
    inner, outer = inner[...].astype(F32), outer[...].astype(F32)
    return pick(odd, inner, outer), pick(odd, outer, inner)


def widened(row_count, rows, row_blocks, column_blocks, emit):
    north, south = row_halo(*row_blocks)
    west, east = column_halo(*column_blocks)
    width = west.shape[1]
    lane = lanes(west.shape)
    for position in range(row_count + 2):
        if position == 0:
            row = north
        elif position == row_count + 1:
            row = south
        else:
            row = rows(position - 1)
        left = rolled(west, -LAST - position)
        right = rolled(east, width - 1 - position)
        emit(
            position,
            jnp.where(lane == 0, left, rolled(row, 1)),
            row,
            jnp.where(lane == width - 1, right, rolled(row, -1)),
        )


def pack_kernel(below, hidden, inner_out, outer_out, wide_out, below_here, hidden_here, arrived):
    first = pltpu.make_async_copy(below, below_here, arrived.at[0])
    second = pltpu.make_async_copy(hidden, hidden_here, arrived.at[1])
    first.start()
    second.start()
    channels, row_count, width = below.shape
    size = channels * row_count
    first.wait()
    wide_out[0:size, :] = below_here[...].astype(F32).reshape(size, width)
    second.wait()
    wide_out[size : 2 * size, :] = hidden_here[...].astype(F32).reshape(size, width)
    edges = [
        wide_out[pl.ds(index, 2 * channels, stride=row_count), :] for index in (0, row_count - 1)
    ]
    row_sends(edges[0], edges[1], inner_out, outer_out)


def down_rows(values, width):
    count = values.shape[0]
    return jnp.broadcast_to(values[None, :], (width, count)).T


def prepare_kernel(
    wide,
    cell_hbm,
    weights_hbm,
    hidden_grad_hbm,
    target_hbm,
    land_hbm,
    fire_hbm,
    gate_bias_hbm,
    readout_hbm,
    rows_out,
    columns_out,
    cell_out,
    weights_out,
    hidden_grad_out,
    target_out,
    land_out,
    fire_out,
    bias_wide_out,
    readout_wide_out,
    hidden_grad_here,
    gate_bias_here,
    readout_here,
    arrived,
):
    copies = [
        pltpu.make_async_copy(source, target, arrived.at[index])
        for index, (source, target) in enumerate(
            (
                (cell_hbm, cell_out),
                (weights_hbm, weights_out),
                (hidden_grad_hbm, hidden_grad_here),
                (target_hbm, target_out),
                (land_hbm, land_out),
                (fire_hbm, fire_out),
                (gate_bias_hbm, gate_bias_here),
                (readout_hbm, readout_here),
            )
        )
    ]
    for copy in copies:
        copy.start()
    row_count, channels, width = rows_out.shape
    columns = jnp.zeros((channels, width), F32)
    for index in range(row_count):
        row = wide[pl.ds(index, channels, stride=row_count), :]
        rows_out[index] = row.astype(BF16)
        columns = edge_columns(row, index + 1, columns)
    columns_out[...] = columns
    for copy in copies:
        copy.wait()
    hidden_grad_out[...] = hidden_grad_here[...].astype(F32).reshape(hidden_grad_out.shape)
    bias_wide_out[...] = down_rows(gate_bias_here[...], width)
    readout_wide_out[...] = down_rows(readout_here[...], width)


def columns_kernel(row_count, columns, inner, outer, out):
    north, south = row_halo(inner, outer)
    value = edge_columns(north, 0, columns[...])
    out[...] = edge_columns(south, row_count + 1, value).astype(BF16)


def pre_columns_kernel(row_count, pre, inner, outer, out):
    width = out.shape[1]
    north, south = row_halo(inner, outer)
    value = edge_columns(north, 0, jnp.zeros(north.shape, F32))
    for index in range(row_count):
        row = pre[:, pl.ds(index * width, width)].astype(F32)
        value = edge_columns(row, index + 1, value)
    out[...] = edge_columns(south, row_count + 1, value).astype(BF16)


def encode(bias):
    high = bias.astype(BF16).astype(F32)
    return jnp.concatenate([high, bias - high], axis=0)


def decode(block):
    return block[0:8] + block[8:16]


def split_sum(place, phase, bias, sums, rows, send_out, keep_out):
    half = rows // 2
    rank = place.rank(phase)
    send_out[0:BIAS_ROWS, :] = encode(bias).astype(BF16)
    away = pl.ds(pl.multiple_of((1 - rank) * half, 8), half)
    send_out[BIAS_ROWS:, :] = sums[away, :].astype(BF16)
    keep_out[...] = sums[pl.ds(pl.multiple_of(rank * half, 8), half), :]


def gates_kernel(
    place,
    rows_in,
    inner_row,
    outer_row,
    inner_column,
    outer_column,
    cell_prev,
    weights,
    hidden_grad,
    target,
    land,
    fire,
    bias_wide,
    readout_wide,
    hidden_hbm,
    cell_hbm,
    grad_cell_hbm,
    pre_out,
    inner_out,
    outer_out,
    send_out,
    keep_out,
    bias_out,
    shifted,
    hidden_wide,
    hidden_low,
    cell_out,
    grad_cell_out,
    sums,
    left,
):
    row_count, channels, width = rows_in.shape
    gate_count = weights.shape[1]
    hid = gate_count // 4

    def emit(position, left, row, right):
        at = pl.ds(position * width, width)
        shifted[0:channels, at] = left.astype(BF16)
        shifted[channels : 2 * channels, at] = row.astype(BF16)
        shifted[2 * channels : 3 * channels, at] = right.astype(BF16)

    widened(
        row_count,
        lambda index: rows_in[index].astype(F32),
        (inner_row, outer_row),
        (inner_column, outer_column),
        emit,
    )

    taps = [
        jnp.concatenate([weights[3 * a], weights[3 * a + 1], weights[3 * a + 2]], axis=1)
        for a in range(3)
    ]
    bias_total = jnp.zeros((gate_count, width), F32)
    edges = []
    readout = readout_wide[...]
    pair = 2 if row_count % 2 == 0 else 1
    for base in range(0, row_count, pair):
        preact = jnp.zeros((gate_count, pair * width), F32)
        for a in range(3):
            preact += jnp.dot(
                taps[a],
                shifted[:, pl.ds((base + a) * width, pair * width)],
                preferred_element_type=F32,
            )
        for offset in range(pair):
            index = base + offset
            strided = pl.ds(index, hid, stride=row_count)
            part = preact[:, offset * width : (offset + 1) * width] + bias_wide[...]
            input_gate = 0.5 + 0.5 * jnp.tanh(0.5 * part[0:hid])
            forget_gate = 0.5 + 0.5 * jnp.tanh(0.5 * part[hid : 2 * hid])
            output_gate = 0.5 + 0.5 * jnp.tanh(0.5 * part[2 * hid : 3 * hid])
            candidate = jnp.tanh(part[3 * hid : 4 * hid])
            cell_before = cell_prev[strided, :]
            land_row = land[index : index + 1, :].astype(F32)
            fire_row = fire[index : index + 1, :].astype(F32)
            cell_next = land_row * (forget_gate * cell_before + input_gate * candidate)
            squashed = jnp.tanh(cell_next)
            hidden_next = (output_gate * squashed).astype(BF16).astype(F32)
            predicted = jnp.sum(readout * hidden_next, axis=0, keepdims=True)
            miss = 2.0 * (fire_row * (predicted - target[index : index + 1, :]))
            total_grad = hidden_grad[strided, :] + miss * readout
            cell_grad = land_row * total_grad * output_gate * (1.0 - squashed * squashed)
            cell_out[strided, :] = cell_next
            hidden_wide[strided, :] = hidden_next
            grad_cell_out[strided, :] = cell_grad * forget_gate
            pre_grad = jnp.concatenate(
                [
                    cell_grad * candidate * input_gate * (1.0 - input_gate),
                    cell_grad * cell_before * forget_gate * (1.0 - forget_gate),
                    total_grad * squashed * output_gate * (1.0 - output_gate),
                    cell_grad * input_gate * (1.0 - candidate * candidate),
                ],
                axis=0,
            )
            bias_total += pre_grad
            pre_out[:, pl.ds(index * width, width)] = pre_grad.astype(BF16)
            if index in (0, row_count - 1):
                edges.append(pre_grad)
    hidden_low[...] = hidden_wide[...].reshape(hidden_low.shape).astype(BF16)
    leaving = [
        pltpu.make_async_copy(source, target, left.at[index])
        for index, (source, target) in enumerate(
            ((hidden_low, hidden_hbm), (cell_out, cell_hbm), (grad_cell_out, grad_cell_hbm))
        )
    ]
    for copy in leaving:
        copy.start()
    row_sends(edges[0], edges[-1], inner_out, outer_out)

    for a in range(3):
        product = lax.dot_general(
            pre_out[...],
            shifted[:, pl.ds(a * width, row_count * width)],
            ACROSS,
            preferred_element_type=F32,
        )
        for b in range(3):
            at = (3 * a + b) * gate_count
            sums[at : at + gate_count, :] = product[:, b * channels : (b + 1) * channels]
    used = 9 * gate_count
    if place.rows > used:
        sums[used:, :] = jnp.zeros((place.rows - used, channels), F32)

    ones = jnp.ones((8, width), BF16)
    high = bias_total.astype(BF16)
    low = (bias_total - high.astype(F32)).astype(BF16)
    flat = lax.dot_general(ones, high, ACROSS, preferred_element_type=F32)
    flat += lax.dot_general(ones, low, ACROSS, preferred_element_type=F32)
    odd = lax.broadcasted_iota(jnp.int32, (8, channels), 0) % 2 == 1
    bias_rows = jnp.where(odd, flat[:, channels : 2 * channels], flat[:, 0:channels])
    bias_out[...] = bias_rows
    split_sum(place, 0, bias_rows, sums, place.rows, send_out, keep_out)
    for copy in leaving:
        copy.wait()


def pair_kernel(place, keep, bias, received, out, scratch):
    chunk = place.chunk
    scratch[...] = keep[...] + received[BIAS_ROWS:, :].astype(F32)
    block = encode(bias[...] + decode(received[0:BIAS_ROWS, :].astype(F32))).astype(BF16)
    for index in range(place.plane):
        out[index, 0:BIAS_ROWS, :] = block
        out[index, BIAS_ROWS:, :] = scratch[index * chunk : (index + 1) * chunk, :].astype(BF16)


def plane_kernel(received, after, out):
    del after
    total = received[0].astype(F32)
    bias = decode(total[0:BIAS_ROWS])
    total = total[BIAS_ROWS:]
    for index in range(1, received.shape[0]):
        value = received[index].astype(F32)
        bias += decode(value[0:BIAS_ROWS])
        total += value[BIAS_ROWS:]
    out[0:BIAS_ROWS, :] = encode(bias).astype(BF16)
    out[BIAS_ROWS:, :] = total.astype(BF16)


def add_kernel(scale, own, received, after, out):
    del after
    here, there = own[...].astype(F32), received[...].astype(F32)
    bias = encode((decode(here[0:BIAS_ROWS]) + decode(there[0:BIAS_ROWS])) * scale).astype(BF16)
    total = ((here[BIAS_ROWS:] + there[BIAS_ROWS:]) * scale).astype(BF16)
    if len(out.shape) == 2:
        out[0:BIAS_ROWS, :] = bias
        out[BIAS_ROWS:, :] = total
    else:
        for index in range(out.shape[0]):
            out[index, 0:BIAS_ROWS, :] = bias
            out[index, BIAS_ROWS:, :] = total


def unpack(blocks, wide):
    chunk = blocks.shape[1] - BIAS_ROWS
    for index in range(blocks.shape[0]):
        wide[index * chunk : (index + 1) * chunk, :] = blocks[index, BIAS_ROWS:, :].astype(F32)


def own_half_kernel(place, own, out, wide, left):
    unpack(own, wide)
    at = pl.ds(pl.multiple_of(place.rank(0) * place.half_rows, 8), place.half_rows)
    copy = pltpu.make_async_copy(wide, out.at[at, :], left.at[0])
    copy.start()
    copy.wait()


def other_half_kernel(place, own, received, out_before, out, bias_out, wide, bias_here, left):
    del out_before
    rank = place.rank(0)
    here, there = own[0, 0:BIAS_ROWS, :].astype(F32), received[0, 0:BIAS_ROWS, :].astype(F32)
    bias = decode(pick(rank == 1, there, here))
    width = bias.shape[1]
    for index in range(bias_here.shape[0] // width):
        bias_here[pl.ds(index * width, width)] = bias[index]
    bias_copy = pltpu.make_async_copy(bias_here, bias_out, left.at[1])
    bias_copy.start()
    unpack(received, wide)
    at = pl.ds(pl.multiple_of((1 - rank) * place.half_rows, 8), place.half_rows)
    copy = pltpu.make_async_copy(wide, out.at[at, :], left.at[0])
    copy.start()
    bias_copy.wait()
    copy.wait()


def field_kernel(
    place,
    pre,
    inner_row,
    outer_row,
    inner_column,
    outer_column,
    weights,
    inputs_out,
    hidden_out,
    done_out,
    shifted,
    turned,
    wide,
):
    gate_count = pre.shape[0]
    channels = weights.shape[2]
    done_out[...] = jnp.zeros(done_out.shape, F32)
    hid, row_count, width = hidden_out.shape

    def emit(position, left, row, right):
        at = pl.ds(position * width, width)
        shifted[0:gate_count, at] = right.astype(BF16)
        shifted[gate_count : 2 * gate_count, at] = row.astype(BF16)
        shifted[2 * gate_count : 3 * gate_count, at] = left.astype(BF16)

    widened(
        row_count,
        lambda index: pre[:, pl.ds(index * width, width)].astype(F32),
        (inner_row, outer_row),
        (inner_column, outer_column),
        emit,
    )
    for a in range(3):
        for b in range(3):
            turned[a, :, b * gate_count : (b + 1) * gate_count] = weights[3 * a + b].T
    lat = place.position()[0]
    top = turned[jnp.where(lat == 0, 0, 2)]
    bottom = turned[jnp.where(lat == place.lat - 1, 2, 0)]

    def product(matrix, position, count):
        return jnp.dot(
            matrix, shifted[:, pl.ds(position * width, count * width)], preferred_element_type=F32
        )

    pair = 2 if row_count % 2 == 0 else 1
    for base in range(0, row_count, pair):
        total = product(turned[1], base + 1, pair)
        if base == 0:
            above = product(top, 0, 1)
            if pair == 2:
                above = jnp.concatenate([above, product(turned[2], 1, 1)], axis=1)
        else:
            above = product(turned[2], base, pair)
        if base + pair == row_count:
            below = product(bottom, row_count + 1, 1)
            if pair == 2:
                below = jnp.concatenate([product(turned[0], row_count, 1), below], axis=1)
        else:
            below = product(turned[0], base + 2, pair)
        total = total + above + below
        for offset in range(pair):
            value = total[:, offset * width : (offset + 1) * width]
            wide[pl.ds(base + offset, channels, stride=row_count), :] = value
    size = (channels - hid) * row_count
    inputs_out[...] = wide[0:size, :].reshape(inputs_out.shape).astype(BF16)
    hidden_out[...] = wide[size:, :].reshape(hidden_out.shape).astype(BF16)


def body(
    place,
    inputs_below,
    hidden_prev,
    cell_prev,
    kernel_weights,
    gate_bias,
    readout,
    target_field,
    land_mask,
    fire_mask,
    hidden_grad,
):
    hid, row_count, width = hidden_prev.shape
    gate_count, channels = kernel_weights.shape[1:]
    cells = row_count * width
    halo_cells = (row_count + 2) * width
    scaling = 1.0 / math.sqrt(cells * place.lat * place.lon)
    bind = functools.partial
    inner_rows, outer_rows = place.pairs(place.inner_rows), place.pairs(place.outer_rows)
    inner_columns = place.pairs(place.inner_columns)
    outer_columns = place.pairs(place.outer_columns)
    flat = sds((hid * row_count, width), F32)

    inner, outer, wide = call(
        pack_kernel,
        (
            sds((channels, width), BF16),
            sds((channels, width), BF16),
            sds((channels * row_count, width), F32),
        ),
        [
            pltpu.VMEM(inputs_below.shape, BF16),
            pltpu.VMEM(hidden_prev.shape, BF16),
            pltpu.SemaphoreType.DMA((2,)),
        ],
        remote=2,
        moved=4 * channels * cells,
    )(inputs_below, hidden_prev)
    inner, outer = permuted(inner, inner_rows), permuted(outer, outer_rows)
    (
        rows,
        columns,
        cell_here,
        weights_here,
        hidden_grad_here,
        target_here,
        land_here,
        fire_here,
        bias_wide,
        readout_wide,
    ) = call(
        prepare_kernel,
        (
            sds((row_count, channels, width), BF16),
            sds((channels, width), F32),
            flat,
            sds(kernel_weights.shape, BF16),
            flat,
            sds(target_field.shape, F32),
            sds(land_mask.shape, jnp.int32),
            sds(fire_mask.shape, jnp.int32),
            sds((gate_count, width), F32),
            sds((hid, width), F32),
        ),
        [
            pltpu.VMEM(hidden_grad.shape, BF16),
            pltpu.VMEM(gate_bias.shape, F32),
            pltpu.VMEM(readout.shape, F32),
            pltpu.SemaphoreType.DMA((8,)),
        ],
        remote=8,
        moved=6_000_000,
    )(
        wide,
        cell_prev.reshape(hid * row_count, width),
        kernel_weights,
        hidden_grad,
        target_field,
        land_mask,
        fire_mask,
        gate_bias,
        readout,
    )
    columns = call(bind(columns_kernel, row_count), sds((channels, width), BF16))(
        columns, inner, outer
    )

    (
        hidden_next,
        cell_next,
        grad_cell,
        pre,
        pre_inner,
        pre_outer,
        send,
        keep,
        bias,
    ) = call(
        bind(gates_kernel, place),
        (
            sds((hid, row_count, width), BF16),
            flat,
            flat,
            sds((gate_count, cells), BF16),
            sds((gate_count, width), BF16),
            sds((gate_count, width), BF16),
            sds((BIAS_ROWS + place.half_rows, channels), BF16),
            sds((place.half_rows, channels), F32),
            sds((8, channels), F32),
        ),
        [
            pltpu.VMEM((3 * channels, halo_cells), BF16),
            pltpu.VMEM((hid * row_count, width), F32),
            pltpu.VMEM((hid, row_count, width), BF16),
            pltpu.VMEM((hid * row_count, width), F32),
            pltpu.VMEM((hid * row_count, width), F32),
            pltpu.VMEM((place.rows, channels), F32),
            pltpu.SemaphoreType.DMA((3,)),
        ],
        leaving=3,
        flops=4 * 9 * gate_count * channels * cells,
        moved=4_000_000,
        transcendentals=5 * hid * cells,
    )(
        rows,
        inner,
        outer,
        permuted(columns, inner_columns),
        permuted(columns, outer_columns),
        cell_here,
        weights_here,
        hidden_grad_here,
        target_here,
        land_here,
        fire_here,
        bias_wide,
        readout_wide,
    )

    pre_inner, pre_outer = permuted(pre_inner, inner_rows), permuted(pre_outer, outer_rows)
    pre_columns = call(bind(pre_columns_kernel, row_count), sds((gate_count, width), BF16))(
        pre, pre_inner, pre_outer
    )
    grad_inputs, grad_hidden, field_done = call(
        bind(field_kernel, place),
        (
            sds((channels - hid, row_count, width), BF16),
            sds((hid, row_count, width), BF16),
            sds((8, width), F32),
        ),
        [
            pltpu.VMEM((3 * gate_count, halo_cells), BF16),
            pltpu.VMEM((3, channels, 3 * gate_count), BF16),
            pltpu.VMEM((channels * row_count, width), F32),
        ],
        flops=2 * 9 * gate_count * channels * cells,
        moved=2_000_000,
    )(
        pre,
        pre_inner,
        pre_outer,
        permuted(pre_columns, inner_columns),
        permuted(pre_columns, outer_columns),
        weights_here,
    )

    def plane_exchange(value):
        return lax.all_to_all(value, PLANE, 0, 0, tiled=True)

    phases = len(place.orders[0])
    after = [target_here] * phases
    after[1] = pre_columns
    after[2] = field_done
    block_shape = (BIAS_ROWS + place.chunk, channels)
    parts = call(
        bind(pair_kernel, place),
        sds((place.plane, *block_shape), BF16),
        [pltpu.VMEM((place.half_rows, channels), F32)],
    )(keep, bias, permuted(send, place.phase_pairs(0)))
    block = call(plane_kernel, sds(block_shape, BF16))(plane_exchange(parts), target_here)
    for phase in range(1, phases):
        received = permuted(block, place.phase_pairs(phase))
        is_last = phase == phases - 1
        shape = (place.plane, *block_shape) if is_last else block_shape
        block = call(bind(add_kernel, scaling if is_last else 1.0), sds(shape, BF16))(
            block, received, after[phase]
        )
    gathered = plane_exchange(block)
    received = permuted(gathered, place.phase_pairs(0))
    half = [pltpu.VMEM((place.half_rows, channels), F32)]
    grad_kernel = call(
        bind(own_half_kernel, place),
        (sds((place.rows, channels), F32),),
        half + [pltpu.SemaphoreType.DMA((1,))],
        leaving=1,
        moved=6 * place.half_rows * channels,
    )(gathered)[0]
    grad_kernel, grad_bias = call(
        bind(other_half_kernel, place),
        (sds((place.rows, channels), F32), sds((gate_count,), F32)),
        half + [pltpu.VMEM((gate_count,), F32), pltpu.SemaphoreType.DMA((2,))],
        remote=1,
        leaving=2,
        aliases={2: 0},
        moved=6 * place.half_rows * channels,
    )(gathered, received, grad_kernel)
    shape = hidden_prev.shape
    return (
        hidden_next,
        cell_next.reshape(shape),
        grad_inputs,
        grad_hidden,
        grad_cell.reshape(shape),
        grad_kernel[: 9 * gate_count].reshape(kernel_weights.shape),
        grad_bias,
    )


def solution(mesh):
    lat_count, lon_count = mesh.shape["lat"], mesh.shape["lon"]
    split = Mesh(mesh.devices.reshape(lat_count // 2, 2, lon_count // 2, 2), AXES)
    field = P(None, ("band", "core"), ("reach", "near"))
    flat = P(("band", "core"), ("reach", "near"))

    def run(*args):
        place = Layout(lat_count, lon_count, args[3].shape[0] * args[3].shape[1])
        return jax.shard_map(
            functools.partial(body, place),
            mesh=split,
            in_specs=(field, field, field, P(), P(), P(), flat, flat, flat, field),
            out_specs=(field, field, field, field, field, P(), P()),
            check_vma=False,
        )(*args)

    return run
```

```python
import functools
import math

import jax
import jax.numpy as jnp
from jax import lax
from jax.experimental import pallas as pl
from jax.experimental.pallas import tpu as pltpu
from jax.sharding import Mesh, PartitionSpec as P

F32 = jnp.float32
BF16 = jnp.bfloat16
AXES = ("band", "core", "reach", "near")
BIAS_ROWS = 16
LAST = 16
VMEM = pl.BlockSpec(memory_space=pltpu.VMEM)
HBM = pl.BlockSpec(memory_space=pltpu.HBM)
ACROSS = (((1,), (1,)), ((), ()))


def sds(shape, dtype):
    return jax.ShapeDtypeStruct(shape, dtype)


def call(
    kernel,
    out_shape,
    scratch=(),
    remote=0,
    leaving=0,
    aliases=None,
    flops=0,
    moved=0,
    transcendentals=0,
):
    several = isinstance(out_shape, tuple)
    shapes = out_shape if several else (out_shape,)
    out_specs = tuple([HBM] * leaving + [VMEM] * (len(shapes) - leaving))

    def run(*args):
        near = len(args) - remote
        far = [pltpu.with_memory_space_constraint(arg, pltpu.HBM) for arg in args[near:]]
        return pl.pallas_call(
            kernel,
            out_shape=out_shape,
            in_specs=[VMEM] * near + [HBM] * remote,
            out_specs=out_specs if several else out_specs[0],
            input_output_aliases=aliases or {},
            scratch_shapes=list(scratch),
            cost_estimate=pl.CostEstimate(
                flops=flops, bytes_accessed=moved, transcendentals=transcendentals
            ),
            compiler_params=pltpu.CompilerParams(vmem_limit_bytes=24 * 1024 * 1024),
        )(*args[:near], *far)

    return run


class Layout:
    def __init__(self, lat_count, lon_count, kernel_rows):
        self.lat, self.lon = lat_count, lon_count
        self.half = lon_count // 2
        self.plane = lat_count
        whole = [("lon", 1 << k) for k in range(1, lon_count.bit_length() - 1)]
        self.orders = ([("lat", 1)] + whole, [("lat", 1)] + whole[::-1])
        step = 16 * self.plane
        self.rows = -(-kernel_rows // step) * step
        self.half_rows = self.rows // 2
        self.chunk = self.half_rows // self.plane

    def position(self):
        lat = 2 * lax.axis_index("band") + lax.axis_index("core")
        return lat, 2 * lax.axis_index("reach") + lax.axis_index("near")

    def rank(self, phase):
        lat, lon = self.position()

        def digit(order):
            axis, bit = order[phase]
            return ((lat if axis == "lat" else lon) // bit) % 2

        return jnp.where(lat % 2 == 0, digit(self.orders[0]), digit(self.orders[1]))

    def pairs(self, partner):
        result = []
        for lat in range(self.lat):
            for lon in range(self.lon):
                there = partner(lat, lon)
                result.append((lat * self.lon + lon, there[0] * self.lon + there[1]))
        return result

    def phase_pairs(self, phase):
        def partner(lat, lon):
            axis, bit = self.orders[lat % 2][phase]
            return (lat ^ bit, lon) if axis == "lat" else (lat, lon ^ bit)

        return self.pairs(partner)

    def plane_rank(self):
        return 2 * lax.axis_index("band") + lax.axis_index("near")

    def plane_pairs(self, step):
        def partner(lat, lon):
            there = (lat // 2 * 2 + lon % 2) ^ step
            return there // 2 * 2 + lat % 2, lon // 2 * 2 + there % 2

        return self.pairs(partner)

    def inner_rows(self, lat, lon):
        return lat ^ 1, lon

    def outer_rows(self, lat, lon):
        there = lat + 1 if lat % 2 else lat - 1
        if 0 <= there < self.lat:
            return there, lon
        return lat, (lon + self.half) % self.lon

    def inner_columns(self, lat, lon):
        return lat, lon ^ 1

    def outer_columns(self, lat, lon):
        return lat, (lon + (1 if lon % 2 else -1)) % self.lon


def permuted(value, pairs):
    return lax.ppermute(value, AXES, pairs)


def lanes(shape):
    return lax.broadcasted_iota(jnp.int32, shape, len(shape) - 1)


def rolled(value, shift):
    shift %= value.shape[1]
    return pltpu.roll(value, shift, 1) if shift else value


def edge_columns(row, position, columns):
    lane = lanes(row.shape)
    columns = jnp.where(lane == position, rolled(row, position), columns)
    return jnp.where(lane == LAST + position, rolled(row, LAST + position + 1), columns)


def pick(flag, yes, no):
    return jnp.where(flag, yes, no)


def is_odd(axis):
    return lax.axis_index(axis) % 2 == 1


def row_sends(first, last, inner_out, outer_out):
    odd = is_odd("core")
    inner_out[...] = pick(odd, first, last).astype(BF16)
    outer_out[...] = pick(odd, last, first).astype(BF16)


def row_halo(inner, outer):
    odd = is_odd("core")
    inner, outer = inner[...].astype(F32), outer[...].astype(F32)
    return pick(odd, inner, outer), pick(odd, outer, inner)


def column_halo(inner, outer):
    odd = is_odd("near")
    inner, outer = inner[...].astype(F32), outer[...].astype(F32)
    return pick(odd, inner, outer), pick(odd, outer, inner)


def widened(row_count, rows, row_blocks, column_blocks, emit):
    north, south = row_halo(*row_blocks)
    west, east = column_halo(*column_blocks)
    width = west.shape[1]
    lane = lanes(west.shape)
    for position in range(row_count + 2):
        if position == 0:
            row = north
        elif position == row_count + 1:
            row = south
        else:
            row = rows(position - 1)
        left = rolled(west, -LAST - position)
        right = rolled(east, width - 1 - position)
        emit(
            position,
            jnp.where(lane == 0, left, rolled(row, 1)),
            row,
            jnp.where(lane == width - 1, right, rolled(row, -1)),
        )


def pack_kernel(below, hidden, inner_out, outer_out, wide_out, below_here, hidden_here, arrived):
    first = pltpu.make_async_copy(below, below_here, arrived.at[0])
    second = pltpu.make_async_copy(hidden, hidden_here, arrived.at[1])
    first.start()
    second.start()
    channels, row_count, width = below.shape
    size = channels * row_count
    first.wait()
    wide_out[0:size, :] = below_here[...].astype(F32).reshape(size, width)
    second.wait()
    wide_out[size : 2 * size, :] = hidden_here[...].astype(F32).reshape(size, width)
    edges = [
        wide_out[pl.ds(index, 2 * channels, stride=row_count), :] for index in (0, row_count - 1)
    ]
    row_sends(edges[0], edges[1], inner_out, outer_out)


def down_rows(values, width):
    count = values.shape[0]
    return jnp.broadcast_to(values[None, :], (width, count)).T


def prepare_kernel(
    wide,
    cell_hbm,
    weights_hbm,
    hidden_grad_hbm,
    target_hbm,
    land_hbm,
    fire_hbm,
    gate_bias_hbm,
    readout_hbm,
    rows_out,
    columns_out,
    cell_out,
    weights_out,
    hidden_grad_out,
    target_out,
    land_out,
    fire_out,
    bias_wide_out,
    readout_wide_out,
    hidden_grad_here,
    gate_bias_here,
    readout_here,
    arrived,
):
    copies = [
        pltpu.make_async_copy(source, target, arrived.at[index])
        for index, (source, target) in enumerate(
            (
                (cell_hbm, cell_out),
                (weights_hbm, weights_out),
                (hidden_grad_hbm, hidden_grad_here),
                (target_hbm, target_out),
                (land_hbm, land_out),
                (fire_hbm, fire_out),
                (gate_bias_hbm, gate_bias_here),
                (readout_hbm, readout_here),
            )
        )
    ]
    for copy in copies:
        copy.start()
    row_count, channels, width = rows_out.shape
    columns = jnp.zeros((channels, width), F32)
    for index in range(row_count):
        row = wide[pl.ds(index, channels, stride=row_count), :]
        rows_out[index] = row.astype(BF16)
        columns = edge_columns(row, index + 1, columns)
    columns_out[...] = columns
    for copy in copies:
        copy.wait()
    hidden_grad_out[...] = hidden_grad_here[...].astype(F32).reshape(hidden_grad_out.shape)
    bias_wide_out[...] = down_rows(gate_bias_here[...], width)
    readout_wide_out[...] = down_rows(readout_here[...], width)


def columns_kernel(row_count, columns, inner, outer, out):
    north, south = row_halo(inner, outer)
    value = edge_columns(north, 0, columns[...])
    out[...] = edge_columns(south, row_count + 1, value).astype(BF16)


def pre_columns_kernel(row_count, pre, inner, outer, out):
    width = out.shape[1]
    north, south = row_halo(inner, outer)
    value = edge_columns(north, 0, jnp.zeros(north.shape, F32))
    for index in range(row_count):
        row = pre[:, pl.ds(index * width, width)].astype(F32)
        value = edge_columns(row, index + 1, value)
    out[...] = edge_columns(south, row_count + 1, value).astype(BF16)


def encode(bias):
    high = bias.astype(BF16).astype(F32)
    return jnp.concatenate([high, bias - high], axis=0)


def decode(block):
    return block[0:8] + block[8:16]


def split_sum(place, phase, bias, sums, rows, send_out, keep_out):
    half = rows // 2
    rank = place.rank(phase)
    send_out[0:BIAS_ROWS, :] = encode(bias).astype(BF16)
    away = pl.ds(pl.multiple_of((1 - rank) * half, 8), half)
    send_out[BIAS_ROWS:, :] = sums[away, :].astype(BF16)
    keep_out[...] = sums[pl.ds(pl.multiple_of(rank * half, 8), half), :]


def gates_kernel(
    place,
    rows_in,
    inner_row,
    outer_row,
    inner_column,
    outer_column,
    cell_prev,
    weights,
    hidden_grad,
    target,
    land,
    fire,
    bias_wide,
    readout_wide,
    hidden_hbm,
    cell_hbm,
    grad_cell_hbm,
    pre_out,
    inner_out,
    outer_out,
    send_out,
    keep_out,
    bias_out,
    shifted,
    hidden_wide,
    hidden_low,
    cell_out,
    grad_cell_out,
    sums,
    left,
):
    row_count, channels, width = rows_in.shape
    gate_count = weights.shape[1]
    hid = gate_count // 4

    def emit(position, left, row, right):
        at = pl.ds(position * width, width)
        shifted[0:channels, at] = left.astype(BF16)
        shifted[channels : 2 * channels, at] = row.astype(BF16)
        shifted[2 * channels : 3 * channels, at] = right.astype(BF16)

    widened(
        row_count,
        lambda index: rows_in[index].astype(F32),
        (inner_row, outer_row),
        (inner_column, outer_column),
        emit,
    )

    taps = [
        jnp.concatenate([weights[3 * a], weights[3 * a + 1], weights[3 * a + 2]], axis=1)
        for a in range(3)
    ]
    bias_total = jnp.zeros((gate_count, width), F32)
    edges = []
    readout = readout_wide[...]
    pair = 2 if row_count % 2 == 0 else 1
    for base in range(0, row_count, pair):
        preact = jnp.zeros((gate_count, pair * width), F32)
        for a in range(3):
            preact += jnp.dot(
                taps[a],
                shifted[:, pl.ds((base + a) * width, pair * width)],
                preferred_element_type=F32,
            )
        for offset in range(pair):
            index = base + offset
            strided = pl.ds(index, hid, stride=row_count)
            part = preact[:, offset * width : (offset + 1) * width] + bias_wide[...]
            input_gate = 0.5 + 0.5 * jnp.tanh(0.5 * part[0:hid])
            forget_gate = 0.5 + 0.5 * jnp.tanh(0.5 * part[hid : 2 * hid])
            output_gate = 0.5 + 0.5 * jnp.tanh(0.5 * part[2 * hid : 3 * hid])
            candidate = jnp.tanh(part[3 * hid : 4 * hid])
            cell_before = cell_prev[strided, :]
            land_row = land[index : index + 1, :].astype(F32)
            fire_row = fire[index : index + 1, :].astype(F32)
            cell_next = land_row * (forget_gate * cell_before + input_gate * candidate)
            squashed = jnp.tanh(cell_next)
            hidden_next = (output_gate * squashed).astype(BF16).astype(F32)
            predicted = jnp.sum(readout * hidden_next, axis=0, keepdims=True)
            miss = 2.0 * (fire_row * (predicted - target[index : index + 1, :]))
            total_grad = hidden_grad[strided, :] + miss * readout
            cell_grad = land_row * total_grad * output_gate * (1.0 - squashed * squashed)
            cell_out[strided, :] = cell_next
            hidden_wide[strided, :] = hidden_next
            grad_cell_out[strided, :] = cell_grad * forget_gate
            pre_grad = jnp.concatenate(
                [
                    cell_grad * candidate * input_gate * (1.0 - input_gate),
                    cell_grad * cell_before * forget_gate * (1.0 - forget_gate),
                    total_grad * squashed * output_gate * (1.0 - output_gate),
                    cell_grad * input_gate * (1.0 - candidate * candidate),
                ],
                axis=0,
            )
            bias_total += pre_grad
            pre_out[:, pl.ds(index * width, width)] = pre_grad.astype(BF16)
            if index in (0, row_count - 1):
                edges.append(pre_grad)
    hidden_low[...] = hidden_wide[...].reshape(hidden_low.shape).astype(BF16)
    leaving = [
        pltpu.make_async_copy(source, target, left.at[index])
        for index, (source, target) in enumerate(
            ((hidden_low, hidden_hbm), (cell_out, cell_hbm), (grad_cell_out, grad_cell_hbm))
        )
    ]
    for copy in leaving:
        copy.start()
    row_sends(edges[0], edges[-1], inner_out, outer_out)

    for a in range(3):
        product = lax.dot_general(
            pre_out[...],
            shifted[:, pl.ds(a * width, row_count * width)],
            ACROSS,
            preferred_element_type=F32,
        )
        for b in range(3):
            at = (3 * a + b) * gate_count
            sums[at : at + gate_count, :] = product[:, b * channels : (b + 1) * channels]
    used = 9 * gate_count
    if place.rows > used:
        sums[used:, :] = jnp.zeros((place.rows - used, channels), F32)

    ones = jnp.ones((8, width), BF16)
    high = bias_total.astype(BF16)
    low = (bias_total - high.astype(F32)).astype(BF16)
    flat = lax.dot_general(ones, high, ACROSS, preferred_element_type=F32)
    flat += lax.dot_general(ones, low, ACROSS, preferred_element_type=F32)
    odd = lax.broadcasted_iota(jnp.int32, (8, channels), 0) % 2 == 1
    bias_rows = jnp.where(odd, flat[:, channels : 2 * channels], flat[:, 0:channels])
    bias_out[...] = bias_rows
    split_sum(place, 0, bias_rows, sums, place.rows, send_out, keep_out)
    for copy in leaving:
        copy.wait()


def pair_kernel(place, keep, bias, received, *outs):
    sends, keep_out, bias_out, scratch = outs[:-3], outs[-3], outs[-2], outs[-1]
    chunk = place.chunk
    rank = place.plane_rank()
    scratch[...] = keep[...] + received[BIAS_ROWS:, :].astype(F32)
    bias_total = bias[...] + decode(received[0:BIAS_ROWS, :].astype(F32))
    block = encode(bias_total).astype(BF16)
    for step, send in enumerate(sends, 1):
        send[0:BIAS_ROWS, :] = block
        at = pl.ds(pl.multiple_of((rank ^ step) * chunk, 8), chunk)
        send[BIAS_ROWS:, :] = scratch[at, :].astype(BF16)
    keep_out[...] = scratch[pl.ds(pl.multiple_of(rank * chunk, 8), chunk), :]
    bias_out[...] = bias_total


def plane_kernel(keep, bias, *refs):
    received, out = refs[:-2], refs[-1]
    total, bias_total = keep[...], bias[...]
    for ref in received:
        total += ref[BIAS_ROWS:, :].astype(F32)
        bias_total += decode(ref[0:BIAS_ROWS, :].astype(F32))
    out[0:BIAS_ROWS, :] = encode(bias_total).astype(BF16)
    out[BIAS_ROWS:, :] = total.astype(BF16)


def join_kernel(place, *refs):
    blocks, out = refs[:-2], refs[-1]
    rank = place.plane_rank()
    for step, block in enumerate(blocks):
        out[rank ^ step] = block[...]


def add_kernel(scale, own, received, out, done_out):
    here, there = own[...].astype(F32), received[...].astype(F32)
    bias = (decode(here[0:BIAS_ROWS]) + decode(there[0:BIAS_ROWS])) * scale
    out[0:BIAS_ROWS, :] = encode(bias).astype(BF16)
    out[BIAS_ROWS:, :] = ((here[BIAS_ROWS:] + there[BIAS_ROWS:]) * scale).astype(BF16)
    done_out[...] = jnp.zeros(done_out.shape, F32)


def unpack(blocks, wide):
    chunk = blocks.shape[1] - BIAS_ROWS
    for index in range(blocks.shape[0]):
        wide[index * chunk : (index + 1) * chunk, :] = blocks[index, BIAS_ROWS:, :].astype(F32)


def own_half_kernel(place, own, out, wide, left):
    unpack(own, wide)
    at = pl.ds(pl.multiple_of(place.rank(0) * place.half_rows, 8), place.half_rows)
    copy = pltpu.make_async_copy(wide, out.at[at, :], left.at[0])
    copy.start()
    copy.wait()


def other_half_kernel(place, own, received, out_before, out, bias_out, wide, bias_here, left):
    del out_before
    rank = place.rank(0)
    here, there = own[0, 0:BIAS_ROWS, :].astype(F32), received[0, 0:BIAS_ROWS, :].astype(F32)
    bias = decode(pick(rank == 1, there, here))
    width = bias.shape[1]
    for index in range(bias_here.shape[0] // width):
        bias_here[pl.ds(index * width, width)] = bias[index]
    bias_copy = pltpu.make_async_copy(bias_here, bias_out, left.at[1])
    bias_copy.start()
    unpack(received, wide)
    at = pl.ds(pl.multiple_of((1 - rank) * place.half_rows, 8), place.half_rows)
    copy = pltpu.make_async_copy(wide, out.at[at, :], left.at[0])
    copy.start()
    bias_copy.wait()
    copy.wait()


def field_kernel(
    place,
    pre,
    inner_row,
    outer_row,
    inner_column,
    outer_column,
    weights,
    after,
    inputs_out,
    hidden_out,
    done_out,
    shifted,
    turned,
    wide,
):
    del after
    gate_count = pre.shape[0]
    channels = weights.shape[2]
    done_out[...] = jnp.zeros(done_out.shape, F32)
    hid, row_count, width = hidden_out.shape

    def emit(position, left, row, right):
        at = pl.ds(position * width, width)
        shifted[0:gate_count, at] = right.astype(BF16)
        shifted[gate_count : 2 * gate_count, at] = row.astype(BF16)
        shifted[2 * gate_count : 3 * gate_count, at] = left.astype(BF16)

    widened(
        row_count,
        lambda index: pre[:, pl.ds(index * width, width)].astype(F32),
        (inner_row, outer_row),
        (inner_column, outer_column),
        emit,
    )
    for a in range(3):
        for b in range(3):
            turned[a, :, b * gate_count : (b + 1) * gate_count] = weights[3 * a + b].T
    lat = place.position()[0]
    top = turned[jnp.where(lat == 0, 0, 2)]
    bottom = turned[jnp.where(lat == place.lat - 1, 2, 0)]

    def product(matrix, position, count):
        return jnp.dot(
            matrix, shifted[:, pl.ds(position * width, count * width)], preferred_element_type=F32
        )

    pair = 2 if row_count % 2 == 0 else 1
    for base in range(0, row_count, pair):
        total = product(turned[1], base + 1, pair)
        if base == 0:
            above = product(top, 0, 1)
            if pair == 2:
                above = jnp.concatenate([above, product(turned[2], 1, 1)], axis=1)
        else:
            above = product(turned[2], base, pair)
        if base + pair == row_count:
            below = product(bottom, row_count + 1, 1)
            if pair == 2:
                below = jnp.concatenate([product(turned[0], row_count, 1), below], axis=1)
        else:
            below = product(turned[0], base + 2, pair)
        total = total + above + below
        for offset in range(pair):
            value = total[:, offset * width : (offset + 1) * width]
            wide[pl.ds(base + offset, channels, stride=row_count), :] = value
    size = (channels - hid) * row_count
    inputs_out[...] = wide[0:size, :].reshape(inputs_out.shape).astype(BF16)
    hidden_out[...] = wide[size:, :].reshape(hidden_out.shape).astype(BF16)


def body(
    place,
    inputs_below,
    hidden_prev,
    cell_prev,
    kernel_weights,
    gate_bias,
    readout,
    target_field,
    land_mask,
    fire_mask,
    hidden_grad,
):
    hid, row_count, width = hidden_prev.shape
    gate_count, channels = kernel_weights.shape[1:]
    cells = row_count * width
    halo_cells = (row_count + 2) * width
    scaling = 1.0 / math.sqrt(cells * place.lat * place.lon)
    bind = functools.partial
    inner_rows, outer_rows = place.pairs(place.inner_rows), place.pairs(place.outer_rows)
    inner_columns = place.pairs(place.inner_columns)
    outer_columns = place.pairs(place.outer_columns)
    flat = sds((hid * row_count, width), F32)

    inner, outer, wide = call(
        pack_kernel,
        (
            sds((channels, width), BF16),
            sds((channels, width), BF16),
            sds((channels * row_count, width), F32),
        ),
        [
            pltpu.VMEM(inputs_below.shape, BF16),
            pltpu.VMEM(hidden_prev.shape, BF16),
            pltpu.SemaphoreType.DMA((2,)),
        ],
        remote=2,
        moved=4 * channels * cells,
    )(inputs_below, hidden_prev)
    inner, outer = permuted(inner, inner_rows), permuted(outer, outer_rows)
    (
        rows,
        columns,
        cell_here,
        weights_here,
        hidden_grad_here,
        target_here,
        land_here,
        fire_here,
        bias_wide,
        readout_wide,
    ) = call(
        prepare_kernel,
        (
            sds((row_count, channels, width), BF16),
            sds((channels, width), F32),
            flat,
            sds(kernel_weights.shape, BF16),
            flat,
            sds(target_field.shape, F32),
            sds(land_mask.shape, jnp.int32),
            sds(fire_mask.shape, jnp.int32),
            sds((gate_count, width), F32),
            sds((hid, width), F32),
        ),
        [
            pltpu.VMEM(hidden_grad.shape, BF16),
            pltpu.VMEM(gate_bias.shape, F32),
            pltpu.VMEM(readout.shape, F32),
            pltpu.SemaphoreType.DMA((8,)),
        ],
        remote=8,
        moved=6_000_000,
    )(
        wide,
        cell_prev.reshape(hid * row_count, width),
        kernel_weights,
        hidden_grad,
        target_field,
        land_mask,
        fire_mask,
        gate_bias,
        readout,
    )
    columns = call(bind(columns_kernel, row_count), sds((channels, width), BF16))(
        columns, inner, outer
    )

    (
        hidden_next,
        cell_next,
        grad_cell,
        pre,
        pre_inner,
        pre_outer,
        send,
        keep,
        bias,
    ) = call(
        bind(gates_kernel, place),
        (
            sds((hid, row_count, width), BF16),
            flat,
            flat,
            sds((gate_count, cells), BF16),
            sds((gate_count, width), BF16),
            sds((gate_count, width), BF16),
            sds((BIAS_ROWS + place.half_rows, channels), BF16),
            sds((place.half_rows, channels), F32),
            sds((8, channels), F32),
        ),
        [
            pltpu.VMEM((3 * channels, halo_cells), BF16),
            pltpu.VMEM((hid * row_count, width), F32),
            pltpu.VMEM((hid, row_count, width), BF16),
            pltpu.VMEM((hid * row_count, width), F32),
            pltpu.VMEM((hid * row_count, width), F32),
            pltpu.VMEM((place.rows, channels), F32),
            pltpu.SemaphoreType.DMA((3,)),
        ],
        leaving=3,
        flops=4 * 9 * gate_count * channels * cells,
        moved=4_000_000,
        transcendentals=5 * hid * cells,
    )(
        rows,
        inner,
        outer,
        permuted(columns, inner_columns),
        permuted(columns, outer_columns),
        cell_here,
        weights_here,
        hidden_grad_here,
        target_here,
        land_here,
        fire_here,
        bias_wide,
        readout_wide,
    )

    pre_inner, pre_outer = permuted(pre_inner, inner_rows), permuted(pre_outer, outer_rows)
    pre_columns = call(bind(pre_columns_kernel, row_count), sds((gate_count, width), BF16))(
        pre, pre_inner, pre_outer
    )
    block = sds((BIAS_ROWS + place.chunk, channels), BF16)
    token = sds((8, width), F32)
    steps = range(1, place.plane)
    *sends, keep, bias = call(
        bind(pair_kernel, place),
        (*[block for _ in steps], sds((place.chunk, channels), F32), sds((8, channels), F32)),
        [pltpu.VMEM((place.half_rows, channels), F32)],
    )(keep, bias, permuted(send, place.phase_pairs(0)))
    received = [permuted(send, place.plane_pairs(step)) for step, send in zip(steps, sends)]
    part = call(plane_kernel, block)(keep, bias, *received, pre_columns)
    pre_inner_columns = permuted(pre_columns, inner_columns)
    pre_outer_columns = permuted(pre_columns, outer_columns)
    phases = len(place.orders[0])
    for phase in range(1, phases):
        is_last = phase == phases - 1
        part, summed = call(bind(add_kernel, scaling if is_last else 1.0), (block, token))(
            part,
            permuted(part, place.phase_pairs(phase)),
        )
    grad_inputs, grad_hidden, field_done = call(
        bind(field_kernel, place),
        (
            sds((channels - hid, row_count, width), BF16),
            sds((hid, row_count, width), BF16),
            sds((8, width), F32),
        ),
        [
            pltpu.VMEM((3 * gate_count, halo_cells), BF16),
            pltpu.VMEM((3, channels, 3 * gate_count), BF16),
            pltpu.VMEM((channels * row_count, width), F32),
        ],
        flops=2 * 9 * gate_count * channels * cells,
        moved=2_000_000,
    )(
        pre,
        pre_inner,
        pre_outer,
        pre_inner_columns,
        pre_outer_columns,
        weights_here,
        summed,
    )
    received = [permuted(part, place.plane_pairs(step)) for step in steps]
    gathered = call(bind(join_kernel, place), sds((place.plane, *block.shape), BF16))(
        part, *received, field_done
    )
    received = permuted(gathered, place.phase_pairs(0))
    half = [pltpu.VMEM((place.half_rows, channels), F32)]
    grad_kernel = call(
        bind(own_half_kernel, place),
        (sds((place.rows, channels), F32),),
        half + [pltpu.SemaphoreType.DMA((1,))],
        leaving=1,
        moved=6 * place.half_rows * channels,
    )(gathered)[0]
    grad_kernel, grad_bias = call(
        bind(other_half_kernel, place),
        (sds((place.rows, channels), F32), sds((gate_count,), F32)),
        half + [pltpu.VMEM((gate_count,), F32), pltpu.SemaphoreType.DMA((2,))],
        remote=1,
        leaving=2,
        aliases={2: 0},
        moved=6 * place.half_rows * channels,
    )(gathered, received, grad_kernel)
    shape = hidden_prev.shape
    return (
        hidden_next,
        cell_next.reshape(shape),
        grad_inputs,
        grad_hidden,
        grad_cell.reshape(shape),
        grad_kernel[: 9 * gate_count].reshape(kernel_weights.shape),
        grad_bias,
    )


def solution(mesh):
    lat_count, lon_count = mesh.shape["lat"], mesh.shape["lon"]
    split = Mesh(mesh.devices.reshape(lat_count // 2, 2, lon_count // 2, 2), AXES)
    field = P(None, ("band", "core"), ("reach", "near"))
    flat = P(("band", "core"), ("reach", "near"))

    def run(*args):
        place = Layout(lat_count, lon_count, args[3].shape[0] * args[3].shape[1])
        return jax.shard_map(
            functools.partial(body, place),
            mesh=split,
            in_specs=(field, field, field, P(), P(), P(), flat, flat, flat, field),
            out_specs=(field, field, field, field, field, P(), P()),
            check_vma=False,
        )(*args)

    return run
```

```python
import functools
import math

import jax
import jax.numpy as jnp
from jax import lax
from jax.experimental import pallas as pl
from jax.experimental.pallas import tpu as pltpu
from jax.sharding import Mesh, PartitionSpec as P

F32 = jnp.float32
BF16 = jnp.bfloat16
AXES = ("band", "core", "reach", "near")
BIAS_ROWS = 16
LAST = 16
VMEM = pl.BlockSpec(memory_space=pltpu.VMEM)
HBM = pl.BlockSpec(memory_space=pltpu.HBM)
ACROSS = (((1,), (1,)), ((), ()))


def sds(shape, dtype):
    return jax.ShapeDtypeStruct(shape, dtype)


def call(
    kernel,
    out_shape,
    scratch=(),
    remote=0,
    leaving=0,
    aliases=None,
    flops=0,
    moved=0,
    transcendentals=0,
):
    several = isinstance(out_shape, tuple)
    shapes = out_shape if several else (out_shape,)
    out_specs = tuple([HBM] * leaving + [VMEM] * (len(shapes) - leaving))

    def run(*args):
        near = len(args) - remote
        far = [pltpu.with_memory_space_constraint(arg, pltpu.HBM) for arg in args[near:]]
        return pl.pallas_call(
            kernel,
            out_shape=out_shape,
            in_specs=[VMEM] * near + [HBM] * remote,
            out_specs=out_specs if several else out_specs[0],
            input_output_aliases=aliases or {},
            scratch_shapes=list(scratch),
            cost_estimate=pl.CostEstimate(
                flops=flops, bytes_accessed=moved, transcendentals=transcendentals
            ),
            compiler_params=pltpu.CompilerParams(vmem_limit_bytes=24 * 1024 * 1024),
        )(*args[:near], *far)

    return run


class Layout:
    def __init__(self, lat_count, lon_count, kernel_rows):
        self.lat, self.lon = lat_count, lon_count
        self.half = lon_count // 2
        self.plane = lat_count
        whole = [("lon", 1 << k) for k in range(1, lon_count.bit_length() - 1)]
        self.orders = ([("lat", 1)] + whole, [("lat", 1)] + whole[::-1])
        step = 16 * self.plane
        self.rows = -(-kernel_rows // step) * step
        self.half_rows = self.rows // 2
        self.chunk = self.half_rows // self.plane

    def position(self):
        lat = 2 * lax.axis_index("band") + lax.axis_index("core")
        return lat, 2 * lax.axis_index("reach") + lax.axis_index("near")

    def rank(self, phase):
        lat, lon = self.position()

        def digit(order):
            axis, bit = order[phase]
            return ((lat if axis == "lat" else lon) // bit) % 2

        return jnp.where(lat % 2 == 0, digit(self.orders[0]), digit(self.orders[1]))

    def pairs(self, partner):
        result = []
        for lat in range(self.lat):
            for lon in range(self.lon):
                there = partner(lat, lon)
                result.append((lat * self.lon + lon, there[0] * self.lon + there[1]))
        return result

    def phase_pairs(self, phase):
        def partner(lat, lon):
            axis, bit = self.orders[lat % 2][phase]
            return (lat ^ bit, lon) if axis == "lat" else (lat, lon ^ bit)

        return self.pairs(partner)

    def plane_rank(self):
        return 2 * lax.axis_index("band") + lax.axis_index("near")

    def plane_pairs(self, step):
        def partner(lat, lon):
            there = (lat // 2 * 2 + lon % 2) ^ step
            return there // 2 * 2 + lat % 2, lon // 2 * 2 + there % 2

        return self.pairs(partner)

    def inner_rows(self, lat, lon):
        return lat ^ 1, lon

    def outer_rows(self, lat, lon):
        there = lat + 1 if lat % 2 else lat - 1
        if 0 <= there < self.lat:
            return there, lon
        return lat, (lon + self.half) % self.lon

    def inner_columns(self, lat, lon):
        return lat, lon ^ 1

    def outer_columns(self, lat, lon):
        return lat, (lon + (1 if lon % 2 else -1)) % self.lon


def permuted(value, pairs):
    return lax.ppermute(value, AXES, pairs)


def lanes(shape):
    return lax.broadcasted_iota(jnp.int32, shape, len(shape) - 1)


def rolled(value, shift):
    shift %= value.shape[1]
    return pltpu.roll(value, shift, 1) if shift else value


def edge_columns(row, position, columns):
    lane = lanes(row.shape)
    columns = jnp.where(lane == position, rolled(row, position), columns)
    return jnp.where(lane == LAST + position, rolled(row, LAST + position + 1), columns)


def pick(flag, yes, no):
    return jnp.where(flag, yes, no)


def is_odd(axis):
    return lax.axis_index(axis) % 2 == 1


def row_sends(first, last, inner_out, outer_out):
    odd = is_odd("core")
    inner_out[...] = pick(odd, first, last).astype(BF16)
    outer_out[...] = pick(odd, last, first).astype(BF16)


def row_halo(inner, outer):
    odd = is_odd("core")
    inner, outer = inner[...].astype(F32), outer[...].astype(F32)
    return pick(odd, inner, outer), pick(odd, outer, inner)


def column_halo(inner, outer):
    odd = is_odd("near")
    inner, outer = inner[...].astype(F32), outer[...].astype(F32)
    return pick(odd, inner, outer), pick(odd, outer, inner)


def widened(row_count, rows, row_blocks, column_blocks, emit):
    north, south = row_halo(*row_blocks)
    west, east = column_halo(*column_blocks)
    width = west.shape[1]
    lane = lanes(west.shape)
    for position in range(row_count + 2):
        if position == 0:
            row = north
        elif position == row_count + 1:
            row = south
        else:
            row = rows(position - 1)
        left = rolled(west, -LAST - position)
        right = rolled(east, width - 1 - position)
        emit(
            position,
            jnp.where(lane == 0, left, rolled(row, 1)),
            row,
            jnp.where(lane == width - 1, right, rolled(row, -1)),
        )


def pack_kernel(below, hidden, inner_out, outer_out, wide_out, below_here, hidden_here, arrived):
    first = pltpu.make_async_copy(below, below_here, arrived.at[0])
    second = pltpu.make_async_copy(hidden, hidden_here, arrived.at[1])
    first.start()
    second.start()
    channels, row_count, width = below.shape
    size = channels * row_count
    first.wait()
    wide_out[0:size, :] = below_here[...].astype(F32).reshape(size, width)
    second.wait()
    wide_out[size : 2 * size, :] = hidden_here[...].astype(F32).reshape(size, width)
    edges = [
        wide_out[pl.ds(index, 2 * channels, stride=row_count), :] for index in (0, row_count - 1)
    ]
    row_sends(edges[0], edges[1], inner_out, outer_out)


def down_rows(values, width):
    count = values.shape[0]
    return jnp.broadcast_to(values[None, :], (width, count)).T


def prepare_kernel(
    wide,
    cell_hbm,
    weights_hbm,
    hidden_grad_hbm,
    target_hbm,
    land_hbm,
    fire_hbm,
    gate_bias_hbm,
    readout_hbm,
    rows_out,
    columns_out,
    cell_out,
    weights_out,
    hidden_grad_out,
    target_out,
    land_out,
    fire_out,
    bias_wide_out,
    readout_wide_out,
    hidden_grad_here,
    gate_bias_here,
    readout_here,
    arrived,
):
    copies = [
        pltpu.make_async_copy(source, target, arrived.at[index])
        for index, (source, target) in enumerate(
            (
                (cell_hbm, cell_out),
                (weights_hbm, weights_out),
                (hidden_grad_hbm, hidden_grad_here),
                (target_hbm, target_out),
                (land_hbm, land_out),
                (fire_hbm, fire_out),
                (gate_bias_hbm, gate_bias_here),
                (readout_hbm, readout_here),
            )
        )
    ]
    for copy in copies:
        copy.start()
    row_count, channels, width = rows_out.shape
    columns = jnp.zeros((channels, width), F32)
    for index in range(row_count):
        row = wide[pl.ds(index, channels, stride=row_count), :]
        rows_out[index] = row.astype(BF16)
        columns = edge_columns(row, index + 1, columns)
    columns_out[...] = columns
    for copy in copies:
        copy.wait()
    hidden_grad_out[...] = hidden_grad_here[...].astype(F32).reshape(hidden_grad_out.shape)
    bias_wide_out[...] = down_rows(gate_bias_here[...], width)
    readout_wide_out[...] = down_rows(readout_here[...], width)


def columns_kernel(row_count, columns, inner, outer, out):
    north, south = row_halo(inner, outer)
    value = edge_columns(north, 0, columns[...])
    out[...] = edge_columns(south, row_count + 1, value).astype(BF16)


def pre_columns_kernel(row_count, pre, inner, outer, out):
    width = out.shape[1]
    north, south = row_halo(inner, outer)
    value = edge_columns(north, 0, jnp.zeros(north.shape, F32))
    for index in range(row_count):
        row = pre[:, pl.ds(index * width, width)].astype(F32)
        value = edge_columns(row, index + 1, value)
    out[...] = edge_columns(south, row_count + 1, value).astype(BF16)


def encode(bias):
    high = bias.astype(BF16).astype(F32)
    return jnp.concatenate([high, bias - high], axis=0)


def decode(block):
    return block[0:8] + block[8:16]


def split_sum(place, phase, bias, sums, rows, send_out, keep_out):
    half = rows // 2
    rank = place.rank(phase)
    send_out[0:BIAS_ROWS, :] = encode(bias).astype(BF16)
    away = pl.ds(pl.multiple_of((1 - rank) * half, 8), half)
    send_out[BIAS_ROWS:, :] = sums[away, :].astype(BF16)
    keep_out[...] = sums[pl.ds(pl.multiple_of(rank * half, 8), half), :]


def gates_kernel(
    place,
    rows_in,
    inner_row,
    outer_row,
    inner_column,
    outer_column,
    cell_prev,
    weights,
    hidden_grad,
    target,
    land,
    fire,
    bias_wide,
    readout_wide,
    hidden_hbm,
    cell_hbm,
    grad_cell_hbm,
    pre_out,
    inner_out,
    outer_out,
    send_out,
    keep_out,
    bias_out,
    shifted,
    hidden_wide,
    hidden_low,
    cell_out,
    grad_cell_out,
    sums,
    left,
):
    row_count, channels, width = rows_in.shape
    gate_count = weights.shape[1]
    hid = gate_count // 4

    def emit(position, left, row, right):
        at = pl.ds(position * width, width)
        shifted[0:channels, at] = left.astype(BF16)
        shifted[channels : 2 * channels, at] = row.astype(BF16)
        shifted[2 * channels : 3 * channels, at] = right.astype(BF16)

    widened(
        row_count,
        lambda index: rows_in[index].astype(F32),
        (inner_row, outer_row),
        (inner_column, outer_column),
        emit,
    )

    taps = [
        jnp.concatenate([weights[3 * a], weights[3 * a + 1], weights[3 * a + 2]], axis=1)
        for a in range(3)
    ]
    bias_total = jnp.zeros((gate_count, width), F32)
    edges = []
    readout = readout_wide[...]
    pair = 2 if row_count % 2 == 0 else 1
    for base in range(0, row_count, pair):
        preact = jnp.zeros((gate_count, pair * width), F32)
        for a in range(3):
            preact += jnp.dot(
                taps[a],
                shifted[:, pl.ds((base + a) * width, pair * width)],
                preferred_element_type=F32,
            )
        for offset in range(pair):
            index = base + offset
            strided = pl.ds(index, hid, stride=row_count)
            part = preact[:, offset * width : (offset + 1) * width] + bias_wide[...]
            input_gate = 0.5 + 0.5 * jnp.tanh(0.5 * part[0:hid])
            forget_gate = 0.5 + 0.5 * jnp.tanh(0.5 * part[hid : 2 * hid])
            output_gate = 0.5 + 0.5 * jnp.tanh(0.5 * part[2 * hid : 3 * hid])
            candidate = jnp.tanh(part[3 * hid : 4 * hid])
            cell_before = cell_prev[strided, :]
            land_row = land[index : index + 1, :].astype(F32)
            fire_row = fire[index : index + 1, :].astype(F32)
            cell_next = land_row * (forget_gate * cell_before + input_gate * candidate)
            squashed = jnp.tanh(cell_next)
            hidden_next = (output_gate * squashed).astype(BF16).astype(F32)
            predicted = jnp.sum(readout * hidden_next, axis=0, keepdims=True)
            miss = 2.0 * (fire_row * (predicted - target[index : index + 1, :]))
            total_grad = hidden_grad[strided, :] + miss * readout
            cell_grad = land_row * total_grad * output_gate * (1.0 - squashed * squashed)
            cell_out[strided, :] = cell_next
            hidden_wide[strided, :] = hidden_next
            grad_cell_out[strided, :] = cell_grad * forget_gate
            pre_grad = jnp.concatenate(
                [
                    cell_grad * candidate * input_gate * (1.0 - input_gate),
                    cell_grad * cell_before * forget_gate * (1.0 - forget_gate),
                    total_grad * squashed * output_gate * (1.0 - output_gate),
                    cell_grad * input_gate * (1.0 - candidate * candidate),
                ],
                axis=0,
            )
            bias_total += pre_grad
            pre_out[:, pl.ds(index * width, width)] = pre_grad.astype(BF16)
            if index in (0, row_count - 1):
                edges.append(pre_grad)
    hidden_low[...] = hidden_wide[...].reshape(hidden_low.shape).astype(BF16)
    leaving = [
        pltpu.make_async_copy(source, target, left.at[index])
        for index, (source, target) in enumerate(
            ((hidden_low, hidden_hbm), (cell_out, cell_hbm), (grad_cell_out, grad_cell_hbm))
        )
    ]
    for copy in leaving:
        copy.start()
    row_sends(edges[0], edges[-1], inner_out, outer_out)

    for a in range(3):
        product = lax.dot_general(
            pre_out[...],
            shifted[:, pl.ds(a * width, row_count * width)],
            ACROSS,
            preferred_element_type=F32,
        )
        for b in range(3):
            at = (3 * a + b) * gate_count
            sums[at : at + gate_count, :] = product[:, b * channels : (b + 1) * channels]
    used = 9 * gate_count
    if place.rows > used:
        sums[used:, :] = jnp.zeros((place.rows - used, channels), F32)

    ones = jnp.ones((8, width), BF16)
    high = bias_total.astype(BF16)
    low = (bias_total - high.astype(F32)).astype(BF16)
    flat = lax.dot_general(ones, high, ACROSS, preferred_element_type=F32)
    flat += lax.dot_general(ones, low, ACROSS, preferred_element_type=F32)
    odd = lax.broadcasted_iota(jnp.int32, (8, channels), 0) % 2 == 1
    bias_rows = jnp.where(odd, flat[:, channels : 2 * channels], flat[:, 0:channels])
    bias_out[...] = bias_rows
    split_sum(place, 0, bias_rows, sums, place.rows, send_out, keep_out)
    for copy in leaving:
        copy.wait()


def pair_kernel(place, keep, bias, received, *outs):
    sends, keep_out, bias_out, scratch = outs[:-3], outs[-3], outs[-2], outs[-1]
    chunk = place.chunk
    rank = place.plane_rank()
    scratch[...] = keep[...] + received[BIAS_ROWS:, :].astype(F32)
    bias_total = bias[...] + decode(received[0:BIAS_ROWS, :].astype(F32))
    block = encode(bias_total).astype(BF16)
    for step, send in enumerate(sends, 1):
        send[0:BIAS_ROWS, :] = block
        at = pl.ds(pl.multiple_of((rank ^ step) * chunk, 8), chunk)
        send[BIAS_ROWS:, :] = scratch[at, :].astype(BF16)
    keep_out[...] = scratch[pl.ds(pl.multiple_of(rank * chunk, 8), chunk), :]
    bias_out[...] = bias_total


def plane_kernel(keep, bias, *refs):
    received, out = refs[:-1], refs[-1]
    total, bias_total = keep[...], bias[...]
    for ref in received:
        total += ref[BIAS_ROWS:, :].astype(F32)
        bias_total += decode(ref[0:BIAS_ROWS, :].astype(F32))
    out[0:BIAS_ROWS, :] = encode(bias_total).astype(BF16)
    out[BIAS_ROWS:, :] = total.astype(BF16)


def join_kernel(place, *refs):
    blocks, out = refs[:-2], refs[-1]
    rank = place.plane_rank()
    for step, block in enumerate(blocks):
        out[rank ^ step] = block[...]


def add_kernel(scale, own, received, out, *done_out):
    here, there = own[...].astype(F32), received[...].astype(F32)
    bias = (decode(here[0:BIAS_ROWS]) + decode(there[0:BIAS_ROWS])) * scale
    out[0:BIAS_ROWS, :] = encode(bias).astype(BF16)
    out[BIAS_ROWS:, :] = ((here[BIAS_ROWS:] + there[BIAS_ROWS:]) * scale).astype(BF16)
    for done in done_out:
        done[...] = jnp.zeros(done.shape, F32)


def unpack(blocks, wide):
    chunk = blocks.shape[1] - BIAS_ROWS
    for index in range(blocks.shape[0]):
        wide[index * chunk : (index + 1) * chunk, :] = blocks[index, BIAS_ROWS:, :].astype(F32)


def own_half_kernel(place, own, out, wide, left):
    unpack(own, wide)
    at = pl.ds(pl.multiple_of(place.rank(0) * place.half_rows, 8), place.half_rows)
    copy = pltpu.make_async_copy(wide, out.at[at, :], left.at[0])
    copy.start()
    copy.wait()


def other_half_kernel(place, own, received, out_before, out, bias_out, wide, bias_here, left):
    del out_before
    rank = place.rank(0)
    here, there = own[0, 0:BIAS_ROWS, :].astype(F32), received[0, 0:BIAS_ROWS, :].astype(F32)
    bias = decode(pick(rank == 1, there, here))
    width = bias.shape[1]
    for index in range(bias_here.shape[0] // width):
        bias_here[pl.ds(index * width, width)] = bias[index]
    bias_copy = pltpu.make_async_copy(bias_here, bias_out, left.at[1])
    bias_copy.start()
    unpack(received, wide)
    at = pl.ds(pl.multiple_of((1 - rank) * place.half_rows, 8), place.half_rows)
    copy = pltpu.make_async_copy(wide, out.at[at, :], left.at[0])
    copy.start()
    bias_copy.wait()
    copy.wait()


def field_kernel(
    place,
    pre,
    inner_row,
    outer_row,
    inner_column,
    outer_column,
    weights,
    after,
    inputs_out,
    hidden_out,
    done_out,
    shifted,
    turned,
    wide,
):
    del after
    gate_count = pre.shape[0]
    channels = weights.shape[2]
    done_out[...] = jnp.zeros(done_out.shape, F32)
    hid, row_count, width = hidden_out.shape

    def emit(position, left, row, right):
        at = pl.ds(position * width, width)
        shifted[0:gate_count, at] = right.astype(BF16)
        shifted[gate_count : 2 * gate_count, at] = row.astype(BF16)
        shifted[2 * gate_count : 3 * gate_count, at] = left.astype(BF16)

    widened(
        row_count,
        lambda index: pre[:, pl.ds(index * width, width)].astype(F32),
        (inner_row, outer_row),
        (inner_column, outer_column),
        emit,
    )
    for a in range(3):
        for b in range(3):
            turned[a, :, b * gate_count : (b + 1) * gate_count] = weights[3 * a + b].T
    lat = place.position()[0]
    top = turned[jnp.where(lat == 0, 0, 2)]
    bottom = turned[jnp.where(lat == place.lat - 1, 2, 0)]

    def product(matrix, position, count):
        return jnp.dot(
            matrix, shifted[:, pl.ds(position * width, count * width)], preferred_element_type=F32
        )

    pair = 2 if row_count % 2 == 0 else 1
    for base in range(0, row_count, pair):
        total = product(turned[1], base + 1, pair)
        if base == 0:
            above = product(top, 0, 1)
            if pair == 2:
                above = jnp.concatenate([above, product(turned[2], 1, 1)], axis=1)
        else:
            above = product(turned[2], base, pair)
        if base + pair == row_count:
            below = product(bottom, row_count + 1, 1)
            if pair == 2:
                below = jnp.concatenate([product(turned[0], row_count, 1), below], axis=1)
        else:
            below = product(turned[0], base + 2, pair)
        total = total + above + below
        for offset in range(pair):
            value = total[:, offset * width : (offset + 1) * width]
            wide[pl.ds(base + offset, channels, stride=row_count), :] = value
    size = (channels - hid) * row_count
    inputs_out[...] = wide[0:size, :].reshape(inputs_out.shape).astype(BF16)
    hidden_out[...] = wide[size:, :].reshape(hidden_out.shape).astype(BF16)


def body(
    place,
    inputs_below,
    hidden_prev,
    cell_prev,
    kernel_weights,
    gate_bias,
    readout,
    target_field,
    land_mask,
    fire_mask,
    hidden_grad,
):
    hid, row_count, width = hidden_prev.shape
    gate_count, channels = kernel_weights.shape[1:]
    cells = row_count * width
    halo_cells = (row_count + 2) * width
    scaling = 1.0 / math.sqrt(cells * place.lat * place.lon)
    bind = functools.partial
    inner_rows, outer_rows = place.pairs(place.inner_rows), place.pairs(place.outer_rows)
    inner_columns = place.pairs(place.inner_columns)
    outer_columns = place.pairs(place.outer_columns)
    flat = sds((hid * row_count, width), F32)

    inner, outer, wide = call(
        pack_kernel,
        (
            sds((channels, width), BF16),
            sds((channels, width), BF16),
            sds((channels * row_count, width), F32),
        ),
        [
            pltpu.VMEM(inputs_below.shape, BF16),
            pltpu.VMEM(hidden_prev.shape, BF16),
            pltpu.SemaphoreType.DMA((2,)),
        ],
        remote=2,
        moved=4 * channels * cells,
    )(inputs_below, hidden_prev)
    inner, outer = permuted(inner, inner_rows), permuted(outer, outer_rows)
    (
        rows,
        columns,
        cell_here,
        weights_here,
        hidden_grad_here,
        target_here,
        land_here,
        fire_here,
        bias_wide,
        readout_wide,
    ) = call(
        prepare_kernel,
        (
            sds((row_count, channels, width), BF16),
            sds((channels, width), F32),
            flat,
            sds(kernel_weights.shape, BF16),
            flat,
            sds(target_field.shape, F32),
            sds(land_mask.shape, jnp.int32),
            sds(fire_mask.shape, jnp.int32),
            sds((gate_count, width), F32),
            sds((hid, width), F32),
        ),
        [
            pltpu.VMEM(hidden_grad.shape, BF16),
            pltpu.VMEM(gate_bias.shape, F32),
            pltpu.VMEM(readout.shape, F32),
            pltpu.SemaphoreType.DMA((8,)),
        ],
        remote=8,
        moved=6_000_000,
    )(
        wide,
        cell_prev.reshape(hid * row_count, width),
        kernel_weights,
        hidden_grad,
        target_field,
        land_mask,
        fire_mask,
        gate_bias,
        readout,
    )
    columns = call(bind(columns_kernel, row_count), sds((channels, width), BF16))(
        columns, inner, outer
    )

    (
        hidden_next,
        cell_next,
        grad_cell,
        pre,
        pre_inner,
        pre_outer,
        send,
        keep,
        bias,
    ) = call(
        bind(gates_kernel, place),
        (
            sds((hid, row_count, width), BF16),
            flat,
            flat,
            sds((gate_count, cells), BF16),
            sds((gate_count, width), BF16),
            sds((gate_count, width), BF16),
            sds((BIAS_ROWS + place.half_rows, channels), BF16),
            sds((place.half_rows, channels), F32),
            sds((8, channels), F32),
        ),
        [
            pltpu.VMEM((3 * channels, halo_cells), BF16),
            pltpu.VMEM((hid * row_count, width), F32),
            pltpu.VMEM((hid, row_count, width), BF16),
            pltpu.VMEM((hid * row_count, width), F32),
            pltpu.VMEM((hid * row_count, width), F32),
            pltpu.VMEM((place.rows, channels), F32),
            pltpu.SemaphoreType.DMA((3,)),
        ],
        leaving=3,
        flops=4 * 9 * gate_count * channels * cells,
        moved=4_000_000,
        transcendentals=5 * hid * cells,
    )(
        rows,
        inner,
        outer,
        permuted(columns, inner_columns),
        permuted(columns, outer_columns),
        cell_here,
        weights_here,
        hidden_grad_here,
        target_here,
        land_here,
        fire_here,
        bias_wide,
        readout_wide,
    )

    pre_inner, pre_outer = permuted(pre_inner, inner_rows), permuted(pre_outer, outer_rows)
    pre_columns = call(bind(pre_columns_kernel, row_count), sds((gate_count, width), BF16))(
        pre, pre_inner, pre_outer
    )
    block = sds((BIAS_ROWS + place.chunk, channels), BF16)
    token = sds((8, width), F32)
    steps = range(1, place.plane)
    *sends, keep, bias = call(
        bind(pair_kernel, place),
        (*[block for _ in steps], sds((place.chunk, channels), F32), sds((8, channels), F32)),
        [pltpu.VMEM((place.half_rows, channels), F32)],
    )(keep, bias, permuted(send, place.phase_pairs(0)))
    received = [permuted(send, place.plane_pairs(step)) for step, send in zip(steps, sends)]
    part = call(plane_kernel, block)(keep, bias, *received)
    pre_inner_columns = permuted(pre_columns, inner_columns)
    pre_outer_columns = permuted(pre_columns, outer_columns)
    phases = len(place.orders[0])
    for phase in range(1, phases):
        is_last = phase == phases - 1
        part, *summed = call(
            bind(add_kernel, scaling if is_last else 1.0), (block, token) if is_last else (block,)
        )(part, permuted(part, place.phase_pairs(phase)))
    grad_inputs, grad_hidden, field_done = call(
        bind(field_kernel, place),
        (
            sds((channels - hid, row_count, width), BF16),
            sds((hid, row_count, width), BF16),
            sds((8, width), F32),
        ),
        [
            pltpu.VMEM((3 * gate_count, halo_cells), BF16),
            pltpu.VMEM((3, channels, 3 * gate_count), BF16),
            pltpu.VMEM((channels * row_count, width), F32),
        ],
        flops=2 * 9 * gate_count * channels * cells,
        moved=2_000_000,
    )(
        pre,
        pre_inner,
        pre_outer,
        pre_inner_columns,
        pre_outer_columns,
        weights_here,
        *summed,
    )
    received = [permuted(part, place.plane_pairs(step)) for step in steps]
    gathered = call(bind(join_kernel, place), sds((place.plane, *block.shape), BF16))(
        part, *received, field_done
    )
    received = permuted(gathered, place.phase_pairs(0))
    half = [pltpu.VMEM((place.half_rows, channels), F32)]
    grad_kernel = call(
        bind(own_half_kernel, place),
        (sds((place.rows, channels), F32),),
        half + [pltpu.SemaphoreType.DMA((1,))],
        leaving=1,
        moved=6 * place.half_rows * channels,
    )(gathered)[0]
    grad_kernel, grad_bias = call(
        bind(other_half_kernel, place),
        (sds((place.rows, channels), F32), sds((gate_count,), F32)),
        half + [pltpu.VMEM((gate_count,), F32), pltpu.SemaphoreType.DMA((2,))],
        remote=1,
        leaving=2,
        aliases={2: 0},
        moved=6 * place.half_rows * channels,
    )(gathered, received, grad_kernel)
    shape = hidden_prev.shape
    return (
        hidden_next,
        cell_next.reshape(shape),
        grad_inputs,
        grad_hidden,
        grad_cell.reshape(shape),
        grad_kernel[: 9 * gate_count].reshape(kernel_weights.shape),
        grad_bias,
    )


def solution(mesh):
    lat_count, lon_count = mesh.shape["lat"], mesh.shape["lon"]
    split = Mesh(mesh.devices.reshape(lat_count // 2, 2, lon_count // 2, 2), AXES)
    field = P(None, ("band", "core"), ("reach", "near"))
    flat = P(("band", "core"), ("reach", "near"))

    def run(*args):
        place = Layout(lat_count, lon_count, args[3].shape[0] * args[3].shape[1])
        return jax.shard_map(
            functools.partial(body, place),
            mesh=split,
            in_specs=(field, field, field, P(), P(), P(), flat, flat, flat, field),
            out_specs=(field, field, field, field, field, P(), P()),
            check_vma=False,
        )(*args)

    return run
```

```python
import functools
import math

import jax
import jax.numpy as jnp
from jax import lax
from jax.experimental import pallas as pl
from jax.experimental.pallas import tpu as pltpu
from jax.sharding import Mesh, PartitionSpec as P

F32 = jnp.float32
BF16 = jnp.bfloat16
AXES = ("band", "core", "reach", "near")
BIAS_ROWS = 16
LAST = 16
VMEM = pl.BlockSpec(memory_space=pltpu.VMEM)
HBM = pl.BlockSpec(memory_space=pltpu.HBM)
ACROSS = (((1,), (1,)), ((), ()))


def sds(shape, dtype):
    return jax.ShapeDtypeStruct(shape, dtype)


def call(
    kernel,
    out_shape,
    scratch=(),
    remote=0,
    leaving=0,
    aliases=None,
    flops=0,
    moved=0,
    transcendentals=0,
):
    several = isinstance(out_shape, tuple)
    shapes = out_shape if several else (out_shape,)
    out_specs = tuple([HBM] * leaving + [VMEM] * (len(shapes) - leaving))

    def run(*args):
        near = len(args) - remote
        far = [pltpu.with_memory_space_constraint(arg, pltpu.HBM) for arg in args[near:]]
        return pl.pallas_call(
            kernel,
            out_shape=out_shape,
            in_specs=[VMEM] * near + [HBM] * remote,
            out_specs=out_specs if several else out_specs[0],
            input_output_aliases=aliases or {},
            scratch_shapes=list(scratch),
            cost_estimate=pl.CostEstimate(
                flops=flops, bytes_accessed=moved, transcendentals=transcendentals
            ),
            compiler_params=pltpu.CompilerParams(vmem_limit_bytes=24 * 1024 * 1024),
        )(*args[:near], *far)

    return run


class Layout:
    def __init__(self, lat_count, lon_count, taps, gate_count):
        self.lat, self.lon = lat_count, lon_count
        self.half = lon_count // 2
        self.taps, self.half_gates = taps, gate_count // 2
        self.plane = lat_count
        whole = [("lon", 1 << k) for k in range(1, lon_count.bit_length() - 1)]
        self.orders = ([("lat", 1)] + whole, [("lat", 1)] + whole[::-1])
        step = 8 * self.plane
        self.half_rows = -(-taps * self.half_gates // step) * step
        self.chunk = self.half_rows // self.plane

    def position(self):
        lat = 2 * lax.axis_index("band") + lax.axis_index("core")
        return lat, 2 * lax.axis_index("reach") + lax.axis_index("near")

    def rank(self, phase):
        lat, lon = self.position()

        def digit(order):
            axis, bit = order[phase]
            return ((lat if axis == "lat" else lon) // bit) % 2

        return jnp.where(lat % 2 == 0, digit(self.orders[0]), digit(self.orders[1]))

    def pairs(self, partner):
        result = []
        for lat in range(self.lat):
            for lon in range(self.lon):
                there = partner(lat, lon)
                result.append((lat * self.lon + lon, there[0] * self.lon + there[1]))
        return result

    def phase_pairs(self, phase):
        def partner(lat, lon):
            axis, bit = self.orders[lat % 2][phase]
            return (lat ^ bit, lon) if axis == "lat" else (lat, lon ^ bit)

        return self.pairs(partner)

    def plane_rank(self):
        return 2 * lax.axis_index("band") + lax.axis_index("near")

    def plane_pairs(self, step):
        def partner(lat, lon):
            there = (lat // 2 * 2 + lon % 2) ^ step
            return there // 2 * 2 + lat % 2, lon // 2 * 2 + there % 2

        return self.pairs(partner)

    def inner_rows(self, lat, lon):
        return lat ^ 1, lon

    def outer_rows(self, lat, lon):
        there = lat + 1 if lat % 2 else lat - 1
        if 0 <= there < self.lat:
            return there, lon
        return lat, (lon + self.half) % self.lon

    def inner_columns(self, lat, lon):
        return lat, lon ^ 1

    def outer_columns(self, lat, lon):
        return lat, (lon + (1 if lon % 2 else -1)) % self.lon


def permuted(value, pairs):
    return lax.ppermute(value, AXES, pairs)


def lanes(shape):
    return lax.broadcasted_iota(jnp.int32, shape, len(shape) - 1)


def rolled(value, shift):
    shift %= value.shape[1]
    return pltpu.roll(value, shift, 1) if shift else value


def edge_columns(row, position, columns):
    lane = lanes(row.shape)
    columns = jnp.where(lane == position, rolled(row, position), columns)
    return jnp.where(lane == LAST + position, rolled(row, LAST + position + 1), columns)


def second_columns(row, position, columns):
    lane = lanes(row.shape)
    columns = jnp.where(lane == position, rolled(row, position - 1), columns)
    return jnp.where(lane == LAST + position, rolled(row, LAST + position + 2), columns)


def at_edges(row, position, columns):
    lane = lanes(row.shape)
    width = row.shape[1]
    row = jnp.where(lane == 0, rolled(columns, -position), row)
    return jnp.where(lane == width - 1, rolled(columns, width - 1 - LAST - position), row)


def pick(flag, yes, no):
    return jnp.where(flag, yes, no)


def is_odd(axis):
    return lax.axis_index(axis) % 2 == 1


def row_sends(first, last, inner_out, outer_out):
    odd = is_odd("core")
    inner_out[...] = pick(odd, first, last).astype(BF16)
    outer_out[...] = pick(odd, last, first).astype(BF16)


def row_halo(inner, outer):
    odd = is_odd("core")
    inner, outer = inner[...].astype(F32), outer[...].astype(F32)
    return pick(odd, inner, outer), pick(odd, outer, inner)


def column_halo(inner, outer):
    odd = is_odd("near")
    inner, outer = inner[...].astype(F32), outer[...].astype(F32)
    return pick(odd, inner, outer), pick(odd, outer, inner)


def widened(row_count, rows, row_blocks, column_blocks, emit):
    north, south = row_halo(*row_blocks)
    west, east = column_halo(*column_blocks)
    width = west.shape[1]
    lane = lanes(west.shape)
    for position in range(row_count + 2):
        if position == 0:
            row = north
        elif position == row_count + 1:
            row = south
        else:
            row = rows(position - 1)
        left = rolled(west, -LAST - position)
        right = rolled(east, width - 1 - position)
        emit(
            position,
            jnp.where(lane == 0, left, rolled(row, 1)),
            row,
            jnp.where(lane == width - 1, right, rolled(row, -1)),
        )


def pack_kernel(below, hidden, inner_out, outer_out, wide_out, below_here, hidden_here, arrived):
    first = pltpu.make_async_copy(below, below_here, arrived.at[0])
    second = pltpu.make_async_copy(hidden, hidden_here, arrived.at[1])
    first.start()
    second.start()
    channels, row_count, width = below.shape
    size = channels * row_count
    first.wait()
    wide_out[0:size, :] = below_here[...].astype(F32).reshape(size, width)
    second.wait()
    wide_out[size : 2 * size, :] = hidden_here[...].astype(F32).reshape(size, width)
    edges = [
        wide_out[pl.ds(index, 2 * channels, stride=row_count), :] for index in (0, row_count - 1)
    ]
    row_sends(edges[0], edges[1], inner_out, outer_out)


def down_rows(values, width):
    count = values.shape[0]
    return jnp.broadcast_to(values[None, :], (width, count)).T


def prepare_kernel(
    wide,
    cell_hbm,
    weights_hbm,
    hidden_grad_hbm,
    target_hbm,
    land_hbm,
    fire_hbm,
    gate_bias_hbm,
    readout_hbm,
    rows_out,
    columns_out,
    second_out,
    cell_strip_out,
    hidden_grad_strip_out,
    fields_strip_out,
    cell_out,
    weights_out,
    hidden_grad_out,
    target_out,
    land_out,
    fire_out,
    bias_wide_out,
    readout_wide_out,
    hidden_grad_here,
    gate_bias_here,
    readout_here,
    arrived,
):
    copies = [
        pltpu.make_async_copy(source, target, arrived.at[index])
        for index, (source, target) in enumerate(
            (
                (cell_hbm, cell_out),
                (weights_hbm, weights_out),
                (hidden_grad_hbm, hidden_grad_here),
                (target_hbm, target_out),
                (land_hbm, land_out),
                (fire_hbm, fire_out),
                (gate_bias_hbm, gate_bias_here),
                (readout_hbm, readout_here),
            )
        )
    ]
    for copy in copies:
        copy.start()
    row_count, channels, width = rows_out.shape
    columns = jnp.zeros((channels, width), F32)
    second = jnp.zeros((channels, width), F32)
    for index in range(row_count):
        row = wide[pl.ds(index, channels, stride=row_count), :]
        rows_out[index] = row.astype(BF16)
        columns = edge_columns(row, index + 1, columns)
        second = second_columns(row, index + 1, second)
    columns_out[...] = columns
    second_out[...] = second
    for copy in copies:
        copy.wait()
    hidden_grad_out[...] = hidden_grad_here[...].astype(F32).reshape(hidden_grad_out.shape)
    bias_wide_out[...] = down_rows(gate_bias_here[...], width)
    readout_wide_out[...] = down_rows(readout_here[...], width)
    hid = hidden_grad_here.shape[0]
    cell_strip = jnp.zeros((hid, width), F32)
    hidden_grad_strip = jnp.zeros((hid, width), F32)
    fields_strip = jnp.zeros((8, width), F32)
    for index in range(row_count):
        strided = pl.ds(index, hid, stride=row_count)
        cell_strip = edge_columns(cell_out[strided, :], index + 1, cell_strip)
        hidden_grad_strip = edge_columns(hidden_grad_out[strided, :], index + 1, hidden_grad_strip)
        at = slice(index, index + 1)
        fields = [target_out[at, :], land_out[at, :].astype(F32), fire_out[at, :].astype(F32)]
        fields = jnp.concatenate(fields + [jnp.zeros((5, width), F32)], axis=0)
        fields_strip = edge_columns(fields, index + 1, fields_strip)
    cell_strip_out[...] = cell_strip
    hidden_grad_strip_out[...] = hidden_grad_strip
    fields_strip_out[...] = fields_strip


def columns_kernel(row_count, columns, inner, outer, out):
    north, south = row_halo(inner, outer)
    value = edge_columns(north, 0, columns[...].astype(F32))
    out[...] = edge_columns(south, row_count + 1, value).astype(BF16)


def encode(bias):
    high = bias.astype(BF16).astype(F32)
    return jnp.concatenate([high, bias - high], axis=0)


def decode(block):
    return block[0:8] + block[8:16]


def cell_step(part, cell_before, hidden_grad, target, land, fire, readout):
    hid = part.shape[0] // 4
    input_gate = 0.5 + 0.5 * jnp.tanh(0.5 * part[0:hid])
    forget_gate = 0.5 + 0.5 * jnp.tanh(0.5 * part[hid : 2 * hid])
    output_gate = 0.5 + 0.5 * jnp.tanh(0.5 * part[2 * hid : 3 * hid])
    candidate = jnp.tanh(part[3 * hid : 4 * hid])
    cell_next = land * (forget_gate * cell_before + input_gate * candidate)
    squashed = jnp.tanh(cell_next)
    hidden_next = (output_gate * squashed).astype(BF16).astype(F32)
    predicted = jnp.sum(readout * hidden_next, axis=0, keepdims=True)
    total_grad = hidden_grad + 2.0 * (fire * (predicted - target)) * readout
    cell_grad = land * total_grad * output_gate * (1.0 - squashed * squashed)
    pre_grad = jnp.concatenate(
        [
            cell_grad * candidate * input_gate * (1.0 - input_gate),
            cell_grad * cell_before * forget_gate * (1.0 - forget_gate),
            total_grad * squashed * output_gate * (1.0 - output_gate),
            cell_grad * input_gate * (1.0 - candidate * candidate),
        ],
        axis=0,
    )
    return hidden_next, cell_next, cell_grad * forget_gate, pre_grad


def gates_kernel(
    place,
    rows_in,
    inner_row,
    outer_row,
    second,
    cell_prev,
    weights,
    hidden_grad,
    target,
    land,
    fire,
    bias_wide,
    readout_wide,
    hidden_out,
    cell_out,
    grad_cell_out,
    pre_out,
    second_out,
    sums,
    bias_out,
    shifted,
):
    row_count, channels, width = rows_in.shape
    gate_count = weights.shape[1]
    hid = gate_count // 4
    half_gates = place.half_gates
    north, south = row_halo(inner_row, outer_row)
    columns = second_columns(north, 0, second[...])
    second_out[...] = second_columns(south, row_count + 1, columns).astype(BF16)
    for position in range(row_count + 2):
        if position == 0:
            row = north
        elif position == row_count + 1:
            row = south
        else:
            row = rows_in[position - 1].astype(F32)
        at = pl.ds(position * width, width)
        shifted[0:channels, at] = rolled(row, 1).astype(BF16)
        shifted[channels : 2 * channels, at] = row.astype(BF16)
        shifted[2 * channels : 3 * channels, at] = rolled(row, -1).astype(BF16)

    taps = [
        jnp.concatenate([weights[3 * a], weights[3 * a + 1], weights[3 * a + 2]], axis=1)
        for a in range(3)
    ]
    bias_total = jnp.zeros((gate_count, width), F32)
    lane = lanes((gate_count, width))
    inside = (lane > 0) & (lane < width - 1)
    readout = readout_wide[...]
    pair = 2 if row_count % 2 == 0 else 1
    for base in range(0, row_count, pair):
        preact = jnp.zeros((gate_count, pair * width), F32)
        for a in range(3):
            preact += jnp.dot(
                taps[a],
                shifted[:, pl.ds((base + a) * width, pair * width)],
                preferred_element_type=F32,
            )
        for offset in range(pair):
            index = base + offset
            strided = pl.ds(index, hid, stride=row_count)
            at = slice(index, index + 1)
            hidden_next, cell_next, grad_cell, pre_grad = cell_step(
                preact[:, offset * width : (offset + 1) * width] + bias_wide[...],
                cell_prev[strided, :],
                hidden_grad[strided, :],
                target[at, :],
                land[at, :].astype(F32),
                fire[at, :].astype(F32),
                readout,
            )
            hidden_out[strided, :] = hidden_next
            cell_out[strided, :] = cell_next
            grad_cell_out[strided, :] = grad_cell
            pre_grad = jnp.where(inside, pre_grad, 0.0)
            bias_total += pre_grad
            pre_out[:, pl.ds(index * width, width)] = pre_grad.astype(BF16)
    bias_out[...] = bias_total

    for a in range(3):
        product = lax.dot_general(
            pre_out[...],
            shifted[:, pl.ds(a * width, row_count * width)],
            ACROSS,
            preferred_element_type=F32,
        )
        for b in range(3):
            for half in range(2):
                at = half * place.half_rows + (3 * a + b) * half_gates
                sums[at : at + half_gates, :] = product[
                    half * half_gates : (half + 1) * half_gates, b * channels : (b + 1) * channels
                ]
    used = place.taps * half_gates
    if place.half_rows > used:
        for half in range(2):
            at = half * place.half_rows
            sums[at + used : at + place.half_rows, :] = jnp.zeros(
                (place.half_rows - used, channels), F32
            )


def add_strip(place, half, sums, pre_strip, patches, out, start):
    half_gates, channels = place.half_gates, sums.shape[1]
    gates = pre_strip[pl.ds(pl.multiple_of(half * half_gates, half_gates), half_gates), :]
    product = lax.dot_general(gates, patches[...], ACROSS, preferred_element_type=F32)
    base = half * place.half_rows
    for tap in range(place.taps):
        at = pl.ds(pl.multiple_of(base + tap * half_gates, 8), half_gates)
        value = sums[at, :] + product[:, tap * channels : (tap + 1) * channels]
        to = start + tap * half_gates
        out[to : to + half_gates, :] = value.astype(out.dtype)
    used = place.taps * half_gates
    if place.half_rows > used:
        rest = jnp.zeros((place.half_rows - used, channels), out.dtype)
        out[start + used : start + place.half_rows, :] = rest


def strip_kernel(
    place,
    row_count,
    edge,
    second,
    inner_column,
    outer_column,
    weights,
    bias_wide,
    readout_wide,
    cell_strip,
    hidden_grad_strip,
    fields_strip,
    sums,
    bias_partial,
    send_out,
    bias_out,
    pre_out,
    patches,
    hidden_out,
    cell_out,
    grad_cell_out,
):
    channels, width = edge.shape
    west, east = column_halo(inner_column, outer_column)
    near_first = lanes((channels, width)) < LAST
    inner = second[...].astype(F32)
    columns = (
        jnp.where(near_first, rolled(west, -LAST), inner),
        edge[...].astype(F32),
        jnp.where(near_first, inner, rolled(east, LAST)),
    )
    for a in range(3):
        for b in range(3):
            at = (3 * a + b) * channels
            patches[at : at + channels, :] = rolled(columns[b], 1 - a).astype(BF16)
    taps = jnp.concatenate([weights[tap] for tap in range(place.taps)], axis=1)
    preact = jnp.dot(taps, patches[...], preferred_element_type=F32) + bias_wide[...]
    hidden_next, cell_next, grad_cell, pre_grad = cell_step(
        preact,
        cell_strip[...],
        hidden_grad_strip[...],
        fields_strip[0:1, :],
        fields_strip[1:2, :],
        fields_strip[2:3, :],
        readout_wide[...],
    )
    hidden_out[...] = hidden_next
    cell_out[...] = cell_next
    grad_cell_out[...] = grad_cell
    lane = lanes(pre_grad.shape)
    lane = jnp.where(lane >= LAST, lane - LAST, lane)
    pre_grad = jnp.where((lane >= 1) & (lane <= row_count), pre_grad, 0.0)
    pre_out[...] = pre_grad.astype(BF16)
    rank = place.rank(0)
    add_strip(place, 1 - rank, sums, pre_out, patches, send_out, BIAS_ROWS)

    bias_total = bias_partial[...] + pre_grad
    ones = jnp.ones((8, width), BF16)
    high = bias_total.astype(BF16)
    low = (bias_total - high.astype(F32)).astype(BF16)
    flat = lax.dot_general(ones, high, ACROSS, preferred_element_type=F32)
    flat += lax.dot_general(ones, low, ACROSS, preferred_element_type=F32)
    odd = lax.broadcasted_iota(jnp.int32, (8, channels), 0) % 2 == 1
    bias_rows = jnp.where(odd, flat[:, channels : 2 * channels], flat[:, 0:channels])
    bias_out[...] = bias_rows
    send_out[0:BIAS_ROWS, :] = encode(bias_rows).astype(BF16)


def keep_kernel(place, sums, pre_strip, patches, out):
    add_strip(place, place.rank(0), sums, pre_strip, patches, out, 0)


def edges_kernel(
    row_count,
    hidden,
    cell,
    grad_cell,
    pre,
    hidden_strip,
    cell_strip,
    grad_cell_strip,
    pre_strip,
    hidden_hbm,
    cell_hbm,
    grad_cell_hbm,
    pre_out,
    inner_out,
    outer_out,
    hidden_low,
    cell_here,
    grad_cell_here,
    left,
):
    hid, _, width = hidden_low.shape
    pairs = (
        (cell, cell_strip, cell_here, cell_hbm),
        (grad_cell, grad_cell_strip, grad_cell_here, grad_cell_hbm),
    )
    leaving = []
    for source, strip, here, target in pairs:
        columns = strip[...]
        for index in range(row_count):
            strided = pl.ds(index, hid, stride=row_count)
            here[strided, :] = at_edges(source[strided, :], index + 1, columns)
        leaving.append(pltpu.make_async_copy(here, target, left.at[len(leaving)]))
        leaving[-1].start()
    first, last = None, None
    columns = pre_strip[...].astype(F32)
    for index in range(row_count):
        at = pl.ds(index * width, width)
        row = at_edges(pre[:, at].astype(F32), index + 1, columns)
        pre_out[:, at] = row.astype(BF16)
        first = row if index == 0 else first
        last = row
    row_sends(first, last, inner_out, outer_out)
    for copy in leaving:
        copy.wait()
    columns = hidden_strip[...]
    for index in range(row_count):
        strided = pl.ds(index, hid, stride=row_count)
        cell_here[strided, :] = at_edges(hidden[strided, :], index + 1, columns)
    hidden_low[...] = cell_here[...].reshape(hidden_low.shape).astype(BF16)
    copy = pltpu.make_async_copy(hidden_low, hidden_hbm, left.at[2])
    copy.start()
    copy.wait()


def pair_kernel(place, keep, bias, received, *outs):
    sends, keep_out, bias_out, scratch = outs[:-3], outs[-3], outs[-2], outs[-1]
    chunk = place.chunk
    rank = place.plane_rank()
    scratch[...] = keep[...] + received[BIAS_ROWS:, :].astype(F32)
    bias_total = bias[...] + decode(received[0:BIAS_ROWS, :].astype(F32))
    block = encode(bias_total).astype(BF16)
    for step, send in zip(range(place.plane - 1, 0, -1), sends):
        send[0:BIAS_ROWS, :] = block
        at = pl.ds(pl.multiple_of((rank ^ step) * chunk, 8), chunk)
        send[BIAS_ROWS:, :] = scratch[at, :].astype(BF16)
    keep_out[...] = scratch[pl.ds(pl.multiple_of(rank * chunk, 8), chunk), :]
    bias_out[...] = bias_total


def plane_kernel(keep, bias, *refs):
    received, out = refs[:-2], refs[-1]
    total, bias_total = keep[...], bias[...]
    for ref in received:
        total += ref[BIAS_ROWS:, :].astype(F32)
        bias_total += decode(ref[0:BIAS_ROWS, :].astype(F32))
    out[0:BIAS_ROWS, :] = encode(bias_total).astype(BF16)
    out[BIAS_ROWS:, :] = total.astype(BF16)


def join_kernel(place, *refs):
    blocks, out = refs[:-2], refs[-1]
    rank = place.plane_rank()
    for step, block in enumerate(blocks):
        out[rank ^ step] = block[...]


def add_kernel(scale, own, received, out, *done_out):
    here, there = own[...].astype(F32), received[...].astype(F32)
    bias = (decode(here[0:BIAS_ROWS]) + decode(there[0:BIAS_ROWS])) * scale
    out[0:BIAS_ROWS, :] = encode(bias).astype(BF16)
    out[BIAS_ROWS:, :] = ((here[BIAS_ROWS:] + there[BIAS_ROWS:]) * scale).astype(BF16)
    for done in done_out:
        done[...] = jnp.zeros(done.shape, F32)


def store_half(place, half, blocks, out, wide, left):
    chunk, half_gates = place.chunk, place.half_gates
    gates = pl.ds(pl.multiple_of(half * half_gates, half_gates), half_gates)
    copies = []
    for index in range(place.plane):
        wide[index * chunk : (index + 1) * chunk, :] = blocks[index, BIAS_ROWS:, :].astype(F32)
        while len(copies) < min(place.taps, (index + 1) * chunk // half_gates):
            tap = len(copies)
            source = wide.at[tap * half_gates : (tap + 1) * half_gates, :]
            copies.append(pltpu.make_async_copy(source, out.at[tap, gates, :], left.at[tap]))
            copies[-1].start()
    return copies


def own_half_kernel(place, own, out, wide, left):
    for copy in store_half(place, place.rank(0), own, out, wide, left):
        copy.wait()


def other_half_kernel(place, own, received, out_before, out, bias_out, wide, bias_here, left):
    del out_before
    rank = place.rank(0)
    here, there = own[0, 0:BIAS_ROWS, :].astype(F32), received[0, 0:BIAS_ROWS, :].astype(F32)
    bias = decode(pick(rank == 1, there, here))
    width = bias.shape[1]
    for index in range(bias_here.shape[0] // width):
        bias_here[pl.ds(index * width, width)] = bias[index]
    bias_copy = pltpu.make_async_copy(bias_here, bias_out, left.at[place.taps])
    bias_copy.start()
    copies = store_half(place, 1 - rank, received, out, wide, left)
    bias_copy.wait()
    for copy in copies:
        copy.wait()


def field_kernel(
    place,
    pre,
    inner_row,
    outer_row,
    inner_column,
    outer_column,
    weights,
    after,
    inputs_out,
    hidden_out,
    done_out,
    shifted,
    turned,
    wide,
):
    del after
    gate_count = pre.shape[0]
    channels = weights.shape[2]
    done_out[...] = jnp.zeros(done_out.shape, F32)
    hid, row_count, width = hidden_out.shape

    def emit(position, left, row, right):
        at = pl.ds(position * width, width)
        shifted[0:gate_count, at] = right.astype(BF16)
        shifted[gate_count : 2 * gate_count, at] = row.astype(BF16)
        shifted[2 * gate_count : 3 * gate_count, at] = left.astype(BF16)

    widened(
        row_count,
        lambda index: pre[:, pl.ds(index * width, width)].astype(F32),
        (inner_row, outer_row),
        (inner_column, outer_column),
        emit,
    )
    for a in range(3):
        for b in range(3):
            turned[a, :, b * gate_count : (b + 1) * gate_count] = weights[3 * a + b].T
    lat = place.position()[0]
    top = turned[jnp.where(lat == 0, 0, 2)]
    bottom = turned[jnp.where(lat == place.lat - 1, 2, 0)]

    def product(matrix, position, count):
        return jnp.dot(
            matrix, shifted[:, pl.ds(position * width, count * width)], preferred_element_type=F32
        )

    pair = 2 if row_count % 2 == 0 else 1
    for base in range(0, row_count, pair):
        total = product(turned[1], base + 1, pair)
        if base == 0:
            above = product(top, 0, 1)
            if pair == 2:
                above = jnp.concatenate([above, product(turned[2], 1, 1)], axis=1)
        else:
            above = product(turned[2], base, pair)
        if base + pair == row_count:
            below = product(bottom, row_count + 1, 1)
            if pair == 2:
                below = jnp.concatenate([product(turned[0], row_count, 1), below], axis=1)
        else:
            below = product(turned[0], base + 2, pair)
        total = total + above + below
        for offset in range(pair):
            value = total[:, offset * width : (offset + 1) * width]
            wide[pl.ds(base + offset, channels, stride=row_count), :] = value
    size = (channels - hid) * row_count
    inputs_out[...] = wide[0:size, :].reshape(inputs_out.shape).astype(BF16)
    hidden_out[...] = wide[size:, :].reshape(hidden_out.shape).astype(BF16)


def body(
    place,
    inputs_below,
    hidden_prev,
    cell_prev,
    kernel_weights,
    gate_bias,
    readout,
    target_field,
    land_mask,
    fire_mask,
    hidden_grad,
):
    hid, row_count, width = hidden_prev.shape
    gate_count, channels = kernel_weights.shape[1:]
    cells = row_count * width
    halo_cells = (row_count + 2) * width
    scaling = 1.0 / math.sqrt(cells * place.lat * place.lon)
    bind = functools.partial
    inner_rows, outer_rows = place.pairs(place.inner_rows), place.pairs(place.outer_rows)
    inner_columns = place.pairs(place.inner_columns)
    outer_columns = place.pairs(place.outer_columns)
    flat = sds((hid * row_count, width), F32)
    strip = sds((hid, width), F32)

    inner, outer, wide = call(
        pack_kernel,
        (
            sds((channels, width), BF16),
            sds((channels, width), BF16),
            sds((channels * row_count, width), F32),
        ),
        [
            pltpu.VMEM(inputs_below.shape, BF16),
            pltpu.VMEM(hidden_prev.shape, BF16),
            pltpu.SemaphoreType.DMA((2,)),
        ],
        remote=2,
        moved=4 * channels * cells,
    )(inputs_below, hidden_prev)
    inner, outer = permuted(inner, inner_rows), permuted(outer, outer_rows)
    (
        rows,
        columns,
        second,
        cell_strip,
        hidden_grad_strip,
        fields_strip,
        cell_here,
        weights_here,
        hidden_grad_here,
        target_here,
        land_here,
        fire_here,
        bias_wide,
        readout_wide,
    ) = call(
        prepare_kernel,
        (
            sds((row_count, channels, width), BF16),
            sds((channels, width), F32),
            sds((channels, width), F32),
            strip,
            strip,
            sds((8, width), F32),
            flat,
            sds(kernel_weights.shape, BF16),
            flat,
            sds(target_field.shape, F32),
            sds(land_mask.shape, jnp.int32),
            sds(fire_mask.shape, jnp.int32),
            sds((gate_count, width), F32),
            sds((hid, width), F32),
        ),
        [
            pltpu.VMEM(hidden_grad.shape, BF16),
            pltpu.VMEM(gate_bias.shape, F32),
            pltpu.VMEM(readout.shape, F32),
            pltpu.SemaphoreType.DMA((8,)),
        ],
        remote=8,
        moved=6_000_000,
    )(
        wide,
        cell_prev.reshape(hid * row_count, width),
        kernel_weights,
        hidden_grad,
        target_field,
        land_mask,
        fire_mask,
        gate_bias,
        readout,
    )
    edge = call(bind(columns_kernel, row_count), sds((channels, width), BF16))(
        columns, inner, outer
    )
    inner_column, outer_column = permuted(edge, inner_columns), permuted(edge, outer_columns)
    hidden_rows, cell_rows, grad_cell_rows, pre, second, sums, bias = call(
        bind(gates_kernel, place),
        (
            flat,
            flat,
            flat,
            sds((gate_count, cells), BF16),
            sds((channels, width), BF16),
            sds((2 * place.half_rows, channels), F32),
            sds((gate_count, width), F32),
        ),
        [pltpu.VMEM((3 * channels, halo_cells), BF16)],
        flops=4 * 9 * gate_count * channels * cells,
        moved=6_000_000,
        transcendentals=5 * hid * cells,
    )(
        rows,
        inner,
        outer,
        second,
        cell_here,
        weights_here,
        hidden_grad_here,
        target_here,
        land_here,
        fire_here,
        bias_wide,
        readout_wide,
    )
    send, bias, pre_strip, patches, *strips = call(
        bind(strip_kernel, place, row_count),
        (
            sds((BIAS_ROWS + place.half_rows, channels), BF16),
            sds((8, channels), F32),
            sds((gate_count, width), BF16),
            sds((place.taps * channels, width), BF16),
            strip,
            strip,
            strip,
        ),
    )(
        edge,
        second,
        inner_column,
        outer_column,
        weights_here,
        bias_wide,
        readout_wide,
        cell_strip,
        hidden_grad_strip,
        fields_strip,
        sums,
        bias,
    )
    keep = call(bind(keep_kernel, place), sds((place.half_rows, channels), F32))(
        sums, pre_strip, patches
    )
    hidden_next, cell_next, grad_cell, pre, pre_inner, pre_outer = call(
        bind(edges_kernel, row_count),
        (
            sds((hid, row_count, width), BF16),
            flat,
            flat,
            sds((gate_count, cells), BF16),
            sds((gate_count, width), BF16),
            sds((gate_count, width), BF16),
        ),
        [
            pltpu.VMEM((hid, row_count, width), BF16),
            pltpu.VMEM(flat.shape, F32),
            pltpu.VMEM(flat.shape, F32),
            pltpu.SemaphoreType.DMA((3,)),
        ],
        leaving=3,
        moved=4_000_000,
    )(hidden_rows, cell_rows, grad_cell_rows, pre, *strips, pre_strip)
    after = pre_inner
    pre_inner, pre_outer = permuted(pre_inner, inner_rows), permuted(pre_outer, outer_rows)
    pre_columns = call(bind(columns_kernel, row_count), sds((gate_count, width), BF16))(
        pre_strip, pre_inner, pre_outer
    )

    block = sds((BIAS_ROWS + place.chunk, channels), BF16)
    token = sds((8, width), F32)
    steps = range(place.plane - 1, 0, -1)
    *sends, keep, bias = call(
        bind(pair_kernel, place),
        (*[block for _ in steps], sds((place.chunk, channels), F32), sds((8, channels), F32)),
        [pltpu.VMEM((place.half_rows, channels), F32)],
    )(keep, bias, permuted(send, place.phase_pairs(0)))
    received = [permuted(send, place.plane_pairs(step)) for step, send in zip(steps, sends)]
    part = call(plane_kernel, block)(keep, bias, *received, after)
    pre_inner_columns = permuted(pre_columns, inner_columns)
    pre_outer_columns = permuted(pre_columns, outer_columns)
    phases = len(place.orders[0])
    for phase in range(1, phases):
        is_last = phase == phases - 1
        part, *summed = call(
            bind(add_kernel, scaling if is_last else 1.0), (block, token) if is_last else (block,)
        )(part, permuted(part, place.phase_pairs(phase)))
    grad_inputs, grad_hidden, field_done = call(
        bind(field_kernel, place),
        (
            sds((channels - hid, row_count, width), BF16),
            sds((hid, row_count, width), BF16),
            sds((8, width), F32),
        ),
        [
            pltpu.VMEM((3 * gate_count, halo_cells), BF16),
            pltpu.VMEM((3, channels, 3 * gate_count), BF16),
            pltpu.VMEM((channels * row_count, width), F32),
        ],
        flops=2 * 9 * gate_count * channels * cells,
        moved=2_000_000,
    )(
        pre,
        pre_inner,
        pre_outer,
        pre_inner_columns,
        pre_outer_columns,
        weights_here,
        *summed,
    )
    received = [permuted(part, place.plane_pairs(step)) for step in steps[::-1]]
    gathered = call(bind(join_kernel, place), sds((place.plane, *block.shape), BF16))(
        part, *received, field_done
    )
    received = permuted(gathered, place.phase_pairs(0))
    half = [pltpu.VMEM((place.half_rows, channels), F32)]
    grad_kernel = call(
        bind(own_half_kernel, place),
        (sds(kernel_weights.shape, F32),),
        half + [pltpu.SemaphoreType.DMA((place.taps,))],
        leaving=1,
        moved=6 * place.half_rows * channels,
    )(gathered)[0]
    grad_kernel, grad_bias = call(
        bind(other_half_kernel, place),
        (sds(kernel_weights.shape, F32), sds((gate_count,), F32)),
        half + [pltpu.VMEM((gate_count,), F32), pltpu.SemaphoreType.DMA((place.taps + 1,))],
        remote=1,
        leaving=2,
        aliases={2: 0},
        moved=6 * place.half_rows * channels,
    )(gathered, received, grad_kernel)
    shape = hidden_prev.shape
    return (
        hidden_next,
        cell_next.reshape(shape),
        grad_inputs,
        grad_hidden,
        grad_cell.reshape(shape),
        grad_kernel,
        grad_bias,
    )


def solution(mesh):
    lat_count, lon_count = mesh.shape["lat"], mesh.shape["lon"]
    split = Mesh(mesh.devices.reshape(lat_count // 2, 2, lon_count // 2, 2), AXES)
    field = P(None, ("band", "core"), ("reach", "near"))
    flat = P(("band", "core"), ("reach", "near"))

    def run(*args):
        place = Layout(lat_count, lon_count, *args[3].shape[:2])
        return jax.shard_map(
            functools.partial(body, place),
            mesh=split,
            in_specs=(field, field, field, P(), P(), P(), flat, flat, flat, field),
            out_specs=(field, field, field, field, field, P(), P()),
            check_vma=False,
        )(*args)

    return run
```

```python
import functools
import math

import jax
import jax.numpy as jnp
from jax import lax
from jax.experimental import pallas as pl
from jax.experimental.pallas import tpu as pltpu
from jax.sharding import Mesh, PartitionSpec as P

F32 = jnp.float32
BF16 = jnp.bfloat16
AXES = ("band", "core", "reach", "near")
BIAS_ROWS = 16
GROUPS = 4
PRE_GROUPS = 1
LAST = 16
VMEM = pl.BlockSpec(memory_space=pltpu.VMEM)
HBM = pl.BlockSpec(memory_space=pltpu.HBM)
ACROSS = (((1,), (1,)), ((), ()))


def sds(shape, dtype):
    return jax.ShapeDtypeStruct(shape, dtype)


def call(
    kernel,
    out_shape,
    scratch=(),
    remote=0,
    leaving=0,
    aliases=None,
    flops=0,
    moved=0,
    transcendentals=0,
):
    several = isinstance(out_shape, tuple)
    shapes = out_shape if several else (out_shape,)
    out_specs = tuple([HBM] * leaving + [VMEM] * (len(shapes) - leaving))

    def run(*args):
        near = len(args) - remote
        far = [pltpu.with_memory_space_constraint(arg, pltpu.HBM) for arg in args[near:]]
        return pl.pallas_call(
            kernel,
            out_shape=out_shape,
            in_specs=[VMEM] * near + [HBM] * remote,
            out_specs=out_specs if several else out_specs[0],
            input_output_aliases=aliases or {},
            scratch_shapes=list(scratch),
            cost_estimate=pl.CostEstimate(
                flops=flops, bytes_accessed=moved, transcendentals=transcendentals
            ),
            compiler_params=pltpu.CompilerParams(vmem_limit_bytes=24 * 1024 * 1024),
        )(*args[:near], *far)

    return run


class Layout:
    def __init__(self, lat_count, lon_count, taps, gate_count):
        self.lat, self.lon = lat_count, lon_count
        self.half = lon_count // 2
        self.taps, self.half_gates = taps, gate_count // 2
        self.plane = lat_count
        whole = [("lon", 1 << k) for k in range(1, lon_count.bit_length() - 1)]
        self.orders = ([("lat", 1)] + whole, [("lat", 1)] + whole[::-1])
        step = 8 * self.plane
        self.half_rows = -(-taps * self.half_gates // step) * step
        self.chunk = self.half_rows // self.plane

    def position(self):
        lat = 2 * lax.axis_index("band") + lax.axis_index("core")
        return lat, 2 * lax.axis_index("reach") + lax.axis_index("near")

    def rank(self, phase):
        lat, lon = self.position()

        def digit(order):
            axis, bit = order[phase]
            return ((lat if axis == "lat" else lon) // bit) % 2

        return jnp.where(lat % 2 == 0, digit(self.orders[0]), digit(self.orders[1]))

    def pairs(self, partner):
        result = []
        for lat in range(self.lat):
            for lon in range(self.lon):
                there = partner(lat, lon)
                result.append((lat * self.lon + lon, there[0] * self.lon + there[1]))
        return result

    def phase_pairs(self, phase):
        def partner(lat, lon):
            axis, bit = self.orders[lat % 2][phase]
            return (lat ^ bit, lon) if axis == "lat" else (lat, lon ^ bit)

        return self.pairs(partner)

    def plane_rank(self):
        return 2 * lax.axis_index("band") + lax.axis_index("near")

    def plane_pairs(self, step):
        def partner(lat, lon):
            there = (lat // 2 * 2 + lon % 2) ^ step
            return there // 2 * 2 + lat % 2, lon // 2 * 2 + there % 2

        return self.pairs(partner)

    def inner_rows(self, lat, lon):
        return lat ^ 1, lon

    def outer_rows(self, lat, lon):
        there = lat + 1 if lat % 2 else lat - 1
        if 0 <= there < self.lat:
            return there, lon
        return lat, (lon + self.half) % self.lon

    def inner_columns(self, lat, lon):
        return lat, lon ^ 1

    def outer_columns(self, lat, lon):
        return lat, (lon + (1 if lon % 2 else -1)) % self.lon


def permuted(value, pairs):
    return lax.ppermute(value, AXES, pairs)


def lanes(shape):
    return lax.broadcasted_iota(jnp.int32, shape, len(shape) - 1)


def rolled(value, shift):
    shift %= value.shape[1]
    return pltpu.roll(value, shift, 1) if shift else value


def edge_columns(row, position, columns):
    lane = lanes(row.shape)
    columns = jnp.where(lane == position, rolled(row, position), columns)
    return jnp.where(lane == LAST + position, rolled(row, LAST + position + 1), columns)


def second_columns(row, position, columns):
    lane = lanes(row.shape)
    columns = jnp.where(lane == position, rolled(row, position - 1), columns)
    return jnp.where(lane == LAST + position, rolled(row, LAST + position + 2), columns)


def at_edges(row, position, columns):
    lane = lanes(row.shape)
    width = row.shape[1]
    row = jnp.where(lane == 0, rolled(columns, -position), row)
    return jnp.where(lane == width - 1, rolled(columns, width - 1 - LAST - position), row)


def pick(flag, yes, no):
    return jnp.where(flag, yes, no)


def is_odd(axis):
    return lax.axis_index(axis) % 2 == 1


def row_sends(first, last, inner_out, outer_out):
    odd = is_odd("core")
    inner_out[...] = pick(odd, first, last).astype(BF16)
    outer_out[...] = pick(odd, last, first).astype(BF16)


def row_halo(inner, outer):
    odd = is_odd("core")
    inner, outer = inner[...].astype(F32), outer[...].astype(F32)
    return pick(odd, inner, outer), pick(odd, outer, inner)


def packed(columns, groups):
    count, width = columns.shape[0] // groups, columns.shape[1] // groups
    lane = lanes((count, columns.shape[1]))
    value = columns[0:count]
    for group in range(1, groups):
        part = rolled(columns[group * count : (group + 1) * count], group * width)
        value = jnp.where(lane >= group * width, part, value)
    return value


def unpacked(value, groups):
    width = value.shape[1] // groups
    return jnp.concatenate([rolled(value, -group * width) for group in range(groups)], axis=0)


def column_halo(inner, outer, groups):
    odd = is_odd("near")
    inner, outer = inner[...].astype(F32), outer[...].astype(F32)
    return unpacked(pick(odd, inner, outer), groups), unpacked(pick(odd, outer, inner), groups)


def widened(row_count, rows, row_blocks, column_blocks, emit):
    north, south = row_halo(*row_blocks)
    west, east = column_halo(*column_blocks, PRE_GROUPS)
    width = west.shape[1]
    lane = lanes(west.shape)
    for position in range(row_count + 2):
        if position == 0:
            row = north
        elif position == row_count + 1:
            row = south
        else:
            row = rows(position - 1)
        left = rolled(west, -LAST - position)
        right = rolled(east, width - 1 - position)
        emit(
            position,
            jnp.where(lane == 0, left, rolled(row, 1)),
            row,
            jnp.where(lane == width - 1, right, rolled(row, -1)),
        )


def pack_kernel(below, hidden, inner_out, outer_out, wide_out, below_here, hidden_here, arrived):
    first = pltpu.make_async_copy(below, below_here, arrived.at[0])
    second = pltpu.make_async_copy(hidden, hidden_here, arrived.at[1])
    first.start()
    second.start()
    channels, row_count, width = below.shape
    size = channels * row_count
    first.wait()
    wide_out[0:size, :] = below_here[...].astype(F32).reshape(size, width)
    second.wait()
    wide_out[size : 2 * size, :] = hidden_here[...].astype(F32).reshape(size, width)
    edges = [
        wide_out[pl.ds(index, 2 * channels, stride=row_count), :] for index in (0, row_count - 1)
    ]
    row_sends(edges[0], edges[1], inner_out, outer_out)


def down_rows(values, width):
    count = values.shape[0]
    return jnp.broadcast_to(values[None, :], (width, count)).T


def prepare_kernel(
    wide,
    cell_hbm,
    weights_hbm,
    hidden_grad_hbm,
    target_hbm,
    land_hbm,
    fire_hbm,
    gate_bias_hbm,
    readout_hbm,
    rows_out,
    columns_out,
    second_out,
    cell_strip_out,
    hidden_grad_strip_out,
    fields_strip_out,
    cell_out,
    weights_out,
    hidden_grad_out,
    target_out,
    land_out,
    fire_out,
    bias_wide_out,
    readout_wide_out,
    hidden_grad_here,
    gate_bias_here,
    readout_here,
    arrived,
):
    copies = [
        pltpu.make_async_copy(source, target, arrived.at[index])
        for index, (source, target) in enumerate(
            (
                (cell_hbm, cell_out),
                (weights_hbm, weights_out),
                (hidden_grad_hbm, hidden_grad_here),
                (target_hbm, target_out),
                (land_hbm, land_out),
                (fire_hbm, fire_out),
                (gate_bias_hbm, gate_bias_here),
                (readout_hbm, readout_here),
            )
        )
    ]
    for copy in copies:
        copy.start()
    row_count, channels, width = rows_out.shape
    columns = jnp.zeros((channels, width), F32)
    second = jnp.zeros((channels, width), F32)
    for index in range(row_count):
        row = wide[pl.ds(index, channels, stride=row_count), :]
        rows_out[index] = row.astype(BF16)
        columns = edge_columns(row, index + 1, columns)
        second = second_columns(row, index + 1, second)
    columns_out[...] = columns
    second_out[...] = second
    for copy in copies:
        copy.wait()
    hidden_grad_out[...] = hidden_grad_here[...].astype(F32).reshape(hidden_grad_out.shape)
    bias_wide_out[...] = down_rows(gate_bias_here[...], width)
    readout_wide_out[...] = down_rows(readout_here[...], width)
    hid = hidden_grad_here.shape[0]
    cell_strip = jnp.zeros((hid, width), F32)
    hidden_grad_strip = jnp.zeros((hid, width), F32)
    fields_strip = jnp.zeros((8, width), F32)
    for index in range(row_count):
        strided = pl.ds(index, hid, stride=row_count)
        cell_strip = edge_columns(cell_out[strided, :], index + 1, cell_strip)
        hidden_grad_strip = edge_columns(hidden_grad_out[strided, :], index + 1, hidden_grad_strip)
        at = slice(index, index + 1)
        fields = [target_out[at, :], land_out[at, :].astype(F32), fire_out[at, :].astype(F32)]
        fields = jnp.concatenate(fields + [jnp.zeros((5, width), F32)], axis=0)
        fields_strip = edge_columns(fields, index + 1, fields_strip)
    cell_strip_out[...] = cell_strip
    hidden_grad_strip_out[...] = hidden_grad_strip
    fields_strip_out[...] = fields_strip


def columns_kernel(row_count, groups, columns, inner, outer, packed_out, *whole_out):
    north, south = row_halo(inner, outer)
    value = edge_columns(north, 0, columns[...].astype(F32))
    value = edge_columns(south, row_count + 1, value)
    packed_out[...] = packed(value, groups).astype(BF16)
    for out in whole_out:
        out[...] = value.astype(BF16)


def encode(bias):
    high = bias.astype(BF16).astype(F32)
    return jnp.concatenate([high, bias - high], axis=0)


def decode(block):
    return block[0:8] + block[8:16]


def cell_step(part, cell_before, hidden_grad, target, land, fire, readout):
    hid = part.shape[0] // 4
    input_gate = 0.5 + 0.5 * jnp.tanh(0.5 * part[0:hid])
    forget_gate = 0.5 + 0.5 * jnp.tanh(0.5 * part[hid : 2 * hid])
    output_gate = 0.5 + 0.5 * jnp.tanh(0.5 * part[2 * hid : 3 * hid])
    candidate = jnp.tanh(part[3 * hid : 4 * hid])
    cell_next = land * (forget_gate * cell_before + input_gate * candidate)
    squashed = jnp.tanh(cell_next)
    hidden_next = (output_gate * squashed).astype(BF16).astype(F32)
    predicted = jnp.sum(readout * hidden_next, axis=0, keepdims=True)
    total_grad = hidden_grad + 2.0 * (fire * (predicted - target)) * readout
    cell_grad = land * total_grad * output_gate * (1.0 - squashed * squashed)
    pre_grad = jnp.concatenate(
        [
            cell_grad * candidate * input_gate * (1.0 - input_gate),
            cell_grad * cell_before * forget_gate * (1.0 - forget_gate),
            total_grad * squashed * output_gate * (1.0 - output_gate),
            cell_grad * input_gate * (1.0 - candidate * candidate),
        ],
        axis=0,
    )
    return hidden_next, cell_next, cell_grad * forget_gate, pre_grad


def gates_kernel(
    place,
    rows_in,
    inner_row,
    outer_row,
    second,
    cell_prev,
    weights,
    hidden_grad,
    target,
    land,
    fire,
    bias_wide,
    readout_wide,
    hidden_out,
    cell_out,
    grad_cell_out,
    pre_out,
    second_out,
    sums,
    bias_out,
    shifted,
):
    row_count, channels, width = rows_in.shape
    gate_count = weights.shape[1]
    hid = gate_count // 4
    half_gates = place.half_gates
    north, south = row_halo(inner_row, outer_row)
    columns = second_columns(north, 0, second[...])
    second_out[...] = second_columns(south, row_count + 1, columns).astype(BF16)
    for position in range(row_count + 2):
        if position == 0:
            row = north
        elif position == row_count + 1:
            row = south
        else:
            row = rows_in[position - 1].astype(F32)
        at = pl.ds(position * width, width)
        shifted[0:channels, at] = rolled(row, 1).astype(BF16)
        shifted[channels : 2 * channels, at] = row.astype(BF16)
        shifted[2 * channels : 3 * channels, at] = rolled(row, -1).astype(BF16)

    taps = [
        jnp.concatenate([weights[3 * a], weights[3 * a + 1], weights[3 * a + 2]], axis=1)
        for a in range(3)
    ]
    bias_total = jnp.zeros((gate_count, width), F32)
    lane = lanes((gate_count, width))
    inside = (lane > 0) & (lane < width - 1)
    readout = readout_wide[...]
    pair = 2 if row_count % 2 == 0 else 1
    for base in range(0, row_count, pair):
        preact = jnp.zeros((gate_count, pair * width), F32)
        for a in range(3):
            preact += jnp.dot(
                taps[a],
                shifted[:, pl.ds((base + a) * width, pair * width)],
                preferred_element_type=F32,
            )
        for offset in range(pair):
            index = base + offset
            strided = pl.ds(index, hid, stride=row_count)
            at = slice(index, index + 1)
            hidden_next, cell_next, grad_cell, pre_grad = cell_step(
                preact[:, offset * width : (offset + 1) * width] + bias_wide[...],
                cell_prev[strided, :],
                hidden_grad[strided, :],
                target[at, :],
                land[at, :].astype(F32),
                fire[at, :].astype(F32),
                readout,
            )
            hidden_out[strided, :] = hidden_next
            cell_out[strided, :] = cell_next
            grad_cell_out[strided, :] = grad_cell
            pre_grad = jnp.where(inside, pre_grad, 0.0)
            bias_total += pre_grad
            pre_out[:, pl.ds(index * width, width)] = pre_grad.astype(BF16)
    bias_out[...] = bias_total

    for a in range(3):
        product = lax.dot_general(
            pre_out[...],
            shifted[:, pl.ds(a * width, row_count * width)],
            ACROSS,
            preferred_element_type=F32,
        )
        for b in range(3):
            for half in range(2):
                at = half * place.half_rows + (3 * a + b) * half_gates
                sums[at : at + half_gates, :] = product[
                    half * half_gates : (half + 1) * half_gates, b * channels : (b + 1) * channels
                ]
    used = place.taps * half_gates
    if place.half_rows > used:
        for half in range(2):
            at = half * place.half_rows
            sums[at + used : at + place.half_rows, :] = jnp.zeros(
                (place.half_rows - used, channels), F32
            )


def add_strip(place, half, sums, pre_strip, patches, out):
    half_gates, channels = place.half_gates, sums.shape[1]
    gates = pre_strip[pl.ds(pl.multiple_of(half * half_gates, half_gates), half_gates), :]
    product = lax.dot_general(gates, patches[...], ACROSS, preferred_element_type=F32)
    base = half * place.half_rows
    for tap in range(place.taps):
        at = pl.ds(pl.multiple_of(base + tap * half_gates, 8), half_gates)
        value = sums[at, :] + product[:, tap * channels : (tap + 1) * channels]
        out[tap * half_gates : (tap + 1) * half_gates, :] = value.astype(out.dtype)
    used = place.taps * half_gates
    if place.half_rows > used:
        rest = jnp.zeros((place.half_rows - used, channels), out.dtype)
        out[used:, :] = rest


def strip_kernel(
    place,
    row_count,
    edge,
    second,
    inner_column,
    outer_column,
    weights,
    bias_wide,
    readout_wide,
    cell_strip,
    hidden_grad_strip,
    fields_strip,
    sums,
    send_out,
    pre_out,
    pre_wide_out,
    patches,
    hidden_out,
    cell_out,
    grad_cell_out,
):
    channels, width = edge.shape
    west, east = column_halo(inner_column, outer_column, GROUPS)
    near_first = lanes((channels, width)) < LAST
    inner = second[...].astype(F32)
    columns = (
        jnp.where(near_first, rolled(west, -LAST), inner),
        edge[...].astype(F32),
        jnp.where(near_first, inner, rolled(east, LAST)),
    )
    for a in range(3):
        for b in range(3):
            at = (3 * a + b) * channels
            patches[at : at + channels, :] = rolled(columns[b], 1 - a).astype(BF16)
    taps = jnp.concatenate([weights[tap] for tap in range(place.taps)], axis=1)
    preact = jnp.dot(taps, patches[...], preferred_element_type=F32) + bias_wide[...]
    hidden_next, cell_next, grad_cell, pre_grad = cell_step(
        preact,
        cell_strip[...],
        hidden_grad_strip[...],
        fields_strip[0:1, :],
        fields_strip[1:2, :],
        fields_strip[2:3, :],
        readout_wide[...],
    )
    hidden_out[...] = hidden_next
    cell_out[...] = cell_next
    grad_cell_out[...] = grad_cell
    lane = lanes(pre_grad.shape)
    lane = jnp.where(lane >= LAST, lane - LAST, lane)
    pre_grad = jnp.where((lane >= 1) & (lane <= row_count), pre_grad, 0.0)
    pre_out[...] = pre_grad.astype(BF16)
    pre_wide_out[...] = pre_grad
    add_strip(place, 1 - place.rank(0), sums, pre_out, patches, send_out)


def keep_kernel(place, sums, pre_strip, patches, bias_partial, pre_wide, out, bias_out):
    add_strip(place, place.rank(0), sums, pre_strip, patches, out)
    channels = sums.shape[1]
    bias_total = bias_partial[...] + pre_wide[...]
    ones = jnp.ones((8, bias_total.shape[1]), BF16)
    high = bias_total.astype(BF16)
    low = (bias_total - high.astype(F32)).astype(BF16)
    flat = lax.dot_general(ones, high, ACROSS, preferred_element_type=F32)
    flat += lax.dot_general(ones, low, ACROSS, preferred_element_type=F32)
    odd = lax.broadcasted_iota(jnp.int32, (8, channels), 0) % 2 == 1
    bias_out[...] = jnp.where(odd, flat[:, channels : 2 * channels], flat[:, 0:channels])


def edges_kernel(
    row_count,
    hidden,
    cell,
    grad_cell,
    pre,
    hidden_strip,
    cell_strip,
    grad_cell_strip,
    pre_strip,
    hidden_hbm,
    cell_hbm,
    grad_cell_hbm,
    pre_out,
    inner_out,
    outer_out,
    hidden_low,
    cell_here,
    grad_cell_here,
    left,
):
    hid, _, width = hidden_low.shape
    pairs = (
        (cell, cell_strip, cell_here, cell_hbm),
        (grad_cell, grad_cell_strip, grad_cell_here, grad_cell_hbm),
    )
    leaving = []
    for source, strip, here, target in pairs:
        columns = strip[...]
        for index in range(row_count):
            strided = pl.ds(index, hid, stride=row_count)
            here[strided, :] = at_edges(source[strided, :], index + 1, columns)
        leaving.append(pltpu.make_async_copy(here, target, left.at[len(leaving)]))
        leaving[-1].start()
    first, last = None, None
    columns = pre_strip[...].astype(F32)
    for index in range(row_count):
        at = pl.ds(index * width, width)
        row = at_edges(pre[:, at].astype(F32), index + 1, columns)
        pre_out[:, at] = row.astype(BF16)
        first = row if index == 0 else first
        last = row
    row_sends(first, last, inner_out, outer_out)
    for copy in leaving:
        copy.wait()
    columns = hidden_strip[...]
    for index in range(row_count):
        strided = pl.ds(index, hid, stride=row_count)
        cell_here[strided, :] = at_edges(hidden[strided, :], index + 1, columns)
    hidden_low[...] = cell_here[...].reshape(hidden_low.shape).astype(BF16)
    copy = pltpu.make_async_copy(hidden_low, hidden_hbm, left.at[2])
    copy.start()
    copy.wait()


def pair_kernel(place, keep, bias, received, *outs):
    sends, keep_out, scratch = outs[:-2], outs[-2], outs[-1]
    chunk = place.chunk
    rank = place.plane_rank()
    scratch[...] = keep[...] + received[...].astype(F32)
    block = encode(bias[...]).astype(BF16)
    for step, send in zip(range(place.plane - 1, 0, -1), sends):
        send[0:BIAS_ROWS, :] = block
        at = pl.ds(pl.multiple_of((rank ^ step) * chunk, 8), chunk)
        send[BIAS_ROWS:, :] = scratch[at, :].astype(BF16)
    keep_out[...] = scratch[pl.ds(pl.multiple_of(rank * chunk, 8), chunk), :]


def plane_kernel(keep, bias, *refs):
    received, out = refs[:-2], refs[-1]
    total, bias_total = keep[...], bias[...]
    for ref in received:
        total += ref[BIAS_ROWS:, :].astype(F32)
        bias_total += decode(ref[0:BIAS_ROWS, :].astype(F32))
    out[0:BIAS_ROWS, :] = encode(bias_total).astype(BF16)
    out[BIAS_ROWS:, :] = total.astype(BF16)


def join_kernel(place, *refs):
    blocks, out = refs[:-2], refs[-1]
    rank = place.plane_rank()
    for step, block in enumerate(blocks):
        out[rank ^ step] = block[...]


def add_kernel(scale, own, received, out, *done_out):
    here, there = own[...].astype(F32), received[...].astype(F32)
    bias = (decode(here[0:BIAS_ROWS]) + decode(there[0:BIAS_ROWS])) * scale
    out[0:BIAS_ROWS, :] = encode(bias).astype(BF16)
    out[BIAS_ROWS:, :] = ((here[BIAS_ROWS:] + there[BIAS_ROWS:]) * scale).astype(BF16)
    for done in done_out:
        done[...] = jnp.zeros(done.shape, F32)


def store_half(place, half, blocks, out, wide, left):
    chunk, half_gates = place.chunk, place.half_gates
    gates = pl.ds(pl.multiple_of(half * half_gates, half_gates), half_gates)
    copies = []
    for index in range(place.plane):
        wide[index * chunk : (index + 1) * chunk, :] = blocks[index, BIAS_ROWS:, :].astype(F32)
        while len(copies) < min(place.taps, (index + 1) * chunk // half_gates):
            tap = len(copies)
            source = wide.at[tap * half_gates : (tap + 1) * half_gates, :]
            copies.append(pltpu.make_async_copy(source, out.at[tap, gates, :], left.at[tap]))
            copies[-1].start()
    return copies


def own_half_kernel(place, own, out, wide, left):
    for copy in store_half(place, place.rank(0), own, out, wide, left):
        copy.wait()


def other_half_kernel(place, own, received, out_before, out, bias_out, wide, bias_here, left):
    del out_before
    rank = place.rank(0)
    here, there = own[0, 0:BIAS_ROWS, :].astype(F32), received[0, 0:BIAS_ROWS, :].astype(F32)
    bias = decode(here) + decode(there)
    width = bias.shape[1]
    for index in range(bias_here.shape[0] // width):
        bias_here[pl.ds(index * width, width)] = bias[index]
    bias_copy = pltpu.make_async_copy(bias_here, bias_out, left.at[place.taps])
    bias_copy.start()
    copies = store_half(place, 1 - rank, received, out, wide, left)
    bias_copy.wait()
    for copy in copies:
        copy.wait()


def field_kernel(
    place,
    pre,
    inner_row,
    outer_row,
    inner_column,
    outer_column,
    weights,
    after,
    inputs_out,
    hidden_out,
    done_out,
    shifted,
    turned,
    wide,
):
    del after
    gate_count = pre.shape[0]
    channels = weights.shape[2]
    done_out[...] = jnp.zeros(done_out.shape, F32)
    hid, row_count, width = hidden_out.shape

    def emit(position, left, row, right):
        at = pl.ds(position * width, width)
        shifted[0:gate_count, at] = right.astype(BF16)
        shifted[gate_count : 2 * gate_count, at] = row.astype(BF16)
        shifted[2 * gate_count : 3 * gate_count, at] = left.astype(BF16)

    widened(
        row_count,
        lambda index: pre[:, pl.ds(index * width, width)].astype(F32),
        (inner_row, outer_row),
        (inner_column, outer_column),
        emit,
    )
    for a in range(3):
        for b in range(3):
            turned[a, :, b * gate_count : (b + 1) * gate_count] = weights[3 * a + b].T
    lat = place.position()[0]
    top = turned[jnp.where(lat == 0, 0, 2)]
    bottom = turned[jnp.where(lat == place.lat - 1, 2, 0)]

    def product(matrix, position, count):
        return jnp.dot(
            matrix, shifted[:, pl.ds(position * width, count * width)], preferred_element_type=F32
        )

    pair = 2 if row_count % 2 == 0 else 1
    for base in range(0, row_count, pair):
        total = product(turned[1], base + 1, pair)
        if base == 0:
            above = product(top, 0, 1)
            if pair == 2:
                above = jnp.concatenate([above, product(turned[2], 1, 1)], axis=1)
        else:
            above = product(turned[2], base, pair)
        if base + pair == row_count:
            below = product(bottom, row_count + 1, 1)
            if pair == 2:
                below = jnp.concatenate([product(turned[0], row_count, 1), below], axis=1)
        else:
            below = product(turned[0], base + 2, pair)
        total = total + above + below
        for offset in range(pair):
            value = total[:, offset * width : (offset + 1) * width]
            wide[pl.ds(base + offset, channels, stride=row_count), :] = value
    size = (channels - hid) * row_count
    inputs_out[...] = wide[0:size, :].reshape(inputs_out.shape).astype(BF16)
    hidden_out[...] = wide[size:, :].reshape(hidden_out.shape).astype(BF16)


def body(
    place,
    inputs_below,
    hidden_prev,
    cell_prev,
    kernel_weights,
    gate_bias,
    readout,
    target_field,
    land_mask,
    fire_mask,
    hidden_grad,
):
    hid, row_count, width = hidden_prev.shape
    gate_count, channels = kernel_weights.shape[1:]
    cells = row_count * width
    halo_cells = (row_count + 2) * width
    scaling = 1.0 / math.sqrt(cells * place.lat * place.lon)
    bind = functools.partial
    inner_rows, outer_rows = place.pairs(place.inner_rows), place.pairs(place.outer_rows)
    inner_columns = place.pairs(place.inner_columns)
    outer_columns = place.pairs(place.outer_columns)
    flat = sds((hid * row_count, width), F32)
    strip = sds((hid, width), F32)

    inner, outer, wide = call(
        pack_kernel,
        (
            sds((channels, width), BF16),
            sds((channels, width), BF16),
            sds((channels * row_count, width), F32),
        ),
        [
            pltpu.VMEM(inputs_below.shape, BF16),
            pltpu.VMEM(hidden_prev.shape, BF16),
            pltpu.SemaphoreType.DMA((2,)),
        ],
        remote=2,
        moved=4 * channels * cells,
    )(inputs_below, hidden_prev)
    inner, outer = permuted(inner, inner_rows), permuted(outer, outer_rows)
    (
        rows,
        columns,
        second,
        cell_strip,
        hidden_grad_strip,
        fields_strip,
        cell_here,
        weights_here,
        hidden_grad_here,
        target_here,
        land_here,
        fire_here,
        bias_wide,
        readout_wide,
    ) = call(
        prepare_kernel,
        (
            sds((row_count, channels, width), BF16),
            sds((channels, width), F32),
            sds((channels, width), F32),
            strip,
            strip,
            sds((8, width), F32),
            flat,
            sds(kernel_weights.shape, BF16),
            flat,
            sds(target_field.shape, F32),
            sds(land_mask.shape, jnp.int32),
            sds(fire_mask.shape, jnp.int32),
            sds((gate_count, width), F32),
            sds((hid, width), F32),
        ),
        [
            pltpu.VMEM(hidden_grad.shape, BF16),
            pltpu.VMEM(gate_bias.shape, F32),
            pltpu.VMEM(readout.shape, F32),
            pltpu.SemaphoreType.DMA((8,)),
        ],
        remote=8,
        moved=6_000_000,
    )(
        wide,
        cell_prev.reshape(hid * row_count, width),
        kernel_weights,
        hidden_grad,
        target_field,
        land_mask,
        fire_mask,
        gate_bias,
        readout,
    )
    columns, edge = call(
        bind(columns_kernel, row_count, GROUPS),
        (sds((channels // GROUPS, width), BF16), sds((channels, width), BF16)),
    )(columns, inner, outer)
    outer_column = permuted(columns, outer_columns)
    inner_column = permuted(columns, inner_columns)
    hidden_rows, cell_rows, grad_cell_rows, pre, second, sums, bias = call(
        bind(gates_kernel, place),
        (
            flat,
            flat,
            flat,
            sds((gate_count, cells), BF16),
            sds((channels, width), BF16),
            sds((2 * place.half_rows, channels), F32),
            sds((gate_count, width), F32),
        ),
        [pltpu.VMEM((3 * channels, halo_cells), BF16)],
        flops=4 * 9 * gate_count * channels * cells,
        moved=6_000_000,
        transcendentals=5 * hid * cells,
    )(
        rows,
        inner,
        outer,
        second,
        cell_here,
        weights_here,
        hidden_grad_here,
        target_here,
        land_here,
        fire_here,
        bias_wide,
        readout_wide,
    )
    send, pre_strip, pre_wide, patches, *strips = call(
        bind(strip_kernel, place, row_count),
        (
            sds((place.half_rows, channels), BF16),
            sds((gate_count, width), BF16),
            sds((gate_count, width), F32),
            sds((place.taps * channels, width), BF16),
            strip,
            strip,
            strip,
        ),
    )(
        edge,
        second,
        inner_column,
        outer_column,
        weights_here,
        bias_wide,
        readout_wide,
        cell_strip,
        hidden_grad_strip,
        fields_strip,
        sums,
    )
    keep, bias = call(
        bind(keep_kernel, place),
        (sds((place.half_rows, channels), F32), sds((8, channels), F32)),
    )(sums, pre_strip, patches, bias, pre_wide)
    hidden_next, cell_next, grad_cell, pre, pre_inner, pre_outer = call(
        bind(edges_kernel, row_count),
        (
            sds((hid, row_count, width), BF16),
            flat,
            flat,
            sds((gate_count, cells), BF16),
            sds((gate_count, width), BF16),
            sds((gate_count, width), BF16),
        ),
        [
            pltpu.VMEM((hid, row_count, width), BF16),
            pltpu.VMEM(flat.shape, F32),
            pltpu.VMEM(flat.shape, F32),
            pltpu.SemaphoreType.DMA((3,)),
        ],
        leaving=3,
        moved=4_000_000,
    )(hidden_rows, cell_rows, grad_cell_rows, pre, *strips, pre_strip)
    after = pre_inner
    pre_inner, pre_outer = permuted(pre_inner, inner_rows), permuted(pre_outer, outer_rows)
    pre_columns = call(
        bind(columns_kernel, row_count, PRE_GROUPS),
        (sds((gate_count // PRE_GROUPS, width), BF16),),
    )(pre_strip, pre_inner, pre_outer)[0]

    block = sds((BIAS_ROWS + place.chunk, channels), BF16)
    token = sds((8, width), F32)
    steps = range(place.plane - 1, 0, -1)
    *sends, keep = call(
        bind(pair_kernel, place),
        (*[block for _ in steps], sds((place.chunk, channels), F32)),
        [pltpu.VMEM((place.half_rows, channels), F32)],
    )(keep, bias, permuted(send, place.phase_pairs(0)))
    received = [permuted(send, place.plane_pairs(step)) for step, send in zip(steps, sends)]
    part = call(plane_kernel, block)(keep, bias, *received, after)
    pre_outer_columns = permuted(pre_columns, outer_columns)
    pre_inner_columns = permuted(pre_columns, inner_columns)
    phases = len(place.orders[0])
    for phase in range(1, phases):
        is_last = phase == phases - 1
        part, *summed = call(
            bind(add_kernel, scaling if is_last else 1.0), (block, token) if is_last else (block,)
        )(part, permuted(part, place.phase_pairs(phase)))
    grad_inputs, grad_hidden, field_done = call(
        bind(field_kernel, place),
        (
            sds((channels - hid, row_count, width), BF16),
            sds((hid, row_count, width), BF16),
            sds((8, width), F32),
        ),
        [
            pltpu.VMEM((3 * gate_count, halo_cells), BF16),
            pltpu.VMEM((3, channels, 3 * gate_count), BF16),
            pltpu.VMEM((channels * row_count, width), F32),
        ],
        flops=2 * 9 * gate_count * channels * cells,
        moved=2_000_000,
    )(
        pre,
        pre_inner,
        pre_outer,
        pre_inner_columns,
        pre_outer_columns,
        weights_here,
        *summed,
    )
    received = [permuted(part, place.plane_pairs(step)) for step in steps[::-1]]
    gathered = call(bind(join_kernel, place), sds((place.plane, *block.shape), BF16))(
        part, *received, field_done
    )
    received = permuted(gathered, place.phase_pairs(0))
    half = [pltpu.VMEM((place.half_rows, channels), F32)]
    grad_kernel = call(
        bind(own_half_kernel, place),
        (sds(kernel_weights.shape, F32),),
        half + [pltpu.SemaphoreType.DMA((place.taps,))],
        leaving=1,
        moved=6 * place.half_rows * channels,
    )(gathered)[0]
    grad_kernel, grad_bias = call(
        bind(other_half_kernel, place),
        (sds(kernel_weights.shape, F32), sds((gate_count,), F32)),
        half + [pltpu.VMEM((gate_count,), F32), pltpu.SemaphoreType.DMA((place.taps + 1,))],
        remote=1,
        leaving=2,
        aliases={2: 0},
        moved=6 * place.half_rows * channels,
    )(gathered, received, grad_kernel)
    shape = hidden_prev.shape
    return (
        hidden_next,
        cell_next.reshape(shape),
        grad_inputs,
        grad_hidden,
        grad_cell.reshape(shape),
        grad_kernel,
        grad_bias,
    )


def solution(mesh):
    lat_count, lon_count = mesh.shape["lat"], mesh.shape["lon"]
    split = Mesh(mesh.devices.reshape(lat_count // 2, 2, lon_count // 2, 2), AXES)
    field = P(None, ("band", "core"), ("reach", "near"))
    flat = P(("band", "core"), ("reach", "near"))

    def run(*args):
        place = Layout(lat_count, lon_count, *args[3].shape[:2])
        return jax.shard_map(
            functools.partial(body, place),
            mesh=split,
            in_specs=(field, field, field, P(), P(), P(), flat, flat, flat, field),
            out_specs=(field, field, field, field, field, P(), P()),
            check_vma=False,
        )(*args)

    return run
```

```python
import functools
import math

import jax
import jax.numpy as jnp
from jax import lax
from jax.experimental import pallas as pl
from jax.experimental.pallas import tpu as pltpu
from jax.sharding import Mesh, PartitionSpec as P

F32 = jnp.float32
BF16 = jnp.bfloat16
AXES = ("band", "core", "reach", "near")
BIAS_ROWS = 16
GROUPS = 4
PRE_GROUPS = 1
LAST = 16
VMEM = pl.BlockSpec(memory_space=pltpu.VMEM)
HBM = pl.BlockSpec(memory_space=pltpu.HBM)
ACROSS = (((1,), (1,)), ((), ()))


def sds(shape, dtype):
    return jax.ShapeDtypeStruct(shape, dtype)


def call(
    kernel,
    out_shape,
    scratch=(),
    remote=0,
    leaving=0,
    aliases=None,
    flops=0,
    moved=0,
    transcendentals=0,
):
    several = isinstance(out_shape, tuple)
    shapes = out_shape if several else (out_shape,)
    out_specs = tuple([HBM] * leaving + [VMEM] * (len(shapes) - leaving))

    def run(*args):
        near = len(args) - remote
        far = [pltpu.with_memory_space_constraint(arg, pltpu.HBM) for arg in args[near:]]
        return pl.pallas_call(
            kernel,
            out_shape=out_shape,
            in_specs=[VMEM] * near + [HBM] * remote,
            out_specs=out_specs if several else out_specs[0],
            input_output_aliases=aliases or {},
            scratch_shapes=list(scratch),
            cost_estimate=pl.CostEstimate(
                flops=flops, bytes_accessed=moved, transcendentals=transcendentals
            ),
            compiler_params=pltpu.CompilerParams(vmem_limit_bytes=24 * 1024 * 1024),
        )(*args[:near], *far)

    return run


class Layout:
    def __init__(self, lat_count, lon_count, taps, gate_count):
        self.lat, self.lon = lat_count, lon_count
        self.half = lon_count // 2
        self.taps, self.half_gates = taps, gate_count // 2
        self.plane = lat_count
        whole = [("lon", 1 << k) for k in range(1, lon_count.bit_length() - 1)]
        self.orders = ([("lat", 1)] + whole, [("lat", 1)] + whole[::-1])
        step = 8 * self.plane
        self.half_rows = -(-taps * self.half_gates // step) * step
        self.chunk = self.half_rows // self.plane

    def position(self):
        lat = 2 * lax.axis_index("band") + lax.axis_index("core")
        return lat, 2 * lax.axis_index("reach") + lax.axis_index("near")

    def rank(self, phase):
        lat, lon = self.position()

        def digit(order):
            axis, bit = order[phase]
            return ((lat if axis == "lat" else lon) // bit) % 2

        return jnp.where(lat % 2 == 0, digit(self.orders[0]), digit(self.orders[1]))

    def pairs(self, partner):
        result = []
        for lat in range(self.lat):
            for lon in range(self.lon):
                there = partner(lat, lon)
                result.append((lat * self.lon + lon, there[0] * self.lon + there[1]))
        return result

    def phase_pairs(self, phase):
        def partner(lat, lon):
            axis, bit = self.orders[lat % 2][phase]
            return (lat ^ bit, lon) if axis == "lat" else (lat, lon ^ bit)

        return self.pairs(partner)

    def plane_rank(self):
        return 2 * lax.axis_index("band") + lax.axis_index("near")

    def plane_pairs(self, step):
        def partner(lat, lon):
            there = (lat // 2 * 2 + lon % 2) ^ step
            return there // 2 * 2 + lat % 2, lon // 2 * 2 + there % 2

        return self.pairs(partner)

    def inner_rows(self, lat, lon):
        return lat ^ 1, lon

    def outer_rows(self, lat, lon):
        there = lat + 1 if lat % 2 else lat - 1
        if 0 <= there < self.lat:
            return there, lon
        return lat, (lon + self.half) % self.lon

    def inner_columns(self, lat, lon):
        return lat, lon ^ 1

    def outer_columns(self, lat, lon):
        return lat, (lon + (1 if lon % 2 else -1)) % self.lon


def permuted(value, pairs):
    return lax.ppermute(value, AXES, pairs)


def lanes(shape):
    return lax.broadcasted_iota(jnp.int32, shape, len(shape) - 1)


def rolled(value, shift):
    shift %= value.shape[1]
    return pltpu.roll(value, shift, 1) if shift else value


def edge_columns(row, position, columns):
    lane = lanes(row.shape)
    columns = jnp.where(lane == position, rolled(row, position), columns)
    return jnp.where(lane == LAST + position, rolled(row, LAST + position + 1), columns)


def second_columns(row, position, columns):
    lane = lanes(row.shape)
    columns = jnp.where(lane == position, rolled(row, position - 1), columns)
    return jnp.where(lane == LAST + position, rolled(row, LAST + position + 2), columns)


def at_edges(row, position, columns):
    lane = lanes(row.shape)
    width = row.shape[1]
    row = jnp.where(lane == 0, rolled(columns, -position), row)
    return jnp.where(lane == width - 1, rolled(columns, width - 1 - LAST - position), row)


def pick(flag, yes, no):
    return jnp.where(flag, yes, no)


def is_odd(axis):
    return lax.axis_index(axis) % 2 == 1


def row_sends(first, last, inner_out, outer_out):
    odd = is_odd("core")
    inner_out[...] = pick(odd, first, last).astype(BF16)
    outer_out[...] = pick(odd, last, first).astype(BF16)


def row_halo(inner, outer):
    odd = is_odd("core")
    inner, outer = inner[...].astype(F32), outer[...].astype(F32)
    return pick(odd, inner, outer), pick(odd, outer, inner)


def packed(columns, groups):
    count, width = columns.shape[0] // groups, columns.shape[1] // groups
    lane = lanes((count, columns.shape[1]))
    value = columns[0:count]
    for group in range(1, groups):
        part = rolled(columns[group * count : (group + 1) * count], group * width)
        value = jnp.where(lane >= group * width, part, value)
    return value


def unpacked(value, groups):
    width = value.shape[1] // groups
    return jnp.concatenate([rolled(value, -group * width) for group in range(groups)], axis=0)


def column_halo(inner, outer, groups):
    odd = is_odd("near")
    inner, outer = inner[...].astype(F32), outer[...].astype(F32)
    return unpacked(pick(odd, inner, outer), groups), unpacked(pick(odd, outer, inner), groups)


def widened(row_count, rows, row_blocks, column_blocks, emit):
    north, south = row_halo(*row_blocks)
    west, east = column_halo(*column_blocks, PRE_GROUPS)
    width = west.shape[1]
    lane = lanes(west.shape)
    for position in range(row_count + 2):
        if position == 0:
            row = north
        elif position == row_count + 1:
            row = south
        else:
            row = rows(position - 1)
        left = rolled(west, -LAST - position)
        right = rolled(east, width - 1 - position)
        emit(
            position,
            jnp.where(lane == 0, left, rolled(row, 1)),
            row,
            jnp.where(lane == width - 1, right, rolled(row, -1)),
        )


def pack_kernel(below, hidden, inner_out, outer_out, wide_out, below_here, hidden_here, arrived):
    first = pltpu.make_async_copy(below, below_here, arrived.at[0])
    second = pltpu.make_async_copy(hidden, hidden_here, arrived.at[1])
    first.start()
    second.start()
    channels, row_count, width = below.shape
    size = channels * row_count
    first.wait()
    wide_out[0:size, :] = below_here[...].astype(F32).reshape(size, width)
    second.wait()
    wide_out[size : 2 * size, :] = hidden_here[...].astype(F32).reshape(size, width)
    edges = [
        wide_out[pl.ds(index, 2 * channels, stride=row_count), :] for index in (0, row_count - 1)
    ]
    row_sends(edges[0], edges[1], inner_out, outer_out)


def down_rows(values, width):
    count = values.shape[0]
    return jnp.broadcast_to(values[None, :], (width, count)).T


def prepare_kernel(
    wide,
    cell_hbm,
    weights_hbm,
    hidden_grad_hbm,
    target_hbm,
    land_hbm,
    fire_hbm,
    gate_bias_hbm,
    readout_hbm,
    rows_out,
    columns_out,
    second_out,
    cell_strip_out,
    hidden_grad_strip_out,
    fields_strip_out,
    cell_out,
    weights_out,
    hidden_grad_out,
    target_out,
    land_out,
    fire_out,
    bias_wide_out,
    readout_wide_out,
    hidden_grad_here,
    gate_bias_here,
    readout_here,
    arrived,
):
    copies = [
        pltpu.make_async_copy(source, target, arrived.at[index])
        for index, (source, target) in enumerate(
            (
                (cell_hbm, cell_out),
                (weights_hbm, weights_out),
                (hidden_grad_hbm, hidden_grad_here),
                (target_hbm, target_out),
                (land_hbm, land_out),
                (fire_hbm, fire_out),
                (gate_bias_hbm, gate_bias_here),
                (readout_hbm, readout_here),
            )
        )
    ]
    for copy in copies:
        copy.start()
    row_count, channels, width = rows_out.shape
    columns = jnp.zeros((channels, width), F32)
    second = jnp.zeros((channels, width), F32)
    for index in range(row_count):
        row = wide[pl.ds(index, channels, stride=row_count), :]
        rows_out[index] = row.astype(BF16)
        columns = edge_columns(row, index + 1, columns)
        second = second_columns(row, index + 1, second)
    columns_out[...] = columns
    second_out[...] = second
    for copy in copies:
        copy.wait()
    hidden_grad_out[...] = hidden_grad_here[...].astype(F32).reshape(hidden_grad_out.shape)
    bias_wide_out[...] = down_rows(gate_bias_here[...], width)
    readout_wide_out[...] = down_rows(readout_here[...], width)
    hid = hidden_grad_here.shape[0]
    cell_strip = jnp.zeros((hid, width), F32)
    hidden_grad_strip = jnp.zeros((hid, width), F32)
    fields_strip = jnp.zeros((8, width), F32)
    for index in range(row_count):
        strided = pl.ds(index, hid, stride=row_count)
        cell_strip = edge_columns(cell_out[strided, :], index + 1, cell_strip)
        hidden_grad_strip = edge_columns(hidden_grad_out[strided, :], index + 1, hidden_grad_strip)
        at = slice(index, index + 1)
        fields = [target_out[at, :], land_out[at, :].astype(F32), fire_out[at, :].astype(F32)]
        fields = jnp.concatenate(fields + [jnp.zeros((5, width), F32)], axis=0)
        fields_strip = edge_columns(fields, index + 1, fields_strip)
    cell_strip_out[...] = cell_strip
    hidden_grad_strip_out[...] = hidden_grad_strip
    fields_strip_out[...] = fields_strip


def columns_kernel(row_count, groups, columns, outer, inner, packed_out, *whole_out):
    north, south = row_halo(inner, outer)
    value = edge_columns(north, 0, columns[...].astype(F32))
    value = edge_columns(south, row_count + 1, value)
    packed_out[...] = packed(value, groups).astype(BF16)
    for out in whole_out:
        out[...] = value.astype(BF16)


def encode(bias):
    high = bias.astype(BF16).astype(F32)
    return jnp.concatenate([high, bias - high], axis=0)


def decode(block):
    return block[0:8] + block[8:16]


def cell_step(part, cell_before, hidden_grad, target, land, fire, readout):
    hid = part.shape[0] // 4
    input_gate = 0.5 + 0.5 * jnp.tanh(0.5 * part[0:hid])
    forget_gate = 0.5 + 0.5 * jnp.tanh(0.5 * part[hid : 2 * hid])
    output_gate = 0.5 + 0.5 * jnp.tanh(0.5 * part[2 * hid : 3 * hid])
    candidate = jnp.tanh(part[3 * hid : 4 * hid])
    cell_next = land * (forget_gate * cell_before + input_gate * candidate)
    squashed = jnp.tanh(cell_next)
    hidden_next = (output_gate * squashed).astype(BF16).astype(F32)
    predicted = jnp.sum(readout * hidden_next, axis=0, keepdims=True)
    total_grad = hidden_grad + 2.0 * (fire * (predicted - target)) * readout
    cell_grad = land * total_grad * output_gate * (1.0 - squashed * squashed)
    pre_grad = jnp.concatenate(
        [
            cell_grad * candidate * input_gate * (1.0 - input_gate),
            cell_grad * cell_before * forget_gate * (1.0 - forget_gate),
            total_grad * squashed * output_gate * (1.0 - output_gate),
            cell_grad * input_gate * (1.0 - candidate * candidate),
        ],
        axis=0,
    )
    return hidden_next, cell_next, cell_grad * forget_gate, pre_grad


def gates_kernel(
    place,
    rows_in,
    inner_row,
    outer_row,
    second,
    cell_prev,
    weights,
    hidden_grad,
    target,
    land,
    fire,
    bias_wide,
    readout_wide,
    hidden_out,
    cell_out,
    grad_cell_out,
    pre_out,
    second_out,
    sums,
    bias_out,
    shifted,
):
    row_count, channels, width = rows_in.shape
    gate_count = weights.shape[1]
    hid = gate_count // 4
    half_gates = place.half_gates
    north, south = row_halo(inner_row, outer_row)
    columns = second_columns(north, 0, second[...])
    second_out[...] = second_columns(south, row_count + 1, columns).astype(BF16)
    for position in range(row_count + 2):
        if position == 0:
            row = north
        elif position == row_count + 1:
            row = south
        else:
            row = rows_in[position - 1].astype(F32)
        at = pl.ds(position * width, width)
        shifted[0:channels, at] = rolled(row, 1).astype(BF16)
        shifted[channels : 2 * channels, at] = row.astype(BF16)
        shifted[2 * channels : 3 * channels, at] = rolled(row, -1).astype(BF16)

    taps = [
        jnp.concatenate([weights[3 * a], weights[3 * a + 1], weights[3 * a + 2]], axis=1)
        for a in range(3)
    ]
    bias_total = jnp.zeros((gate_count, width), F32)
    lane = lanes((gate_count, width))
    inside = (lane > 0) & (lane < width - 1)
    readout = readout_wide[...]
    pair = 2 if row_count % 2 == 0 else 1
    for base in range(0, row_count, pair):
        preact = jnp.zeros((gate_count, pair * width), F32)
        for a in range(3):
            preact += jnp.dot(
                taps[a],
                shifted[:, pl.ds((base + a) * width, pair * width)],
                preferred_element_type=F32,
            )
        for offset in range(pair):
            index = base + offset
            strided = pl.ds(index, hid, stride=row_count)
            at = slice(index, index + 1)
            hidden_next, cell_next, grad_cell, pre_grad = cell_step(
                preact[:, offset * width : (offset + 1) * width] + bias_wide[...],
                cell_prev[strided, :],
                hidden_grad[strided, :],
                target[at, :],
                land[at, :].astype(F32),
                fire[at, :].astype(F32),
                readout,
            )
            hidden_out[strided, :] = hidden_next
            cell_out[strided, :] = cell_next
            grad_cell_out[strided, :] = grad_cell
            pre_grad = jnp.where(inside, pre_grad, 0.0)
            bias_total += pre_grad
            pre_out[:, pl.ds(index * width, width)] = pre_grad.astype(BF16)
    bias_out[...] = bias_total

    for a in range(3):
        product = lax.dot_general(
            pre_out[...],
            shifted[:, pl.ds(a * width, row_count * width)],
            ACROSS,
            preferred_element_type=F32,
        )
        for b in range(3):
            for half in range(2):
                at = half * place.half_rows + (3 * a + b) * half_gates
                sums[at : at + half_gates, :] = product[
                    half * half_gates : (half + 1) * half_gates, b * channels : (b + 1) * channels
                ]
    used = place.taps * half_gates
    if place.half_rows > used:
        for half in range(2):
            at = half * place.half_rows
            sums[at + used : at + place.half_rows, :] = jnp.zeros(
                (place.half_rows - used, channels), F32
            )


def add_strip(place, half, sums, pre_strip, patches, out):
    half_gates, channels = place.half_gates, sums.shape[1]
    gates = pre_strip[pl.ds(pl.multiple_of(half * half_gates, half_gates), half_gates), :]
    product = lax.dot_general(gates, patches[...], ACROSS, preferred_element_type=F32)
    base = half * place.half_rows
    for tap in range(place.taps):
        at = pl.ds(pl.multiple_of(base + tap * half_gates, 8), half_gates)
        value = sums[at, :] + product[:, tap * channels : (tap + 1) * channels]
        out[tap * half_gates : (tap + 1) * half_gates, :] = value.astype(out.dtype)
    used = place.taps * half_gates
    if place.half_rows > used:
        rest = jnp.zeros((place.half_rows - used, channels), out.dtype)
        out[used:, :] = rest


def strip_kernel(
    place,
    row_count,
    edge,
    second,
    outer_column,
    inner_column,
    weights,
    bias_wide,
    readout_wide,
    cell_strip,
    hidden_grad_strip,
    fields_strip,
    sums,
    send_out,
    pre_out,
    pre_wide_out,
    patches,
    hidden_out,
    cell_out,
    grad_cell_out,
):
    channels, width = edge.shape
    west, east = column_halo(inner_column, outer_column, GROUPS)
    near_first = lanes((channels, width)) < LAST
    inner = second[...].astype(F32)
    columns = (
        jnp.where(near_first, rolled(west, -LAST), inner),
        edge[...].astype(F32),
        jnp.where(near_first, inner, rolled(east, LAST)),
    )
    for a in range(3):
        for b in range(3):
            at = (3 * a + b) * channels
            patches[at : at + channels, :] = rolled(columns[b], 1 - a).astype(BF16)
    taps = jnp.concatenate([weights[tap] for tap in range(place.taps)], axis=1)
    preact = jnp.dot(taps, patches[...], preferred_element_type=F32) + bias_wide[...]
    hidden_next, cell_next, grad_cell, pre_grad = cell_step(
        preact,
        cell_strip[...],
        hidden_grad_strip[...],
        fields_strip[0:1, :],
        fields_strip[1:2, :],
        fields_strip[2:3, :],
        readout_wide[...],
    )
    hidden_out[...] = hidden_next
    cell_out[...] = cell_next
    grad_cell_out[...] = grad_cell
    lane = lanes(pre_grad.shape)
    lane = jnp.where(lane >= LAST, lane - LAST, lane)
    pre_grad = jnp.where((lane >= 1) & (lane <= row_count), pre_grad, 0.0)
    pre_out[...] = pre_grad.astype(BF16)
    pre_wide_out[...] = pre_grad
    add_strip(place, 1 - place.rank(0), sums, pre_out, patches, send_out)


def keep_kernel(place, sums, pre_strip, patches, bias_partial, pre_wide, out, bias_out):
    add_strip(place, place.rank(0), sums, pre_strip, patches, out)
    channels = sums.shape[1]
    bias_total = bias_partial[...] + pre_wide[...]
    ones = jnp.ones((8, bias_total.shape[1]), BF16)
    high = bias_total.astype(BF16)
    low = (bias_total - high.astype(F32)).astype(BF16)
    flat = lax.dot_general(ones, high, ACROSS, preferred_element_type=F32)
    flat += lax.dot_general(ones, low, ACROSS, preferred_element_type=F32)
    odd = lax.broadcasted_iota(jnp.int32, (8, channels), 0) % 2 == 1
    bias_out[...] = jnp.where(odd, flat[:, channels : 2 * channels], flat[:, 0:channels])


def edges_kernel(
    row_count,
    hidden,
    cell,
    grad_cell,
    pre,
    hidden_strip,
    cell_strip,
    grad_cell_strip,
    pre_strip,
    hidden_hbm,
    cell_hbm,
    grad_cell_hbm,
    pre_out,
    inner_out,
    outer_out,
    hidden_low,
    cell_here,
    grad_cell_here,
    left,
):
    hid, _, width = hidden_low.shape
    pairs = (
        (cell, cell_strip, cell_here, cell_hbm),
        (grad_cell, grad_cell_strip, grad_cell_here, grad_cell_hbm),
    )
    leaving = []
    for source, strip, here, target in pairs:
        columns = strip[...]
        for index in range(row_count):
            strided = pl.ds(index, hid, stride=row_count)
            here[strided, :] = at_edges(source[strided, :], index + 1, columns)
        leaving.append(pltpu.make_async_copy(here, target, left.at[len(leaving)]))
        leaving[-1].start()
    first, last = None, None
    columns = pre_strip[...].astype(F32)
    for index in range(row_count):
        at = pl.ds(index * width, width)
        row = at_edges(pre[:, at].astype(F32), index + 1, columns)
        pre_out[:, at] = row.astype(BF16)
        first = row if index == 0 else first
        last = row
    row_sends(first, last, inner_out, outer_out)
    for copy in leaving:
        copy.wait()
    columns = hidden_strip[...]
    for index in range(row_count):
        strided = pl.ds(index, hid, stride=row_count)
        cell_here[strided, :] = at_edges(hidden[strided, :], index + 1, columns)
    hidden_low[...] = cell_here[...].reshape(hidden_low.shape).astype(BF16)
    copy = pltpu.make_async_copy(hidden_low, hidden_hbm, left.at[2])
    copy.start()
    copy.wait()


def pair_kernel(place, keep, bias, received, *outs):
    sends, keep_out, scratch = outs[:-2], outs[-2], outs[-1]
    chunk = place.chunk
    rank = place.plane_rank()
    scratch[...] = keep[...] + received[...].astype(F32)
    block = encode(bias[...]).astype(BF16)
    for step, send in zip(range(place.plane - 1, 0, -1), sends):
        send[0:BIAS_ROWS, :] = block
        at = pl.ds(pl.multiple_of((rank ^ step) * chunk, 8), chunk)
        send[BIAS_ROWS:, :] = scratch[at, :].astype(BF16)
    keep_out[...] = scratch[pl.ds(pl.multiple_of(rank * chunk, 8), chunk), :]


def plane_kernel(keep, bias, *refs):
    received, out = refs[:-2], refs[-1]
    total, bias_total = keep[...], bias[...]
    for ref in received:
        total += ref[BIAS_ROWS:, :].astype(F32)
        bias_total += decode(ref[0:BIAS_ROWS, :].astype(F32))
    out[0:BIAS_ROWS, :] = encode(bias_total).astype(BF16)
    out[BIAS_ROWS:, :] = total.astype(BF16)


def join_kernel(place, *refs):
    blocks, out = refs[:-2], refs[-1]
    rank = place.plane_rank()
    for step, block in enumerate(blocks):
        out[rank ^ step] = block[...]


def add_kernel(scale, own, received, out, *done_out):
    here, there = own[...].astype(F32), received[...].astype(F32)
    bias = (decode(here[0:BIAS_ROWS]) + decode(there[0:BIAS_ROWS])) * scale
    out[0:BIAS_ROWS, :] = encode(bias).astype(BF16)
    out[BIAS_ROWS:, :] = ((here[BIAS_ROWS:] + there[BIAS_ROWS:]) * scale).astype(BF16)
    for done in done_out:
        done[...] = jnp.zeros(done.shape, F32)


def store_half(place, half, blocks, out, wide, left):
    chunk, half_gates = place.chunk, place.half_gates
    gates = pl.ds(pl.multiple_of(half * half_gates, half_gates), half_gates)
    copies = []
    for index in range(place.plane):
        wide[index * chunk : (index + 1) * chunk, :] = blocks[index, BIAS_ROWS:, :].astype(F32)
        while len(copies) < min(place.taps, (index + 1) * chunk // half_gates):
            tap = len(copies)
            source = wide.at[tap * half_gates : (tap + 1) * half_gates, :]
            copies.append(pltpu.make_async_copy(source, out.at[tap, gates, :], left.at[tap]))
            copies[-1].start()
    return copies


def own_half_kernel(place, own, out, wide, left):
    for copy in store_half(place, place.rank(0), own, out, wide, left):
        copy.wait()


def other_half_kernel(place, own, received, out_before, out, bias_out, wide, bias_here, left):
    del out_before
    rank = place.rank(0)
    here, there = own[0, 0:BIAS_ROWS, :].astype(F32), received[0, 0:BIAS_ROWS, :].astype(F32)
    bias = decode(here) + decode(there)
    width = bias.shape[1]
    for index in range(bias_here.shape[0] // width):
        bias_here[pl.ds(index * width, width)] = bias[index]
    bias_copy = pltpu.make_async_copy(bias_here, bias_out, left.at[place.taps])
    bias_copy.start()
    copies = store_half(place, 1 - rank, received, out, wide, left)
    bias_copy.wait()
    for copy in copies:
        copy.wait()


def field_kernel(
    place,
    pre,
    outer_row,
    inner_row,
    outer_column,
    inner_column,
    weights,
    after,
    inputs_out,
    hidden_out,
    done_out,
    shifted,
    turned,
    wide,
):
    del after
    gate_count = pre.shape[0]
    channels = weights.shape[2]
    done_out[...] = jnp.zeros(done_out.shape, F32)
    hid, row_count, width = hidden_out.shape

    def emit(position, left, row, right):
        at = pl.ds(position * width, width)
        shifted[0:gate_count, at] = right.astype(BF16)
        shifted[gate_count : 2 * gate_count, at] = row.astype(BF16)
        shifted[2 * gate_count : 3 * gate_count, at] = left.astype(BF16)

    widened(
        row_count,
        lambda index: pre[:, pl.ds(index * width, width)].astype(F32),
        (inner_row, outer_row),
        (inner_column, outer_column),
        emit,
    )
    for a in range(3):
        for b in range(3):
            turned[a, :, b * gate_count : (b + 1) * gate_count] = weights[3 * a + b].T
    lat = place.position()[0]
    top = turned[jnp.where(lat == 0, 0, 2)]
    bottom = turned[jnp.where(lat == place.lat - 1, 2, 0)]

    def product(matrix, position, count):
        return jnp.dot(
            matrix, shifted[:, pl.ds(position * width, count * width)], preferred_element_type=F32
        )

    pair = 2 if row_count % 2 == 0 else 1
    for base in range(0, row_count, pair):
        total = product(turned[1], base + 1, pair)
        if base == 0:
            above = product(top, 0, 1)
            if pair == 2:
                above = jnp.concatenate([above, product(turned[2], 1, 1)], axis=1)
        else:
            above = product(turned[2], base, pair)
        if base + pair == row_count:
            below = product(bottom, row_count + 1, 1)
            if pair == 2:
                below = jnp.concatenate([product(turned[0], row_count, 1), below], axis=1)
        else:
            below = product(turned[0], base + 2, pair)
        total = total + above + below
        for offset in range(pair):
            value = total[:, offset * width : (offset + 1) * width]
            wide[pl.ds(base + offset, channels, stride=row_count), :] = value
    size = (channels - hid) * row_count
    inputs_out[...] = wide[0:size, :].reshape(inputs_out.shape).astype(BF16)
    hidden_out[...] = wide[size:, :].reshape(hidden_out.shape).astype(BF16)


def body(
    place,
    inputs_below,
    hidden_prev,
    cell_prev,
    kernel_weights,
    gate_bias,
    readout,
    target_field,
    land_mask,
    fire_mask,
    hidden_grad,
):
    hid, row_count, width = hidden_prev.shape
    gate_count, channels = kernel_weights.shape[1:]
    cells = row_count * width
    halo_cells = (row_count + 2) * width
    scaling = 1.0 / math.sqrt(cells * place.lat * place.lon)
    bind = functools.partial
    inner_rows, outer_rows = place.pairs(place.inner_rows), place.pairs(place.outer_rows)
    inner_columns = place.pairs(place.inner_columns)
    outer_columns = place.pairs(place.outer_columns)
    flat = sds((hid * row_count, width), F32)
    strip = sds((hid, width), F32)

    inner, outer, wide = call(
        pack_kernel,
        (
            sds((channels, width), BF16),
            sds((channels, width), BF16),
            sds((channels * row_count, width), F32),
        ),
        [
            pltpu.VMEM(inputs_below.shape, BF16),
            pltpu.VMEM(hidden_prev.shape, BF16),
            pltpu.SemaphoreType.DMA((2,)),
        ],
        remote=2,
        moved=4 * channels * cells,
    )(inputs_below, hidden_prev)
    inner, outer = permuted(inner, inner_rows), permuted(outer, outer_rows)
    (
        rows,
        columns,
        second,
        cell_strip,
        hidden_grad_strip,
        fields_strip,
        cell_here,
        weights_here,
        hidden_grad_here,
        target_here,
        land_here,
        fire_here,
        bias_wide,
        readout_wide,
    ) = call(
        prepare_kernel,
        (
            sds((row_count, channels, width), BF16),
            sds((channels, width), F32),
            sds((channels, width), F32),
            strip,
            strip,
            sds((8, width), F32),
            flat,
            sds(kernel_weights.shape, BF16),
            flat,
            sds(target_field.shape, F32),
            sds(land_mask.shape, jnp.int32),
            sds(fire_mask.shape, jnp.int32),
            sds((gate_count, width), F32),
            sds((hid, width), F32),
        ),
        [
            pltpu.VMEM(hidden_grad.shape, BF16),
            pltpu.VMEM(gate_bias.shape, F32),
            pltpu.VMEM(readout.shape, F32),
            pltpu.SemaphoreType.DMA((8,)),
        ],
        remote=8,
        moved=6_000_000,
    )(
        wide,
        cell_prev.reshape(hid * row_count, width),
        kernel_weights,
        hidden_grad,
        target_field,
        land_mask,
        fire_mask,
        gate_bias,
        readout,
    )
    columns, edge = call(
        bind(columns_kernel, row_count, GROUPS),
        (sds((channels // GROUPS, width), BF16), sds((channels, width), BF16)),
    )(columns, outer, inner)
    inner_column = permuted(columns, inner_columns)
    outer_column = permuted(columns, outer_columns)
    hidden_rows, cell_rows, grad_cell_rows, pre, second, sums, bias = call(
        bind(gates_kernel, place),
        (
            flat,
            flat,
            flat,
            sds((gate_count, cells), BF16),
            sds((channels, width), BF16),
            sds((2 * place.half_rows, channels), F32),
            sds((gate_count, width), F32),
        ),
        [pltpu.VMEM((3 * channels, halo_cells), BF16)],
        flops=4 * 9 * gate_count * channels * cells,
        moved=6_000_000,
        transcendentals=5 * hid * cells,
    )(
        rows,
        inner,
        outer,
        second,
        cell_here,
        weights_here,
        hidden_grad_here,
        target_here,
        land_here,
        fire_here,
        bias_wide,
        readout_wide,
    )
    send, pre_strip, pre_wide, patches, *strips = call(
        bind(strip_kernel, place, row_count),
        (
            sds((place.half_rows, channels), BF16),
            sds((gate_count, width), BF16),
            sds((gate_count, width), F32),
            sds((place.taps * channels, width), BF16),
            strip,
            strip,
            strip,
        ),
    )(
        edge,
        second,
        outer_column,
        inner_column,
        weights_here,
        bias_wide,
        readout_wide,
        cell_strip,
        hidden_grad_strip,
        fields_strip,
        sums,
    )
    keep, bias = call(
        bind(keep_kernel, place),
        (sds((place.half_rows, channels), F32), sds((8, channels), F32)),
    )(sums, pre_strip, patches, bias, pre_wide)
    hidden_next, cell_next, grad_cell, pre, pre_inner, pre_outer = call(
        bind(edges_kernel, row_count),
        (
            sds((hid, row_count, width), BF16),
            flat,
            flat,
            sds((gate_count, cells), BF16),
            sds((gate_count, width), BF16),
            sds((gate_count, width), BF16),
        ),
        [
            pltpu.VMEM((hid, row_count, width), BF16),
            pltpu.VMEM(flat.shape, F32),
            pltpu.VMEM(flat.shape, F32),
            pltpu.SemaphoreType.DMA((3,)),
        ],
        leaving=3,
        moved=4_000_000,
    )(hidden_rows, cell_rows, grad_cell_rows, pre, *strips, pre_strip)
    after = pre_inner
    pre_inner, pre_outer = permuted(pre_inner, inner_rows), permuted(pre_outer, outer_rows)
    pre_columns = call(
        bind(columns_kernel, row_count, PRE_GROUPS),
        (sds((gate_count // PRE_GROUPS, width), BF16),),
    )(pre_strip, pre_outer, pre_inner)[0]

    block = sds((BIAS_ROWS + place.chunk, channels), BF16)
    token = sds((8, width), F32)
    steps = range(place.plane - 1, 0, -1)
    *sends, keep = call(
        bind(pair_kernel, place),
        (*[block for _ in steps], sds((place.chunk, channels), F32)),
        [pltpu.VMEM((place.half_rows, channels), F32)],
    )(keep, bias, permuted(send, place.phase_pairs(0)))
    received = [permuted(send, place.plane_pairs(step)) for step, send in zip(steps, sends)]
    part = call(plane_kernel, block)(keep, bias, *received, after)
    pre_inner_columns = permuted(pre_columns, inner_columns)
    pre_outer_columns = permuted(pre_columns, outer_columns)
    phases = len(place.orders[0])
    for phase in range(1, phases):
        is_last = phase == phases - 1
        part, *summed = call(
            bind(add_kernel, scaling if is_last else 1.0), (block, token) if is_last else (block,)
        )(part, permuted(part, place.phase_pairs(phase)))
    grad_inputs, grad_hidden, field_done = call(
        bind(field_kernel, place),
        (
            sds((channels - hid, row_count, width), BF16),
            sds((hid, row_count, width), BF16),
            sds((8, width), F32),
        ),
        [
            pltpu.VMEM((3 * gate_count, halo_cells), BF16),
            pltpu.VMEM((3, channels, 3 * gate_count), BF16),
            pltpu.VMEM((channels * row_count, width), F32),
        ],
        flops=2 * 9 * gate_count * channels * cells,
        moved=2_000_000,
    )(
        pre,
        pre_outer,
        pre_inner,
        pre_outer_columns,
        pre_inner_columns,
        weights_here,
        *summed,
    )
    received = [permuted(part, place.plane_pairs(step)) for step in steps[::-1]]
    gathered = call(bind(join_kernel, place), sds((place.plane, *block.shape), BF16))(
        part, *received, field_done
    )
    received = permuted(gathered, place.phase_pairs(0))
    half = [pltpu.VMEM((place.half_rows, channels), F32)]
    grad_kernel = call(
        bind(own_half_kernel, place),
        (sds(kernel_weights.shape, F32),),
        half + [pltpu.SemaphoreType.DMA((place.taps,))],
        leaving=1,
        moved=6 * place.half_rows * channels,
    )(gathered)[0]
    grad_kernel, grad_bias = call(
        bind(other_half_kernel, place),
        (sds(kernel_weights.shape, F32), sds((gate_count,), F32)),
        half + [pltpu.VMEM((gate_count,), F32), pltpu.SemaphoreType.DMA((place.taps + 1,))],
        remote=1,
        leaving=2,
        aliases={2: 0},
        moved=6 * place.half_rows * channels,
    )(gathered, received, grad_kernel)
    shape = hidden_prev.shape
    return (
        hidden_next,
        cell_next.reshape(shape),
        grad_inputs,
        grad_hidden,
        grad_cell.reshape(shape),
        grad_kernel,
        grad_bias,
    )


def solution(mesh):
    lat_count, lon_count = mesh.shape["lat"], mesh.shape["lon"]
    split = Mesh(mesh.devices.reshape(lat_count // 2, 2, lon_count // 2, 2), AXES)
    field = P(None, ("band", "core"), ("reach", "near"))
    flat = P(("band", "core"), ("reach", "near"))

    def run(*args):
        place = Layout(lat_count, lon_count, *args[3].shape[:2])
        return jax.shard_map(
            functools.partial(body, place),
            mesh=split,
            in_specs=(field, field, field, P(), P(), P(), flat, flat, flat, field),
            out_specs=(field, field, field, field, field, P(), P()),
            check_vma=False,
        )(*args)

    return run
```

```python
import functools
import math

import jax
import jax.numpy as jnp
from jax import lax
from jax.experimental import pallas as pl
from jax.experimental.pallas import tpu as pltpu
from jax.sharding import Mesh, PartitionSpec as P

F32 = jnp.float32
BF16 = jnp.bfloat16
AXES = ("band", "core", "reach", "near")
BIAS_ROWS = 16
GROUPS = 4
PRE_GROUPS = 4
LAST = 16
VMEM = pl.BlockSpec(memory_space=pltpu.VMEM)
HBM = pl.BlockSpec(memory_space=pltpu.HBM)
ACROSS = (((1,), (1,)), ((), ()))


def sds(shape, dtype):
    return jax.ShapeDtypeStruct(shape, dtype)


def call(
    kernel,
    out_shape,
    scratch=(),
    remote=0,
    leaving=0,
    aliases=None,
    flops=0,
    moved=0,
    transcendentals=0,
):
    several = isinstance(out_shape, tuple)
    shapes = out_shape if several else (out_shape,)
    out_specs = tuple([HBM] * leaving + [VMEM] * (len(shapes) - leaving))

    def run(*args):
        near = len(args) - remote
        far = [pltpu.with_memory_space_constraint(arg, pltpu.HBM) for arg in args[near:]]
        return pl.pallas_call(
            kernel,
            out_shape=out_shape,
            in_specs=[VMEM] * near + [HBM] * remote,
            out_specs=out_specs if several else out_specs[0],
            input_output_aliases=aliases or {},
            scratch_shapes=list(scratch),
            cost_estimate=pl.CostEstimate(
                flops=flops, bytes_accessed=moved, transcendentals=transcendentals
            ),
            compiler_params=pltpu.CompilerParams(vmem_limit_bytes=24 * 1024 * 1024),
        )(*args[:near], *far)

    return run


class Layout:
    def __init__(self, lat_count, lon_count, taps, gate_count):
        self.lat, self.lon = lat_count, lon_count
        self.half = lon_count // 2
        self.taps, self.half_gates = taps, gate_count // 2
        self.plane = lat_count
        whole = [("lon", 1 << k) for k in range(1, lon_count.bit_length() - 1)]
        self.orders = ([("lat", 1)] + whole, [("lat", 1)] + whole[::-1])
        step = 8 * self.plane
        self.half_rows = -(-taps * self.half_gates // step) * step
        self.chunk = self.half_rows // self.plane

    def position(self):
        lat = 2 * lax.axis_index("band") + lax.axis_index("core")
        return lat, 2 * lax.axis_index("reach") + lax.axis_index("near")

    def rank(self, phase):
        lat, lon = self.position()

        def digit(order):
            axis, bit = order[phase]
            return ((lat if axis == "lat" else lon) // bit) % 2

        return jnp.where(lat % 2 == 0, digit(self.orders[0]), digit(self.orders[1]))

    def pairs(self, partner):
        result = []
        for lat in range(self.lat):
            for lon in range(self.lon):
                there = partner(lat, lon)
                result.append((lat * self.lon + lon, there[0] * self.lon + there[1]))
        return result

    def phase_pairs(self, phase):
        def partner(lat, lon):
            axis, bit = self.orders[lat % 2][phase]
            return (lat ^ bit, lon) if axis == "lat" else (lat, lon ^ bit)

        return self.pairs(partner)

    def plane_rank(self):
        return 2 * lax.axis_index("band") + lax.axis_index("near")

    def plane_pairs(self, step):
        def partner(lat, lon):
            there = (lat // 2 * 2 + lon % 2) ^ step
            return there // 2 * 2 + lat % 2, lon // 2 * 2 + there % 2

        return self.pairs(partner)

    def inner_rows(self, lat, lon):
        return lat ^ 1, lon

    def outer_rows(self, lat, lon):
        there = lat + 1 if lat % 2 else lat - 1
        if 0 <= there < self.lat:
            return there, lon
        return lat, (lon + self.half) % self.lon

    def inner_columns(self, lat, lon):
        return lat, lon ^ 1

    def outer_columns(self, lat, lon):
        return lat, (lon + (1 if lon % 2 else -1)) % self.lon


def permuted(value, pairs):
    return lax.ppermute(value, AXES, pairs)


def lanes(shape):
    return lax.broadcasted_iota(jnp.int32, shape, len(shape) - 1)


def rolled(value, shift):
    shift %= value.shape[1]
    return pltpu.roll(value, shift, 1) if shift else value


def edge_columns(row, position, columns):
    lane = lanes(row.shape)
    columns = jnp.where(lane == position, rolled(row, position), columns)
    return jnp.where(lane == LAST + position, rolled(row, LAST + position + 1), columns)


def second_columns(row, position, columns):
    lane = lanes(row.shape)
    columns = jnp.where(lane == position, rolled(row, position - 1), columns)
    return jnp.where(lane == LAST + position, rolled(row, LAST + position + 2), columns)


def at_edges(row, position, columns):
    lane = lanes(row.shape)
    width = row.shape[1]
    row = jnp.where(lane == 0, rolled(columns, -position), row)
    return jnp.where(lane == width - 1, rolled(columns, width - 1 - LAST - position), row)


def pick(flag, yes, no):
    return jnp.where(flag, yes, no)


def is_odd(axis):
    return lax.axis_index(axis) % 2 == 1


def row_sends(first, last, inner_out, outer_out):
    odd = is_odd("core")
    inner_out[...] = pick(odd, first, last).astype(BF16)
    outer_out[...] = pick(odd, last, first).astype(BF16)


def row_halo(inner, outer):
    odd = is_odd("core")
    inner, outer = inner[...].astype(F32), outer[...].astype(F32)
    return pick(odd, inner, outer), pick(odd, outer, inner)


def packed(columns, groups):
    count, width = columns.shape[0] // groups, columns.shape[1] // groups
    lane = lanes((count, columns.shape[1]))
    value = columns[0:count]
    for group in range(1, groups):
        part = rolled(columns[group * count : (group + 1) * count], group * width)
        value = jnp.where(lane >= group * width, part, value)
    return value


def unpacked(value, groups):
    width = value.shape[1] // groups
    return jnp.concatenate([rolled(value, -group * width) for group in range(groups)], axis=0)


def column_halo(inner, outer, groups):
    odd = is_odd("near")
    inner, outer = inner[...].astype(F32), outer[...].astype(F32)
    return unpacked(pick(odd, inner, outer), groups), unpacked(pick(odd, outer, inner), groups)


def pack_kernel(below, hidden, inner_out, outer_out, wide_out, below_here, hidden_here, arrived):
    first = pltpu.make_async_copy(below, below_here, arrived.at[0])
    second = pltpu.make_async_copy(hidden, hidden_here, arrived.at[1])
    first.start()
    second.start()
    channels, row_count, width = below.shape
    size = channels * row_count
    first.wait()
    wide_out[0:size, :] = below_here[...].astype(F32).reshape(size, width)
    second.wait()
    wide_out[size : 2 * size, :] = hidden_here[...].astype(F32).reshape(size, width)
    edges = [
        wide_out[pl.ds(index, 2 * channels, stride=row_count), :] for index in (0, row_count - 1)
    ]
    row_sends(edges[0], edges[1], inner_out, outer_out)


def down_rows(values, width):
    count = values.shape[0]
    return jnp.broadcast_to(values[None, :], (width, count)).T


def prepare_kernel(
    wide,
    cell_hbm,
    weights_hbm,
    hidden_grad_hbm,
    target_hbm,
    land_hbm,
    fire_hbm,
    gate_bias_hbm,
    readout_hbm,
    rows_out,
    columns_out,
    second_out,
    cell_strip_out,
    hidden_grad_strip_out,
    fields_strip_out,
    cell_out,
    weights_out,
    hidden_grad_out,
    target_out,
    land_out,
    fire_out,
    bias_wide_out,
    readout_wide_out,
    hidden_grad_here,
    gate_bias_here,
    readout_here,
    arrived,
):
    copies = [
        pltpu.make_async_copy(source, target, arrived.at[index])
        for index, (source, target) in enumerate(
            (
                (cell_hbm, cell_out),
                (weights_hbm, weights_out),
                (hidden_grad_hbm, hidden_grad_here),
                (target_hbm, target_out),
                (land_hbm, land_out),
                (fire_hbm, fire_out),
                (gate_bias_hbm, gate_bias_here),
                (readout_hbm, readout_here),
            )
        )
    ]
    for copy in copies:
        copy.start()
    row_count, channels, width = rows_out.shape
    columns = jnp.zeros((channels, width), F32)
    second = jnp.zeros((channels, width), F32)
    for index in range(row_count):
        row = wide[pl.ds(index, channels, stride=row_count), :]
        rows_out[index] = row.astype(BF16)
        columns = edge_columns(row, index + 1, columns)
        second = second_columns(row, index + 1, second)
    columns_out[...] = columns
    second_out[...] = second
    for copy in copies:
        copy.wait()
    hidden_grad_out[...] = hidden_grad_here[...].astype(F32).reshape(hidden_grad_out.shape)
    bias_wide_out[...] = down_rows(gate_bias_here[...], width)
    readout_wide_out[...] = down_rows(readout_here[...], width)
    hid = hidden_grad_here.shape[0]
    cell_strip = jnp.zeros((hid, width), F32)
    hidden_grad_strip = jnp.zeros((hid, width), F32)
    fields_strip = jnp.zeros((8, width), F32)
    for index in range(row_count):
        strided = pl.ds(index, hid, stride=row_count)
        cell_strip = edge_columns(cell_out[strided, :], index + 1, cell_strip)
        hidden_grad_strip = edge_columns(hidden_grad_out[strided, :], index + 1, hidden_grad_strip)
        at = slice(index, index + 1)
        fields = [target_out[at, :], land_out[at, :].astype(F32), fire_out[at, :].astype(F32)]
        fields = jnp.concatenate(fields + [jnp.zeros((5, width), F32)], axis=0)
        fields_strip = edge_columns(fields, index + 1, fields_strip)
    cell_strip_out[...] = cell_strip
    hidden_grad_strip_out[...] = hidden_grad_strip
    fields_strip_out[...] = fields_strip


def columns_kernel(row_count, groups, columns, outer, inner, packed_out, *whole_out):
    north, south = row_halo(inner, outer)
    value = edge_columns(north, 0, columns[...].astype(F32))
    value = edge_columns(south, row_count + 1, value)
    packed_out[...] = packed(value, groups).astype(BF16)
    for out in whole_out:
        out[...] = value.astype(BF16)


def encode(bias):
    high = bias.astype(BF16).astype(F32)
    return jnp.concatenate([high, bias - high], axis=0)


def decode(block):
    return block[0:8] + block[8:16]


def cell_step(part, cell_before, hidden_grad, target, land, fire, readout):
    hid = part.shape[0] // 4
    input_gate = 0.5 + 0.5 * jnp.tanh(0.5 * part[0:hid])
    forget_gate = 0.5 + 0.5 * jnp.tanh(0.5 * part[hid : 2 * hid])
    output_gate = 0.5 + 0.5 * jnp.tanh(0.5 * part[2 * hid : 3 * hid])
    candidate = jnp.tanh(part[3 * hid : 4 * hid])
    cell_next = land * (forget_gate * cell_before + input_gate * candidate)
    squashed = jnp.tanh(cell_next)
    hidden_next = (output_gate * squashed).astype(BF16).astype(F32)
    predicted = jnp.sum(readout * hidden_next, axis=0, keepdims=True)
    total_grad = hidden_grad + 2.0 * (fire * (predicted - target)) * readout
    cell_grad = land * total_grad * output_gate * (1.0 - squashed * squashed)
    pre_grad = jnp.concatenate(
        [
            cell_grad * candidate * input_gate * (1.0 - input_gate),
            cell_grad * cell_before * forget_gate * (1.0 - forget_gate),
            total_grad * squashed * output_gate * (1.0 - output_gate),
            cell_grad * input_gate * (1.0 - candidate * candidate),
        ],
        axis=0,
    )
    return hidden_next, cell_next, cell_grad * forget_gate, pre_grad


def gates_kernel(
    place,
    rows_in,
    inner_row,
    outer_row,
    second,
    cell_prev,
    weights,
    hidden_grad,
    target,
    land,
    fire,
    bias_wide,
    readout_wide,
    hidden_out,
    cell_out,
    grad_cell_out,
    pre_out,
    second_out,
    sums,
    bias_out,
    shifted,
):
    row_count, channels, width = rows_in.shape
    gate_count = weights.shape[1]
    hid = gate_count // 4
    half_gates = place.half_gates
    north, south = row_halo(inner_row, outer_row)
    columns = second_columns(north, 0, second[...])
    second_out[...] = second_columns(south, row_count + 1, columns).astype(BF16)
    for position in range(row_count + 2):
        if position == 0:
            row = north
        elif position == row_count + 1:
            row = south
        else:
            row = rows_in[position - 1].astype(F32)
        at = pl.ds(position * width, width)
        shifted[0:channels, at] = rolled(row, 1).astype(BF16)
        shifted[channels : 2 * channels, at] = row.astype(BF16)
        shifted[2 * channels : 3 * channels, at] = rolled(row, -1).astype(BF16)

    taps = [
        jnp.concatenate([weights[3 * a], weights[3 * a + 1], weights[3 * a + 2]], axis=1)
        for a in range(3)
    ]
    bias_total = jnp.zeros((gate_count, width), F32)
    lane = lanes((gate_count, width))
    inside = (lane > 0) & (lane < width - 1)
    readout = readout_wide[...]
    pair = 2 if row_count % 2 == 0 else 1
    for base in range(0, row_count, pair):
        preact = jnp.zeros((gate_count, pair * width), F32)
        for a in range(3):
            preact += jnp.dot(
                taps[a],
                shifted[:, pl.ds((base + a) * width, pair * width)],
                preferred_element_type=F32,
            )
        for offset in range(pair):
            index = base + offset
            strided = pl.ds(index, hid, stride=row_count)
            at = slice(index, index + 1)
            hidden_next, cell_next, grad_cell, pre_grad = cell_step(
                preact[:, offset * width : (offset + 1) * width] + bias_wide[...],
                cell_prev[strided, :],
                hidden_grad[strided, :],
                target[at, :],
                land[at, :].astype(F32),
                fire[at, :].astype(F32),
                readout,
            )
            hidden_out[strided, :] = hidden_next
            cell_out[strided, :] = cell_next
            grad_cell_out[strided, :] = grad_cell
            pre_grad = jnp.where(inside, pre_grad, 0.0)
            bias_total += pre_grad
            pre_out[:, pl.ds(index * width, width)] = pre_grad.astype(BF16)
    bias_out[...] = bias_total

    for a in range(3):
        product = lax.dot_general(
            pre_out[...],
            shifted[:, pl.ds(a * width, row_count * width)],
            ACROSS,
            preferred_element_type=F32,
        )
        for b in range(3):
            for half in range(2):
                at = half * place.half_rows + (3 * a + b) * half_gates
                sums[at : at + half_gates, :] = product[
                    half * half_gates : (half + 1) * half_gates, b * channels : (b + 1) * channels
                ]
    used = place.taps * half_gates
    if place.half_rows > used:
        for half in range(2):
            at = half * place.half_rows
            sums[at + used : at + place.half_rows, :] = jnp.zeros(
                (place.half_rows - used, channels), F32
            )


def add_strip(place, half, sums, pre_strip, patches, out):
    half_gates, channels = place.half_gates, sums.shape[1]
    gates = pre_strip[pl.ds(pl.multiple_of(half * half_gates, half_gates), half_gates), :]
    product = lax.dot_general(gates, patches[...], ACROSS, preferred_element_type=F32)
    base = half * place.half_rows
    for tap in range(place.taps):
        at = pl.ds(pl.multiple_of(base + tap * half_gates, 8), half_gates)
        value = sums[at, :] + product[:, tap * channels : (tap + 1) * channels]
        out[tap * half_gates : (tap + 1) * half_gates, :] = value.astype(out.dtype)
    used = place.taps * half_gates
    if place.half_rows > used:
        rest = jnp.zeros((place.half_rows - used, channels), out.dtype)
        out[used:, :] = rest


def strip_kernel(
    place,
    row_count,
    edge,
    second,
    outer_column,
    inner_column,
    weights,
    bias_wide,
    readout_wide,
    cell_strip,
    hidden_grad_strip,
    fields_strip,
    sums,
    send_out,
    pre_out,
    pre_wide_out,
    patches,
    hidden_out,
    cell_out,
    grad_cell_out,
):
    channels, width = edge.shape
    west, east = column_halo(inner_column, outer_column, GROUPS)
    near_first = lanes((channels, width)) < LAST
    inner = second[...].astype(F32)
    columns = (
        jnp.where(near_first, rolled(west, -LAST), inner),
        edge[...].astype(F32),
        jnp.where(near_first, inner, rolled(east, LAST)),
    )
    for a in range(3):
        for b in range(3):
            at = (3 * a + b) * channels
            patches[at : at + channels, :] = rolled(columns[b], 1 - a).astype(BF16)
    taps = jnp.concatenate([weights[tap] for tap in range(place.taps)], axis=1)
    preact = jnp.dot(taps, patches[...], preferred_element_type=F32) + bias_wide[...]
    hidden_next, cell_next, grad_cell, pre_grad = cell_step(
        preact,
        cell_strip[...],
        hidden_grad_strip[...],
        fields_strip[0:1, :],
        fields_strip[1:2, :],
        fields_strip[2:3, :],
        readout_wide[...],
    )
    hidden_out[...] = hidden_next
    cell_out[...] = cell_next
    grad_cell_out[...] = grad_cell
    lane = lanes(pre_grad.shape)
    lane = jnp.where(lane >= LAST, lane - LAST, lane)
    pre_grad = jnp.where((lane >= 1) & (lane <= row_count), pre_grad, 0.0)
    pre_out[...] = pre_grad.astype(BF16)
    pre_wide_out[...] = pre_grad
    add_strip(place, 1 - place.rank(0), sums, pre_out, patches, send_out)


def keep_kernel(place, sums, pre_strip, patches, bias_partial, pre_wide, out, bias_out):
    add_strip(place, place.rank(0), sums, pre_strip, patches, out)
    channels = sums.shape[1]
    bias_total = bias_partial[...] + pre_wide[...]
    ones = jnp.ones((8, bias_total.shape[1]), BF16)
    high = bias_total.astype(BF16)
    low = (bias_total - high.astype(F32)).astype(BF16)
    flat = lax.dot_general(ones, high, ACROSS, preferred_element_type=F32)
    flat += lax.dot_general(ones, low, ACROSS, preferred_element_type=F32)
    odd = lax.broadcasted_iota(jnp.int32, (8, channels), 0) % 2 == 1
    bias_out[...] = jnp.where(odd, flat[:, channels : 2 * channels], flat[:, 0:channels])


def edges_kernel(
    row_count,
    hidden,
    cell,
    grad_cell,
    pre,
    hidden_strip,
    cell_strip,
    grad_cell_strip,
    pre_strip,
    hidden_hbm,
    cell_hbm,
    grad_cell_hbm,
    pre_out,
    inner_out,
    outer_out,
    hidden_low,
    hidden_here,
    cell_here,
    grad_cell_here,
    left,
):
    hid, _, width = hidden_low.shape
    leaving = []
    for source, strip, here, ready, target in (
        (cell, cell_strip, cell_here, cell_here, cell_hbm),
        (grad_cell, grad_cell_strip, grad_cell_here, grad_cell_here, grad_cell_hbm),
        (hidden, hidden_strip, hidden_here, hidden_low, hidden_hbm),
    ):
        columns = strip[...]
        for index in range(row_count):
            strided = pl.ds(index, hid, stride=row_count)
            here[strided, :] = at_edges(source[strided, :], index + 1, columns)
        if ready is hidden_low:
            hidden_low[...] = here[...].reshape(hidden_low.shape).astype(BF16)
        leaving.append(pltpu.make_async_copy(ready, target, left.at[len(leaving)]))
        leaving[-1].start()
    first, last = None, None
    columns = pre_strip[...].astype(F32)
    for index in range(row_count):
        at = pl.ds(index * width, width)
        row = at_edges(pre[:, at].astype(F32), index + 1, columns)
        pre_out[:, at] = row.astype(BF16)
        first = row if index == 0 else first
        last = row
    row_sends(first, last, inner_out, outer_out)
    for copy in leaving:
        copy.wait()


def pair_kernel(place, keep, bias, received, *outs):
    sends, keep_out, scratch = outs[:-2], outs[-2], outs[-1]
    chunk = place.chunk
    rank = place.plane_rank()
    scratch[...] = keep[...] + received[...].astype(F32)
    block = encode(bias[...]).astype(BF16)
    for step, send in zip(range(place.plane - 1, 0, -1), sends):
        send[0:BIAS_ROWS, :] = block
        at = pl.ds(pl.multiple_of((rank ^ step) * chunk, 8), chunk)
        send[BIAS_ROWS:, :] = scratch[at, :].astype(BF16)
    keep_out[...] = scratch[pl.ds(pl.multiple_of(rank * chunk, 8), chunk), :]


def plane_kernel(keep, bias, *refs):
    received, out = refs[:-2], refs[-1]
    total, bias_total = keep[...], bias[...]
    for ref in received:
        total += ref[BIAS_ROWS:, :].astype(F32)
        bias_total += decode(ref[0:BIAS_ROWS, :].astype(F32))
    out[0:BIAS_ROWS, :] = encode(bias_total).astype(BF16)
    out[BIAS_ROWS:, :] = total.astype(BF16)


def join_kernel(place, *refs):
    blocks, out = refs[:-2], refs[-1]
    rank = place.plane_rank()
    for step, block in enumerate(blocks):
        out[rank ^ step] = block[...]


def add_kernel(scale, own, received, out):
    here, there = own[...].astype(F32), received[...].astype(F32)
    bias = (decode(here[0:BIAS_ROWS]) + decode(there[0:BIAS_ROWS])) * scale
    out[0:BIAS_ROWS, :] = encode(bias).astype(BF16)
    out[BIAS_ROWS:, :] = ((here[BIAS_ROWS:] + there[BIAS_ROWS:]) * scale).astype(BF16)


def store_half(place, half, blocks, out, wide, left):
    chunk, half_gates = place.chunk, place.half_gates
    gates = pl.ds(pl.multiple_of(half * half_gates, half_gates), half_gates)
    copies = []
    for index in range(place.plane):
        wide[index * chunk : (index + 1) * chunk, :] = blocks[index, BIAS_ROWS:, :].astype(F32)
        while len(copies) < min(place.taps, (index + 1) * chunk // half_gates):
            tap = len(copies)
            source = wide.at[tap * half_gates : (tap + 1) * half_gates, :]
            copies.append(pltpu.make_async_copy(source, out.at[tap, gates, :], left.at[tap]))
            copies[-1].start()
    return copies


def own_half_kernel(place, own, out, wide, left):
    for copy in store_half(place, place.rank(0), own, out, wide, left):
        copy.wait()


def other_half_kernel(
    place, own, received, after, out_before, out, bias_out, wide, bias_here, left
):
    del after, out_before
    rank = place.rank(0)
    here, there = own[0, 0:BIAS_ROWS, :].astype(F32), received[0, 0:BIAS_ROWS, :].astype(F32)
    bias = decode(here) + decode(there)
    width = bias.shape[1]
    for index in range(bias_here.shape[0] // width):
        bias_here[pl.ds(index * width, width)] = bias[index]
    bias_copy = pltpu.make_async_copy(bias_here, bias_out, left.at[place.taps])
    bias_copy.start()
    copies = store_half(place, 1 - rank, received, out, wide, left)
    bias_copy.wait()
    for copy in copies:
        copy.wait()


def field_kernel(pre, weights, wide_out, turned_out, done_out, shifted):
    done_out[...] = jnp.zeros(done_out.shape, F32)
    gate_count, cells = pre.shape
    channels, width = weights.shape[2], wide_out.shape[1]
    row_count = cells // width
    lane = lanes((gate_count, width))
    for index in range(row_count):
        at = pl.ds(index * width, width)
        row = pre[:, at].astype(F32)
        left = jnp.where(lane == 0, 0.0, rolled(row, 1))
        right = jnp.where(lane == width - 1, 0.0, rolled(row, -1))
        shifted[0:gate_count, at] = right.astype(BF16)
        shifted[gate_count : 2 * gate_count, at] = pre[:, at]
        shifted[2 * gate_count : 3 * gate_count, at] = left.astype(BF16)
    for a in range(3):
        for b in range(3):
            turned_out[a, :, b * gate_count : (b + 1) * gate_count] = weights[3 * a + b].T

    def product(a, index, count):
        return jnp.dot(
            turned_out[a],
            shifted[:, pl.ds(index * width, count * width)],
            preferred_element_type=F32,
        )

    pair = 2 if row_count % 2 == 0 else 1
    for base in range(0, row_count, pair):
        total = product(1, base, pair)
        for a, first in ((2, base - 1), (0, base + 1)):
            low, high = max(first, 0), min(first + pair, row_count)
            if low >= high:
                continue
            part = product(a, low, high - low)
            blank = jnp.zeros((channels, width), F32)
            parts = [blank] * (low - first) + [part] + [blank] * (first + pair - high)
            total += jnp.concatenate(parts, axis=1)
        for offset in range(pair):
            value = total[:, offset * width : (offset + 1) * width]
            wide_out[pl.ds(base + offset, channels, stride=row_count), :] = value


def field_halo_kernel(
    place,
    wide,
    turned,
    outer_row,
    inner_row,
    outer_column,
    inner_column,
    inputs_out,
    hidden_out,
    done_out,
    total,
):
    done_out[...] = jnp.zeros(done_out.shape, F32)
    hid, row_count, width = hidden_out.shape
    channels = turned.shape[1]
    gate_count = turned.shape[2] // 3
    north, south = row_halo(inner_row, outer_row)
    west, east = column_halo(inner_column, outer_column, PRE_GROUPS)
    lane = lanes((gate_count, width))
    lat = place.position()[0]

    def row_part(taps, row, position):
        left = jnp.where(lane == 0, rolled(west, -LAST - position), rolled(row, 1))
        right = rolled(east, width - 1 - position)
        right = jnp.where(lane == width - 1, right, rolled(row, -1))
        stack = jnp.concatenate([right, row, left], axis=0).astype(BF16)
        return jnp.dot(taps, stack, preferred_element_type=F32)

    above = row_part(turned[jnp.where(lat == 0, 0, 2)], north, 0)
    below = row_part(turned[jnp.where(lat == place.lat - 1, 2, 0)], south, row_count + 1)

    inside = (lane >= 1) & (lane <= row_count)
    west = jnp.where(inside, rolled(west, -LAST), 0.0)
    east = jnp.where(inside, east, 0.0)
    sides = [rolled(west, a - 1) for a in range(3)] + [rolled(east, LAST + a - 1) for a in range(3)]
    taps = [turned[a, :, 2 * gate_count : 3 * gate_count] for a in range(3)]
    taps += [turned[a, :, 0:gate_count] for a in range(3)]
    columns = jnp.dot(
        jnp.concatenate(taps, axis=1),
        jnp.concatenate(sides, axis=0).astype(BF16),
        preferred_element_type=F32,
    )
    blank = jnp.zeros((channels, width), F32)
    for index in range(row_count):
        strided = pl.ds(index, channels, stride=row_count)
        value = wide[strided, :] + at_edges(blank, index + 1, columns)
        if index == 0:
            value += above
        if index == row_count - 1:
            value += below
        total[strided, :] = value
    size = (channels - hid) * row_count
    inputs_out[...] = total[0:size, :].reshape(inputs_out.shape).astype(BF16)
    hidden_out[...] = total[size:, :].reshape(hidden_out.shape).astype(BF16)


def body(
    place,
    inputs_below,
    hidden_prev,
    cell_prev,
    kernel_weights,
    gate_bias,
    readout,
    target_field,
    land_mask,
    fire_mask,
    hidden_grad,
):
    hid, row_count, width = hidden_prev.shape
    gate_count, channels = kernel_weights.shape[1:]
    cells = row_count * width
    halo_cells = (row_count + 2) * width
    scaling = 1.0 / math.sqrt(cells * place.lat * place.lon)
    bind = functools.partial
    inner_rows, outer_rows = place.pairs(place.inner_rows), place.pairs(place.outer_rows)
    inner_columns = place.pairs(place.inner_columns)
    outer_columns = place.pairs(place.outer_columns)
    flat = sds((hid * row_count, width), F32)
    strip = sds((hid, width), F32)

    inner, outer, wide = call(
        pack_kernel,
        (
            sds((channels, width), BF16),
            sds((channels, width), BF16),
            sds((channels * row_count, width), F32),
        ),
        [
            pltpu.VMEM(inputs_below.shape, BF16),
            pltpu.VMEM(hidden_prev.shape, BF16),
            pltpu.SemaphoreType.DMA((2,)),
        ],
        remote=2,
        moved=4 * channels * cells,
    )(inputs_below, hidden_prev)
    inner, outer = permuted(inner, inner_rows), permuted(outer, outer_rows)
    (
        rows,
        columns,
        second,
        cell_strip,
        hidden_grad_strip,
        fields_strip,
        cell_here,
        weights_here,
        hidden_grad_here,
        target_here,
        land_here,
        fire_here,
        bias_wide,
        readout_wide,
    ) = call(
        prepare_kernel,
        (
            sds((row_count, channels, width), BF16),
            sds((channels, width), F32),
            sds((channels, width), F32),
            strip,
            strip,
            sds((8, width), F32),
            flat,
            sds(kernel_weights.shape, BF16),
            flat,
            sds(target_field.shape, F32),
            sds(land_mask.shape, jnp.int32),
            sds(fire_mask.shape, jnp.int32),
            sds((gate_count, width), F32),
            sds((hid, width), F32),
        ),
        [
            pltpu.VMEM(hidden_grad.shape, BF16),
            pltpu.VMEM(gate_bias.shape, F32),
            pltpu.VMEM(readout.shape, F32),
            pltpu.SemaphoreType.DMA((8,)),
        ],
        remote=8,
        moved=6_000_000,
    )(
        wide,
        cell_prev.reshape(hid * row_count, width),
        kernel_weights,
        hidden_grad,
        target_field,
        land_mask,
        fire_mask,
        gate_bias,
        readout,
    )
    columns, edge = call(
        bind(columns_kernel, row_count, GROUPS),
        (sds((channels // GROUPS, width), BF16), sds((channels, width), BF16)),
    )(columns, outer, inner)
    inner_column = permuted(columns, inner_columns)
    outer_column = permuted(columns, outer_columns)
    hidden_rows, cell_rows, grad_cell_rows, pre, second, sums, bias = call(
        bind(gates_kernel, place),
        (
            flat,
            flat,
            flat,
            sds((gate_count, cells), BF16),
            sds((channels, width), BF16),
            sds((2 * place.half_rows, channels), F32),
            sds((gate_count, width), F32),
        ),
        [pltpu.VMEM((3 * channels, halo_cells), BF16)],
        flops=4 * 9 * gate_count * channels * cells,
        moved=6_000_000,
        transcendentals=5 * hid * cells,
    )(
        rows,
        inner,
        outer,
        second,
        cell_here,
        weights_here,
        hidden_grad_here,
        target_here,
        land_here,
        fire_here,
        bias_wide,
        readout_wide,
    )
    send, pre_strip, pre_wide, patches, *strips = call(
        bind(strip_kernel, place, row_count),
        (
            sds((place.half_rows, channels), BF16),
            sds((gate_count, width), BF16),
            sds((gate_count, width), F32),
            sds((place.taps * channels, width), BF16),
            strip,
            strip,
            strip,
        ),
    )(
        edge,
        second,
        outer_column,
        inner_column,
        weights_here,
        bias_wide,
        readout_wide,
        cell_strip,
        hidden_grad_strip,
        fields_strip,
        sums,
    )
    keep, bias = call(
        bind(keep_kernel, place),
        (sds((place.half_rows, channels), F32), sds((8, channels), F32)),
    )(sums, pre_strip, patches, bias, pre_wide)
    hidden_next, cell_next, grad_cell, pre, pre_inner, pre_outer = call(
        bind(edges_kernel, row_count),
        (
            sds((hid, row_count, width), BF16),
            flat,
            flat,
            sds((gate_count, cells), BF16),
            sds((gate_count, width), BF16),
            sds((gate_count, width), BF16),
        ),
        [
            pltpu.VMEM((hid, row_count, width), BF16),
            pltpu.VMEM(flat.shape, F32),
            pltpu.VMEM(flat.shape, F32),
            pltpu.VMEM(flat.shape, F32),
            pltpu.SemaphoreType.DMA((3,)),
        ],
        leaving=3,
        moved=4_000_000,
    )(hidden_rows, cell_rows, grad_cell_rows, pre, *strips, pre_strip)
    pre_inner, pre_outer = permuted(pre_inner, inner_rows), permuted(pre_outer, outer_rows)
    pre_columns = call(
        bind(columns_kernel, row_count, PRE_GROUPS),
        (sds((gate_count // PRE_GROUPS, width), BF16),),
    )(pre_strip, pre_outer, pre_inner)[0]

    block = sds((BIAS_ROWS + place.chunk, channels), BF16)
    token = sds((8, width), F32)
    steps = range(place.plane - 1, 0, -1)
    *sends, keep = call(
        bind(pair_kernel, place),
        (*[block for _ in steps], sds((place.chunk, channels), F32)),
        [pltpu.VMEM((place.half_rows, channels), F32)],
    )(keep, bias, permuted(send, place.phase_pairs(0)))
    received = [permuted(send, place.plane_pairs(step)) for step, send in zip(steps, sends)]
    field, turned, field_done = call(
        field_kernel,
        (
            sds((channels * row_count, width), F32),
            sds((3, channels, 3 * gate_count), BF16),
            token,
        ),
        [pltpu.VMEM((3 * gate_count, cells), BF16)],
        flops=2 * 9 * gate_count * channels * cells,
        moved=3_000_000,
    )(pre, weights_here)
    part = call(plane_kernel, block)(keep, bias, *received, field_done)
    pre_inner_columns = permuted(pre_columns, inner_columns)
    pre_outer_columns = permuted(pre_columns, outer_columns)
    phases = len(place.orders[0])
    for phase in range(1, phases):
        is_last = phase == phases - 1
        part = call(bind(add_kernel, scaling if is_last else 1.0), block)(
            part, permuted(part, place.phase_pairs(phase))
        )
    received = [permuted(part, place.plane_pairs(step)) for step in steps[::-1]]
    grad_inputs, grad_hidden, field_done = call(
        bind(field_halo_kernel, place),
        (
            sds((channels - hid, row_count, width), BF16),
            sds((hid, row_count, width), BF16),
            token,
        ),
        [pltpu.VMEM((channels * row_count, width), F32)],
        flops=40 * gate_count * channels * cells * 9,
        moved=2_000_000,
    )(field, turned, pre_outer, pre_inner, pre_outer_columns, pre_inner_columns)
    gathered = call(bind(join_kernel, place), sds((place.plane, *block.shape), BF16))(
        part, *received, field_done
    )
    received = permuted(gathered, place.phase_pairs(0))
    half = [pltpu.VMEM((place.half_rows, channels), F32)]
    grad_kernel = call(
        bind(own_half_kernel, place),
        (sds(kernel_weights.shape, F32),),
        half + [pltpu.SemaphoreType.DMA((place.taps,))],
        leaving=1,
        moved=6 * place.half_rows * channels,
    )(gathered)[0]
    grad_kernel, grad_bias = call(
        bind(other_half_kernel, place),
        (sds(kernel_weights.shape, F32), sds((gate_count,), F32)),
        half + [pltpu.VMEM((gate_count,), F32), pltpu.SemaphoreType.DMA((place.taps + 1,))],
        remote=1,
        leaving=2,
        aliases={3: 0},
        moved=6 * place.half_rows * channels,
    )(gathered, received, target_here, grad_kernel)
    shape = hidden_prev.shape
    return (
        hidden_next,
        cell_next.reshape(shape),
        grad_inputs,
        grad_hidden,
        grad_cell.reshape(shape),
        grad_kernel,
        grad_bias,
    )


def solution(mesh):
    lat_count, lon_count = mesh.shape["lat"], mesh.shape["lon"]
    split = Mesh(mesh.devices.reshape(lat_count // 2, 2, lon_count // 2, 2), AXES)
    field = P(None, ("band", "core"), ("reach", "near"))
    flat = P(("band", "core"), ("reach", "near"))

    def run(*args):
        place = Layout(lat_count, lon_count, *args[3].shape[:2])
        return jax.shard_map(
            functools.partial(body, place),
            mesh=split,
            in_specs=(field, field, field, P(), P(), P(), flat, flat, flat, field),
            out_specs=(field, field, field, field, field, P(), P()),
            check_vma=False,
        )(*args)

    return run
```

```python
import functools
import math

import jax
import jax.numpy as jnp
from jax import lax
from jax.experimental import pallas as pl
from jax.experimental.pallas import tpu as pltpu
from jax.sharding import Mesh, PartitionSpec as P

F32 = jnp.float32
BF16 = jnp.bfloat16
AXES = ("band", "core", "reach", "near")
BIAS_ROWS = 16
GROUPS = 4
PRE_GROUPS = 4
LAST = 16
VMEM = pl.BlockSpec(memory_space=pltpu.VMEM)
HBM = pl.BlockSpec(memory_space=pltpu.HBM)
ACROSS = (((1,), (1,)), ((), ()))


def sds(shape, dtype):
    return jax.ShapeDtypeStruct(shape, dtype)


def call(
    kernel,
    out_shape,
    scratch=(),
    remote=0,
    leaving=0,
    aliases=None,
    flops=0,
    moved=0,
    transcendentals=0,
):
    several = isinstance(out_shape, tuple)
    shapes = out_shape if several else (out_shape,)
    out_specs = tuple([HBM] * leaving + [VMEM] * (len(shapes) - leaving))

    def run(*args):
        near = len(args) - remote
        far = [pltpu.with_memory_space_constraint(arg, pltpu.HBM) for arg in args[near:]]
        return pl.pallas_call(
            kernel,
            out_shape=out_shape,
            in_specs=[VMEM] * near + [HBM] * remote,
            out_specs=out_specs if several else out_specs[0],
            input_output_aliases=aliases or {},
            scratch_shapes=list(scratch),
            cost_estimate=pl.CostEstimate(
                flops=flops, bytes_accessed=moved, transcendentals=transcendentals
            ),
            compiler_params=pltpu.CompilerParams(vmem_limit_bytes=24 * 1024 * 1024),
        )(*args[:near], *far)

    return run


class Layout:
    def __init__(self, lat_count, lon_count, taps, gate_count):
        self.lat, self.lon = lat_count, lon_count
        self.half = lon_count // 2
        self.taps, self.half_gates = taps, gate_count // 2
        self.plane = lat_count
        whole = [("lon", 1 << k) for k in range(1, lon_count.bit_length() - 1)]
        self.orders = ([("lat", 1)] + whole[::-1], [("lat", 1)] + whole)
        step = 8 * self.plane
        self.half_rows = -(-taps * self.half_gates // step) * step
        self.chunk = self.half_rows // self.plane

    def position(self):
        lat = 2 * lax.axis_index("band") + lax.axis_index("core")
        return lat, 2 * lax.axis_index("reach") + lax.axis_index("near")

    def rank(self, phase):
        lat, lon = self.position()

        def digit(order):
            axis, bit = order[phase]
            return ((lat if axis == "lat" else lon) // bit) % 2

        return jnp.where(lat % 2 == 0, digit(self.orders[0]), digit(self.orders[1]))

    def pairs(self, partner):
        result = []
        for lat in range(self.lat):
            for lon in range(self.lon):
                there = partner(lat, lon)
                result.append((lat * self.lon + lon, there[0] * self.lon + there[1]))
        return result

    def phase_pairs(self, phase):
        def partner(lat, lon):
            axis, bit = self.orders[lat % 2][phase]
            return (lat ^ bit, lon) if axis == "lat" else (lat, lon ^ bit)

        return self.pairs(partner)

    def plane_rank(self):
        return 2 * lax.axis_index("band") + lax.axis_index("near")

    def plane_pairs(self, step):
        def partner(lat, lon):
            there = (lat // 2 * 2 + lon % 2) ^ step
            return there // 2 * 2 + lat % 2, lon // 2 * 2 + there % 2

        return self.pairs(partner)

    def inner_rows(self, lat, lon):
        return lat ^ 1, lon

    def outer_rows(self, lat, lon):
        there = lat + 1 if lat % 2 else lat - 1
        if 0 <= there < self.lat:
            return there, lon
        return lat, (lon + self.half) % self.lon

    def inner_columns(self, lat, lon):
        return lat, lon ^ 1

    def outer_columns(self, lat, lon):
        return lat, (lon + (1 if lon % 2 else -1)) % self.lon


def permuted(value, pairs):
    return lax.ppermute(value, AXES, pairs)


def lanes(shape):
    return lax.broadcasted_iota(jnp.int32, shape, len(shape) - 1)


def rolled(value, shift):
    shift %= value.shape[1]
    return pltpu.roll(value, shift, 1) if shift else value


def edge_columns(row, position, columns):
    lane = lanes(row.shape)
    columns = jnp.where(lane == position, rolled(row, position), columns)
    return jnp.where(lane == LAST + position, rolled(row, LAST + position + 1), columns)


def second_columns(row, position, columns):
    lane = lanes(row.shape)
    columns = jnp.where(lane == position, rolled(row, position - 1), columns)
    return jnp.where(lane == LAST + position, rolled(row, LAST + position + 2), columns)


def at_edges(row, position, columns):
    lane = lanes(row.shape)
    width = row.shape[1]
    row = jnp.where(lane == 0, rolled(columns, -position), row)
    return jnp.where(lane == width - 1, rolled(columns, width - 1 - LAST - position), row)


def pick(flag, yes, no):
    return jnp.where(flag, yes, no)


def is_odd(axis):
    return lax.axis_index(axis) % 2 == 1


def row_sends(first, last, inner_out, outer_out):
    odd = is_odd("core")
    inner_out[...] = pick(odd, first, last).astype(BF16)
    outer_out[...] = pick(odd, last, first).astype(BF16)


def row_halo(inner, outer):
    odd = is_odd("core")
    inner, outer = inner[...].astype(F32), outer[...].astype(F32)
    return pick(odd, inner, outer), pick(odd, outer, inner)


def packed(columns, groups):
    count, width = columns.shape[0] // groups, columns.shape[1] // groups
    lane = lanes((count, columns.shape[1]))
    value = columns[0:count]
    for group in range(1, groups):
        part = rolled(columns[group * count : (group + 1) * count], group * width)
        value = jnp.where(lane >= group * width, part, value)
    return value


def unpacked(value, groups):
    width = value.shape[1] // groups
    return jnp.concatenate([rolled(value, -group * width) for group in range(groups)], axis=0)


def column_halo(inner, outer, groups):
    odd = is_odd("near")
    inner, outer = inner[...].astype(F32), outer[...].astype(F32)
    return unpacked(pick(odd, inner, outer), groups), unpacked(pick(odd, outer, inner), groups)


def pack_kernel(below, hidden, inner_out, outer_out, wide_out, below_here, hidden_here, arrived):
    first = pltpu.make_async_copy(below, below_here, arrived.at[0])
    second = pltpu.make_async_copy(hidden, hidden_here, arrived.at[1])
    first.start()
    second.start()
    channels, row_count, width = below.shape
    size = channels * row_count
    first.wait()
    wide_out[0:size, :] = below_here[...].astype(F32).reshape(size, width)
    second.wait()
    wide_out[size : 2 * size, :] = hidden_here[...].astype(F32).reshape(size, width)
    edges = [
        wide_out[pl.ds(index, 2 * channels, stride=row_count), :] for index in (0, row_count - 1)
    ]
    row_sends(edges[0], edges[1], inner_out, outer_out)


def down_rows(values, width):
    count = values.shape[0]
    return jnp.broadcast_to(values[None, :], (width, count)).T


def prepare_kernel(
    wide,
    cell_hbm,
    weights_hbm,
    hidden_grad_hbm,
    target_hbm,
    land_hbm,
    fire_hbm,
    gate_bias_hbm,
    readout_hbm,
    rows_out,
    columns_out,
    second_out,
    cell_strip_out,
    hidden_grad_strip_out,
    fields_strip_out,
    cell_out,
    weights_out,
    hidden_grad_out,
    target_out,
    land_out,
    fire_out,
    bias_wide_out,
    readout_wide_out,
    hidden_grad_here,
    gate_bias_here,
    readout_here,
    arrived,
):
    copies = [
        pltpu.make_async_copy(source, target, arrived.at[index])
        for index, (source, target) in enumerate(
            (
                (cell_hbm, cell_out),
                (weights_hbm, weights_out),
                (hidden_grad_hbm, hidden_grad_here),
                (target_hbm, target_out),
                (land_hbm, land_out),
                (fire_hbm, fire_out),
                (gate_bias_hbm, gate_bias_here),
                (readout_hbm, readout_here),
            )
        )
    ]
    for copy in copies:
        copy.start()
    row_count, channels, width = rows_out.shape
    columns = jnp.zeros((channels, width), F32)
    second = jnp.zeros((channels, width), F32)
    for index in range(row_count):
        row = wide[pl.ds(index, channels, stride=row_count), :]
        rows_out[index] = row.astype(BF16)
        columns = edge_columns(row, index + 1, columns)
        second = second_columns(row, index + 1, second)
    columns_out[...] = columns
    second_out[...] = second
    for copy in copies:
        copy.wait()
    hidden_grad_out[...] = hidden_grad_here[...].astype(F32).reshape(hidden_grad_out.shape)
    bias_wide_out[...] = down_rows(gate_bias_here[...], width)
    readout_wide_out[...] = down_rows(readout_here[...], width)
    hid = hidden_grad_here.shape[0]
    cell_strip = jnp.zeros((hid, width), F32)
    hidden_grad_strip = jnp.zeros((hid, width), F32)
    fields_strip = jnp.zeros((8, width), F32)
    for index in range(row_count):
        strided = pl.ds(index, hid, stride=row_count)
        cell_strip = edge_columns(cell_out[strided, :], index + 1, cell_strip)
        hidden_grad_strip = edge_columns(hidden_grad_out[strided, :], index + 1, hidden_grad_strip)
        at = slice(index, index + 1)
        fields = [target_out[at, :], land_out[at, :].astype(F32), fire_out[at, :].astype(F32)]
        fields = jnp.concatenate(fields + [jnp.zeros((5, width), F32)], axis=0)
        fields_strip = edge_columns(fields, index + 1, fields_strip)
    cell_strip_out[...] = cell_strip
    hidden_grad_strip_out[...] = hidden_grad_strip
    fields_strip_out[...] = fields_strip


def columns_kernel(row_count, groups, columns, outer, inner, packed_out, *whole_out):
    north, south = row_halo(inner, outer)
    value = edge_columns(north, 0, columns[...].astype(F32))
    value = edge_columns(south, row_count + 1, value)
    packed_out[...] = packed(value, groups).astype(BF16)
    for out in whole_out:
        out[...] = value.astype(BF16)


def encode(bias):
    high = bias.astype(BF16).astype(F32)
    return jnp.concatenate([high, bias - high], axis=0)


def decode(block):
    return block[0:8] + block[8:16]


def cell_step(part, cell_before, hidden_grad, target, land, fire, readout):
    hid = part.shape[0] // 4
    input_gate = 0.5 + 0.5 * jnp.tanh(0.5 * part[0:hid])
    forget_gate = 0.5 + 0.5 * jnp.tanh(0.5 * part[hid : 2 * hid])
    output_gate = 0.5 + 0.5 * jnp.tanh(0.5 * part[2 * hid : 3 * hid])
    candidate = jnp.tanh(part[3 * hid : 4 * hid])
    cell_next = land * (forget_gate * cell_before + input_gate * candidate)
    squashed = jnp.tanh(cell_next)
    hidden_next = (output_gate * squashed).astype(BF16).astype(F32)
    predicted = jnp.sum(readout * hidden_next, axis=0, keepdims=True)
    total_grad = hidden_grad + 2.0 * (fire * (predicted - target)) * readout
    cell_grad = land * total_grad * output_gate * (1.0 - squashed * squashed)
    pre_grad = jnp.concatenate(
        [
            cell_grad * candidate * input_gate * (1.0 - input_gate),
            cell_grad * cell_before * forget_gate * (1.0 - forget_gate),
            total_grad * squashed * output_gate * (1.0 - output_gate),
            cell_grad * input_gate * (1.0 - candidate * candidate),
        ],
        axis=0,
    )
    return hidden_next, cell_next, cell_grad * forget_gate, pre_grad


def gates_kernel(
    place,
    rows_in,
    inner_row,
    outer_row,
    second,
    cell_prev,
    weights,
    hidden_grad,
    target,
    land,
    fire,
    bias_wide,
    readout_wide,
    hidden_out,
    cell_out,
    grad_cell_out,
    pre_out,
    second_out,
    sums,
    bias_out,
    shifted,
):
    row_count, channels, width = rows_in.shape
    gate_count = weights.shape[1]
    hid = gate_count // 4
    half_gates = place.half_gates
    north, south = row_halo(inner_row, outer_row)
    columns = second_columns(north, 0, second[...])
    second_out[...] = second_columns(south, row_count + 1, columns).astype(BF16)
    for position in range(row_count + 2):
        if position == 0:
            row = north
        elif position == row_count + 1:
            row = south
        else:
            row = rows_in[position - 1].astype(F32)
        at = pl.ds(position * width, width)
        shifted[0:channels, at] = rolled(row, 1).astype(BF16)
        shifted[channels : 2 * channels, at] = row.astype(BF16)
        shifted[2 * channels : 3 * channels, at] = rolled(row, -1).astype(BF16)

    taps = [
        jnp.concatenate([weights[3 * a], weights[3 * a + 1], weights[3 * a + 2]], axis=1)
        for a in range(3)
    ]
    bias_total = jnp.zeros((gate_count, width), F32)
    lane = lanes((gate_count, width))
    inside = (lane > 0) & (lane < width - 1)
    readout = readout_wide[...]
    pair = 2 if row_count % 2 == 0 else 1
    for base in range(0, row_count, pair):
        preact = jnp.zeros((gate_count, pair * width), F32)
        for a in range(3):
            preact += jnp.dot(
                taps[a],
                shifted[:, pl.ds((base + a) * width, pair * width)],
                preferred_element_type=F32,
            )
        for offset in range(pair):
            index = base + offset
            strided = pl.ds(index, hid, stride=row_count)
            at = slice(index, index + 1)
            hidden_next, cell_next, grad_cell, pre_grad = cell_step(
                preact[:, offset * width : (offset + 1) * width] + bias_wide[...],
                cell_prev[strided, :],
                hidden_grad[strided, :],
                target[at, :],
                land[at, :].astype(F32),
                fire[at, :].astype(F32),
                readout,
            )
            hidden_out[strided, :] = hidden_next
            cell_out[strided, :] = cell_next
            grad_cell_out[strided, :] = grad_cell
            pre_grad = jnp.where(inside, pre_grad, 0.0)
            bias_total += pre_grad
            pre_out[:, pl.ds(index * width, width)] = pre_grad.astype(BF16)
    bias_out[...] = bias_total

    for a in range(3):
        product = lax.dot_general(
            pre_out[...],
            shifted[:, pl.ds(a * width, row_count * width)],
            ACROSS,
            preferred_element_type=F32,
        )
        for b in range(3):
            for half in range(2):
                at = half * place.half_rows + (3 * a + b) * half_gates
                sums[at : at + half_gates, :] = product[
                    half * half_gates : (half + 1) * half_gates, b * channels : (b + 1) * channels
                ]
    used = place.taps * half_gates
    if place.half_rows > used:
        for half in range(2):
            at = half * place.half_rows
            sums[at + used : at + place.half_rows, :] = jnp.zeros(
                (place.half_rows - used, channels), F32
            )


def add_strip(place, half, sums, pre_strip, patches, out):
    half_gates, channels = place.half_gates, sums.shape[1]
    gates = pre_strip[pl.ds(pl.multiple_of(half * half_gates, half_gates), half_gates), :]
    product = lax.dot_general(gates, patches[...], ACROSS, preferred_element_type=F32)
    base = half * place.half_rows
    for tap in range(place.taps):
        at = pl.ds(pl.multiple_of(base + tap * half_gates, 8), half_gates)
        value = sums[at, :] + product[:, tap * channels : (tap + 1) * channels]
        out[tap * half_gates : (tap + 1) * half_gates, :] = value.astype(out.dtype)
    used = place.taps * half_gates
    if place.half_rows > used:
        rest = jnp.zeros((place.half_rows - used, channels), out.dtype)
        out[used:, :] = rest


def strip_kernel(
    place,
    row_count,
    edge,
    second,
    outer_column,
    inner_column,
    weights,
    bias_wide,
    readout_wide,
    cell_strip,
    hidden_grad_strip,
    fields_strip,
    sums,
    send_out,
    pre_out,
    pre_wide_out,
    patches,
    hidden_out,
    cell_out,
    grad_cell_out,
):
    channels, width = edge.shape
    west, east = column_halo(inner_column, outer_column, GROUPS)
    near_first = lanes((channels, width)) < LAST
    inner = second[...].astype(F32)
    columns = (
        jnp.where(near_first, rolled(west, -LAST), inner),
        edge[...].astype(F32),
        jnp.where(near_first, inner, rolled(east, LAST)),
    )
    for a in range(3):
        for b in range(3):
            at = (3 * a + b) * channels
            patches[at : at + channels, :] = rolled(columns[b], 1 - a).astype(BF16)
    taps = jnp.concatenate([weights[tap] for tap in range(place.taps)], axis=1)
    preact = jnp.dot(taps, patches[...], preferred_element_type=F32) + bias_wide[...]
    hidden_next, cell_next, grad_cell, pre_grad = cell_step(
        preact,
        cell_strip[...],
        hidden_grad_strip[...],
        fields_strip[0:1, :],
        fields_strip[1:2, :],
        fields_strip[2:3, :],
        readout_wide[...],
    )
    hidden_out[...] = hidden_next
    cell_out[...] = cell_next
    grad_cell_out[...] = grad_cell
    lane = lanes(pre_grad.shape)
    lane = jnp.where(lane >= LAST, lane - LAST, lane)
    pre_grad = jnp.where((lane >= 1) & (lane <= row_count), pre_grad, 0.0)
    pre_out[...] = pre_grad.astype(BF16)
    pre_wide_out[...] = pre_grad
    add_strip(place, 1 - place.rank(0), sums, pre_out, patches, send_out)


def keep_kernel(place, sums, pre_strip, patches, bias_partial, pre_wide, out, bias_out):
    add_strip(place, place.rank(0), sums, pre_strip, patches, out)
    channels = sums.shape[1]
    bias_total = bias_partial[...] + pre_wide[...]
    ones = jnp.ones((8, bias_total.shape[1]), BF16)
    high = bias_total.astype(BF16)
    low = (bias_total - high.astype(F32)).astype(BF16)
    flat = lax.dot_general(ones, high, ACROSS, preferred_element_type=F32)
    flat += lax.dot_general(ones, low, ACROSS, preferred_element_type=F32)
    odd = lax.broadcasted_iota(jnp.int32, (8, channels), 0) % 2 == 1
    bias_out[...] = jnp.where(odd, flat[:, channels : 2 * channels], flat[:, 0:channels])


def edges_kernel(
    row_count,
    hidden,
    cell,
    grad_cell,
    pre,
    hidden_strip,
    cell_strip,
    grad_cell_strip,
    pre_strip,
    hidden_hbm,
    cell_hbm,
    grad_cell_hbm,
    pre_out,
    inner_out,
    outer_out,
    hidden_low,
    hidden_here,
    cell_here,
    grad_cell_here,
    left,
):
    hid, _, width = hidden_low.shape
    leaving = []
    for source, strip, here, ready, target in (
        (cell, cell_strip, cell_here, cell_here, cell_hbm),
        (grad_cell, grad_cell_strip, grad_cell_here, grad_cell_here, grad_cell_hbm),
        (hidden, hidden_strip, hidden_here, hidden_low, hidden_hbm),
    ):
        columns = strip[...]
        for index in range(row_count):
            strided = pl.ds(index, hid, stride=row_count)
            here[strided, :] = at_edges(source[strided, :], index + 1, columns)
        if ready is hidden_low:
            hidden_low[...] = here[...].reshape(hidden_low.shape).astype(BF16)
        leaving.append(pltpu.make_async_copy(ready, target, left.at[len(leaving)]))
        leaving[-1].start()
    first, last = None, None
    columns = pre_strip[...].astype(F32)
    for index in range(row_count):
        at = pl.ds(index * width, width)
        row = at_edges(pre[:, at].astype(F32), index + 1, columns)
        pre_out[:, at] = row.astype(BF16)
        first = row if index == 0 else first
        last = row
    row_sends(first, last, inner_out, outer_out)
    for copy in leaving:
        copy.wait()


def pair_kernel(place, keep, bias, received, *outs):
    sends, keep_out, scratch = outs[:-2], outs[-2], outs[-1]
    chunk = place.chunk
    rank = place.plane_rank()
    scratch[...] = keep[...] + received[...].astype(F32)
    block = encode(bias[...]).astype(BF16)
    for step, send in zip(range(place.plane - 1, 0, -1), sends):
        send[0:BIAS_ROWS, :] = block
        at = pl.ds(pl.multiple_of((rank ^ step) * chunk, 8), chunk)
        send[BIAS_ROWS:, :] = scratch[at, :].astype(BF16)
    keep_out[...] = scratch[pl.ds(pl.multiple_of(rank * chunk, 8), chunk), :]


def plane_kernel(keep, bias, *refs):
    received, out = refs[:-2], refs[-1]
    total, bias_total = keep[...], bias[...]
    for ref in received:
        total += ref[BIAS_ROWS:, :].astype(F32)
        bias_total += decode(ref[0:BIAS_ROWS, :].astype(F32))
    out[0:BIAS_ROWS, :] = encode(bias_total).astype(BF16)
    out[BIAS_ROWS:, :] = total.astype(BF16)


def join_kernel(place, *refs):
    blocks, out = refs[:-2], refs[-1]
    rank = place.plane_rank()
    for step, block in enumerate(blocks):
        out[rank ^ step] = block[...]


def add_kernel(scale, own, received, out):
    here, there = own[...].astype(F32), received[...].astype(F32)
    bias = (decode(here[0:BIAS_ROWS]) + decode(there[0:BIAS_ROWS])) * scale
    out[0:BIAS_ROWS, :] = encode(bias).astype(BF16)
    out[BIAS_ROWS:, :] = ((here[BIAS_ROWS:] + there[BIAS_ROWS:]) * scale).astype(BF16)


def store_half(place, half, blocks, out, wide, left):
    chunk, half_gates = place.chunk, place.half_gates
    gates = pl.ds(pl.multiple_of(half * half_gates, half_gates), half_gates)
    copies = []
    for index in range(place.plane):
        wide[index * chunk : (index + 1) * chunk, :] = blocks[index, BIAS_ROWS:, :].astype(F32)
        while len(copies) < min(place.taps, (index + 1) * chunk // half_gates):
            tap = len(copies)
            source = wide.at[tap * half_gates : (tap + 1) * half_gates, :]
            copies.append(pltpu.make_async_copy(source, out.at[tap, gates, :], left.at[tap]))
            copies[-1].start()
    return copies


def own_half_kernel(place, own, out, wide, left):
    for copy in store_half(place, place.rank(0), own, out, wide, left):
        copy.wait()


def other_half_kernel(
    place, own, received, after, out_before, out, bias_out, wide, bias_here, left
):
    del after, out_before
    rank = place.rank(0)
    here, there = own[0, 0:BIAS_ROWS, :].astype(F32), received[0, 0:BIAS_ROWS, :].astype(F32)
    bias = decode(here) + decode(there)
    width = bias.shape[1]
    for index in range(bias_here.shape[0] // width):
        bias_here[pl.ds(index * width, width)] = bias[index]
    bias_copy = pltpu.make_async_copy(bias_here, bias_out, left.at[place.taps])
    bias_copy.start()
    copies = store_half(place, 1 - rank, received, out, wide, left)
    bias_copy.wait()
    for copy in copies:
        copy.wait()


def field_kernel(pre, weights, wide_out, turned_out, done_out, shifted):
    done_out[...] = jnp.zeros(done_out.shape, F32)
    gate_count, cells = pre.shape
    channels, width = weights.shape[2], wide_out.shape[1]
    row_count = cells // width
    lane = lanes((gate_count, width))
    for index in range(row_count):
        at = pl.ds(index * width, width)
        row = pre[:, at].astype(F32)
        left = jnp.where(lane == 0, 0.0, rolled(row, 1))
        right = jnp.where(lane == width - 1, 0.0, rolled(row, -1))
        shifted[0:gate_count, at] = right.astype(BF16)
        shifted[gate_count : 2 * gate_count, at] = pre[:, at]
        shifted[2 * gate_count : 3 * gate_count, at] = left.astype(BF16)
    for a in range(3):
        for b in range(3):
            turned_out[a, :, b * gate_count : (b + 1) * gate_count] = weights[3 * a + b].T

    def product(a, index, count):
        return jnp.dot(
            turned_out[a],
            shifted[:, pl.ds(index * width, count * width)],
            preferred_element_type=F32,
        )

    pair = 2 if row_count % 2 == 0 else 1
    for base in range(0, row_count, pair):
        total = product(1, base, pair)
        for a, first in ((2, base - 1), (0, base + 1)):
            low, high = max(first, 0), min(first + pair, row_count)
            if low >= high:
                continue
            part = product(a, low, high - low)
            blank = jnp.zeros((channels, width), F32)
            parts = [blank] * (low - first) + [part] + [blank] * (first + pair - high)
            total += jnp.concatenate(parts, axis=1)
        for offset in range(pair):
            value = total[:, offset * width : (offset + 1) * width]
            wide_out[pl.ds(base + offset, channels, stride=row_count), :] = value


def field_halo_kernel(
    place,
    wide,
    turned,
    outer_row,
    inner_row,
    outer_column,
    inner_column,
    inputs_out,
    hidden_out,
    done_out,
    total,
):
    done_out[...] = jnp.zeros(done_out.shape, F32)
    hid, row_count, width = hidden_out.shape
    channels = turned.shape[1]
    gate_count = turned.shape[2] // 3
    north, south = row_halo(inner_row, outer_row)
    west, east = column_halo(inner_column, outer_column, PRE_GROUPS)
    lane = lanes((gate_count, width))
    lat = place.position()[0]

    def row_part(taps, row, position):
        left = jnp.where(lane == 0, rolled(west, -LAST - position), rolled(row, 1))
        right = rolled(east, width - 1 - position)
        right = jnp.where(lane == width - 1, right, rolled(row, -1))
        stack = jnp.concatenate([right, row, left], axis=0).astype(BF16)
        return jnp.dot(taps, stack, preferred_element_type=F32)

    above = row_part(turned[jnp.where(lat == 0, 0, 2)], north, 0)
    below = row_part(turned[jnp.where(lat == place.lat - 1, 2, 0)], south, row_count + 1)

    inside = (lane >= 1) & (lane <= row_count)
    west = jnp.where(inside, rolled(west, -LAST), 0.0)
    east = jnp.where(inside, east, 0.0)
    sides = [rolled(west, a - 1) for a in range(3)] + [rolled(east, LAST + a - 1) for a in range(3)]
    taps = [turned[a, :, 2 * gate_count : 3 * gate_count] for a in range(3)]
    taps += [turned[a, :, 0:gate_count] for a in range(3)]
    columns = jnp.dot(
        jnp.concatenate(taps, axis=1),
        jnp.concatenate(sides, axis=0).astype(BF16),
        preferred_element_type=F32,
    )
    blank = jnp.zeros((channels, width), F32)
    for index in range(row_count):
        strided = pl.ds(index, channels, stride=row_count)
        value = wide[strided, :] + at_edges(blank, index + 1, columns)
        if index == 0:
            value += above
        if index == row_count - 1:
            value += below
        total[strided, :] = value
    size = (channels - hid) * row_count
    inputs_out[...] = total[0:size, :].reshape(inputs_out.shape).astype(BF16)
    hidden_out[...] = total[size:, :].reshape(hidden_out.shape).astype(BF16)


def body(
    place,
    inputs_below,
    hidden_prev,
    cell_prev,
    kernel_weights,
    gate_bias,
    readout,
    target_field,
    land_mask,
    fire_mask,
    hidden_grad,
):
    hid, row_count, width = hidden_prev.shape
    gate_count, channels = kernel_weights.shape[1:]
    cells = row_count * width
    halo_cells = (row_count + 2) * width
    scaling = 1.0 / math.sqrt(cells * place.lat * place.lon)
    bind = functools.partial
    inner_rows, outer_rows = place.pairs(place.inner_rows), place.pairs(place.outer_rows)
    inner_columns = place.pairs(place.inner_columns)
    outer_columns = place.pairs(place.outer_columns)
    flat = sds((hid * row_count, width), F32)
    strip = sds((hid, width), F32)

    inner, outer, wide = call(
        pack_kernel,
        (
            sds((channels, width), BF16),
            sds((channels, width), BF16),
            sds((channels * row_count, width), F32),
        ),
        [
            pltpu.VMEM(inputs_below.shape, BF16),
            pltpu.VMEM(hidden_prev.shape, BF16),
            pltpu.SemaphoreType.DMA((2,)),
        ],
        remote=2,
        moved=4 * channels * cells,
    )(inputs_below, hidden_prev)
    inner, outer = permuted(inner, inner_rows), permuted(outer, outer_rows)
    (
        rows,
        columns,
        second,
        cell_strip,
        hidden_grad_strip,
        fields_strip,
        cell_here,
        weights_here,
        hidden_grad_here,
        target_here,
        land_here,
        fire_here,
        bias_wide,
        readout_wide,
    ) = call(
        prepare_kernel,
        (
            sds((row_count, channels, width), BF16),
            sds((channels, width), F32),
            sds((channels, width), F32),
            strip,
            strip,
            sds((8, width), F32),
            flat,
            sds(kernel_weights.shape, BF16),
            flat,
            sds(target_field.shape, F32),
            sds(land_mask.shape, jnp.int32),
            sds(fire_mask.shape, jnp.int32),
            sds((gate_count, width), F32),
            sds((hid, width), F32),
        ),
        [
            pltpu.VMEM(hidden_grad.shape, BF16),
            pltpu.VMEM(gate_bias.shape, F32),
            pltpu.VMEM(readout.shape, F32),
            pltpu.SemaphoreType.DMA((8,)),
        ],
        remote=8,
        moved=6_000_000,
    )(
        wide,
        cell_prev.reshape(hid * row_count, width),
        kernel_weights,
        hidden_grad,
        target_field,
        land_mask,
        fire_mask,
        gate_bias,
        readout,
    )
    columns, edge = call(
        bind(columns_kernel, row_count, GROUPS),
        (sds((channels // GROUPS, width), BF16), sds((channels, width), BF16)),
    )(columns, outer, inner)
    inner_column = permuted(columns, inner_columns)
    outer_column = permuted(columns, outer_columns)
    hidden_rows, cell_rows, grad_cell_rows, pre, second, sums, bias = call(
        bind(gates_kernel, place),
        (
            flat,
            flat,
            flat,
            sds((gate_count, cells), BF16),
            sds((channels, width), BF16),
            sds((2 * place.half_rows, channels), F32),
            sds((gate_count, width), F32),
        ),
        [pltpu.VMEM((3 * channels, halo_cells), BF16)],
        flops=4 * 9 * gate_count * channels * cells,
        moved=6_000_000,
        transcendentals=5 * hid * cells,
    )(
        rows,
        inner,
        outer,
        second,
        cell_here,
        weights_here,
        hidden_grad_here,
        target_here,
        land_here,
        fire_here,
        bias_wide,
        readout_wide,
    )
    send, pre_strip, pre_wide, patches, *strips = call(
        bind(strip_kernel, place, row_count),
        (
            sds((place.half_rows, channels), BF16),
            sds((gate_count, width), BF16),
            sds((gate_count, width), F32),
            sds((place.taps * channels, width), BF16),
            strip,
            strip,
            strip,
        ),
    )(
        edge,
        second,
        outer_column,
        inner_column,
        weights_here,
        bias_wide,
        readout_wide,
        cell_strip,
        hidden_grad_strip,
        fields_strip,
        sums,
    )
    keep, bias = call(
        bind(keep_kernel, place),
        (sds((place.half_rows, channels), F32), sds((8, channels), F32)),
    )(sums, pre_strip, patches, bias, pre_wide)
    hidden_next, cell_next, grad_cell, pre, pre_inner, pre_outer = call(
        bind(edges_kernel, row_count),
        (
            sds((hid, row_count, width), BF16),
            flat,
            flat,
            sds((gate_count, cells), BF16),
            sds((gate_count, width), BF16),
            sds((gate_count, width), BF16),
        ),
        [
            pltpu.VMEM((hid, row_count, width), BF16),
            pltpu.VMEM(flat.shape, F32),
            pltpu.VMEM(flat.shape, F32),
            pltpu.VMEM(flat.shape, F32),
            pltpu.SemaphoreType.DMA((3,)),
        ],
        leaving=3,
        moved=4_000_000,
    )(hidden_rows, cell_rows, grad_cell_rows, pre, *strips, pre_strip)
    pre_inner, pre_outer = permuted(pre_inner, inner_rows), permuted(pre_outer, outer_rows)
    pre_columns = call(
        bind(columns_kernel, row_count, PRE_GROUPS),
        (sds((gate_count // PRE_GROUPS, width), BF16),),
    )(pre_strip, pre_outer, pre_inner)[0]

    block = sds((BIAS_ROWS + place.chunk, channels), BF16)
    token = sds((8, width), F32)
    steps = range(place.plane - 1, 0, -1)
    *sends, keep = call(
        bind(pair_kernel, place),
        (*[block for _ in steps], sds((place.chunk, channels), F32)),
        [pltpu.VMEM((place.half_rows, channels), F32)],
    )(keep, bias, permuted(send, place.phase_pairs(0)))
    received = [permuted(send, place.plane_pairs(step)) for step, send in zip(steps, sends)]
    field, turned, field_done = call(
        field_kernel,
        (
            sds((channels * row_count, width), F32),
            sds((3, channels, 3 * gate_count), BF16),
            token,
        ),
        [pltpu.VMEM((3 * gate_count, cells), BF16)],
        flops=2 * 9 * gate_count * channels * cells,
        moved=3_000_000,
    )(pre, weights_here)
    part = call(plane_kernel, block)(keep, bias, *received, field_done)
    pre_inner_columns = permuted(pre_columns, inner_columns)
    pre_outer_columns = permuted(pre_columns, outer_columns)
    phases = len(place.orders[0])
    for phase in range(1, phases):
        is_last = phase == phases - 1
        part = call(bind(add_kernel, scaling if is_last else 1.0), block)(
            part, permuted(part, place.phase_pairs(phase))
        )
    received = [permuted(part, place.plane_pairs(step)) for step in steps[::-1]]
    grad_inputs, grad_hidden, field_done = call(
        bind(field_halo_kernel, place),
        (
            sds((channels - hid, row_count, width), BF16),
            sds((hid, row_count, width), BF16),
            token,
        ),
        [pltpu.VMEM((channels * row_count, width), F32)],
        flops=40 * gate_count * channels * cells * 9,
        moved=2_000_000,
    )(field, turned, pre_outer, pre_inner, pre_outer_columns, pre_inner_columns)
    gathered = call(bind(join_kernel, place), sds((place.plane, *block.shape), BF16))(
        part, *received, field_done
    )
    received = permuted(gathered, place.phase_pairs(0))
    half = [pltpu.VMEM((place.half_rows, channels), F32)]
    grad_kernel = call(
        bind(own_half_kernel, place),
        (sds(kernel_weights.shape, F32),),
        half + [pltpu.SemaphoreType.DMA((place.taps,))],
        leaving=1,
        moved=6 * place.half_rows * channels,
    )(gathered)[0]
    grad_kernel, grad_bias = call(
        bind(other_half_kernel, place),
        (sds(kernel_weights.shape, F32), sds((gate_count,), F32)),
        half + [pltpu.VMEM((gate_count,), F32), pltpu.SemaphoreType.DMA((place.taps + 1,))],
        remote=1,
        leaving=2,
        aliases={3: 0},
        moved=6 * place.half_rows * channels,
    )(gathered, received, target_here, grad_kernel)
    shape = hidden_prev.shape
    return (
        hidden_next,
        cell_next.reshape(shape),
        grad_inputs,
        grad_hidden,
        grad_cell.reshape(shape),
        grad_kernel,
        grad_bias,
    )


def solution(mesh):
    lat_count, lon_count = mesh.shape["lat"], mesh.shape["lon"]
    split = Mesh(mesh.devices.reshape(lat_count // 2, 2, lon_count // 2, 2), AXES)
    field = P(None, ("band", "core"), ("reach", "near"))
    flat = P(("band", "core"), ("reach", "near"))

    def run(*args):
        place = Layout(lat_count, lon_count, *args[3].shape[:2])
        return jax.shard_map(
            functools.partial(body, place),
            mesh=split,
            in_specs=(field, field, field, P(), P(), P(), flat, flat, flat, field),
            out_specs=(field, field, field, field, field, P(), P()),
            check_vma=False,
        )(*args)

    return run
```

```python
import functools
import math

import jax
import jax.numpy as jnp
from jax import lax
from jax.experimental import pallas as pl
from jax.experimental.pallas import tpu as pltpu
from jax.sharding import Mesh, PartitionSpec as P

F32 = jnp.float32
BF16 = jnp.bfloat16
AXES = ("band", "core", "reach", "near")
BIAS_ROWS = 16
GROUPS = 4
PRE_GROUPS = 4
LAST = 16
VMEM = pl.BlockSpec(memory_space=pltpu.VMEM)
HBM = pl.BlockSpec(memory_space=pltpu.HBM)
ACROSS = (((1,), (1,)), ((), ()))


def sds(shape, dtype):
    return jax.ShapeDtypeStruct(shape, dtype)


def call(
    kernel,
    out_shape,
    scratch=(),
    remote=0,
    leaving=0,
    aliases=None,
    flops=0,
    moved=0,
    transcendentals=0,
):
    several = isinstance(out_shape, tuple)
    shapes = out_shape if several else (out_shape,)
    out_specs = tuple([HBM] * leaving + [VMEM] * (len(shapes) - leaving))

    def run(*args):
        near = len(args) - remote
        far = [pltpu.with_memory_space_constraint(arg, pltpu.HBM) for arg in args[near:]]
        return pl.pallas_call(
            kernel,
            out_shape=out_shape,
            in_specs=[VMEM] * near + [HBM] * remote,
            out_specs=out_specs if several else out_specs[0],
            input_output_aliases=aliases or {},
            scratch_shapes=list(scratch),
            cost_estimate=pl.CostEstimate(
                flops=flops, bytes_accessed=moved, transcendentals=transcendentals
            ),
            compiler_params=pltpu.CompilerParams(vmem_limit_bytes=24 * 1024 * 1024),
        )(*args[:near], *far)

    return run


class Layout:
    def __init__(self, lat_count, lon_count, taps, gate_count):
        self.lat, self.lon = lat_count, lon_count
        self.half = lon_count // 2
        self.taps, self.half_gates = taps, gate_count // 2
        self.plane = lat_count
        whole = [("lon", 1 << k) for k in range(1, lon_count.bit_length() - 1)]
        self.orders = ([("lat", 1)] + whole, [("lat", 1)] + whole[::-1])
        step = 8 * self.plane
        self.half_rows = -(-taps * self.half_gates // step) * step
        self.chunk = self.half_rows // self.plane

    def position(self):
        lat = 2 * lax.axis_index("band") + lax.axis_index("core")
        return lat, 2 * lax.axis_index("reach") + lax.axis_index("near")

    def rank(self, phase):
        lat, lon = self.position()

        def digit(order):
            axis, bit = order[phase]
            return ((lat if axis == "lat" else lon) // bit) % 2

        return jnp.where(lat % 2 == 0, digit(self.orders[0]), digit(self.orders[1]))

    def pairs(self, partner):
        result = []
        for lat in range(self.lat):
            for lon in range(self.lon):
                there = partner(lat, lon)
                result.append((lat * self.lon + lon, there[0] * self.lon + there[1]))
        return result

    def phase_pairs(self, phase):
        def partner(lat, lon):
            axis, bit = self.orders[lat % 2][phase]
            return (lat ^ bit, lon) if axis == "lat" else (lat, lon ^ bit)

        return self.pairs(partner)

    def plane_rank(self):
        return 2 * lax.axis_index("band") + lax.axis_index("near")

    def plane_pairs(self, step):
        def partner(lat, lon):
            there = (lat // 2 * 2 + lon % 2) ^ step
            return there // 2 * 2 + lat % 2, lon // 2 * 2 + there % 2

        return self.pairs(partner)

    def inner_rows(self, lat, lon):
        return lat ^ 1, lon

    def outer_rows(self, lat, lon):
        there = lat + 1 if lat % 2 else lat - 1
        if 0 <= there < self.lat:
            return there, lon
        return lat, (lon + self.half) % self.lon

    def inner_columns(self, lat, lon):
        return lat, lon ^ 1

    def outer_columns(self, lat, lon):
        return lat, (lon + (1 if lon % 2 else -1)) % self.lon


def permuted(value, pairs):
    return lax.ppermute(value, AXES, pairs)


def lanes(shape):
    return lax.broadcasted_iota(jnp.int32, shape, len(shape) - 1)


def rolled(value, shift):
    shift %= value.shape[1]
    return pltpu.roll(value, shift, 1) if shift else value


def edge_columns(row, position, columns):
    lane = lanes(row.shape)
    columns = jnp.where(lane == position, rolled(row, position), columns)
    return jnp.where(lane == LAST + position, rolled(row, LAST + position + 1), columns)


def second_columns(row, position, columns):
    lane = lanes(row.shape)
    columns = jnp.where(lane == position, rolled(row, position - 1), columns)
    return jnp.where(lane == LAST + position, rolled(row, LAST + position + 2), columns)


def at_edges(row, position, columns):
    lane = lanes(row.shape)
    width = row.shape[1]
    row = jnp.where(lane == 0, rolled(columns, -position), row)
    return jnp.where(lane == width - 1, rolled(columns, width - 1 - LAST - position), row)


def pick(flag, yes, no):
    return jnp.where(flag, yes, no)


def is_odd(axis):
    return lax.axis_index(axis) % 2 == 1


def row_sends(first, last, inner_out, outer_out):
    odd = is_odd("core")
    inner_out[...] = pick(odd, first, last).astype(BF16)
    outer_out[...] = pick(odd, last, first).astype(BF16)


def row_halo(inner, outer):
    odd = is_odd("core")
    inner, outer = inner[...].astype(F32), outer[...].astype(F32)
    return pick(odd, inner, outer), pick(odd, outer, inner)


def packed(columns, groups):
    count, width = columns.shape[0] // groups, columns.shape[1] // groups
    lane = lanes((count, columns.shape[1]))
    value = columns[0:count]
    for group in range(1, groups):
        part = rolled(columns[group * count : (group + 1) * count], group * width)
        value = jnp.where(lane >= group * width, part, value)
    return value


def unpacked(value, groups):
    width = value.shape[1] // groups
    return jnp.concatenate([rolled(value, -group * width) for group in range(groups)], axis=0)


def column_halo(inner, outer, groups):
    odd = is_odd("near")
    inner, outer = inner[...].astype(F32), outer[...].astype(F32)
    return unpacked(pick(odd, inner, outer), groups), unpacked(pick(odd, outer, inner), groups)


def pack_kernel(below, hidden, inner_out, outer_out, wide_out, below_here, hidden_here, arrived):
    first = pltpu.make_async_copy(below, below_here, arrived.at[0])
    second = pltpu.make_async_copy(hidden, hidden_here, arrived.at[1])
    first.start()
    second.start()
    channels, row_count, width = below.shape
    size = channels * row_count
    first.wait()
    wide_out[0:size, :] = below_here[...].astype(F32).reshape(size, width)
    second.wait()
    wide_out[size : 2 * size, :] = hidden_here[...].astype(F32).reshape(size, width)
    edges = [
        wide_out[pl.ds(index, 2 * channels, stride=row_count), :] for index in (0, row_count - 1)
    ]
    row_sends(edges[0], edges[1], inner_out, outer_out)


def down_rows(values, width):
    count = values.shape[0]
    return jnp.broadcast_to(values[None, :], (width, count)).T


def prepare_kernel(
    wide,
    cell_hbm,
    weights_hbm,
    hidden_grad_hbm,
    target_hbm,
    land_hbm,
    fire_hbm,
    gate_bias_hbm,
    readout_hbm,
    rows_out,
    columns_out,
    second_out,
    cell_strip_out,
    hidden_grad_strip_out,
    fields_strip_out,
    cell_out,
    weights_out,
    hidden_grad_out,
    target_out,
    land_out,
    fire_out,
    bias_wide_out,
    readout_wide_out,
    hidden_grad_here,
    gate_bias_here,
    readout_here,
    arrived,
):
    copies = [
        pltpu.make_async_copy(source, target, arrived.at[index])
        for index, (source, target) in enumerate(
            (
                (cell_hbm, cell_out),
                (weights_hbm, weights_out),
                (hidden_grad_hbm, hidden_grad_here),
                (target_hbm, target_out),
                (land_hbm, land_out),
                (fire_hbm, fire_out),
                (gate_bias_hbm, gate_bias_here),
                (readout_hbm, readout_here),
            )
        )
    ]
    for copy in copies:
        copy.start()
    row_count, channels, width = rows_out.shape
    columns = jnp.zeros((channels, width), F32)
    second = jnp.zeros((channels, width), F32)
    for index in range(row_count):
        row = wide[pl.ds(index, channels, stride=row_count), :]
        rows_out[index] = row.astype(BF16)
        columns = edge_columns(row, index + 1, columns)
        second = second_columns(row, index + 1, second)
    columns_out[...] = columns
    second_out[...] = second
    for copy in copies:
        copy.wait()
    hidden_grad_out[...] = hidden_grad_here[...].astype(F32).reshape(hidden_grad_out.shape)
    bias_wide_out[...] = down_rows(gate_bias_here[...], width)
    readout_wide_out[...] = down_rows(readout_here[...], width)
    hid = hidden_grad_here.shape[0]
    cell_strip = jnp.zeros((hid, width), F32)
    hidden_grad_strip = jnp.zeros((hid, width), F32)
    fields_strip = jnp.zeros((8, width), F32)
    for index in range(row_count):
        strided = pl.ds(index, hid, stride=row_count)
        cell_strip = edge_columns(cell_out[strided, :], index + 1, cell_strip)
        hidden_grad_strip = edge_columns(hidden_grad_out[strided, :], index + 1, hidden_grad_strip)
        at = slice(index, index + 1)
        fields = [target_out[at, :], land_out[at, :].astype(F32), fire_out[at, :].astype(F32)]
        fields = jnp.concatenate(fields + [jnp.zeros((5, width), F32)], axis=0)
        fields_strip = edge_columns(fields, index + 1, fields_strip)
    cell_strip_out[...] = cell_strip
    hidden_grad_strip_out[...] = hidden_grad_strip
    fields_strip_out[...] = fields_strip


def columns_kernel(row_count, groups, columns, outer, inner, packed_out, *whole_out):
    north, south = row_halo(inner, outer)
    value = edge_columns(north, 0, columns[...].astype(F32))
    value = edge_columns(south, row_count + 1, value)
    packed_out[...] = packed(value, groups).astype(BF16)
    for out in whole_out:
        out[...] = value.astype(BF16)


def encode(bias):
    high = bias.astype(BF16).astype(F32)
    return jnp.concatenate([high, bias - high], axis=0)


def decode(block):
    return block[0:8] + block[8:16]


def cell_step(part, cell_before, hidden_grad, target, land, fire, readout):
    hid = part.shape[0] // 4
    input_gate = 0.5 + 0.5 * jnp.tanh(0.5 * part[0:hid])
    forget_gate = 0.5 + 0.5 * jnp.tanh(0.5 * part[hid : 2 * hid])
    output_gate = 0.5 + 0.5 * jnp.tanh(0.5 * part[2 * hid : 3 * hid])
    candidate = jnp.tanh(part[3 * hid : 4 * hid])
    cell_next = land * (forget_gate * cell_before + input_gate * candidate)
    squashed = jnp.tanh(cell_next)
    hidden_next = (output_gate * squashed).astype(BF16).astype(F32)
    predicted = jnp.sum(readout * hidden_next, axis=0, keepdims=True)
    total_grad = hidden_grad + 2.0 * (fire * (predicted - target)) * readout
    cell_grad = land * total_grad * output_gate * (1.0 - squashed * squashed)
    pre_grad = jnp.concatenate(
        [
            cell_grad * candidate * input_gate * (1.0 - input_gate),
            cell_grad * cell_before * forget_gate * (1.0 - forget_gate),
            total_grad * squashed * output_gate * (1.0 - output_gate),
            cell_grad * input_gate * (1.0 - candidate * candidate),
        ],
        axis=0,
    )
    return hidden_next, cell_next, cell_grad * forget_gate, pre_grad


def gates_kernel(
    place,
    rows_in,
    inner_row,
    outer_row,
    second,
    cell_prev,
    weights,
    hidden_grad,
    target,
    land,
    fire,
    bias_wide,
    readout_wide,
    hidden_out,
    cell_out,
    grad_cell_out,
    pre_out,
    second_out,
    sums,
    bias_out,
    shifted,
):
    row_count, channels, width = rows_in.shape
    gate_count = weights.shape[1]
    hid = gate_count // 4
    half_gates = place.half_gates
    north, south = row_halo(inner_row, outer_row)
    columns = second_columns(north, 0, second[...])
    second_out[...] = second_columns(south, row_count + 1, columns).astype(BF16)
    for position in range(row_count + 2):
        if position == 0:
            row = north
        elif position == row_count + 1:
            row = south
        else:
            row = rows_in[position - 1].astype(F32)
        at = pl.ds(position * width, width)
        shifted[0:channels, at] = rolled(row, 1).astype(BF16)
        shifted[channels : 2 * channels, at] = row.astype(BF16)
        shifted[2 * channels : 3 * channels, at] = rolled(row, -1).astype(BF16)

    taps = [
        jnp.concatenate([weights[3 * a], weights[3 * a + 1], weights[3 * a + 2]], axis=1)
        for a in range(3)
    ]
    bias_total = jnp.zeros((gate_count, width), F32)
    lane = lanes((gate_count, width))
    inside = (lane > 0) & (lane < width - 1)
    readout = readout_wide[...]
    pair = 2 if row_count % 2 == 0 else 1
    for base in range(0, row_count, pair):
        preact = jnp.zeros((gate_count, pair * width), F32)
        for a in range(3):
            preact += jnp.dot(
                taps[a],
                shifted[:, pl.ds((base + a) * width, pair * width)],
                preferred_element_type=F32,
            )
        for offset in range(pair):
            index = base + offset
            strided = pl.ds(index, hid, stride=row_count)
            at = slice(index, index + 1)
            hidden_next, cell_next, grad_cell, pre_grad = cell_step(
                preact[:, offset * width : (offset + 1) * width] + bias_wide[...],
                cell_prev[strided, :],
                hidden_grad[strided, :],
                target[at, :],
                land[at, :].astype(F32),
                fire[at, :].astype(F32),
                readout,
            )
            hidden_out[strided, :] = hidden_next
            cell_out[strided, :] = cell_next
            grad_cell_out[strided, :] = grad_cell
            pre_grad = jnp.where(inside, pre_grad, 0.0)
            bias_total += pre_grad
            pre_out[:, pl.ds(index * width, width)] = pre_grad.astype(BF16)
    bias_out[...] = bias_total

    for a in range(3):
        product = lax.dot_general(
            pre_out[...],
            shifted[:, pl.ds(a * width, row_count * width)],
            ACROSS,
            preferred_element_type=F32,
        )
        for b in range(3):
            for half in range(2):
                at = half * place.half_rows + (3 * a + b) * half_gates
                sums[at : at + half_gates, :] = product[
                    half * half_gates : (half + 1) * half_gates, b * channels : (b + 1) * channels
                ]
    used = place.taps * half_gates
    if place.half_rows > used:
        for half in range(2):
            at = half * place.half_rows
            sums[at + used : at + place.half_rows, :] = jnp.zeros(
                (place.half_rows - used, channels), F32
            )


def add_strip(place, half, sums, pre_strip, patches, out):
    half_gates, channels = place.half_gates, sums.shape[1]
    gates = pre_strip[pl.ds(pl.multiple_of(half * half_gates, half_gates), half_gates), :]
    product = lax.dot_general(gates, patches[...], ACROSS, preferred_element_type=F32)
    base = half * place.half_rows
    for tap in range(place.taps):
        at = pl.ds(pl.multiple_of(base + tap * half_gates, 8), half_gates)
        value = sums[at, :] + product[:, tap * channels : (tap + 1) * channels]
        out[tap * half_gates : (tap + 1) * half_gates, :] = value.astype(out.dtype)
    used = place.taps * half_gates
    if place.half_rows > used:
        rest = jnp.zeros((place.half_rows - used, channels), out.dtype)
        out[used:, :] = rest


def strip_kernel(
    place,
    row_count,
    edge,
    second,
    inner_column,
    outer_column,
    weights,
    bias_wide,
    readout_wide,
    cell_strip,
    hidden_grad_strip,
    fields_strip,
    sums,
    send_out,
    pre_out,
    pre_wide_out,
    patches,
    hidden_out,
    cell_out,
    grad_cell_out,
):
    channels, width = edge.shape
    west, east = column_halo(inner_column, outer_column, GROUPS)
    near_first = lanes((channels, width)) < LAST
    inner = second[...].astype(F32)
    columns = (
        jnp.where(near_first, rolled(west, -LAST), inner),
        edge[...].astype(F32),
        jnp.where(near_first, inner, rolled(east, LAST)),
    )
    for a in range(3):
        for b in range(3):
            at = (3 * a + b) * channels
            patches[at : at + channels, :] = rolled(columns[b], 1 - a).astype(BF16)
    taps = jnp.concatenate([weights[tap] for tap in range(place.taps)], axis=1)
    preact = jnp.dot(taps, patches[...], preferred_element_type=F32) + bias_wide[...]
    hidden_next, cell_next, grad_cell, pre_grad = cell_step(
        preact,
        cell_strip[...],
        hidden_grad_strip[...],
        fields_strip[0:1, :],
        fields_strip[1:2, :],
        fields_strip[2:3, :],
        readout_wide[...],
    )
    hidden_out[...] = hidden_next
    cell_out[...] = cell_next
    grad_cell_out[...] = grad_cell
    lane = lanes(pre_grad.shape)
    lane = jnp.where(lane >= LAST, lane - LAST, lane)
    pre_grad = jnp.where((lane >= 1) & (lane <= row_count), pre_grad, 0.0)
    pre_out[...] = pre_grad.astype(BF16)
    pre_wide_out[...] = pre_grad
    add_strip(place, 1 - place.rank(0), sums, pre_out, patches, send_out)


def keep_kernel(place, sums, pre_strip, patches, bias_partial, pre_wide, out, bias_out):
    add_strip(place, place.rank(0), sums, pre_strip, patches, out)
    channels = sums.shape[1]
    bias_total = bias_partial[...] + pre_wide[...]
    ones = jnp.ones((8, bias_total.shape[1]), BF16)
    high = bias_total.astype(BF16)
    low = (bias_total - high.astype(F32)).astype(BF16)
    flat = lax.dot_general(ones, high, ACROSS, preferred_element_type=F32)
    flat += lax.dot_general(ones, low, ACROSS, preferred_element_type=F32)
    odd = lax.broadcasted_iota(jnp.int32, (8, channels), 0) % 2 == 1
    bias_out[...] = jnp.where(odd, flat[:, channels : 2 * channels], flat[:, 0:channels])


def edges_kernel(
    row_count,
    hidden,
    cell,
    grad_cell,
    pre,
    hidden_strip,
    cell_strip,
    grad_cell_strip,
    pre_strip,
    hidden_hbm,
    cell_hbm,
    grad_cell_hbm,
    pre_out,
    inner_out,
    outer_out,
    hidden_low,
    hidden_here,
    cell_here,
    grad_cell_here,
    left,
):
    hid, _, width = hidden_low.shape
    leaving = []
    for source, strip, here, ready, target in (
        (cell, cell_strip, cell_here, cell_here, cell_hbm),
        (grad_cell, grad_cell_strip, grad_cell_here, grad_cell_here, grad_cell_hbm),
        (hidden, hidden_strip, hidden_here, hidden_low, hidden_hbm),
    ):
        columns = strip[...]
        for index in range(row_count):
            strided = pl.ds(index, hid, stride=row_count)
            here[strided, :] = at_edges(source[strided, :], index + 1, columns)
        if ready is hidden_low:
            hidden_low[...] = here[...].reshape(hidden_low.shape).astype(BF16)
        leaving.append(pltpu.make_async_copy(ready, target, left.at[len(leaving)]))
        leaving[-1].start()
    first, last = None, None
    columns = pre_strip[...].astype(F32)
    for index in range(row_count):
        at = pl.ds(index * width, width)
        row = at_edges(pre[:, at].astype(F32), index + 1, columns)
        pre_out[:, at] = row.astype(BF16)
        first = row if index == 0 else first
        last = row
    row_sends(first, last, inner_out, outer_out)
    for copy in leaving:
        copy.wait()


def pair_kernel(place, keep, bias, received, *outs):
    sends, keep_out, scratch = outs[:-2], outs[-2], outs[-1]
    chunk = place.chunk
    rank = place.plane_rank()
    scratch[...] = keep[...] + received[...].astype(F32)
    block = encode(bias[...]).astype(BF16)
    for step, send in zip(range(place.plane - 1, 0, -1), sends):
        send[0:BIAS_ROWS, :] = block
        at = pl.ds(pl.multiple_of((rank ^ step) * chunk, 8), chunk)
        send[BIAS_ROWS:, :] = scratch[at, :].astype(BF16)
    keep_out[...] = scratch[pl.ds(pl.multiple_of(rank * chunk, 8), chunk), :]


def plane_kernel(keep, bias, *refs):
    received, out = refs[:-2], refs[-1]
    total, bias_total = keep[...], bias[...]
    for ref in received:
        total += ref[BIAS_ROWS:, :].astype(F32)
        bias_total += decode(ref[0:BIAS_ROWS, :].astype(F32))
    out[0:BIAS_ROWS, :] = encode(bias_total).astype(BF16)
    out[BIAS_ROWS:, :] = total.astype(BF16)


def join_kernel(place, *refs):
    blocks, out = refs[:-2], refs[-1]
    rank = place.plane_rank()
    for step, block in enumerate(blocks):
        out[rank ^ step] = block[...]


def add_kernel(scale, own, received, out):
    here, there = own[...].astype(F32), received[...].astype(F32)
    bias = (decode(here[0:BIAS_ROWS]) + decode(there[0:BIAS_ROWS])) * scale
    out[0:BIAS_ROWS, :] = encode(bias).astype(BF16)
    out[BIAS_ROWS:, :] = ((here[BIAS_ROWS:] + there[BIAS_ROWS:]) * scale).astype(BF16)


def store_half(place, half, blocks, out, wide, left):
    chunk, half_gates = place.chunk, place.half_gates
    gates = pl.ds(pl.multiple_of(half * half_gates, half_gates), half_gates)
    copies = []
    for index in range(place.plane):
        wide[index * chunk : (index + 1) * chunk, :] = blocks[index, BIAS_ROWS:, :].astype(F32)
        while len(copies) < min(place.taps, (index + 1) * chunk // half_gates):
            tap = len(copies)
            source = wide.at[tap * half_gates : (tap + 1) * half_gates, :]
            copies.append(pltpu.make_async_copy(source, out.at[tap, gates, :], left.at[tap]))
            copies[-1].start()
    return copies


def own_half_kernel(place, own, out, wide, left):
    for copy in store_half(place, place.rank(0), own, out, wide, left):
        copy.wait()


def other_half_kernel(
    place, own, received, after, out_before, out, bias_out, wide, bias_here, left
):
    del after, out_before
    rank = place.rank(0)
    here, there = own[0, 0:BIAS_ROWS, :].astype(F32), received[0, 0:BIAS_ROWS, :].astype(F32)
    bias = decode(here) + decode(there)
    width = bias.shape[1]
    for index in range(bias_here.shape[0] // width):
        bias_here[pl.ds(index * width, width)] = bias[index]
    bias_copy = pltpu.make_async_copy(bias_here, bias_out, left.at[place.taps])
    bias_copy.start()
    copies = store_half(place, 1 - rank, received, out, wide, left)
    bias_copy.wait()
    for copy in copies:
        copy.wait()


def field_kernel(pre, weights, wide_out, turned_out, done_out, shifted):
    done_out[...] = jnp.zeros(done_out.shape, F32)
    gate_count, cells = pre.shape
    channels, width = weights.shape[2], wide_out.shape[1]
    row_count = cells // width
    lane = lanes((gate_count, width))
    for index in range(row_count):
        at = pl.ds(index * width, width)
        row = pre[:, at].astype(F32)
        left = jnp.where(lane == 0, 0.0, rolled(row, 1))
        right = jnp.where(lane == width - 1, 0.0, rolled(row, -1))
        shifted[0:gate_count, at] = right.astype(BF16)
        shifted[gate_count : 2 * gate_count, at] = pre[:, at]
        shifted[2 * gate_count : 3 * gate_count, at] = left.astype(BF16)
    for a in range(3):
        for b in range(3):
            turned_out[a, :, b * gate_count : (b + 1) * gate_count] = weights[3 * a + b].T

    def product(a, index, count):
        return jnp.dot(
            turned_out[a],
            shifted[:, pl.ds(index * width, count * width)],
            preferred_element_type=F32,
        )

    pair = 2 if row_count % 2 == 0 else 1
    for base in range(0, row_count, pair):
        total = product(1, base, pair)
        for a, first in ((2, base - 1), (0, base + 1)):
            low, high = max(first, 0), min(first + pair, row_count)
            if low >= high:
                continue
            part = product(a, low, high - low)
            blank = jnp.zeros((channels, width), F32)
            parts = [blank] * (low - first) + [part] + [blank] * (first + pair - high)
            total += jnp.concatenate(parts, axis=1)
        for offset in range(pair):
            value = total[:, offset * width : (offset + 1) * width]
            wide_out[pl.ds(base + offset, channels, stride=row_count), :] = value


def field_halo_kernel(
    place,
    wide,
    turned,
    outer_row,
    inner_row,
    outer_column,
    inner_column,
    inputs_out,
    hidden_out,
    done_out,
    total,
):
    done_out[...] = jnp.zeros(done_out.shape, F32)
    hid, row_count, width = hidden_out.shape
    channels = turned.shape[1]
    gate_count = turned.shape[2] // 3
    north, south = row_halo(inner_row, outer_row)
    west, east = column_halo(inner_column, outer_column, PRE_GROUPS)
    lane = lanes((gate_count, width))
    lat = place.position()[0]

    def row_part(taps, row, position):
        left = jnp.where(lane == 0, rolled(west, -LAST - position), rolled(row, 1))
        right = rolled(east, width - 1 - position)
        right = jnp.where(lane == width - 1, right, rolled(row, -1))
        stack = jnp.concatenate([right, row, left], axis=0).astype(BF16)
        return jnp.dot(taps, stack, preferred_element_type=F32)

    above = row_part(turned[jnp.where(lat == 0, 0, 2)], north, 0)
    below = row_part(turned[jnp.where(lat == place.lat - 1, 2, 0)], south, row_count + 1)

    inside = (lane >= 1) & (lane <= row_count)
    west = jnp.where(inside, rolled(west, -LAST), 0.0)
    east = jnp.where(inside, east, 0.0)
    sides = [rolled(west, a - 1) for a in range(3)] + [rolled(east, LAST + a - 1) for a in range(3)]
    taps = [turned[a, :, 2 * gate_count : 3 * gate_count] for a in range(3)]
    taps += [turned[a, :, 0:gate_count] for a in range(3)]
    columns = jnp.dot(
        jnp.concatenate(taps, axis=1),
        jnp.concatenate(sides, axis=0).astype(BF16),
        preferred_element_type=F32,
    )
    blank = jnp.zeros((channels, width), F32)
    for index in range(row_count):
        strided = pl.ds(index, channels, stride=row_count)
        value = wide[strided, :] + at_edges(blank, index + 1, columns)
        if index == 0:
            value += above
        if index == row_count - 1:
            value += below
        total[strided, :] = value
    size = (channels - hid) * row_count
    inputs_out[...] = total[0:size, :].reshape(inputs_out.shape).astype(BF16)
    hidden_out[...] = total[size:, :].reshape(hidden_out.shape).astype(BF16)


def body(
    place,
    inputs_below,
    hidden_prev,
    cell_prev,
    kernel_weights,
    gate_bias,
    readout,
    target_field,
    land_mask,
    fire_mask,
    hidden_grad,
):
    hid, row_count, width = hidden_prev.shape
    gate_count, channels = kernel_weights.shape[1:]
    cells = row_count * width
    halo_cells = (row_count + 2) * width
    scaling = 1.0 / math.sqrt(cells * place.lat * place.lon)
    bind = functools.partial
    inner_rows, outer_rows = place.pairs(place.inner_rows), place.pairs(place.outer_rows)
    inner_columns = place.pairs(place.inner_columns)
    outer_columns = place.pairs(place.outer_columns)
    flat = sds((hid * row_count, width), F32)
    strip = sds((hid, width), F32)

    inner, outer, wide = call(
        pack_kernel,
        (
            sds((channels, width), BF16),
            sds((channels, width), BF16),
            sds((channels * row_count, width), F32),
        ),
        [
            pltpu.VMEM(inputs_below.shape, BF16),
            pltpu.VMEM(hidden_prev.shape, BF16),
            pltpu.SemaphoreType.DMA((2,)),
        ],
        remote=2,
        moved=4 * channels * cells,
    )(inputs_below, hidden_prev)
    inner, outer = permuted(inner, inner_rows), permuted(outer, outer_rows)
    (
        rows,
        columns,
        second,
        cell_strip,
        hidden_grad_strip,
        fields_strip,
        cell_here,
        weights_here,
        hidden_grad_here,
        target_here,
        land_here,
        fire_here,
        bias_wide,
        readout_wide,
    ) = call(
        prepare_kernel,
        (
            sds((row_count, channels, width), BF16),
            sds((channels, width), F32),
            sds((channels, width), F32),
            strip,
            strip,
            sds((8, width), F32),
            flat,
            sds(kernel_weights.shape, BF16),
            flat,
            sds(target_field.shape, F32),
            sds(land_mask.shape, jnp.int32),
            sds(fire_mask.shape, jnp.int32),
            sds((gate_count, width), F32),
            sds((hid, width), F32),
        ),
        [
            pltpu.VMEM(hidden_grad.shape, BF16),
            pltpu.VMEM(gate_bias.shape, F32),
            pltpu.VMEM(readout.shape, F32),
            pltpu.SemaphoreType.DMA((8,)),
        ],
        remote=8,
        moved=6_000_000,
    )(
        wide,
        cell_prev.reshape(hid * row_count, width),
        kernel_weights,
        hidden_grad,
        target_field,
        land_mask,
        fire_mask,
        gate_bias,
        readout,
    )
    columns, edge = call(
        bind(columns_kernel, row_count, GROUPS),
        (sds((channels // GROUPS, width), BF16), sds((channels, width), BF16)),
    )(columns, outer, inner)
    inner_column = permuted(columns, inner_columns)
    outer_column = permuted(columns, outer_columns)
    hidden_rows, cell_rows, grad_cell_rows, pre, second, sums, bias = call(
        bind(gates_kernel, place),
        (
            flat,
            flat,
            flat,
            sds((gate_count, cells), BF16),
            sds((channels, width), BF16),
            sds((2 * place.half_rows, channels), F32),
            sds((gate_count, width), F32),
        ),
        [pltpu.VMEM((3 * channels, halo_cells), BF16)],
        flops=4 * 9 * gate_count * channels * cells,
        moved=6_000_000,
        transcendentals=5 * hid * cells,
    )(
        rows,
        inner,
        outer,
        second,
        cell_here,
        weights_here,
        hidden_grad_here,
        target_here,
        land_here,
        fire_here,
        bias_wide,
        readout_wide,
    )
    send, pre_strip, pre_wide, patches, *strips = call(
        bind(strip_kernel, place, row_count),
        (
            sds((place.half_rows, channels), BF16),
            sds((gate_count, width), BF16),
            sds((gate_count, width), F32),
            sds((place.taps * channels, width), BF16),
            strip,
            strip,
            strip,
        ),
    )(
        edge,
        second,
        inner_column,
        outer_column,
        weights_here,
        bias_wide,
        readout_wide,
        cell_strip,
        hidden_grad_strip,
        fields_strip,
        sums,
    )
    keep, bias = call(
        bind(keep_kernel, place),
        (sds((place.half_rows, channels), F32), sds((8, channels), F32)),
    )(sums, pre_strip, patches, bias, pre_wide)
    hidden_next, cell_next, grad_cell, pre, pre_inner, pre_outer = call(
        bind(edges_kernel, row_count),
        (
            sds((hid, row_count, width), BF16),
            flat,
            flat,
            sds((gate_count, cells), BF16),
            sds((gate_count, width), BF16),
            sds((gate_count, width), BF16),
        ),
        [
            pltpu.VMEM((hid, row_count, width), BF16),
            pltpu.VMEM(flat.shape, F32),
            pltpu.VMEM(flat.shape, F32),
            pltpu.VMEM(flat.shape, F32),
            pltpu.SemaphoreType.DMA((3,)),
        ],
        leaving=3,
        moved=4_000_000,
    )(hidden_rows, cell_rows, grad_cell_rows, pre, *strips, pre_strip)
    pre_inner, pre_outer = permuted(pre_inner, inner_rows), permuted(pre_outer, outer_rows)
    pre_columns = call(
        bind(columns_kernel, row_count, PRE_GROUPS),
        (sds((gate_count // PRE_GROUPS, width), BF16),),
    )(pre_strip, pre_outer, pre_inner)[0]

    block = sds((BIAS_ROWS + place.chunk, channels), BF16)
    token = sds((8, width), F32)
    steps = range(place.plane - 1, 0, -1)
    *sends, keep = call(
        bind(pair_kernel, place),
        (*[block for _ in steps], sds((place.chunk, channels), F32)),
        [pltpu.VMEM((place.half_rows, channels), F32)],
    )(keep, bias, permuted(send, place.phase_pairs(0)))
    received = [permuted(send, place.plane_pairs(step)) for step, send in zip(steps, sends)]
    field, turned, field_done = call(
        field_kernel,
        (
            sds((channels * row_count, width), F32),
            sds((3, channels, 3 * gate_count), BF16),
            token,
        ),
        [pltpu.VMEM((3 * gate_count, cells), BF16)],
        flops=2 * 9 * gate_count * channels * cells,
        moved=3_000_000,
    )(pre, weights_here)
    part = call(plane_kernel, block)(keep, bias, *received, field_done)
    pre_inner_columns = permuted(pre_columns, inner_columns)
    pre_outer_columns = permuted(pre_columns, outer_columns)
    phases = len(place.orders[0])
    for phase in range(1, phases):
        is_last = phase == phases - 1
        part = call(bind(add_kernel, scaling if is_last else 1.0), block)(
            part, permuted(part, place.phase_pairs(phase))
        )
    received = [permuted(part, place.plane_pairs(step)) for step in steps[::-1]]
    grad_inputs, grad_hidden, field_done = call(
        bind(field_halo_kernel, place),
        (
            sds((channels - hid, row_count, width), BF16),
            sds((hid, row_count, width), BF16),
            token,
        ),
        [pltpu.VMEM((channels * row_count, width), F32)],
        flops=40 * gate_count * channels * cells * 9,
        moved=2_000_000,
    )(field, turned, pre_outer, pre_inner, pre_outer_columns, pre_inner_columns)
    gathered = call(bind(join_kernel, place), sds((place.plane, *block.shape), BF16))(
        part, *received, field_done
    )
    received = permuted(gathered, place.phase_pairs(0))
    half = [pltpu.VMEM((place.half_rows, channels), F32)]
    grad_kernel = call(
        bind(own_half_kernel, place),
        (sds(kernel_weights.shape, F32),),
        half + [pltpu.SemaphoreType.DMA((place.taps,))],
        leaving=1,
        moved=6 * place.half_rows * channels,
    )(gathered)[0]
    grad_kernel, grad_bias = call(
        bind(other_half_kernel, place),
        (sds(kernel_weights.shape, F32), sds((gate_count,), F32)),
        half + [pltpu.VMEM((gate_count,), F32), pltpu.SemaphoreType.DMA((place.taps + 1,))],
        remote=1,
        leaving=2,
        aliases={3: 0},
        moved=6 * place.half_rows * channels,
    )(gathered, received, target_here, grad_kernel)
    shape = hidden_prev.shape
    return (
        hidden_next,
        cell_next.reshape(shape),
        grad_inputs,
        grad_hidden,
        grad_cell.reshape(shape),
        grad_kernel,
        grad_bias,
    )


def solution(mesh):
    lat_count, lon_count = mesh.shape["lat"], mesh.shape["lon"]
    split = Mesh(mesh.devices.reshape(lat_count // 2, 2, lon_count // 2, 2), AXES)
    field = P(None, ("band", "core"), ("reach", "near"))
    flat = P(("band", "core"), ("reach", "near"))

    def run(*args):
        place = Layout(lat_count, lon_count, *args[3].shape[:2])
        return jax.shard_map(
            functools.partial(body, place),
            mesh=split,
            in_specs=(field, field, field, P(), P(), P(), flat, flat, flat, field),
            out_specs=(field, field, field, field, field, P(), P()),
            check_vma=False,
        )(*args)

    return run
```

```python
import functools
import math

import jax
import jax.numpy as jnp
from jax import lax
from jax.experimental import pallas as pl
from jax.experimental.pallas import tpu as pltpu
from jax.sharding import Mesh, PartitionSpec as P

F32 = jnp.float32
BF16 = jnp.bfloat16
AXES = ("band", "core", "reach", "near")
BIAS_ROWS = 16
GROUPS = 4
PRE_GROUPS = 4
LAST = 16
VMEM = pl.BlockSpec(memory_space=pltpu.VMEM)
HBM = pl.BlockSpec(memory_space=pltpu.HBM)
ACROSS = (((1,), (1,)), ((), ()))


def sds(shape, dtype):
    return jax.ShapeDtypeStruct(shape, dtype)


def call(
    kernel,
    out_shape,
    scratch=(),
    remote=0,
    leaving=0,
    aliases=None,
    flops=0,
    moved=0,
    transcendentals=0,
):
    several = isinstance(out_shape, tuple)
    shapes = out_shape if several else (out_shape,)
    out_specs = tuple([HBM] * leaving + [VMEM] * (len(shapes) - leaving))

    def run(*args):
        near = len(args) - remote
        far = [pltpu.with_memory_space_constraint(arg, pltpu.HBM) for arg in args[near:]]
        return pl.pallas_call(
            kernel,
            out_shape=out_shape,
            in_specs=[VMEM] * near + [HBM] * remote,
            out_specs=out_specs if several else out_specs[0],
            input_output_aliases=aliases or {},
            scratch_shapes=list(scratch),
            cost_estimate=pl.CostEstimate(
                flops=flops, bytes_accessed=moved, transcendentals=transcendentals
            ),
            compiler_params=pltpu.CompilerParams(vmem_limit_bytes=24 * 1024 * 1024),
        )(*args[:near], *far)

    return run


class Layout:
    def __init__(self, lat_count, lon_count, taps, gate_count):
        self.lat, self.lon = lat_count, lon_count
        self.half = lon_count // 2
        self.taps, self.half_gates = taps, gate_count // 2
        self.plane = lat_count
        whole = [("lon", 1 << k) for k in range(1, lon_count.bit_length() - 1)]
        self.orders = ([("lat", 1)] + whole, [("lat", 1)] + whole[::-1])
        step = 8 * self.plane
        self.half_rows = -(-taps * self.half_gates // step) * step
        self.chunk = self.half_rows // self.plane

    def position(self):
        lat = 2 * lax.axis_index("band") + lax.axis_index("core")
        return lat, 2 * lax.axis_index("reach") + lax.axis_index("near")

    def rank(self, phase):
        lat, lon = self.position()

        def digit(order):
            axis, bit = order[phase]
            return ((lat if axis == "lat" else lon) // bit) % 2

        return jnp.where(lat % 2 == 0, digit(self.orders[0]), digit(self.orders[1]))

    def pairs(self, partner):
        result = []
        for lat in range(self.lat):
            for lon in range(self.lon):
                there = partner(lat, lon)
                result.append((lat * self.lon + lon, there[0] * self.lon + there[1]))
        return result

    def phase_pairs(self, phase):
        def partner(lat, lon):
            axis, bit = self.orders[lat % 2][phase]
            return (lat ^ bit, lon) if axis == "lat" else (lat, lon ^ bit)

        return self.pairs(partner)

    def plane_rank(self):
        return 2 * lax.axis_index("band") + lax.axis_index("near")

    def plane_pairs(self, step):
        def partner(lat, lon):
            there = (lat // 2 * 2 + lon % 2) ^ step
            return there // 2 * 2 + lat % 2, lon // 2 * 2 + there % 2

        return self.pairs(partner)

    def inner_rows(self, lat, lon):
        return lat ^ 1, lon

    def outer_rows(self, lat, lon):
        there = lat + 1 if lat % 2 else lat - 1
        if 0 <= there < self.lat:
            return there, lon
        return lat, (lon + self.half) % self.lon

    def inner_columns(self, lat, lon):
        return lat, lon ^ 1

    def outer_columns(self, lat, lon):
        return lat, (lon + (1 if lon % 2 else -1)) % self.lon


def permuted(value, pairs):
    return lax.ppermute(value, AXES, pairs)


def lanes(shape):
    return lax.broadcasted_iota(jnp.int32, shape, len(shape) - 1)


def rolled(value, shift):
    shift %= value.shape[1]
    return pltpu.roll(value, shift, 1) if shift else value


def edge_columns(row, position, columns):
    lane = lanes(row.shape)
    columns = jnp.where(lane == position, rolled(row, position), columns)
    return jnp.where(lane == LAST + position, rolled(row, LAST + position + 1), columns)


def second_columns(row, position, columns):
    lane = lanes(row.shape)
    columns = jnp.where(lane == position, rolled(row, position - 1), columns)
    return jnp.where(lane == LAST + position, rolled(row, LAST + position + 2), columns)


def at_edges(row, position, columns):
    lane = lanes(row.shape)
    width = row.shape[1]
    row = jnp.where(lane == 0, rolled(columns, -position), row)
    return jnp.where(lane == width - 1, rolled(columns, width - 1 - LAST - position), row)


def pick(flag, yes, no):
    return jnp.where(flag, yes, no)


def is_odd(axis):
    return lax.axis_index(axis) % 2 == 1


def row_sends(first, last, inner_out, outer_out):
    odd = is_odd("core")
    inner_out[...] = pick(odd, first, last).astype(BF16)
    outer_out[...] = pick(odd, last, first).astype(BF16)


def row_halo(inner, outer):
    odd = is_odd("core")
    inner, outer = inner[...].astype(F32), outer[...].astype(F32)
    return pick(odd, inner, outer), pick(odd, outer, inner)


def packed(columns, groups):
    count, width = columns.shape[0] // groups, columns.shape[1] // groups
    lane = lanes((count, columns.shape[1]))
    value = columns[0:count]
    for group in range(1, groups):
        part = rolled(columns[group * count : (group + 1) * count], group * width)
        value = jnp.where(lane >= group * width, part, value)
    return value


def unpacked(value, groups):
    width = value.shape[1] // groups
    return jnp.concatenate([rolled(value, -group * width) for group in range(groups)], axis=0)


def column_halo(inner, outer, groups):
    odd = is_odd("near")
    inner, outer = inner[...].astype(F32), outer[...].astype(F32)
    return unpacked(pick(odd, inner, outer), groups), unpacked(pick(odd, outer, inner), groups)


def pack_kernel(below, hidden, inner_out, outer_out, wide_out, below_here, hidden_here, arrived):
    first = pltpu.make_async_copy(below, below_here, arrived.at[0])
    second = pltpu.make_async_copy(hidden, hidden_here, arrived.at[1])
    first.start()
    second.start()
    channels, row_count, width = below.shape
    size = channels * row_count
    first.wait()
    wide_out[0:size, :] = below_here[...].astype(F32).reshape(size, width)
    second.wait()
    wide_out[size : 2 * size, :] = hidden_here[...].astype(F32).reshape(size, width)
    edges = [
        wide_out[pl.ds(index, 2 * channels, stride=row_count), :] for index in (0, row_count - 1)
    ]
    row_sends(edges[0], edges[1], inner_out, outer_out)


def down_rows(values, width):
    count = values.shape[0]
    return jnp.broadcast_to(values[None, :], (width, count)).T


def prepare_kernel(
    wide,
    cell_hbm,
    weights_hbm,
    hidden_grad_hbm,
    target_hbm,
    land_hbm,
    fire_hbm,
    gate_bias_hbm,
    readout_hbm,
    rows_out,
    columns_out,
    second_out,
    cell_strip_out,
    hidden_grad_strip_out,
    fields_strip_out,
    cell_out,
    weights_out,
    hidden_grad_out,
    target_out,
    land_out,
    fire_out,
    bias_wide_out,
    readout_wide_out,
    hidden_grad_here,
    gate_bias_here,
    readout_here,
    arrived,
):
    copies = [
        pltpu.make_async_copy(source, target, arrived.at[index])
        for index, (source, target) in enumerate(
            (
                (cell_hbm, cell_out),
                (weights_hbm, weights_out),
                (hidden_grad_hbm, hidden_grad_here),
                (target_hbm, target_out),
                (land_hbm, land_out),
                (fire_hbm, fire_out),
                (gate_bias_hbm, gate_bias_here),
                (readout_hbm, readout_here),
            )
        )
    ]
    for copy in copies:
        copy.start()
    row_count, channels, width = rows_out.shape
    columns = jnp.zeros((channels, width), F32)
    second = jnp.zeros((channels, width), F32)
    for index in range(row_count):
        row = wide[pl.ds(index, channels, stride=row_count), :]
        rows_out[index] = row.astype(BF16)
        columns = edge_columns(row, index + 1, columns)
        second = second_columns(row, index + 1, second)
    columns_out[...] = columns
    second_out[...] = second
    for copy in copies:
        copy.wait()
    hidden_grad_out[...] = hidden_grad_here[...].astype(F32).reshape(hidden_grad_out.shape)
    bias_wide_out[...] = down_rows(gate_bias_here[...], width)
    readout_wide_out[...] = down_rows(readout_here[...], width)
    hid = hidden_grad_here.shape[0]
    cell_strip = jnp.zeros((hid, width), F32)
    hidden_grad_strip = jnp.zeros((hid, width), F32)
    fields_strip = jnp.zeros((8, width), F32)
    for index in range(row_count):
        strided = pl.ds(index, hid, stride=row_count)
        cell_strip = edge_columns(cell_out[strided, :], index + 1, cell_strip)
        hidden_grad_strip = edge_columns(hidden_grad_out[strided, :], index + 1, hidden_grad_strip)
        at = slice(index, index + 1)
        fields = [target_out[at, :], land_out[at, :].astype(F32), fire_out[at, :].astype(F32)]
        fields = jnp.concatenate(fields + [jnp.zeros((5, width), F32)], axis=0)
        fields_strip = edge_columns(fields, index + 1, fields_strip)
    cell_strip_out[...] = cell_strip
    hidden_grad_strip_out[...] = hidden_grad_strip
    fields_strip_out[...] = fields_strip


def columns_kernel(row_count, groups, columns, outer, inner, packed_out, *whole_out):
    north, south = row_halo(inner, outer)
    value = edge_columns(north, 0, columns[...].astype(F32))
    value = edge_columns(south, row_count + 1, value)
    packed_out[...] = packed(value, groups).astype(BF16)
    for out in whole_out:
        out[...] = value.astype(BF16)


def encode(bias):
    high = bias.astype(BF16).astype(F32)
    return jnp.concatenate([high, bias - high], axis=0)


def decode(block):
    return block[0:8] + block[8:16]


def cell_step(part, cell_before, hidden_grad, target, land, fire, readout):
    hid = part.shape[0] // 4
    input_gate = 0.5 + 0.5 * jnp.tanh(0.5 * part[0:hid])
    forget_gate = 0.5 + 0.5 * jnp.tanh(0.5 * part[hid : 2 * hid])
    output_gate = 0.5 + 0.5 * jnp.tanh(0.5 * part[2 * hid : 3 * hid])
    candidate = jnp.tanh(part[3 * hid : 4 * hid])
    cell_next = land * (forget_gate * cell_before + input_gate * candidate)
    squashed = jnp.tanh(cell_next)
    hidden_next = (output_gate * squashed).astype(BF16).astype(F32)
    predicted = jnp.sum(readout * hidden_next, axis=0, keepdims=True)
    total_grad = hidden_grad + 2.0 * (fire * (predicted - target)) * readout
    cell_grad = land * total_grad * output_gate * (1.0 - squashed * squashed)
    pre_grad = jnp.concatenate(
        [
            cell_grad * candidate * input_gate * (1.0 - input_gate),
            cell_grad * cell_before * forget_gate * (1.0 - forget_gate),
            total_grad * squashed * output_gate * (1.0 - output_gate),
            cell_grad * input_gate * (1.0 - candidate * candidate),
        ],
        axis=0,
    )
    return hidden_next, cell_next, cell_grad * forget_gate, pre_grad


def gates_kernel(
    place,
    rows_in,
    inner_row,
    outer_row,
    second,
    cell_prev,
    weights,
    hidden_grad,
    target,
    land,
    fire,
    bias_wide,
    readout_wide,
    hidden_out,
    cell_out,
    grad_cell_out,
    pre_out,
    second_out,
    sums,
    bias_out,
    shifted,
):
    row_count, channels, width = rows_in.shape
    gate_count = weights.shape[1]
    hid = gate_count // 4
    half_gates = place.half_gates
    north, south = row_halo(inner_row, outer_row)
    columns = second_columns(north, 0, second[...])
    second_out[...] = second_columns(south, row_count + 1, columns).astype(BF16)
    for position in range(row_count + 2):
        if position == 0:
            row = north
        elif position == row_count + 1:
            row = south
        else:
            row = rows_in[position - 1].astype(F32)
        at = pl.ds(position * width, width)
        shifted[0:channels, at] = rolled(row, 1).astype(BF16)
        shifted[channels : 2 * channels, at] = row.astype(BF16)
        shifted[2 * channels : 3 * channels, at] = rolled(row, -1).astype(BF16)

    taps = [
        jnp.concatenate([weights[3 * a], weights[3 * a + 1], weights[3 * a + 2]], axis=1)
        for a in range(3)
    ]
    bias_total = jnp.zeros((gate_count, width), F32)
    lane = lanes((gate_count, width))
    inside = (lane > 0) & (lane < width - 1)
    readout = readout_wide[...]
    pair = 2 if row_count % 2 == 0 else 1
    for base in range(0, row_count, pair):
        preact = jnp.zeros((gate_count, pair * width), F32)
        for a in range(3):
            preact += jnp.dot(
                taps[a],
                shifted[:, pl.ds((base + a) * width, pair * width)],
                preferred_element_type=F32,
            )
        for offset in range(pair):
            index = base + offset
            strided = pl.ds(index, hid, stride=row_count)
            at = slice(index, index + 1)
            hidden_next, cell_next, grad_cell, pre_grad = cell_step(
                preact[:, offset * width : (offset + 1) * width] + bias_wide[...],
                cell_prev[strided, :],
                hidden_grad[strided, :],
                target[at, :],
                land[at, :].astype(F32),
                fire[at, :].astype(F32),
                readout,
            )
            hidden_out[strided, :] = hidden_next
            cell_out[strided, :] = cell_next
            grad_cell_out[strided, :] = grad_cell
            pre_grad = jnp.where(inside, pre_grad, 0.0)
            bias_total += pre_grad
            pre_out[:, pl.ds(index * width, width)] = pre_grad.astype(BF16)
    bias_out[...] = bias_total

    for a in range(3):
        product = lax.dot_general(
            pre_out[...],
            shifted[:, pl.ds(a * width, row_count * width)],
            ACROSS,
            preferred_element_type=F32,
        )
        for b in range(3):
            for half in range(2):
                at = half * place.half_rows + (3 * a + b) * half_gates
                sums[at : at + half_gates, :] = product[
                    half * half_gates : (half + 1) * half_gates, b * channels : (b + 1) * channels
                ]
    used = place.taps * half_gates
    if place.half_rows > used:
        for half in range(2):
            at = half * place.half_rows
            sums[at + used : at + place.half_rows, :] = jnp.zeros(
                (place.half_rows - used, channels), F32
            )


def add_strip(place, half, sums, pre_strip, patches, out):
    half_gates, channels = place.half_gates, sums.shape[1]
    gates = pre_strip[pl.ds(pl.multiple_of(half * half_gates, half_gates), half_gates), :]
    product = lax.dot_general(gates, patches[...], ACROSS, preferred_element_type=F32)
    base = half * place.half_rows
    for tap in range(place.taps):
        at = pl.ds(pl.multiple_of(base + tap * half_gates, 8), half_gates)
        value = sums[at, :] + product[:, tap * channels : (tap + 1) * channels]
        out[tap * half_gates : (tap + 1) * half_gates, :] = value.astype(out.dtype)
    used = place.taps * half_gates
    if place.half_rows > used:
        rest = jnp.zeros((place.half_rows - used, channels), out.dtype)
        out[used:, :] = rest


def strip_kernel(
    place,
    row_count,
    edge,
    second,
    outer_column,
    inner_column,
    weights,
    bias_wide,
    readout_wide,
    cell_strip,
    hidden_grad_strip,
    fields_strip,
    sums,
    send_out,
    pre_out,
    pre_wide_out,
    patches,
    hidden_out,
    cell_out,
    grad_cell_out,
):
    channels, width = edge.shape
    west, east = column_halo(inner_column, outer_column, GROUPS)
    near_first = lanes((channels, width)) < LAST
    inner = second[...].astype(F32)
    columns = (
        jnp.where(near_first, rolled(west, -LAST), inner),
        edge[...].astype(F32),
        jnp.where(near_first, inner, rolled(east, LAST)),
    )
    for a in range(3):
        for b in range(3):
            at = (3 * a + b) * channels
            patches[at : at + channels, :] = rolled(columns[b], 1 - a).astype(BF16)
    taps = jnp.concatenate([weights[tap] for tap in range(place.taps)], axis=1)
    preact = jnp.dot(taps, patches[...], preferred_element_type=F32) + bias_wide[...]
    hidden_next, cell_next, grad_cell, pre_grad = cell_step(
        preact,
        cell_strip[...],
        hidden_grad_strip[...],
        fields_strip[0:1, :],
        fields_strip[1:2, :],
        fields_strip[2:3, :],
        readout_wide[...],
    )
    hidden_out[...] = hidden_next
    cell_out[...] = cell_next
    grad_cell_out[...] = grad_cell
    lane = lanes(pre_grad.shape)
    lane = jnp.where(lane >= LAST, lane - LAST, lane)
    pre_grad = jnp.where((lane >= 1) & (lane <= row_count), pre_grad, 0.0)
    pre_out[...] = pre_grad.astype(BF16)
    pre_wide_out[...] = pre_grad
    add_strip(place, 1 - place.rank(0), sums, pre_out, patches, send_out)


def keep_kernel(place, sums, pre_strip, patches, bias_partial, pre_wide, out, bias_out):
    add_strip(place, place.rank(0), sums, pre_strip, patches, out)
    channels = sums.shape[1]
    bias_total = bias_partial[...] + pre_wide[...]
    ones = jnp.ones((8, bias_total.shape[1]), BF16)
    high = bias_total.astype(BF16)
    low = (bias_total - high.astype(F32)).astype(BF16)
    flat = lax.dot_general(ones, high, ACROSS, preferred_element_type=F32)
    flat += lax.dot_general(ones, low, ACROSS, preferred_element_type=F32)
    odd = lax.broadcasted_iota(jnp.int32, (8, channels), 0) % 2 == 1
    bias_out[...] = jnp.where(odd, flat[:, channels : 2 * channels], flat[:, 0:channels])


def edges_kernel(
    row_count,
    hidden,
    cell,
    grad_cell,
    pre,
    hidden_strip,
    cell_strip,
    grad_cell_strip,
    pre_strip,
    hidden_hbm,
    cell_hbm,
    grad_cell_hbm,
    pre_out,
    inner_out,
    outer_out,
    hidden_low,
    hidden_here,
    cell_here,
    grad_cell_here,
    left,
):
    hid, _, width = hidden_low.shape
    leaving = []
    for source, strip, here, ready, target in (
        (cell, cell_strip, cell_here, cell_here, cell_hbm),
        (grad_cell, grad_cell_strip, grad_cell_here, grad_cell_here, grad_cell_hbm),
        (hidden, hidden_strip, hidden_here, hidden_low, hidden_hbm),
    ):
        columns = strip[...]
        for index in range(row_count):
            strided = pl.ds(index, hid, stride=row_count)
            here[strided, :] = at_edges(source[strided, :], index + 1, columns)
        if ready is hidden_low:
            hidden_low[...] = here[...].reshape(hidden_low.shape).astype(BF16)
        leaving.append(pltpu.make_async_copy(ready, target, left.at[len(leaving)]))
        leaving[-1].start()
    first, last = None, None
    columns = pre_strip[...].astype(F32)
    for index in range(row_count):
        at = pl.ds(index * width, width)
        row = at_edges(pre[:, at].astype(F32), index + 1, columns)
        pre_out[:, at] = row.astype(BF16)
        first = row if index == 0 else first
        last = row
    row_sends(first, last, inner_out, outer_out)
    for copy in leaving:
        copy.wait()


def pair_kernel(place, keep, bias, received, *outs):
    sends, keep_out, scratch = outs[:-2], outs[-2], outs[-1]
    chunk = place.chunk
    rank = place.plane_rank()
    scratch[...] = keep[...] + received[...].astype(F32)
    block = encode(bias[...]).astype(BF16)
    for step, send in zip(range(place.plane - 1, 0, -1), sends):
        send[0:BIAS_ROWS, :] = block
        at = pl.ds(pl.multiple_of((rank ^ step) * chunk, 8), chunk)
        send[BIAS_ROWS:, :] = scratch[at, :].astype(BF16)
    keep_out[...] = scratch[pl.ds(pl.multiple_of(rank * chunk, 8), chunk), :]


def plane_kernel(keep, bias, *refs):
    received, out = refs[:-2], refs[-1]
    total, bias_total = keep[...], bias[...]
    for ref in received:
        total += ref[BIAS_ROWS:, :].astype(F32)
        bias_total += decode(ref[0:BIAS_ROWS, :].astype(F32))
    out[0:BIAS_ROWS, :] = encode(bias_total).astype(BF16)
    out[BIAS_ROWS:, :] = total.astype(BF16)


def join_kernel(*refs):
    blocks, out = refs[:-2], refs[-1]
    for index, block in enumerate(blocks):
        out[index] = block[...]


def add_kernel(scale, own, received, out):
    here, there = own[...].astype(F32), received[...].astype(F32)
    bias = (decode(here[0:BIAS_ROWS]) + decode(there[0:BIAS_ROWS])) * scale
    out[0:BIAS_ROWS, :] = encode(bias).astype(BF16)
    out[BIAS_ROWS:, :] = ((here[BIAS_ROWS:] + there[BIAS_ROWS:]) * scale).astype(BF16)


def store_half(place, half, blocks, out, wide, left):
    chunk, half_gates = place.chunk, place.half_gates
    gates = pl.ds(pl.multiple_of(half * half_gates, half_gates), half_gates)
    rank = place.plane_rank()
    for step, block in enumerate(blocks):
        at = pl.ds(pl.multiple_of((rank ^ step) * chunk, 8), chunk)
        wide[at, :] = block[BIAS_ROWS:, :].astype(F32)
    copies = []
    for tap in range(place.taps):
        source = wide.at[tap * half_gates : (tap + 1) * half_gates, :]
        copies.append(pltpu.make_async_copy(source, out.at[tap, gates, :], left.at[tap]))
        copies[-1].start()
    return copies


def in_steps(place, early, late):
    return [early.at[0], late] + [early.at[index] for index in range(1, place.plane - 1)]


def own_half_kernel(place, late, early, out, bias_out, wide, left):
    blocks = in_steps(place, early, late)
    copies = store_half(place, place.rank(0), blocks, out, wide, left)
    rank = place.plane_rank()
    bias = decode(blocks[0][0:BIAS_ROWS, :].astype(F32))
    for step in range(1, place.plane):
        bias = pick(rank == step, decode(blocks[step][0:BIAS_ROWS, :].astype(F32)), bias)
    bias_out[...] = bias
    for copy in copies:
        copy.wait()


def other_half_kernel(
    place, bias_own, early, late, after, out_before, out, bias_out, wide, bias_here, left
):
    del after, out_before
    blocks = in_steps(place, early, late)
    copies = store_half(place, 1 - place.rank(0), blocks, out, wide, left)
    rank = place.plane_rank()
    bias = decode(blocks[0][0:BIAS_ROWS, :].astype(F32))
    for step in range(1, place.plane):
        bias = pick(rank == step, decode(blocks[step][0:BIAS_ROWS, :].astype(F32)), bias)
    bias += bias_own[...]
    width = bias.shape[1]
    for index in range(bias_here.shape[0] // width):
        bias_here[pl.ds(index * width, width)] = bias[index]
    bias_copy = pltpu.make_async_copy(bias_here, bias_out, left.at[place.taps])
    bias_copy.start()
    bias_copy.wait()
    for copy in copies:
        copy.wait()


def field_kernel(pre, weights, wide_out, turned_out, done_out, shifted):
    done_out[...] = jnp.zeros(done_out.shape, F32)
    gate_count, cells = pre.shape
    channels, width = weights.shape[2], wide_out.shape[1]
    row_count = cells // width
    lane = lanes((gate_count, width))
    for index in range(row_count):
        at = pl.ds(index * width, width)
        row = pre[:, at].astype(F32)
        left = jnp.where(lane == 0, 0.0, rolled(row, 1))
        right = jnp.where(lane == width - 1, 0.0, rolled(row, -1))
        shifted[0:gate_count, at] = right.astype(BF16)
        shifted[gate_count : 2 * gate_count, at] = pre[:, at]
        shifted[2 * gate_count : 3 * gate_count, at] = left.astype(BF16)
    for a in range(3):
        for b in range(3):
            turned_out[a, :, b * gate_count : (b + 1) * gate_count] = weights[3 * a + b].T

    def product(a, index, count):
        return jnp.dot(
            turned_out[a],
            shifted[:, pl.ds(index * width, count * width)],
            preferred_element_type=F32,
        )

    pair = 2 if row_count % 2 == 0 else 1
    for base in range(0, row_count, pair):
        total = product(1, base, pair)
        for a, first in ((2, base - 1), (0, base + 1)):
            low, high = max(first, 0), min(first + pair, row_count)
            if low >= high:
                continue
            part = product(a, low, high - low)
            blank = jnp.zeros((channels, width), F32)
            parts = [blank] * (low - first) + [part] + [blank] * (first + pair - high)
            total += jnp.concatenate(parts, axis=1)
        for offset in range(pair):
            value = total[:, offset * width : (offset + 1) * width]
            wide_out[pl.ds(base + offset, channels, stride=row_count), :] = value


def field_halo_kernel(
    place,
    wide,
    turned,
    outer_row,
    inner_row,
    outer_column,
    inner_column,
    inputs_out,
    hidden_out,
    done_out,
    total,
):
    done_out[...] = jnp.zeros(done_out.shape, F32)
    hid, row_count, width = hidden_out.shape
    channels = turned.shape[1]
    gate_count = turned.shape[2] // 3
    north, south = row_halo(inner_row, outer_row)
    west, east = column_halo(inner_column, outer_column, PRE_GROUPS)
    lane = lanes((gate_count, width))
    lat = place.position()[0]

    def row_part(taps, row, position):
        left = jnp.where(lane == 0, rolled(west, -LAST - position), rolled(row, 1))
        right = rolled(east, width - 1 - position)
        right = jnp.where(lane == width - 1, right, rolled(row, -1))
        stack = jnp.concatenate([right, row, left], axis=0).astype(BF16)
        return jnp.dot(taps, stack, preferred_element_type=F32)

    above = row_part(turned[jnp.where(lat == 0, 0, 2)], north, 0)
    below = row_part(turned[jnp.where(lat == place.lat - 1, 2, 0)], south, row_count + 1)

    inside = (lane >= 1) & (lane <= row_count)
    west = jnp.where(inside, rolled(west, -LAST), 0.0)
    east = jnp.where(inside, east, 0.0)
    sides = [rolled(west, a - 1) for a in range(3)] + [rolled(east, LAST + a - 1) for a in range(3)]
    taps = [turned[a, :, 2 * gate_count : 3 * gate_count] for a in range(3)]
    taps += [turned[a, :, 0:gate_count] for a in range(3)]
    columns = jnp.dot(
        jnp.concatenate(taps, axis=1),
        jnp.concatenate(sides, axis=0).astype(BF16),
        preferred_element_type=F32,
    )
    blank = jnp.zeros((channels, width), F32)
    for index in range(row_count):
        strided = pl.ds(index, channels, stride=row_count)
        value = wide[strided, :] + at_edges(blank, index + 1, columns)
        if index == 0:
            value += above
        if index == row_count - 1:
            value += below
        total[strided, :] = value
    size = (channels - hid) * row_count
    inputs_out[...] = total[0:size, :].reshape(inputs_out.shape).astype(BF16)
    hidden_out[...] = total[size:, :].reshape(hidden_out.shape).astype(BF16)


def body(
    place,
    inputs_below,
    hidden_prev,
    cell_prev,
    kernel_weights,
    gate_bias,
    readout,
    target_field,
    land_mask,
    fire_mask,
    hidden_grad,
):
    hid, row_count, width = hidden_prev.shape
    gate_count, channels = kernel_weights.shape[1:]
    cells = row_count * width
    halo_cells = (row_count + 2) * width
    scaling = 1.0 / math.sqrt(cells * place.lat * place.lon)
    bind = functools.partial
    inner_rows, outer_rows = place.pairs(place.inner_rows), place.pairs(place.outer_rows)
    inner_columns = place.pairs(place.inner_columns)
    outer_columns = place.pairs(place.outer_columns)
    flat = sds((hid * row_count, width), F32)
    strip = sds((hid, width), F32)

    inner, outer, wide = call(
        pack_kernel,
        (
            sds((channels, width), BF16),
            sds((channels, width), BF16),
            sds((channels * row_count, width), F32),
        ),
        [
            pltpu.VMEM(inputs_below.shape, BF16),
            pltpu.VMEM(hidden_prev.shape, BF16),
            pltpu.SemaphoreType.DMA((2,)),
        ],
        remote=2,
        moved=4 * channels * cells,
    )(inputs_below, hidden_prev)
    inner, outer = permuted(inner, inner_rows), permuted(outer, outer_rows)
    (
        rows,
        columns,
        second,
        cell_strip,
        hidden_grad_strip,
        fields_strip,
        cell_here,
        weights_here,
        hidden_grad_here,
        target_here,
        land_here,
        fire_here,
        bias_wide,
        readout_wide,
    ) = call(
        prepare_kernel,
        (
            sds((row_count, channels, width), BF16),
            sds((channels, width), F32),
            sds((channels, width), F32),
            strip,
            strip,
            sds((8, width), F32),
            flat,
            sds(kernel_weights.shape, BF16),
            flat,
            sds(target_field.shape, F32),
            sds(land_mask.shape, jnp.int32),
            sds(fire_mask.shape, jnp.int32),
            sds((gate_count, width), F32),
            sds((hid, width), F32),
        ),
        [
            pltpu.VMEM(hidden_grad.shape, BF16),
            pltpu.VMEM(gate_bias.shape, F32),
            pltpu.VMEM(readout.shape, F32),
            pltpu.SemaphoreType.DMA((8,)),
        ],
        remote=8,
        moved=6_000_000,
    )(
        wide,
        cell_prev.reshape(hid * row_count, width),
        kernel_weights,
        hidden_grad,
        target_field,
        land_mask,
        fire_mask,
        gate_bias,
        readout,
    )
    columns, edge = call(
        bind(columns_kernel, row_count, GROUPS),
        (sds((channels // GROUPS, width), BF16), sds((channels, width), BF16)),
    )(columns, outer, inner)
    inner_column = permuted(columns, inner_columns)
    outer_column = permuted(columns, outer_columns)
    hidden_rows, cell_rows, grad_cell_rows, pre, second, sums, bias = call(
        bind(gates_kernel, place),
        (
            flat,
            flat,
            flat,
            sds((gate_count, cells), BF16),
            sds((channels, width), BF16),
            sds((2 * place.half_rows, channels), F32),
            sds((gate_count, width), F32),
        ),
        [pltpu.VMEM((3 * channels, halo_cells), BF16)],
        flops=4 * 9 * gate_count * channels * cells,
        moved=6_000_000,
        transcendentals=5 * hid * cells,
    )(
        rows,
        inner,
        outer,
        second,
        cell_here,
        weights_here,
        hidden_grad_here,
        target_here,
        land_here,
        fire_here,
        bias_wide,
        readout_wide,
    )
    send, pre_strip, pre_wide, patches, *strips = call(
        bind(strip_kernel, place, row_count),
        (
            sds((place.half_rows, channels), BF16),
            sds((gate_count, width), BF16),
            sds((gate_count, width), F32),
            sds((place.taps * channels, width), BF16),
            strip,
            strip,
            strip,
        ),
    )(
        edge,
        second,
        outer_column,
        inner_column,
        weights_here,
        bias_wide,
        readout_wide,
        cell_strip,
        hidden_grad_strip,
        fields_strip,
        sums,
    )
    keep, bias = call(
        bind(keep_kernel, place),
        (sds((place.half_rows, channels), F32), sds((8, channels), F32)),
    )(sums, pre_strip, patches, bias, pre_wide)
    hidden_next, cell_next, grad_cell, pre, pre_inner, pre_outer = call(
        bind(edges_kernel, row_count),
        (
            sds((hid, row_count, width), BF16),
            flat,
            flat,
            sds((gate_count, cells), BF16),
            sds((gate_count, width), BF16),
            sds((gate_count, width), BF16),
        ),
        [
            pltpu.VMEM((hid, row_count, width), BF16),
            pltpu.VMEM(flat.shape, F32),
            pltpu.VMEM(flat.shape, F32),
            pltpu.VMEM(flat.shape, F32),
            pltpu.SemaphoreType.DMA((3,)),
        ],
        leaving=3,
        moved=4_000_000,
    )(hidden_rows, cell_rows, grad_cell_rows, pre, *strips, pre_strip)
    pre_inner, pre_outer = permuted(pre_inner, inner_rows), permuted(pre_outer, outer_rows)
    pre_columns = call(
        bind(columns_kernel, row_count, PRE_GROUPS),
        (sds((gate_count // PRE_GROUPS, width), BF16),),
    )(pre_strip, pre_outer, pre_inner)[0]

    block = sds((BIAS_ROWS + place.chunk, channels), BF16)
    token = sds((8, width), F32)
    steps = range(place.plane - 1, 0, -1)
    *sends, keep = call(
        bind(pair_kernel, place),
        (*[block for _ in steps], sds((place.chunk, channels), F32)),
        [pltpu.VMEM((place.half_rows, channels), F32)],
    )(keep, bias, permuted(send, place.phase_pairs(0)))
    received = [permuted(send, place.plane_pairs(step)) for step, send in zip(steps, sends)]
    field, turned, field_done = call(
        field_kernel,
        (
            sds((channels * row_count, width), F32),
            sds((3, channels, 3 * gate_count), BF16),
            token,
        ),
        [pltpu.VMEM((3 * gate_count, cells), BF16)],
        flops=2 * 9 * gate_count * channels * cells,
        moved=3_000_000,
    )(pre, weights_here)
    part = call(plane_kernel, block)(keep, bias, *received, field_done)
    pre_inner_columns = permuted(pre_columns, inner_columns)
    pre_outer_columns = permuted(pre_columns, outer_columns)
    phases = len(place.orders[0])
    for phase in range(1, phases):
        is_last = phase == phases - 1
        part = call(bind(add_kernel, scaling if is_last else 1.0), block)(
            part, permuted(part, place.phase_pairs(phase))
        )
    received = [permuted(part, place.plane_pairs(step)) for step in steps[::-1]]
    grad_inputs, grad_hidden, field_done = call(
        bind(field_halo_kernel, place),
        (
            sds((channels - hid, row_count, width), BF16),
            sds((hid, row_count, width), BF16),
            token,
        ),
        [pltpu.VMEM((channels * row_count, width), F32)],
        flops=40 * gate_count * channels * cells * 9,
        moved=2_000_000,
    )(field, turned, pre_outer, pre_inner, pre_outer_columns, pre_inner_columns)
    early = call(join_kernel, sds((place.plane - 1, *block.shape), BF16))(
        part, *received[1:], field_done
    )
    late = received[0]
    early_other = permuted(early, place.phase_pairs(0))
    late_other = permuted(late, place.phase_pairs(0))
    half = [pltpu.VMEM((place.half_rows, channels), F32)]
    grad_kernel, bias = call(
        bind(own_half_kernel, place),
        (sds(kernel_weights.shape, F32), sds((8, channels), F32)),
        half + [pltpu.SemaphoreType.DMA((place.taps,))],
        leaving=1,
        flops=40 * gate_count * channels * cells * 9,
        moved=6 * place.half_rows * channels,
    )(late, early)
    grad_kernel, grad_bias = call(
        bind(other_half_kernel, place),
        (sds(kernel_weights.shape, F32), sds((gate_count,), F32)),
        half + [pltpu.VMEM((gate_count,), F32), pltpu.SemaphoreType.DMA((place.taps + 1,))],
        remote=1,
        leaving=2,
        aliases={4: 0},
        moved=6 * place.half_rows * channels,
    )(bias, early_other, late_other, target_here, grad_kernel)
    shape = hidden_prev.shape
    return (
        hidden_next,
        cell_next.reshape(shape),
        grad_inputs,
        grad_hidden,
        grad_cell.reshape(shape),
        grad_kernel,
        grad_bias,
    )


def solution(mesh):
    lat_count, lon_count = mesh.shape["lat"], mesh.shape["lon"]
    split = Mesh(mesh.devices.reshape(lat_count // 2, 2, lon_count // 2, 2), AXES)
    field = P(None, ("band", "core"), ("reach", "near"))
    flat = P(("band", "core"), ("reach", "near"))

    def run(*args):
        place = Layout(lat_count, lon_count, *args[3].shape[:2])
        return jax.shard_map(
            functools.partial(body, place),
            mesh=split,
            in_specs=(field, field, field, P(), P(), P(), flat, flat, flat, field),
            out_specs=(field, field, field, field, field, P(), P()),
            check_vma=False,
        )(*args)

    return run
```

```python
import functools
import math

import jax
import jax.numpy as jnp
from jax import lax
from jax.experimental import pallas as pl
from jax.experimental.pallas import tpu as pltpu
from jax.sharding import Mesh, PartitionSpec as P

F32 = jnp.float32
BF16 = jnp.bfloat16
AXES = ("band", "core", "reach", "near")
BIAS_ROWS = 16
GROUPS = 4
PRE_GROUPS = 4
LAST = 16
VMEM = pl.BlockSpec(memory_space=pltpu.VMEM)
HBM = pl.BlockSpec(memory_space=pltpu.HBM)
ACROSS = (((1,), (1,)), ((), ()))


def sds(shape, dtype):
    return jax.ShapeDtypeStruct(shape, dtype)


def call(
    kernel,
    out_shape,
    scratch=(),
    remote=0,
    leaving=0,
    aliases=None,
    flops=0,
    moved=0,
    transcendentals=0,
):
    several = isinstance(out_shape, tuple)
    shapes = out_shape if several else (out_shape,)
    out_specs = tuple([HBM] * leaving + [VMEM] * (len(shapes) - leaving))

    def run(*args):
        near = len(args) - remote
        far = [pltpu.with_memory_space_constraint(arg, pltpu.HBM) for arg in args[near:]]
        return pl.pallas_call(
            kernel,
            out_shape=out_shape,
            in_specs=[VMEM] * near + [HBM] * remote,
            out_specs=out_specs if several else out_specs[0],
            input_output_aliases=aliases or {},
            scratch_shapes=list(scratch),
            cost_estimate=pl.CostEstimate(
                flops=flops, bytes_accessed=moved, transcendentals=transcendentals
            ),
            compiler_params=pltpu.CompilerParams(vmem_limit_bytes=24 * 1024 * 1024),
        )(*args[:near], *far)

    return run


class Layout:
    def __init__(self, lat_count, lon_count, taps, gate_count):
        self.lat, self.lon = lat_count, lon_count
        self.half = lon_count // 2
        self.taps, self.half_gates = taps, gate_count // 2
        self.plane = lat_count
        whole = [("lon", 1 << k) for k in range(1, lon_count.bit_length() - 1)]
        self.orders = ([("lat", 1)] + whole, [("lat", 1)] + whole[::-1])
        step = 8 * self.plane
        self.half_rows = -(-taps * self.half_gates // step) * step
        self.chunk = self.half_rows // self.plane

    def position(self):
        lat = 2 * lax.axis_index("band") + lax.axis_index("core")
        return lat, 2 * lax.axis_index("reach") + lax.axis_index("near")

    def rank(self, phase):
        lat, lon = self.position()

        def digit(order):
            axis, bit = order[phase]
            return ((lat if axis == "lat" else lon) // bit) % 2

        return jnp.where(lat % 2 == 0, digit(self.orders[0]), digit(self.orders[1]))

    def pairs(self, partner):
        result = []
        for lat in range(self.lat):
            for lon in range(self.lon):
                there = partner(lat, lon)
                result.append((lat * self.lon + lon, there[0] * self.lon + there[1]))
        return result

    def phase_pairs(self, phase):
        def partner(lat, lon):
            axis, bit = self.orders[lat % 2][phase]
            return (lat ^ bit, lon) if axis == "lat" else (lat, lon ^ bit)

        return self.pairs(partner)

    def plane_rank(self):
        return 2 * lax.axis_index("band") + lax.axis_index("near")

    def plane_pairs(self, step):
        def partner(lat, lon):
            there = (lat // 2 * 2 + lon % 2) ^ step
            return there // 2 * 2 + lat % 2, lon // 2 * 2 + there % 2

        return self.pairs(partner)

    def inner_rows(self, lat, lon):
        return lat ^ 1, lon

    def outer_rows(self, lat, lon):
        there = lat + 1 if lat % 2 else lat - 1
        if 0 <= there < self.lat:
            return there, lon
        return lat, (lon + self.half) % self.lon

    def inner_columns(self, lat, lon):
        return lat, lon ^ 1

    def outer_columns(self, lat, lon):
        return lat, (lon + (1 if lon % 2 else -1)) % self.lon


def permuted(value, pairs):
    return lax.ppermute(value, AXES, pairs)


def lanes(shape):
    return lax.broadcasted_iota(jnp.int32, shape, len(shape) - 1)


def rolled(value, shift):
    shift %= value.shape[1]
    return pltpu.roll(value, shift, 1) if shift else value


def edge_columns(row, position, columns):
    lane = lanes(row.shape)
    columns = jnp.where(lane == position, rolled(row, position), columns)
    return jnp.where(lane == LAST + position, rolled(row, LAST + position + 1), columns)


def second_columns(row, position, columns):
    lane = lanes(row.shape)
    columns = jnp.where(lane == position, rolled(row, position - 1), columns)
    return jnp.where(lane == LAST + position, rolled(row, LAST + position + 2), columns)


def at_edges(row, position, columns):
    lane = lanes(row.shape)
    width = row.shape[1]
    row = jnp.where(lane == 0, rolled(columns, -position), row)
    return jnp.where(lane == width - 1, rolled(columns, width - 1 - LAST - position), row)


def pick(flag, yes, no):
    return jnp.where(flag, yes, no)


def is_odd(axis):
    return lax.axis_index(axis) % 2 == 1


def row_sends(first, last, inner_out, outer_out):
    odd = is_odd("core")
    inner_out[...] = pick(odd, first, last).astype(BF16)
    outer_out[...] = pick(odd, last, first).astype(BF16)


def row_halo(inner, outer):
    odd = is_odd("core")
    inner, outer = inner[...].astype(F32), outer[...].astype(F32)
    return pick(odd, inner, outer), pick(odd, outer, inner)


def packed(columns, groups):
    count, width = columns.shape[0] // groups, columns.shape[1] // groups
    lane = lanes((count, columns.shape[1]))
    value = columns[0:count]
    for group in range(1, groups):
        part = rolled(columns[group * count : (group + 1) * count], group * width)
        value = jnp.where(lane >= group * width, part, value)
    return value


def unpacked(value, groups):
    width = value.shape[1] // groups
    return jnp.concatenate([rolled(value, -group * width) for group in range(groups)], axis=0)


def column_halo(inner, outer, groups):
    odd = is_odd("near")
    inner, outer = inner[...].astype(F32), outer[...].astype(F32)
    return unpacked(pick(odd, inner, outer), groups), unpacked(pick(odd, outer, inner), groups)


def pack_kernel(below, hidden, inner_out, outer_out, wide_out, below_here, hidden_here, arrived):
    first = pltpu.make_async_copy(below, below_here, arrived.at[0])
    second = pltpu.make_async_copy(hidden, hidden_here, arrived.at[1])
    first.start()
    second.start()
    channels, row_count, width = below.shape
    size = channels * row_count
    first.wait()
    wide_out[0:size, :] = below_here[...].astype(F32).reshape(size, width)
    second.wait()
    wide_out[size : 2 * size, :] = hidden_here[...].astype(F32).reshape(size, width)
    edges = [
        wide_out[pl.ds(index, 2 * channels, stride=row_count), :] for index in (0, row_count - 1)
    ]
    row_sends(edges[0], edges[1], inner_out, outer_out)


def down_rows(values, width):
    count = values.shape[0]
    return jnp.broadcast_to(values[None, :], (width, count)).T


def prepare_kernel(
    wide,
    cell_hbm,
    weights_hbm,
    hidden_grad_hbm,
    target_hbm,
    land_hbm,
    fire_hbm,
    gate_bias_hbm,
    readout_hbm,
    rows_out,
    columns_out,
    second_out,
    cell_strip_out,
    hidden_grad_strip_out,
    fields_strip_out,
    cell_out,
    weights_out,
    hidden_grad_out,
    target_out,
    land_out,
    fire_out,
    bias_wide_out,
    readout_wide_out,
    hidden_grad_here,
    gate_bias_here,
    readout_here,
    arrived,
):
    copies = [
        pltpu.make_async_copy(source, target, arrived.at[index])
        for index, (source, target) in enumerate(
            (
                (cell_hbm, cell_out),
                (weights_hbm, weights_out),
                (hidden_grad_hbm, hidden_grad_here),
                (target_hbm, target_out),
                (land_hbm, land_out),
                (fire_hbm, fire_out),
                (gate_bias_hbm, gate_bias_here),
                (readout_hbm, readout_here),
            )
        )
    ]
    for copy in copies:
        copy.start()
    row_count, channels, width = rows_out.shape
    columns = jnp.zeros((channels, width), F32)
    second = jnp.zeros((channels, width), F32)
    for index in range(row_count):
        row = wide[pl.ds(index, channels, stride=row_count), :]
        rows_out[index] = row.astype(BF16)
        columns = edge_columns(row, index + 1, columns)
        second = second_columns(row, index + 1, second)
    columns_out[...] = columns
    second_out[...] = second
    for copy in copies:
        copy.wait()
    hidden_grad_out[...] = hidden_grad_here[...].astype(F32).reshape(hidden_grad_out.shape)
    bias_wide_out[...] = down_rows(gate_bias_here[...], width)
    readout_wide_out[...] = down_rows(readout_here[...], width)
    hid = hidden_grad_here.shape[0]
    cell_strip = jnp.zeros((hid, width), F32)
    hidden_grad_strip = jnp.zeros((hid, width), F32)
    fields_strip = jnp.zeros((8, width), F32)
    for index in range(row_count):
        strided = pl.ds(index, hid, stride=row_count)
        cell_strip = edge_columns(cell_out[strided, :], index + 1, cell_strip)
        hidden_grad_strip = edge_columns(hidden_grad_out[strided, :], index + 1, hidden_grad_strip)
        at = slice(index, index + 1)
        fields = [target_out[at, :], land_out[at, :].astype(F32), fire_out[at, :].astype(F32)]
        fields = jnp.concatenate(fields + [jnp.zeros((5, width), F32)], axis=0)
        fields_strip = edge_columns(fields, index + 1, fields_strip)
    cell_strip_out[...] = cell_strip
    hidden_grad_strip_out[...] = hidden_grad_strip
    fields_strip_out[...] = fields_strip


def columns_kernel(row_count, groups, columns, outer, inner, packed_out, *whole_out):
    north, south = row_halo(inner, outer)
    value = edge_columns(north, 0, columns[...].astype(F32))
    value = edge_columns(south, row_count + 1, value)
    packed_out[...] = packed(value, groups).astype(BF16)
    for out in whole_out:
        out[...] = value.astype(BF16)


def encode(bias):
    high = bias.astype(BF16).astype(F32)
    return jnp.concatenate([high, bias - high], axis=0)


def decode(block):
    return block[0:8] + block[8:16]


def cell_step(part, cell_before, hidden_grad, target, land, fire, readout):
    hid = part.shape[0] // 4
    input_gate = 0.5 + 0.5 * jnp.tanh(0.5 * part[0:hid])
    forget_gate = 0.5 + 0.5 * jnp.tanh(0.5 * part[hid : 2 * hid])
    output_gate = 0.5 + 0.5 * jnp.tanh(0.5 * part[2 * hid : 3 * hid])
    candidate = jnp.tanh(part[3 * hid : 4 * hid])
    cell_next = land * (forget_gate * cell_before + input_gate * candidate)
    squashed = jnp.tanh(cell_next)
    hidden_next = (output_gate * squashed).astype(BF16).astype(F32)
    predicted = jnp.sum(readout * hidden_next, axis=0, keepdims=True)
    total_grad = hidden_grad + 2.0 * (fire * (predicted - target)) * readout
    cell_grad = land * total_grad * output_gate * (1.0 - squashed * squashed)
    pre_grad = jnp.concatenate(
        [
            cell_grad * candidate * input_gate * (1.0 - input_gate),
            cell_grad * cell_before * forget_gate * (1.0 - forget_gate),
            total_grad * squashed * output_gate * (1.0 - output_gate),
            cell_grad * input_gate * (1.0 - candidate * candidate),
        ],
        axis=0,
    )
    return hidden_next, cell_next, cell_grad * forget_gate, pre_grad


def gates_kernel(
    place,
    rows_in,
    inner_row,
    outer_row,
    second,
    cell_prev,
    weights,
    hidden_grad,
    target,
    land,
    fire,
    bias_wide,
    readout_wide,
    hidden_out,
    cell_out,
    grad_cell_out,
    pre_out,
    second_out,
    sums,
    bias_out,
    shifted,
):
    row_count, channels, width = rows_in.shape
    gate_count = weights.shape[1]
    hid = gate_count // 4
    half_gates = place.half_gates
    north, south = row_halo(inner_row, outer_row)
    columns = second_columns(north, 0, second[...])
    second_out[...] = second_columns(south, row_count + 1, columns).astype(BF16)
    for position in range(row_count + 2):
        if position == 0:
            row = north
        elif position == row_count + 1:
            row = south
        else:
            row = rows_in[position - 1].astype(F32)
        at = pl.ds(position * width, width)
        shifted[0:channels, at] = rolled(row, 1).astype(BF16)
        shifted[channels : 2 * channels, at] = row.astype(BF16)
        shifted[2 * channels : 3 * channels, at] = rolled(row, -1).astype(BF16)

    taps = [
        jnp.concatenate([weights[3 * a], weights[3 * a + 1], weights[3 * a + 2]], axis=1)
        for a in range(3)
    ]
    bias_total = jnp.zeros((gate_count, width), F32)
    lane = lanes((gate_count, width))
    inside = (lane > 0) & (lane < width - 1)
    readout = readout_wide[...]
    pair = 2 if row_count % 2 == 0 else 1
    for base in range(0, row_count, pair):
        preact = jnp.zeros((gate_count, pair * width), F32)
        for a in range(3):
            preact += jnp.dot(
                taps[a],
                shifted[:, pl.ds((base + a) * width, pair * width)],
                preferred_element_type=F32,
            )
        for offset in range(pair):
            index = base + offset
            strided = pl.ds(index, hid, stride=row_count)
            at = slice(index, index + 1)
            hidden_next, cell_next, grad_cell, pre_grad = cell_step(
                preact[:, offset * width : (offset + 1) * width] + bias_wide[...],
                cell_prev[strided, :],
                hidden_grad[strided, :],
                target[at, :],
                land[at, :].astype(F32),
                fire[at, :].astype(F32),
                readout,
            )
            hidden_out[strided, :] = hidden_next
            cell_out[strided, :] = cell_next
            grad_cell_out[strided, :] = grad_cell
            pre_grad = jnp.where(inside, pre_grad, 0.0)
            bias_total += pre_grad
            pre_out[:, pl.ds(index * width, width)] = pre_grad.astype(BF16)
    bias_out[...] = bias_total

    for a in range(3):
        product = lax.dot_general(
            pre_out[...],
            shifted[:, pl.ds(a * width, row_count * width)],
            ACROSS,
            preferred_element_type=F32,
        )
        for b in range(3):
            for half in range(2):
                at = half * place.half_rows + (3 * a + b) * half_gates
                sums[at : at + half_gates, :] = product[
                    half * half_gates : (half + 1) * half_gates, b * channels : (b + 1) * channels
                ]
    used = place.taps * half_gates
    if place.half_rows > used:
        for half in range(2):
            at = half * place.half_rows
            sums[at + used : at + place.half_rows, :] = jnp.zeros(
                (place.half_rows - used, channels), F32
            )


def add_strip(place, half, sums, pre_strip, patches, out):
    half_gates, channels = place.half_gates, sums.shape[1]
    gates = pre_strip[pl.ds(pl.multiple_of(half * half_gates, half_gates), half_gates), :]
    product = lax.dot_general(gates, patches[...], ACROSS, preferred_element_type=F32)
    base = half * place.half_rows
    for tap in range(place.taps):
        at = pl.ds(pl.multiple_of(base + tap * half_gates, 8), half_gates)
        value = sums[at, :] + product[:, tap * channels : (tap + 1) * channels]
        out[tap * half_gates : (tap + 1) * half_gates, :] = value.astype(out.dtype)
    used = place.taps * half_gates
    if place.half_rows > used:
        rest = jnp.zeros((place.half_rows - used, channels), out.dtype)
        out[used:, :] = rest


def strip_kernel(
    place,
    row_count,
    edge,
    second,
    outer_column,
    inner_column,
    weights,
    bias_wide,
    readout_wide,
    cell_strip,
    hidden_grad_strip,
    fields_strip,
    sums,
    send_out,
    pre_out,
    pre_wide_out,
    patches,
    hidden_out,
    cell_out,
    grad_cell_out,
):
    channels, width = edge.shape
    west, east = column_halo(inner_column, outer_column, GROUPS)
    near_first = lanes((channels, width)) < LAST
    inner = second[...].astype(F32)
    columns = (
        jnp.where(near_first, rolled(west, -LAST), inner),
        edge[...].astype(F32),
        jnp.where(near_first, inner, rolled(east, LAST)),
    )
    for a in range(3):
        for b in range(3):
            at = (3 * a + b) * channels
            patches[at : at + channels, :] = rolled(columns[b], 1 - a).astype(BF16)
    taps = jnp.concatenate([weights[tap] for tap in range(place.taps)], axis=1)
    preact = jnp.dot(taps, patches[...], preferred_element_type=F32) + bias_wide[...]
    hidden_next, cell_next, grad_cell, pre_grad = cell_step(
        preact,
        cell_strip[...],
        hidden_grad_strip[...],
        fields_strip[0:1, :],
        fields_strip[1:2, :],
        fields_strip[2:3, :],
        readout_wide[...],
    )
    hidden_out[...] = hidden_next
    cell_out[...] = cell_next
    grad_cell_out[...] = grad_cell
    lane = lanes(pre_grad.shape)
    lane = jnp.where(lane >= LAST, lane - LAST, lane)
    pre_grad = jnp.where((lane >= 1) & (lane <= row_count), pre_grad, 0.0)
    pre_out[...] = pre_grad.astype(BF16)
    pre_wide_out[...] = pre_grad
    add_strip(place, 1 - place.rank(0), sums, pre_out, patches, send_out)


def keep_kernel(place, sums, pre_strip, patches, bias_partial, pre_wide, out, bias_out):
    add_strip(place, place.rank(0), sums, pre_strip, patches, out)
    channels = sums.shape[1]
    bias_total = bias_partial[...] + pre_wide[...]
    ones = jnp.ones((8, bias_total.shape[1]), BF16)
    high = bias_total.astype(BF16)
    low = (bias_total - high.astype(F32)).astype(BF16)
    flat = lax.dot_general(ones, high, ACROSS, preferred_element_type=F32)
    flat += lax.dot_general(ones, low, ACROSS, preferred_element_type=F32)
    odd = lax.broadcasted_iota(jnp.int32, (8, channels), 0) % 2 == 1
    bias_out[...] = jnp.where(odd, flat[:, channels : 2 * channels], flat[:, 0:channels])


def edges_kernel(
    row_count,
    hidden,
    cell,
    grad_cell,
    pre,
    hidden_strip,
    cell_strip,
    grad_cell_strip,
    pre_strip,
    hidden_hbm,
    cell_hbm,
    grad_cell_hbm,
    pre_out,
    inner_out,
    outer_out,
    hidden_low,
    hidden_here,
    cell_here,
    grad_cell_here,
    left,
):
    hid, _, width = hidden_low.shape
    leaving = []
    for source, strip, here, ready, target in (
        (cell, cell_strip, cell_here, cell_here, cell_hbm),
        (grad_cell, grad_cell_strip, grad_cell_here, grad_cell_here, grad_cell_hbm),
        (hidden, hidden_strip, hidden_here, hidden_low, hidden_hbm),
    ):
        columns = strip[...]
        for index in range(row_count):
            strided = pl.ds(index, hid, stride=row_count)
            here[strided, :] = at_edges(source[strided, :], index + 1, columns)
        if ready is hidden_low:
            hidden_low[...] = here[...].reshape(hidden_low.shape).astype(BF16)
        leaving.append(pltpu.make_async_copy(ready, target, left.at[len(leaving)]))
        leaving[-1].start()
    first, last = None, None
    columns = pre_strip[...].astype(F32)
    for index in range(row_count):
        at = pl.ds(index * width, width)
        row = at_edges(pre[:, at].astype(F32), index + 1, columns)
        pre_out[:, at] = row.astype(BF16)
        first = row if index == 0 else first
        last = row
    row_sends(first, last, inner_out, outer_out)
    for copy in leaving:
        copy.wait()


def pair_kernel(place, keep, bias, received, *outs):
    sends, keep_out, scratch = outs[:-2], outs[-2], outs[-1]
    chunk = place.chunk
    rank = place.plane_rank()
    scratch[...] = keep[...] + received[...].astype(F32)
    block = encode(bias[...]).astype(BF16)
    for step, send in zip([*range(2, place.plane), 1], sends):
        send[0:BIAS_ROWS, :] = block
        at = pl.ds(pl.multiple_of((rank ^ step) * chunk, 8), chunk)
        send[BIAS_ROWS:, :] = scratch[at, :].astype(BF16)
    keep_out[...] = scratch[pl.ds(pl.multiple_of(rank * chunk, 8), chunk), :]


def plane_kernel(keep, bias, *refs):
    received, out = refs[:-2], refs[-1]
    total, bias_total = keep[...], bias[...]
    for ref in received:
        total += ref[BIAS_ROWS:, :].astype(F32)
        bias_total += decode(ref[0:BIAS_ROWS, :].astype(F32))
    out[0:BIAS_ROWS, :] = encode(bias_total).astype(BF16)
    out[BIAS_ROWS:, :] = total.astype(BF16)


def join_kernel(*refs):
    blocks, out = refs[:-2], refs[-1]
    for index, block in enumerate(blocks):
        out[index] = block[...]


def add_kernel(scale, own, received, out):
    here, there = own[...].astype(F32), received[...].astype(F32)
    bias = (decode(here[0:BIAS_ROWS]) + decode(there[0:BIAS_ROWS])) * scale
    out[0:BIAS_ROWS, :] = encode(bias).astype(BF16)
    out[BIAS_ROWS:, :] = ((here[BIAS_ROWS:] + there[BIAS_ROWS:]) * scale).astype(BF16)


def store_half(place, half, blocks, out, wide, left):
    chunk, half_gates = place.chunk, place.half_gates
    gates = pl.ds(pl.multiple_of(half * half_gates, half_gates), half_gates)
    rank = place.plane_rank()
    for step, block in enumerate(blocks):
        at = pl.ds(pl.multiple_of((rank ^ step) * chunk, 8), chunk)
        wide[at, :] = block[BIAS_ROWS:, :].astype(F32)
    copies = []
    for tap in range(place.taps):
        source = wide.at[tap * half_gates : (tap + 1) * half_gates, :]
        copies.append(pltpu.make_async_copy(source, out.at[tap, gates, :], left.at[tap]))
        copies[-1].start()
    return copies


def in_steps(place, early, late):
    return [early.at[0], late] + [early.at[index] for index in range(place.plane - 2, 0, -1)]


def own_half_kernel(place, late, early, out, bias_out, wide, left):
    blocks = in_steps(place, early, late)
    copies = store_half(place, place.rank(0), blocks, out, wide, left)
    rank = place.plane_rank()
    bias = decode(blocks[0][0:BIAS_ROWS, :].astype(F32))
    for step in range(1, place.plane):
        bias = pick(rank == step, decode(blocks[step][0:BIAS_ROWS, :].astype(F32)), bias)
    bias_out[...] = bias
    for copy in copies:
        copy.wait()


def other_half_kernel(
    place, bias_own, early, late, after, out_before, out, bias_out, wide, bias_here, left
):
    del after, out_before
    blocks = in_steps(place, early, late)
    copies = store_half(place, 1 - place.rank(0), blocks, out, wide, left)
    rank = place.plane_rank()
    bias = decode(blocks[0][0:BIAS_ROWS, :].astype(F32))
    for step in range(1, place.plane):
        bias = pick(rank == step, decode(blocks[step][0:BIAS_ROWS, :].astype(F32)), bias)
    bias += bias_own[...]
    width = bias.shape[1]
    for index in range(bias_here.shape[0] // width):
        bias_here[pl.ds(index * width, width)] = bias[index]
    bias_copy = pltpu.make_async_copy(bias_here, bias_out, left.at[place.taps])
    bias_copy.start()
    bias_copy.wait()
    for copy in copies:
        copy.wait()


def field_kernel(pre, weights, wide_out, turned_out, done_out, shifted):
    done_out[...] = jnp.zeros(done_out.shape, F32)
    gate_count, cells = pre.shape
    channels, width = weights.shape[2], wide_out.shape[1]
    row_count = cells // width
    lane = lanes((gate_count, width))
    for index in range(row_count):
        at = pl.ds(index * width, width)
        row = pre[:, at].astype(F32)
        left = jnp.where(lane == 0, 0.0, rolled(row, 1))
        right = jnp.where(lane == width - 1, 0.0, rolled(row, -1))
        shifted[0:gate_count, at] = right.astype(BF16)
        shifted[gate_count : 2 * gate_count, at] = pre[:, at]
        shifted[2 * gate_count : 3 * gate_count, at] = left.astype(BF16)
    for a in range(3):
        for b in range(3):
            turned_out[a, :, b * gate_count : (b + 1) * gate_count] = weights[3 * a + b].T

    def product(a, index, count):
        return jnp.dot(
            turned_out[a],
            shifted[:, pl.ds(index * width, count * width)],
            preferred_element_type=F32,
        )

    pair = 2 if row_count % 2 == 0 else 1
    for base in range(0, row_count, pair):
        total = product(1, base, pair)
        for a, first in ((2, base - 1), (0, base + 1)):
            low, high = max(first, 0), min(first + pair, row_count)
            if low >= high:
                continue
            part = product(a, low, high - low)
            blank = jnp.zeros((channels, width), F32)
            parts = [blank] * (low - first) + [part] + [blank] * (first + pair - high)
            total += jnp.concatenate(parts, axis=1)
        for offset in range(pair):
            value = total[:, offset * width : (offset + 1) * width]
            wide_out[pl.ds(base + offset, channels, stride=row_count), :] = value


def field_halo_kernel(
    place,
    wide,
    turned,
    outer_row,
    inner_row,
    outer_column,
    inner_column,
    inputs_out,
    hidden_out,
    done_out,
    total,
):
    done_out[...] = jnp.zeros(done_out.shape, F32)
    hid, row_count, width = hidden_out.shape
    channels = turned.shape[1]
    gate_count = turned.shape[2] // 3
    north, south = row_halo(inner_row, outer_row)
    west, east = column_halo(inner_column, outer_column, PRE_GROUPS)
    lane = lanes((gate_count, width))
    lat = place.position()[0]

    def row_part(taps, row, position):
        left = jnp.where(lane == 0, rolled(west, -LAST - position), rolled(row, 1))
        right = rolled(east, width - 1 - position)
        right = jnp.where(lane == width - 1, right, rolled(row, -1))
        stack = jnp.concatenate([right, row, left], axis=0).astype(BF16)
        return jnp.dot(taps, stack, preferred_element_type=F32)

    above = row_part(turned[jnp.where(lat == 0, 0, 2)], north, 0)
    below = row_part(turned[jnp.where(lat == place.lat - 1, 2, 0)], south, row_count + 1)

    inside = (lane >= 1) & (lane <= row_count)
    west = jnp.where(inside, rolled(west, -LAST), 0.0)
    east = jnp.where(inside, east, 0.0)
    sides = [rolled(west, a - 1) for a in range(3)] + [rolled(east, LAST + a - 1) for a in range(3)]
    taps = [turned[a, :, 2 * gate_count : 3 * gate_count] for a in range(3)]
    taps += [turned[a, :, 0:gate_count] for a in range(3)]
    columns = jnp.dot(
        jnp.concatenate(taps, axis=1),
        jnp.concatenate(sides, axis=0).astype(BF16),
        preferred_element_type=F32,
    )
    blank = jnp.zeros((channels, width), F32)
    for index in range(row_count):
        strided = pl.ds(index, channels, stride=row_count)
        value = wide[strided, :] + at_edges(blank, index + 1, columns)
        if index == 0:
            value += above
        if index == row_count - 1:
            value += below
        total[strided, :] = value
    size = (channels - hid) * row_count
    inputs_out[...] = total[0:size, :].reshape(inputs_out.shape).astype(BF16)
    hidden_out[...] = total[size:, :].reshape(hidden_out.shape).astype(BF16)


def body(
    place,
    inputs_below,
    hidden_prev,
    cell_prev,
    kernel_weights,
    gate_bias,
    readout,
    target_field,
    land_mask,
    fire_mask,
    hidden_grad,
):
    hid, row_count, width = hidden_prev.shape
    gate_count, channels = kernel_weights.shape[1:]
    cells = row_count * width
    halo_cells = (row_count + 2) * width
    scaling = 1.0 / math.sqrt(cells * place.lat * place.lon)
    bind = functools.partial
    inner_rows, outer_rows = place.pairs(place.inner_rows), place.pairs(place.outer_rows)
    inner_columns = place.pairs(place.inner_columns)
    outer_columns = place.pairs(place.outer_columns)
    flat = sds((hid * row_count, width), F32)
    strip = sds((hid, width), F32)

    inner, outer, wide = call(
        pack_kernel,
        (
            sds((channels, width), BF16),
            sds((channels, width), BF16),
            sds((channels * row_count, width), F32),
        ),
        [
            pltpu.VMEM(inputs_below.shape, BF16),
            pltpu.VMEM(hidden_prev.shape, BF16),
            pltpu.SemaphoreType.DMA((2,)),
        ],
        remote=2,
        moved=4 * channels * cells,
    )(inputs_below, hidden_prev)
    inner, outer = permuted(inner, inner_rows), permuted(outer, outer_rows)
    (
        rows,
        columns,
        second,
        cell_strip,
        hidden_grad_strip,
        fields_strip,
        cell_here,
        weights_here,
        hidden_grad_here,
        target_here,
        land_here,
        fire_here,
        bias_wide,
        readout_wide,
    ) = call(
        prepare_kernel,
        (
            sds((row_count, channels, width), BF16),
            sds((channels, width), F32),
            sds((channels, width), F32),
            strip,
            strip,
            sds((8, width), F32),
            flat,
            sds(kernel_weights.shape, BF16),
            flat,
            sds(target_field.shape, F32),
            sds(land_mask.shape, jnp.int32),
            sds(fire_mask.shape, jnp.int32),
            sds((gate_count, width), F32),
            sds((hid, width), F32),
        ),
        [
            pltpu.VMEM(hidden_grad.shape, BF16),
            pltpu.VMEM(gate_bias.shape, F32),
            pltpu.VMEM(readout.shape, F32),
            pltpu.SemaphoreType.DMA((8,)),
        ],
        remote=8,
        moved=6_000_000,
    )(
        wide,
        cell_prev.reshape(hid * row_count, width),
        kernel_weights,
        hidden_grad,
        target_field,
        land_mask,
        fire_mask,
        gate_bias,
        readout,
    )
    columns, edge = call(
        bind(columns_kernel, row_count, GROUPS),
        (sds((channels // GROUPS, width), BF16), sds((channels, width), BF16)),
    )(columns, outer, inner)
    inner_column = permuted(columns, inner_columns)
    outer_column = permuted(columns, outer_columns)
    hidden_rows, cell_rows, grad_cell_rows, pre, second, sums, bias = call(
        bind(gates_kernel, place),
        (
            flat,
            flat,
            flat,
            sds((gate_count, cells), BF16),
            sds((channels, width), BF16),
            sds((2 * place.half_rows, channels), F32),
            sds((gate_count, width), F32),
        ),
        [pltpu.VMEM((3 * channels, halo_cells), BF16)],
        flops=4 * 9 * gate_count * channels * cells,
        moved=6_000_000,
        transcendentals=5 * hid * cells,
    )(
        rows,
        inner,
        outer,
        second,
        cell_here,
        weights_here,
        hidden_grad_here,
        target_here,
        land_here,
        fire_here,
        bias_wide,
        readout_wide,
    )
    send, pre_strip, pre_wide, patches, *strips = call(
        bind(strip_kernel, place, row_count),
        (
            sds((place.half_rows, channels), BF16),
            sds((gate_count, width), BF16),
            sds((gate_count, width), F32),
            sds((place.taps * channels, width), BF16),
            strip,
            strip,
            strip,
        ),
    )(
        edge,
        second,
        outer_column,
        inner_column,
        weights_here,
        bias_wide,
        readout_wide,
        cell_strip,
        hidden_grad_strip,
        fields_strip,
        sums,
    )
    keep, bias = call(
        bind(keep_kernel, place),
        (sds((place.half_rows, channels), F32), sds((8, channels), F32)),
    )(sums, pre_strip, patches, bias, pre_wide)
    hidden_next, cell_next, grad_cell, pre, pre_inner, pre_outer = call(
        bind(edges_kernel, row_count),
        (
            sds((hid, row_count, width), BF16),
            flat,
            flat,
            sds((gate_count, cells), BF16),
            sds((gate_count, width), BF16),
            sds((gate_count, width), BF16),
        ),
        [
            pltpu.VMEM((hid, row_count, width), BF16),
            pltpu.VMEM(flat.shape, F32),
            pltpu.VMEM(flat.shape, F32),
            pltpu.VMEM(flat.shape, F32),
            pltpu.SemaphoreType.DMA((3,)),
        ],
        leaving=3,
        moved=4_000_000,
    )(hidden_rows, cell_rows, grad_cell_rows, pre, *strips, pre_strip)
    pre_inner, pre_outer = permuted(pre_inner, inner_rows), permuted(pre_outer, outer_rows)
    pre_columns = call(
        bind(columns_kernel, row_count, PRE_GROUPS),
        (sds((gate_count // PRE_GROUPS, width), BF16),),
    )(pre_strip, pre_outer, pre_inner)[0]

    block = sds((BIAS_ROWS + place.chunk, channels), BF16)
    token = sds((8, width), F32)
    steps = [*range(2, place.plane), 1]
    *sends, keep = call(
        bind(pair_kernel, place),
        (*[block for _ in steps], sds((place.chunk, channels), F32)),
        [pltpu.VMEM((place.half_rows, channels), F32)],
    )(keep, bias, permuted(send, place.phase_pairs(0)))
    received = [permuted(send, place.plane_pairs(step)) for step, send in zip(steps, sends)]
    field, turned, field_done = call(
        field_kernel,
        (
            sds((channels * row_count, width), F32),
            sds((3, channels, 3 * gate_count), BF16),
            token,
        ),
        [pltpu.VMEM((3 * gate_count, cells), BF16)],
        flops=2 * 9 * gate_count * channels * cells,
        moved=3_000_000,
    )(pre, weights_here)
    part = call(plane_kernel, block)(keep, bias, *received, field_done)
    pre_inner_columns = permuted(pre_columns, inner_columns)
    pre_outer_columns = permuted(pre_columns, outer_columns)
    phases = len(place.orders[0])
    for phase in range(1, phases):
        is_last = phase == phases - 1
        part = call(bind(add_kernel, scaling if is_last else 1.0), block)(
            part, permuted(part, place.phase_pairs(phase))
        )
    late, *received = [permuted(part, place.plane_pairs(step)) for step in steps[::-1]]
    grad_inputs, grad_hidden, field_done = call(
        bind(field_halo_kernel, place),
        (
            sds((channels - hid, row_count, width), BF16),
            sds((hid, row_count, width), BF16),
            token,
        ),
        [pltpu.VMEM((channels * row_count, width), F32)],
        flops=40 * gate_count * channels * cells * 9,
        moved=2_000_000,
    )(field, turned, pre_outer, pre_inner, pre_outer_columns, pre_inner_columns)
    early = call(join_kernel, sds((place.plane - 1, *block.shape), BF16))(
        part, *received, field_done
    )
    early_other = permuted(early, place.phase_pairs(0))
    late_other = permuted(late, place.phase_pairs(0))
    half = [pltpu.VMEM((place.half_rows, channels), F32)]
    grad_kernel, bias = call(
        bind(own_half_kernel, place),
        (sds(kernel_weights.shape, F32), sds((8, channels), F32)),
        half + [pltpu.SemaphoreType.DMA((place.taps,))],
        leaving=1,
        flops=40 * gate_count * channels * cells * 9,
        moved=6 * place.half_rows * channels,
    )(late, early)
    grad_kernel, grad_bias = call(
        bind(other_half_kernel, place),
        (sds(kernel_weights.shape, F32), sds((gate_count,), F32)),
        half + [pltpu.VMEM((gate_count,), F32), pltpu.SemaphoreType.DMA((place.taps + 1,))],
        remote=1,
        leaving=2,
        aliases={4: 0},
        moved=6 * place.half_rows * channels,
    )(bias, early_other, late_other, target_here, grad_kernel)
    shape = hidden_prev.shape
    return (
        hidden_next,
        cell_next.reshape(shape),
        grad_inputs,
        grad_hidden,
        grad_cell.reshape(shape),
        grad_kernel,
        grad_bias,
    )


def solution(mesh):
    lat_count, lon_count = mesh.shape["lat"], mesh.shape["lon"]
    split = Mesh(mesh.devices.reshape(lat_count // 2, 2, lon_count // 2, 2), AXES)
    field = P(None, ("band", "core"), ("reach", "near"))
    flat = P(("band", "core"), ("reach", "near"))

    def run(*args):
        place = Layout(lat_count, lon_count, *args[3].shape[:2])
        return jax.shard_map(
            functools.partial(body, place),
            mesh=split,
            in_specs=(field, field, field, P(), P(), P(), flat, flat, flat, field),
            out_specs=(field, field, field, field, field, P(), P()),
            check_vma=False,
        )(*args)

    return run
```

```python
import functools
import math

import jax
import jax.numpy as jnp
from jax import lax
from jax.experimental import pallas as pl
from jax.experimental.pallas import tpu as pltpu
from jax.sharding import Mesh, PartitionSpec as P

F32 = jnp.float32
BF16 = jnp.bfloat16
AXES = ("band", "core", "reach", "near")
BIAS_ROWS = 16
GROUPS = 4
PRE_GROUPS = 4
LAST = 16
VMEM = pl.BlockSpec(memory_space=pltpu.VMEM)
HBM = pl.BlockSpec(memory_space=pltpu.HBM)
ACROSS = (((1,), (1,)), ((), ()))


def sds(shape, dtype):
    return jax.ShapeDtypeStruct(shape, dtype)


def call(
    kernel,
    out_shape,
    scratch=(),
    remote=0,
    leaving=0,
    aliases=None,
    flops=0,
    moved=0,
    transcendentals=0,
):
    several = isinstance(out_shape, tuple)
    shapes = out_shape if several else (out_shape,)
    out_specs = tuple([HBM] * leaving + [VMEM] * (len(shapes) - leaving))

    def run(*args):
        near = len(args) - remote
        far = [pltpu.with_memory_space_constraint(arg, pltpu.HBM) for arg in args[near:]]
        return pl.pallas_call(
            kernel,
            out_shape=out_shape,
            in_specs=[VMEM] * near + [HBM] * remote,
            out_specs=out_specs if several else out_specs[0],
            input_output_aliases=aliases or {},
            scratch_shapes=list(scratch),
            cost_estimate=pl.CostEstimate(
                flops=flops, bytes_accessed=moved, transcendentals=transcendentals
            ),
            compiler_params=pltpu.CompilerParams(vmem_limit_bytes=24 * 1024 * 1024),
        )(*args[:near], *far)

    return run


class Layout:
    def __init__(self, lat_count, lon_count, taps, gate_count):
        self.lat, self.lon = lat_count, lon_count
        self.half = lon_count // 2
        self.taps, self.half_gates = taps, gate_count // 2
        self.plane = lat_count
        whole = [("lon", 1 << k) for k in range(1, lon_count.bit_length() - 1)]
        self.orders = ([("lat", 1)] + whole, [("lat", 1)] + whole[::-1])
        step = 8 * self.plane
        self.half_rows = -(-taps * self.half_gates // step) * step
        self.chunk = self.half_rows // self.plane

    def position(self):
        lat = 2 * lax.axis_index("band") + lax.axis_index("core")
        return lat, 2 * lax.axis_index("reach") + lax.axis_index("near")

    def rank(self, phase):
        lat, lon = self.position()

        def digit(order):
            axis, bit = order[phase]
            return ((lat if axis == "lat" else lon) // bit) % 2

        return jnp.where(lat % 2 == 0, digit(self.orders[0]), digit(self.orders[1]))

    def pairs(self, partner):
        result = []
        for lat in range(self.lat):
            for lon in range(self.lon):
                there = partner(lat, lon)
                result.append((lat * self.lon + lon, there[0] * self.lon + there[1]))
        return result

    def phase_pairs(self, phase):
        def partner(lat, lon):
            axis, bit = self.orders[lat % 2][phase]
            return (lat ^ bit, lon) if axis == "lat" else (lat, lon ^ bit)

        return self.pairs(partner)

    def plane_rank(self):
        return 2 * lax.axis_index("band") + lax.axis_index("near")

    def plane_pairs(self, step):
        def partner(lat, lon):
            there = (lat // 2 * 2 + lon % 2) ^ step
            return there // 2 * 2 + lat % 2, lon // 2 * 2 + there % 2

        return self.pairs(partner)

    def inner_rows(self, lat, lon):
        return lat ^ 1, lon

    def outer_rows(self, lat, lon):
        there = lat + 1 if lat % 2 else lat - 1
        if 0 <= there < self.lat:
            return there, lon
        return lat, (lon + self.half) % self.lon

    def inner_columns(self, lat, lon):
        return lat, lon ^ 1

    def outer_columns(self, lat, lon):
        return lat, (lon + (1 if lon % 2 else -1)) % self.lon


def permuted(value, pairs):
    return lax.ppermute(value, AXES, pairs)


def lanes(shape):
    return lax.broadcasted_iota(jnp.int32, shape, len(shape) - 1)


def rolled(value, shift):
    shift %= value.shape[1]
    return pltpu.roll(value, shift, 1) if shift else value


def edge_columns(row, position, columns):
    lane = lanes(row.shape)
    columns = jnp.where(lane == position, rolled(row, position), columns)
    return jnp.where(lane == LAST + position, rolled(row, LAST + position + 1), columns)


def at_edges(row, position, columns):
    lane = lanes(row.shape)
    width = row.shape[1]
    row = jnp.where(lane == 0, rolled(columns, -position), row)
    return jnp.where(lane == width - 1, rolled(columns, width - 1 - LAST - position), row)


def pick(flag, yes, no):
    return jnp.where(flag, yes, no)


def is_odd(axis):
    return lax.axis_index(axis) % 2 == 1


def row_sends(first, last, inner_out, outer_out):
    odd = is_odd("core")
    first, last = first.astype(F32), last.astype(F32)
    inner_out[...] = pick(odd, first, last).astype(BF16)
    outer_out[...] = pick(odd, last, first).astype(BF16)


def row_halo(inner, outer):
    odd = is_odd("core")
    inner, outer = inner[...].astype(F32), outer[...].astype(F32)
    return pick(odd, inner, outer), pick(odd, outer, inner)


def packed(columns, groups):
    count, width = columns.shape[0] // groups, columns.shape[1] // groups
    lane = lanes((count, columns.shape[1]))
    value = columns[0:count]
    for group in range(1, groups):
        part = rolled(columns[group * count : (group + 1) * count], group * width)
        value = jnp.where(lane >= group * width, part, value)
    return value


def unpacked(value, groups):
    width = value.shape[1] // groups
    return jnp.concatenate([rolled(value, -group * width) for group in range(groups)], axis=0)


def column_halo(inner, outer, groups):
    odd = is_odd("near")
    inner, outer = inner[...].astype(F32), outer[...].astype(F32)
    return unpacked(pick(odd, inner, outer), groups), unpacked(pick(odd, outer, inner), groups)


def pack_kernel(below, hidden, columns_out, wide_out, below_here, hidden_here, arrived):
    first = pltpu.make_async_copy(below, below_here, arrived.at[0])
    second = pltpu.make_async_copy(hidden, hidden_here, arrived.at[1])
    first.start()
    second.start()
    channels, row_count, width = below.shape
    size = channels * row_count
    first.wait()
    wide_out[0:size, :] = below_here[...].astype(F32).reshape(size, width)
    second.wait()
    wide_out[size : 2 * size, :] = hidden_here[...].astype(F32).reshape(size, width)
    columns = jnp.zeros((2 * channels, width), F32)
    for index in range(row_count):
        row = wide_out[pl.ds(index, 2 * channels, stride=row_count), :]
        columns = edge_columns(row, index + 1, columns)
    columns_out[...] = packed(columns, GROUPS).astype(BF16)


def rows_kernel(row_count, wide, inner_column, outer_column, inner_out, outer_out):
    west, east = column_halo(inner_column, outer_column, GROUPS)
    channels = west.shape[0]
    lane = lanes(west.shape)
    edges = []
    for index in (0, row_count - 1):
        row = wide[pl.ds(index, channels, stride=row_count), :]
        ends = jnp.where(lane == 0, rolled(west, -LAST - index - 1), 0.0)
        ends = jnp.where(lane == LAST, rolled(east, LAST - index - 1), ends)
        edges.append(jnp.concatenate([row, packed(ends, GROUPS)], axis=0))
    row_sends(edges[0], edges[1], inner_out, outer_out)


def down_rows(values, width):
    count = values.shape[0]
    return jnp.broadcast_to(values[None, :], (width, count)).T


def prepare_kernel(
    wide,
    cell_hbm,
    weights_hbm,
    hidden_grad_hbm,
    target_hbm,
    land_hbm,
    fire_hbm,
    gate_bias_hbm,
    readout_hbm,
    rows_out,
    cell_out,
    weights_out,
    hidden_grad_out,
    target_out,
    land_out,
    fire_out,
    bias_wide_out,
    readout_wide_out,
    hidden_grad_here,
    gate_bias_here,
    readout_here,
    arrived,
):
    copies = [
        pltpu.make_async_copy(source, target, arrived.at[index])
        for index, (source, target) in enumerate(
            (
                (cell_hbm, cell_out),
                (weights_hbm, weights_out),
                (hidden_grad_hbm, hidden_grad_here),
                (target_hbm, target_out),
                (land_hbm, land_out),
                (fire_hbm, fire_out),
                (gate_bias_hbm, gate_bias_here),
                (readout_hbm, readout_here),
            )
        )
    ]
    for copy in copies:
        copy.start()
    row_count, channels, width = rows_out.shape
    for index in range(row_count):
        rows_out[index] = wide[pl.ds(index, channels, stride=row_count), :].astype(BF16)
    for copy in copies:
        copy.wait()
    hidden_grad_out[...] = hidden_grad_here[...].astype(F32).reshape(hidden_grad_out.shape)
    bias_wide_out[...] = down_rows(gate_bias_here[...], width)
    readout_wide_out[...] = down_rows(readout_here[...], width)


def columns_kernel(row_count, groups, columns, outer, inner, packed_out):
    north, south = row_halo(inner, outer)
    value = edge_columns(north, 0, columns[...].astype(F32))
    value = edge_columns(south, row_count + 1, value)
    packed_out[...] = packed(value, groups).astype(BF16)


def encode(bias):
    high = bias.astype(BF16).astype(F32)
    return jnp.concatenate([high, bias - high], axis=0)


def decode(block):
    return block[0:8] + block[8:16]


def cell_step(part, cell_before, hidden_grad, target, land, fire, readout):
    hid = part.shape[0] // 4
    input_gate = 0.5 + 0.5 * jnp.tanh(0.5 * part[0:hid])
    forget_gate = 0.5 + 0.5 * jnp.tanh(0.5 * part[hid : 2 * hid])
    output_gate = 0.5 + 0.5 * jnp.tanh(0.5 * part[2 * hid : 3 * hid])
    candidate = jnp.tanh(part[3 * hid : 4 * hid])
    cell_next = land * (forget_gate * cell_before + input_gate * candidate)
    squashed = jnp.tanh(cell_next)
    hidden_next = (output_gate * squashed).astype(BF16).astype(F32)
    predicted = jnp.sum(readout * hidden_next, axis=0, keepdims=True)
    total_grad = hidden_grad + 2.0 * (fire * (predicted - target)) * readout
    cell_grad = land * total_grad * output_gate * (1.0 - squashed * squashed)
    pre_grad = jnp.concatenate(
        [
            cell_grad * candidate * input_gate * (1.0 - input_gate),
            cell_grad * cell_before * forget_gate * (1.0 - forget_gate),
            total_grad * squashed * output_gate * (1.0 - output_gate),
            cell_grad * input_gate * (1.0 - candidate * candidate),
        ],
        axis=0,
    )
    return hidden_next, cell_next, cell_grad * forget_gate, pre_grad


def beside(row, left, right):
    lane = lanes(row.shape)
    width = row.shape[1]
    return jnp.concatenate(
        [
            jnp.where(lane == 0, left, rolled(row, 1)),
            row,
            jnp.where(lane == width - 1, right, rolled(row, -1)),
        ],
        axis=0,
    ).astype(BF16)


def gates_kernel(
    place,
    rows_in,
    outer_column,
    inner_column,
    cell_prev,
    weights,
    hidden_grad,
    target,
    land,
    fire,
    bias_wide,
    readout_wide,
    hidden_out,
    cell_out,
    grad_cell_out,
    pre_out,
    shifted,
    sums,
    bias_out,
):
    row_count, channels, width = rows_in.shape
    gate_count = weights.shape[1]
    hid = gate_count // 4
    half_gates = place.half_gates
    west, east = column_halo(inner_column, outer_column, GROUPS)
    for index in range(row_count):
        shifted[:, pl.ds((index + 1) * width, width)] = beside(
            rows_in[index].astype(F32),
            rolled(west, -LAST - index - 1),
            rolled(east, width - 2 - index),
        )

    taps = [
        jnp.concatenate([weights[3 * a], weights[3 * a + 1], weights[3 * a + 2]], axis=1)
        for a in range(3)
    ]
    bias_total = jnp.zeros((gate_count, width), F32)
    readout = readout_wide[...]
    pair = 2 if row_count % 2 == 0 else 1
    for base in range(1, row_count - 1, pair):
        preact = jnp.zeros((gate_count, pair * width), F32)
        for a in range(3):
            preact += jnp.dot(
                taps[a],
                shifted[:, pl.ds((base + a) * width, pair * width)],
                preferred_element_type=F32,
            )
        for offset in range(pair):
            index = base + offset
            strided = pl.ds(index, hid, stride=row_count)
            at = slice(index, index + 1)
            hidden_next, cell_next, grad_cell, pre_grad = cell_step(
                preact[:, offset * width : (offset + 1) * width] + bias_wide[...],
                cell_prev[strided, :],
                hidden_grad[strided, :],
                target[at, :],
                land[at, :].astype(F32),
                fire[at, :].astype(F32),
                readout,
            )
            hidden_out[strided, :] = hidden_next
            cell_out[strided, :] = cell_next
            grad_cell_out[strided, :] = grad_cell
            bias_total += pre_grad
            pre_out[:, pl.ds(index * width, width)] = pre_grad.astype(BF16)
    bias_out[...] = bias_total

    for a in range(3):
        product = lax.dot_general(
            pre_out[:, pl.ds(width, (row_count - 2) * width)],
            shifted[:, pl.ds((a + 1) * width, (row_count - 2) * width)],
            ACROSS,
            preferred_element_type=F32,
        )
        for b in range(3):
            for half in range(2):
                at = half * place.half_rows + (3 * a + b) * half_gates
                sums[at : at + half_gates, :] = product[
                    half * half_gates : (half + 1) * half_gates, b * channels : (b + 1) * channels
                ]
    used = place.taps * half_gates
    if place.half_rows > used:
        for half in range(2):
            at = half * place.half_rows
            sums[at + used : at + place.half_rows, :] = jnp.zeros(
                (place.half_rows - used, channels), F32
            )


def add_strip(place, half, sums, pre_strip, patches, out):
    half_gates, channels = place.half_gates, sums.shape[1]
    gates = pre_strip[pl.ds(pl.multiple_of(half * half_gates, half_gates), half_gates), :]
    product = lax.dot_general(gates, patches[...], ACROSS, preferred_element_type=F32)
    base = half * place.half_rows
    for tap in range(place.taps):
        at = pl.ds(pl.multiple_of(base + tap * half_gates, 8), half_gates)
        value = sums[at, :] + product[:, tap * channels : (tap + 1) * channels]
        out[tap * half_gates : (tap + 1) * half_gates, :] = value.astype(out.dtype)
    used = place.taps * half_gates
    if place.half_rows > used:
        rest = jnp.zeros((place.half_rows - used, channels), out.dtype)
        out[used:, :] = rest


def strip_kernel(
    place,
    row_count,
    outer_row,
    inner_row,
    shifted,
    weights,
    bias_wide,
    readout_wide,
    cell_prev,
    hidden_grad,
    target,
    land,
    fire,
    sums,
    send_out,
    pre_out,
    pre_wide_out,
    patches,
    hidden_out,
    cell_out,
    grad_cell_out,
):
    channels = weights.shape[2]
    hid, width = readout_wide.shape
    block = 3 * channels
    halo = []
    for value in row_halo(inner_row, outer_row):
        ends = unpacked(value[channels:], GROUPS)
        halo.append(beside(value[0:channels], ends, rolled(ends, width - 1 - LAST)))
    for a in range(3):
        at = slice(a * block, (a + 1) * block)
        north = a == 0
        south = a == 2
        patches[at, 0:width] = halo[0] if north else shifted[:, a * width : (a + 1) * width]
        from_row = (row_count - 1 + a) * width
        patches[at, width : 2 * width] = (
            halo[1] if south else shifted[:, from_row : from_row + width]
        )
    taps = jnp.concatenate([weights[tap] for tap in range(place.taps)], axis=1)
    preact = jnp.dot(taps, patches[...], preferred_element_type=F32)

    def both(value):
        return jnp.concatenate([value, value], axis=1)

    def edges(ref):
        return jnp.concatenate(
            [ref[pl.ds(index, hid, stride=row_count), :] for index in (0, row_count - 1)], axis=1
        )

    def edge_fields(ref):
        rows = [ref[index : index + 1, :].astype(F32) for index in (0, row_count - 1)]
        return jnp.concatenate(rows, axis=1)

    hidden_next, cell_next, grad_cell, pre_grad = cell_step(
        preact + both(bias_wide[...]),
        edges(cell_prev),
        edges(hidden_grad),
        edge_fields(target),
        edge_fields(land),
        edge_fields(fire),
        both(readout_wide[...]),
    )
    hidden_out[...] = hidden_next
    cell_out[...] = cell_next
    grad_cell_out[...] = grad_cell
    pre_out[...] = pre_grad.astype(BF16)
    pre_wide_out[...] = pre_grad
    add_strip(place, 1 - place.rank(0), sums, pre_out, patches, send_out)


def keep_kernel(place, sums, pre_strip, patches, bias_partial, pre_wide, out, bias_out):
    add_strip(place, place.rank(0), sums, pre_strip, patches, out)
    channels = sums.shape[1]
    width = bias_partial.shape[1]
    bias_total = bias_partial[...] + pre_wide[:, 0:width] + pre_wide[:, width : 2 * width]
    ones = jnp.ones((8, bias_total.shape[1]), BF16)
    high = bias_total.astype(BF16)
    low = (bias_total - high.astype(F32)).astype(BF16)
    flat = lax.dot_general(ones, high, ACROSS, preferred_element_type=F32)
    flat += lax.dot_general(ones, low, ACROSS, preferred_element_type=F32)
    odd = lax.broadcasted_iota(jnp.int32, (8, channels), 0) % 2 == 1
    bias_out[...] = jnp.where(odd, flat[:, channels : 2 * channels], flat[:, 0:channels])


def edges_kernel(
    row_count,
    hidden,
    cell,
    grad_cell,
    pre,
    hidden_strip,
    cell_strip,
    grad_cell_strip,
    pre_strip,
    hidden_hbm,
    cell_hbm,
    grad_cell_hbm,
    pre_out,
    columns_out,
    inner_out,
    outer_out,
    hidden_low,
    hidden_here,
    cell_here,
    grad_cell_here,
    left,
):
    hid, _, width = hidden_low.shape
    halves = ((0, slice(0, width)), (row_count - 1, slice(width, 2 * width)))
    leaving = []
    for source, strip, here, ready, target in (
        (cell, cell_strip, cell_here, cell_here, cell_hbm),
        (grad_cell, grad_cell_strip, grad_cell_here, grad_cell_here, grad_cell_hbm),
        (hidden, hidden_strip, hidden_here, hidden_low, hidden_hbm),
    ):
        here[...] = source[...]
        for index, half in halves:
            here[pl.ds(index, hid, stride=row_count), :] = strip[:, half]
        if ready is hidden_low:
            hidden_low[...] = here[...].reshape(hidden_low.shape).astype(BF16)
        leaving.append(pltpu.make_async_copy(ready, target, left.at[len(leaving)]))
        leaving[-1].start()
    pre_out[...] = pre[...]
    for index, half in halves:
        pre_out[:, pl.ds(index * width, width)] = pre_strip[:, half]
    row_sends(pre_strip[:, 0:width], pre_strip[:, width : 2 * width], inner_out, outer_out)
    columns = jnp.zeros(columns_out.shape, F32)
    for index in range(row_count):
        row = pre_out[:, pl.ds(index * width, width)].astype(F32)
        columns = edge_columns(row, index + 1, columns)
    columns_out[...] = columns.astype(BF16)
    for copy in leaving:
        copy.wait()


def pair_kernel(place, keep, bias, received, *outs):
    sends, keep_out, scratch = outs[:-2], outs[-2], outs[-1]
    chunk = place.chunk
    rank = place.plane_rank()
    scratch[...] = keep[...] + received[...].astype(F32)
    block = encode(bias[...]).astype(BF16)
    for step, send in zip(range(place.plane - 1, 0, -1), sends):
        send[0:BIAS_ROWS, :] = block
        at = pl.ds(pl.multiple_of((rank ^ step) * chunk, 8), chunk)
        send[BIAS_ROWS:, :] = scratch[at, :].astype(BF16)
    keep_out[...] = scratch[pl.ds(pl.multiple_of(rank * chunk, 8), chunk), :]


def plane_kernel(keep, bias, *refs):
    received, out = refs[:-2], refs[-1]
    total, bias_total = keep[...], bias[...]
    for ref in received:
        total += ref[BIAS_ROWS:, :].astype(F32)
        bias_total += decode(ref[0:BIAS_ROWS, :].astype(F32))
    out[0:BIAS_ROWS, :] = encode(bias_total).astype(BF16)
    out[BIAS_ROWS:, :] = total.astype(BF16)


def join_kernel(*refs):
    blocks, out = refs[:-2], refs[-1]
    for index, block in enumerate(blocks):
        out[index] = block[...]


def add_kernel(scale, own, received, out):
    here, there = own[...].astype(F32), received[...].astype(F32)
    bias = (decode(here[0:BIAS_ROWS]) + decode(there[0:BIAS_ROWS])) * scale
    out[0:BIAS_ROWS, :] = encode(bias).astype(BF16)
    out[BIAS_ROWS:, :] = ((here[BIAS_ROWS:] + there[BIAS_ROWS:]) * scale).astype(BF16)


def store_half(place, half, blocks, out, wide, left):
    chunk, half_gates = place.chunk, place.half_gates
    gates = pl.ds(pl.multiple_of(half * half_gates, half_gates), half_gates)
    rank = place.plane_rank()
    for step, block in enumerate(blocks):
        at = pl.ds(pl.multiple_of((rank ^ step) * chunk, 8), chunk)
        wide[at, :] = block[BIAS_ROWS:, :].astype(F32)
    copies = []
    for tap in range(place.taps):
        source = wide.at[tap * half_gates : (tap + 1) * half_gates, :]
        copies.append(pltpu.make_async_copy(source, out.at[tap, gates, :], left.at[tap]))
        copies[-1].start()
    return copies


def in_steps(place, early, late):
    return [early.at[0], late] + [early.at[index] for index in range(1, place.plane - 1)]


def own_half_kernel(place, late, early, out, bias_out, wide, left):
    blocks = in_steps(place, early, late)
    copies = store_half(place, place.rank(0), blocks, out, wide, left)
    rank = place.plane_rank()
    bias = decode(blocks[0][0:BIAS_ROWS, :].astype(F32))
    for step in range(1, place.plane):
        bias = pick(rank == step, decode(blocks[step][0:BIAS_ROWS, :].astype(F32)), bias)
    bias_out[...] = bias
    for copy in copies:
        copy.wait()


def other_half_kernel(
    place, bias_own, early, late, after, out_before, out, bias_out, wide, bias_here, left
):
    del after, out_before
    blocks = in_steps(place, early, late)
    copies = store_half(place, 1 - place.rank(0), blocks, out, wide, left)
    rank = place.plane_rank()
    bias = decode(blocks[0][0:BIAS_ROWS, :].astype(F32))
    for step in range(1, place.plane):
        bias = pick(rank == step, decode(blocks[step][0:BIAS_ROWS, :].astype(F32)), bias)
    bias += bias_own[...]
    width = bias.shape[1]
    for index in range(bias_here.shape[0] // width):
        bias_here[pl.ds(index * width, width)] = bias[index]
    bias_copy = pltpu.make_async_copy(bias_here, bias_out, left.at[place.taps])
    bias_copy.start()
    bias_copy.wait()
    for copy in copies:
        copy.wait()


def field_kernel(pre, weights, wide_out, turned_out, done_out, shifted):
    done_out[...] = jnp.zeros(done_out.shape, F32)
    gate_count, cells = pre.shape
    channels, width = weights.shape[2], wide_out.shape[1]
    row_count = cells // width
    lane = lanes((gate_count, width))
    for index in range(row_count):
        at = pl.ds(index * width, width)
        row = pre[:, at].astype(F32)
        left = jnp.where(lane == 0, 0.0, rolled(row, 1))
        right = jnp.where(lane == width - 1, 0.0, rolled(row, -1))
        shifted[0:gate_count, at] = right.astype(BF16)
        shifted[gate_count : 2 * gate_count, at] = pre[:, at]
        shifted[2 * gate_count : 3 * gate_count, at] = left.astype(BF16)
    for a in range(3):
        for b in range(3):
            turned_out[a, :, b * gate_count : (b + 1) * gate_count] = weights[3 * a + b].T

    def product(a, index, count):
        return jnp.dot(
            turned_out[a],
            shifted[:, pl.ds(index * width, count * width)],
            preferred_element_type=F32,
        )

    pair = 2 if row_count % 2 == 0 else 1
    for base in range(0, row_count, pair):
        total = product(1, base, pair)
        for a, first in ((2, base - 1), (0, base + 1)):
            low, high = max(first, 0), min(first + pair, row_count)
            if low >= high:
                continue
            part = product(a, low, high - low)
            blank = jnp.zeros((channels, width), F32)
            parts = [blank] * (low - first) + [part] + [blank] * (first + pair - high)
            total += jnp.concatenate(parts, axis=1)
        for offset in range(pair):
            value = total[:, offset * width : (offset + 1) * width]
            wide_out[pl.ds(base + offset, channels, stride=row_count), :] = value


def field_halo_kernel(
    place,
    wide,
    turned,
    outer_row,
    inner_row,
    outer_column,
    inner_column,
    inputs_out,
    hidden_out,
    done_out,
    total,
):
    done_out[...] = jnp.zeros(done_out.shape, F32)
    hid, row_count, width = hidden_out.shape
    channels = turned.shape[1]
    gate_count = turned.shape[2] // 3
    north, south = row_halo(inner_row, outer_row)
    west, east = column_halo(inner_column, outer_column, PRE_GROUPS)
    lane = lanes((gate_count, width))
    lat = place.position()[0]

    def row_part(taps, row, position):
        left = jnp.where(lane == 0, rolled(west, -LAST - position), rolled(row, 1))
        right = rolled(east, width - 1 - position)
        right = jnp.where(lane == width - 1, right, rolled(row, -1))
        stack = jnp.concatenate([right, row, left], axis=0).astype(BF16)
        return jnp.dot(taps, stack, preferred_element_type=F32)

    above = row_part(turned[jnp.where(lat == 0, 0, 2)], north, 0)
    below = row_part(turned[jnp.where(lat == place.lat - 1, 2, 0)], south, row_count + 1)

    inside = (lane >= 1) & (lane <= row_count)
    west = jnp.where(inside, rolled(west, -LAST), 0.0)
    east = jnp.where(inside, east, 0.0)
    sides = [rolled(west, a - 1) for a in range(3)] + [rolled(east, LAST + a - 1) for a in range(3)]
    taps = [turned[a, :, 2 * gate_count : 3 * gate_count] for a in range(3)]
    taps += [turned[a, :, 0:gate_count] for a in range(3)]
    columns = jnp.dot(
        jnp.concatenate(taps, axis=1),
        jnp.concatenate(sides, axis=0).astype(BF16),
        preferred_element_type=F32,
    )
    blank = jnp.zeros((channels, width), F32)
    for index in range(row_count):
        strided = pl.ds(index, channels, stride=row_count)
        value = wide[strided, :] + at_edges(blank, index + 1, columns)
        if index == 0:
            value += above
        if index == row_count - 1:
            value += below
        total[strided, :] = value
    size = (channels - hid) * row_count
    inputs_out[...] = total[0:size, :].reshape(inputs_out.shape).astype(BF16)
    hidden_out[...] = total[size:, :].reshape(hidden_out.shape).astype(BF16)


def body(
    place,
    inputs_below,
    hidden_prev,
    cell_prev,
    kernel_weights,
    gate_bias,
    readout,
    target_field,
    land_mask,
    fire_mask,
    hidden_grad,
):
    hid, row_count, width = hidden_prev.shape
    gate_count, channels = kernel_weights.shape[1:]
    cells = row_count * width
    halo_cells = (row_count + 2) * width
    scaling = 1.0 / math.sqrt(cells * place.lat * place.lon)
    bind = functools.partial
    inner_rows, outer_rows = place.pairs(place.inner_rows), place.pairs(place.outer_rows)
    inner_columns = place.pairs(place.inner_columns)
    outer_columns = place.pairs(place.outer_columns)
    flat = sds((hid * row_count, width), F32)
    strip = sds((hid, 2 * width), F32)

    columns, wide = call(
        pack_kernel,
        (
            sds((channels // GROUPS, width), BF16),
            sds((channels * row_count, width), F32),
        ),
        [
            pltpu.VMEM(inputs_below.shape, BF16),
            pltpu.VMEM(hidden_prev.shape, BF16),
            pltpu.SemaphoreType.DMA((2,)),
        ],
        remote=2,
        moved=4 * channels * cells,
    )(inputs_below, hidden_prev)
    inner_column = permuted(columns, inner_columns)
    outer_column = permuted(columns, outer_columns)
    (
        rows,
        cell_here,
        weights_here,
        hidden_grad_here,
        target_here,
        land_here,
        fire_here,
        bias_wide,
        readout_wide,
    ) = call(
        prepare_kernel,
        (
            sds((row_count, channels, width), BF16),
            flat,
            sds(kernel_weights.shape, BF16),
            flat,
            sds(target_field.shape, F32),
            sds(land_mask.shape, jnp.int32),
            sds(fire_mask.shape, jnp.int32),
            sds((gate_count, width), F32),
            sds((hid, width), F32),
        ),
        [
            pltpu.VMEM(hidden_grad.shape, BF16),
            pltpu.VMEM(gate_bias.shape, F32),
            pltpu.VMEM(readout.shape, F32),
            pltpu.SemaphoreType.DMA((8,)),
        ],
        remote=8,
        moved=6_000_000,
    )(
        wide,
        cell_prev.reshape(hid * row_count, width),
        kernel_weights,
        hidden_grad,
        target_field,
        land_mask,
        fire_mask,
        gate_bias,
        readout,
    )
    edge = sds((channels + channels // GROUPS, width), BF16)
    inner, outer = call(bind(rows_kernel, row_count), (edge, edge))(
        wide, inner_column, outer_column
    )
    inner, outer = permuted(inner, inner_rows), permuted(outer, outer_rows)
    hidden_rows, cell_rows, grad_cell_rows, pre, shifted, sums, bias = call(
        bind(gates_kernel, place),
        (
            flat,
            flat,
            flat,
            sds((gate_count, cells), BF16),
            sds((3 * channels, halo_cells), BF16),
            sds((2 * place.half_rows, channels), F32),
            sds((gate_count, width), F32),
        ),
        flops=4 * 9 * gate_count * channels * cells,
        moved=6_000_000,
        transcendentals=5 * hid * cells,
    )(
        rows,
        outer_column,
        inner_column,
        cell_here,
        weights_here,
        hidden_grad_here,
        target_here,
        land_here,
        fire_here,
        bias_wide,
        readout_wide,
    )
    send, pre_strip, pre_wide, patches, *strips = call(
        bind(strip_kernel, place, row_count),
        (
            sds((place.half_rows, channels), BF16),
            sds((gate_count, 2 * width), BF16),
            sds((gate_count, 2 * width), F32),
            sds((place.taps * channels, 2 * width), BF16),
            strip,
            strip,
            strip,
        ),
    )(
        outer,
        inner,
        shifted,
        weights_here,
        bias_wide,
        readout_wide,
        cell_here,
        hidden_grad_here,
        target_here,
        land_here,
        fire_here,
        sums,
    )
    keep, bias = call(
        bind(keep_kernel, place),
        (sds((place.half_rows, channels), F32), sds((8, channels), F32)),
    )(sums, pre_strip, patches, bias, pre_wide)
    hidden_next, cell_next, grad_cell, pre, pre_columns, pre_inner, pre_outer = call(
        bind(edges_kernel, row_count),
        (
            sds((hid, row_count, width), BF16),
            flat,
            flat,
            sds((gate_count, cells), BF16),
            sds((gate_count, width), BF16),
            sds((gate_count, width), BF16),
            sds((gate_count, width), BF16),
        ),
        [
            pltpu.VMEM((hid, row_count, width), BF16),
            pltpu.VMEM(flat.shape, F32),
            pltpu.VMEM(flat.shape, F32),
            pltpu.VMEM(flat.shape, F32),
            pltpu.SemaphoreType.DMA((3,)),
        ],
        leaving=3,
        moved=4_000_000,
    )(hidden_rows, cell_rows, grad_cell_rows, pre, *strips, pre_strip)
    pre_inner, pre_outer = permuted(pre_inner, inner_rows), permuted(pre_outer, outer_rows)
    pre_columns = call(
        bind(columns_kernel, row_count, PRE_GROUPS),
        (sds((gate_count // PRE_GROUPS, width), BF16),),
    )(pre_columns, pre_outer, pre_inner)[0]

    block = sds((BIAS_ROWS + place.chunk, channels), BF16)
    token = sds((8, width), F32)
    steps = range(place.plane - 1, 0, -1)
    *sends, keep = call(
        bind(pair_kernel, place),
        (*[block for _ in steps], sds((place.chunk, channels), F32)),
        [pltpu.VMEM((place.half_rows, channels), F32)],
    )(keep, bias, permuted(send, place.phase_pairs(0)))
    received = [permuted(send, place.plane_pairs(step)) for step, send in zip(steps, sends)]
    field, turned, field_done = call(
        field_kernel,
        (
            sds((channels * row_count, width), F32),
            sds((3, channels, 3 * gate_count), BF16),
            token,
        ),
        [pltpu.VMEM((3 * gate_count, cells), BF16)],
        flops=2 * 9 * gate_count * channels * cells,
        moved=3_000_000,
    )(pre, weights_here)
    part = call(plane_kernel, block)(keep, bias, *received, field_done)
    pre_inner_columns = permuted(pre_columns, inner_columns)
    pre_outer_columns = permuted(pre_columns, outer_columns)
    phases = len(place.orders[0])
    for phase in range(1, phases):
        is_last = phase == phases - 1
        part = call(bind(add_kernel, scaling if is_last else 1.0), block)(
            part, permuted(part, place.phase_pairs(phase))
        )
    received = [permuted(part, place.plane_pairs(step)) for step in steps[::-1]]
    grad_inputs, grad_hidden, field_done = call(
        bind(field_halo_kernel, place),
        (
            sds((channels - hid, row_count, width), BF16),
            sds((hid, row_count, width), BF16),
            token,
        ),
        [pltpu.VMEM((channels * row_count, width), F32)],
        flops=40 * gate_count * channels * cells * 9,
        moved=2_000_000,
    )(field, turned, pre_outer, pre_inner, pre_outer_columns, pre_inner_columns)
    early = call(join_kernel, sds((place.plane - 1, *block.shape), BF16))(
        part, *received[1:], field_done
    )
    late = received[0]
    early_other = permuted(early, place.phase_pairs(0))
    late_other = permuted(late, place.phase_pairs(0))
    half = [pltpu.VMEM((place.half_rows, channels), F32)]
    grad_kernel, bias = call(
        bind(own_half_kernel, place),
        (sds(kernel_weights.shape, F32), sds((8, channels), F32)),
        half + [pltpu.SemaphoreType.DMA((place.taps,))],
        leaving=1,
        flops=40 * gate_count * channels * cells * 9,
        moved=6 * place.half_rows * channels,
    )(late, early)
    grad_kernel, grad_bias = call(
        bind(other_half_kernel, place),
        (sds(kernel_weights.shape, F32), sds((gate_count,), F32)),
        half + [pltpu.VMEM((gate_count,), F32), pltpu.SemaphoreType.DMA((place.taps + 1,))],
        remote=1,
        leaving=2,
        aliases={4: 0},
        moved=6 * place.half_rows * channels,
    )(bias, early_other, late_other, target_here, grad_kernel)
    shape = hidden_prev.shape
    return (
        hidden_next,
        cell_next.reshape(shape),
        grad_inputs,
        grad_hidden,
        grad_cell.reshape(shape),
        grad_kernel,
        grad_bias,
    )


def solution(mesh):
    lat_count, lon_count = mesh.shape["lat"], mesh.shape["lon"]
    split = Mesh(mesh.devices.reshape(lat_count // 2, 2, lon_count // 2, 2), AXES)
    field = P(None, ("band", "core"), ("reach", "near"))
    flat = P(("band", "core"), ("reach", "near"))

    def run(*args):
        place = Layout(lat_count, lon_count, *args[3].shape[:2])
        return jax.shard_map(
            functools.partial(body, place),
            mesh=split,
            in_specs=(field, field, field, P(), P(), P(), flat, flat, flat, field),
            out_specs=(field, field, field, field, field, P(), P()),
            check_vma=False,
        )(*args)

    return run
```

```python
import functools
import math

import jax
import jax.numpy as jnp
from jax import lax
from jax.experimental import pallas as pl
from jax.experimental.pallas import tpu as pltpu
from jax.sharding import Mesh, PartitionSpec as P

F32 = jnp.float32
BF16 = jnp.bfloat16
AXES = ("band", "core", "reach", "near")
BIAS_ROWS = 16
GROUPS = 4
PRE_GROUPS = 4
LAST = 16
VMEM = pl.BlockSpec(memory_space=pltpu.VMEM)
HBM = pl.BlockSpec(memory_space=pltpu.HBM)
ACROSS = (((1,), (1,)), ((), ()))


def sds(shape, dtype):
    return jax.ShapeDtypeStruct(shape, dtype)


def call(
    kernel,
    out_shape,
    scratch=(),
    remote=0,
    leaving=0,
    aliases=None,
    flops=0,
    moved=0,
    transcendentals=0,
):
    several = isinstance(out_shape, tuple)
    shapes = out_shape if several else (out_shape,)
    out_specs = tuple([HBM] * leaving + [VMEM] * (len(shapes) - leaving))

    def run(*args):
        near = len(args) - remote
        far = [pltpu.with_memory_space_constraint(arg, pltpu.HBM) for arg in args[near:]]
        return pl.pallas_call(
            kernel,
            out_shape=out_shape,
            in_specs=[VMEM] * near + [HBM] * remote,
            out_specs=out_specs if several else out_specs[0],
            input_output_aliases=aliases or {},
            scratch_shapes=list(scratch),
            cost_estimate=pl.CostEstimate(
                flops=flops, bytes_accessed=moved, transcendentals=transcendentals
            ),
            compiler_params=pltpu.CompilerParams(vmem_limit_bytes=24 * 1024 * 1024),
        )(*args[:near], *far)

    return run


class Layout:
    def __init__(self, lat_count, lon_count, taps, gate_count):
        self.lat, self.lon = lat_count, lon_count
        self.half = lon_count // 2
        self.taps, self.half_gates = taps, gate_count // 2
        self.plane = lat_count
        whole = [("lon", 1 << k) for k in range(1, lon_count.bit_length() - 1)]
        self.orders = ([("lat", 1)] + whole, [("lat", 1)] + whole[::-1])
        step = 8 * self.plane
        self.half_rows = -(-taps * self.half_gates // step) * step
        self.chunk = self.half_rows // self.plane

    def position(self):
        lat = 2 * lax.axis_index("band") + lax.axis_index("core")
        return lat, 2 * lax.axis_index("reach") + lax.axis_index("near")

    def rank(self, phase):
        lat, lon = self.position()

        def digit(order):
            axis, bit = order[phase]
            return ((lat if axis == "lat" else lon) // bit) % 2

        return jnp.where(lat % 2 == 0, digit(self.orders[0]), digit(self.orders[1]))

    def pairs(self, partner):
        result = []
        for lat in range(self.lat):
            for lon in range(self.lon):
                there = partner(lat, lon)
                result.append((lat * self.lon + lon, there[0] * self.lon + there[1]))
        return result

    def phase_pairs(self, phase):
        def partner(lat, lon):
            axis, bit = self.orders[lat % 2][phase]
            return (lat ^ bit, lon) if axis == "lat" else (lat, lon ^ bit)

        return self.pairs(partner)

    def plane_rank(self):
        return 2 * lax.axis_index("band") + lax.axis_index("near")

    def plane_pairs(self, step):
        def partner(lat, lon):
            there = (lat // 2 * 2 + lon % 2) ^ step
            return there // 2 * 2 + lat % 2, lon // 2 * 2 + there % 2

        return self.pairs(partner)

    def inner_rows(self, lat, lon):
        return lat ^ 1, lon

    def outer_rows(self, lat, lon):
        there = lat + 1 if lat % 2 else lat - 1
        if 0 <= there < self.lat:
            return there, lon
        return lat, (lon + self.half) % self.lon

    def inner_columns(self, lat, lon):
        return lat, lon ^ 1

    def outer_columns(self, lat, lon):
        return lat, (lon + (1 if lon % 2 else -1)) % self.lon


def permuted(value, pairs):
    return lax.ppermute(value, AXES, pairs)


def lanes(shape):
    return lax.broadcasted_iota(jnp.int32, shape, len(shape) - 1)


def rolled(value, shift):
    shift %= value.shape[1]
    return pltpu.roll(value, shift, 1) if shift else value


def edge_columns(row, position, columns):
    lane = lanes(row.shape)
    columns = jnp.where(lane == position, rolled(row, position), columns)
    return jnp.where(lane == LAST + position, rolled(row, LAST + position + 1), columns)


def second_columns(row, position, columns):
    lane = lanes(row.shape)
    columns = jnp.where(lane == position, rolled(row, position - 1), columns)
    return jnp.where(lane == LAST + position, rolled(row, LAST + position + 2), columns)


def at_edges(row, position, columns):
    lane = lanes(row.shape)
    width = row.shape[1]
    row = jnp.where(lane == 0, rolled(columns, -position), row)
    return jnp.where(lane == width - 1, rolled(columns, width - 1 - LAST - position), row)


def pick(flag, yes, no):
    return jnp.where(flag, yes, no)


def is_odd(axis):
    return lax.axis_index(axis) % 2 == 1


def row_sends(first, last, inner_out, outer_out):
    odd = is_odd("core")
    inner_out[...] = pick(odd, first, last).astype(BF16)
    outer_out[...] = pick(odd, last, first).astype(BF16)


def row_halo(inner, outer):
    odd = is_odd("core")
    inner, outer = inner[...].astype(F32), outer[...].astype(F32)
    return pick(odd, inner, outer), pick(odd, outer, inner)


def packed(columns, groups):
    count, width = columns.shape[0] // groups, columns.shape[1] // groups
    lane = lanes((count, columns.shape[1]))
    value = columns[0:count]
    for group in range(1, groups):
        part = rolled(columns[group * count : (group + 1) * count], group * width)
        value = jnp.where(lane >= group * width, part, value)
    return value


def unpacked(value, groups):
    width = value.shape[1] // groups
    return jnp.concatenate([rolled(value, -group * width) for group in range(groups)], axis=0)


def column_halo(inner, outer, groups):
    odd = is_odd("near")
    inner, outer = inner[...].astype(F32), outer[...].astype(F32)
    return unpacked(pick(odd, inner, outer), groups), unpacked(pick(odd, outer, inner), groups)


def pack_kernel(below, hidden, inner_out, outer_out, wide_out, below_here, hidden_here, arrived):
    channels, row_count, width = below.shape
    size = channels * row_count
    part = channels // 2
    copies = []
    for source, here in ((below, below_here), (hidden, hidden_here)):
        for at in (pl.ds(0, part), pl.ds(part, part)):
            copies.append(
                pltpu.make_async_copy(source.at[at], here.at[at], arrived.at[len(copies)])
            )
            copies[-1].start()
    for index, copy in enumerate(copies):
        here = (below_here, hidden_here)[index // 2]
        copy.wait()
        value = here[pl.ds(index % 2 * part, part)].astype(F32)
        at = pl.ds(index * part * row_count, part * row_count)
        wide_out[at, :] = value.reshape(part * row_count, width)
    edges = [
        wide_out[pl.ds(index, 2 * channels, stride=row_count), :] for index in (0, row_count - 1)
    ]
    row_sends(edges[0], edges[1], inner_out, outer_out)


def down_rows(values, width):
    count = values.shape[0]
    return jnp.broadcast_to(values[None, :], (width, count)).T


def prepare_kernel(
    wide,
    cell_hbm,
    weights_hbm,
    hidden_grad_hbm,
    target_hbm,
    land_hbm,
    fire_hbm,
    gate_bias_hbm,
    readout_hbm,
    rows_out,
    columns_out,
    second_out,
    cell_strip_out,
    hidden_grad_strip_out,
    fields_strip_out,
    cell_out,
    weights_out,
    hidden_grad_out,
    target_out,
    land_out,
    fire_out,
    bias_wide_out,
    readout_wide_out,
    hidden_grad_here,
    gate_bias_here,
    readout_here,
    arrived,
):
    row_count, channels, width = rows_out.shape
    copies = [
        pltpu.make_async_copy(source, target, arrived.at[index])
        for index, (source, target) in enumerate(
            (
                (cell_hbm, cell_out),
                *(
                    (weights_hbm.at[tap], weights_out.at[:, pl.ds(tap * channels, channels)])
                    for tap in range(weights_hbm.shape[0])
                ),
                (hidden_grad_hbm, hidden_grad_here),
                (target_hbm, target_out),
                (land_hbm, land_out),
                (fire_hbm, fire_out),
                (gate_bias_hbm, gate_bias_here),
                (readout_hbm, readout_here),
            )
        )
    ]
    for copy in copies:
        copy.start()
    columns = jnp.zeros((channels, width), F32)
    second = jnp.zeros((channels, width), F32)
    for index in range(row_count):
        row = wide[pl.ds(index, channels, stride=row_count), :]
        rows_out[index] = row.astype(BF16)
        columns = edge_columns(row, index + 1, columns)
        second = second_columns(row, index + 1, second)
    columns_out[...] = columns
    second_out[...] = second
    for copy in copies:
        copy.wait()
    hidden_grad_out[...] = hidden_grad_here[...].astype(F32).reshape(hidden_grad_out.shape)
    bias_wide_out[...] = down_rows(gate_bias_here[...], width)
    readout_wide_out[...] = down_rows(readout_here[...], width)
    hid = hidden_grad_here.shape[0]
    cell_strip = jnp.zeros((hid, width), F32)
    hidden_grad_strip = jnp.zeros((hid, width), F32)
    fields_strip = jnp.zeros((8, width), F32)
    for index in range(row_count):
        strided = pl.ds(index, hid, stride=row_count)
        cell_strip = edge_columns(cell_out[strided, :], index + 1, cell_strip)
        hidden_grad_strip = edge_columns(hidden_grad_out[strided, :], index + 1, hidden_grad_strip)
        at = slice(index, index + 1)
        fields = [target_out[at, :], land_out[at, :].astype(F32), fire_out[at, :].astype(F32)]
        fields = jnp.concatenate(fields + [jnp.zeros((5, width), F32)], axis=0)
        fields_strip = edge_columns(fields, index + 1, fields_strip)
    cell_strip_out[...] = cell_strip
    hidden_grad_strip_out[...] = hidden_grad_strip
    fields_strip_out[...] = fields_strip


def columns_kernel(row_count, groups, columns, outer, inner, packed_out, *whole_out):
    north, south = row_halo(inner, outer)
    value = edge_columns(north, 0, columns[...].astype(F32))
    value = edge_columns(south, row_count + 1, value)
    packed_out[...] = packed(value, groups).astype(BF16)
    for out in whole_out:
        out[...] = value.astype(BF16)


def encode(bias):
    high = bias.astype(BF16).astype(F32)
    return jnp.concatenate([high, bias - high], axis=0)


def decode(block):
    return block[0:8] + block[8:16]


def cell_step(part, cell_before, hidden_grad, target, land, fire, readout):
    hid = part.shape[0] // 4
    input_gate = 0.5 + 0.5 * jnp.tanh(0.5 * part[0:hid])
    forget_gate = 0.5 + 0.5 * jnp.tanh(0.5 * part[hid : 2 * hid])
    output_gate = 0.5 + 0.5 * jnp.tanh(0.5 * part[2 * hid : 3 * hid])
    candidate = jnp.tanh(part[3 * hid : 4 * hid])
    cell_next = land * (forget_gate * cell_before + input_gate * candidate)
    squashed = jnp.tanh(cell_next)
    hidden_next = (output_gate * squashed).astype(BF16).astype(F32)
    predicted = jnp.sum(readout * hidden_next, axis=0, keepdims=True)
    total_grad = hidden_grad + 2.0 * (fire * (predicted - target)) * readout
    cell_grad = land * total_grad * output_gate * (1.0 - squashed * squashed)
    pre_grad = jnp.concatenate(
        [
            cell_grad * candidate * input_gate * (1.0 - input_gate),
            cell_grad * cell_before * forget_gate * (1.0 - forget_gate),
            total_grad * squashed * output_gate * (1.0 - output_gate),
            cell_grad * input_gate * (1.0 - candidate * candidate),
        ],
        axis=0,
    )
    return hidden_next, cell_next, cell_grad * forget_gate, pre_grad


def gates_kernel(
    place,
    rows_in,
    inner_row,
    outer_row,
    second,
    cell_prev,
    weights,
    hidden_grad,
    target,
    land,
    fire,
    bias_wide,
    readout_wide,
    hidden_out,
    cell_out,
    grad_cell_out,
    pre_out,
    second_out,
    sums,
    bias_out,
    shifted,
):
    row_count, channels, width = rows_in.shape
    gate_count = weights.shape[0]
    hid = gate_count // 4
    half_gates = place.half_gates
    north, south = row_halo(inner_row, outer_row)
    columns = second_columns(north, 0, second[...])
    second_out[...] = second_columns(south, row_count + 1, columns).astype(BF16)
    for position in range(row_count + 2):
        if position == 0:
            row = north
        elif position == row_count + 1:
            row = south
        else:
            row = rows_in[position - 1].astype(F32)
        at = pl.ds(position * width, width)
        shifted[0:channels, at] = rolled(row, 1).astype(BF16)
        shifted[channels : 2 * channels, at] = row.astype(BF16)
        shifted[2 * channels : 3 * channels, at] = rolled(row, -1).astype(BF16)

    bias_total = jnp.zeros((gate_count, width), F32)
    lane = lanes((gate_count, width))
    inside = (lane > 0) & (lane < width - 1)
    readout = readout_wide[...]
    pair = 2 if row_count % 2 == 0 else 1
    for base in range(0, row_count, pair):
        preact = jnp.zeros((gate_count, pair * width), F32)
        for a in range(3):
            preact += jnp.dot(
                weights[:, pl.ds(3 * a * channels, 3 * channels)],
                shifted[:, pl.ds((base + a) * width, pair * width)],
                preferred_element_type=F32,
            )
        for offset in range(pair):
            index = base + offset
            strided = pl.ds(index, hid, stride=row_count)
            at = slice(index, index + 1)
            hidden_next, cell_next, grad_cell, pre_grad = cell_step(
                preact[:, offset * width : (offset + 1) * width] + bias_wide[...],
                cell_prev[strided, :],
                hidden_grad[strided, :],
                target[at, :],
                land[at, :].astype(F32),
                fire[at, :].astype(F32),
                readout,
            )
            hidden_out[strided, :] = hidden_next
            cell_out[strided, :] = cell_next
            grad_cell_out[strided, :] = grad_cell
            pre_grad = jnp.where(inside, pre_grad, 0.0)
            bias_total += pre_grad
            pre_out[:, pl.ds(index * width, width)] = pre_grad.astype(BF16)
    bias_out[...] = bias_total

    for a in range(3):
        product = lax.dot_general(
            pre_out[...],
            shifted[:, pl.ds(a * width, row_count * width)],
            ACROSS,
            preferred_element_type=F32,
        )
        for b in range(3):
            for half in range(2):
                at = half * place.half_rows + (3 * a + b) * half_gates
                sums[at : at + half_gates, :] = product[
                    half * half_gates : (half + 1) * half_gates, b * channels : (b + 1) * channels
                ]
    used = place.taps * half_gates
    if place.half_rows > used:
        for half in range(2):
            at = half * place.half_rows
            sums[at + used : at + place.half_rows, :] = jnp.zeros(
                (place.half_rows - used, channels), F32
            )


def add_strip(place, half, sums, pre_strip, patches, out):
    half_gates, channels = place.half_gates, sums.shape[1]
    gates = pre_strip[pl.ds(pl.multiple_of(half * half_gates, half_gates), half_gates), :]
    product = lax.dot_general(gates, patches[...], ACROSS, preferred_element_type=F32)
    base = half * place.half_rows
    for tap in range(place.taps):
        at = pl.ds(pl.multiple_of(base + tap * half_gates, 8), half_gates)
        value = sums[at, :] + product[:, tap * channels : (tap + 1) * channels]
        out[tap * half_gates : (tap + 1) * half_gates, :] = value.astype(out.dtype)
    used = place.taps * half_gates
    if place.half_rows > used:
        rest = jnp.zeros((place.half_rows - used, channels), out.dtype)
        out[used:, :] = rest


def strip_kernel(
    place,
    row_count,
    edge,
    second,
    outer_column,
    inner_column,
    weights,
    bias_wide,
    readout_wide,
    cell_strip,
    hidden_grad_strip,
    fields_strip,
    sums,
    send_out,
    pre_out,
    pre_wide_out,
    patches,
    hidden_out,
    cell_out,
    grad_cell_out,
):
    channels, width = edge.shape
    west, east = column_halo(inner_column, outer_column, GROUPS)
    near_first = lanes((channels, width)) < LAST
    inner = second[...].astype(F32)
    columns = (
        jnp.where(near_first, rolled(west, -LAST), inner),
        edge[...].astype(F32),
        jnp.where(near_first, inner, rolled(east, LAST)),
    )
    for a in range(3):
        for b in range(3):
            at = (3 * a + b) * channels
            patches[at : at + channels, :] = rolled(columns[b], 1 - a).astype(BF16)
    preact = jnp.dot(weights[...], patches[...], preferred_element_type=F32) + bias_wide[...]
    hidden_next, cell_next, grad_cell, pre_grad = cell_step(
        preact,
        cell_strip[...],
        hidden_grad_strip[...],
        fields_strip[0:1, :],
        fields_strip[1:2, :],
        fields_strip[2:3, :],
        readout_wide[...],
    )
    hidden_out[...] = hidden_next
    cell_out[...] = cell_next
    grad_cell_out[...] = grad_cell
    lane = lanes(pre_grad.shape)
    lane = jnp.where(lane >= LAST, lane - LAST, lane)
    pre_grad = jnp.where((lane >= 1) & (lane <= row_count), pre_grad, 0.0)
    pre_out[...] = pre_grad.astype(BF16)
    pre_wide_out[...] = pre_grad
    add_strip(place, 1 - place.rank(0), sums, pre_out, patches, send_out)


def keep_kernel(place, sums, pre_strip, patches, bias_partial, pre_wide, out, bias_out):
    add_strip(place, place.rank(0), sums, pre_strip, patches, out)
    channels = sums.shape[1]
    bias_total = bias_partial[...] + pre_wide[...]
    ones = jnp.ones((8, bias_total.shape[1]), BF16)
    high = bias_total.astype(BF16)
    low = (bias_total - high.astype(F32)).astype(BF16)
    flat = lax.dot_general(ones, high, ACROSS, preferred_element_type=F32)
    flat += lax.dot_general(ones, low, ACROSS, preferred_element_type=F32)
    odd = lax.broadcasted_iota(jnp.int32, (8, channels), 0) % 2 == 1
    bias_out[...] = jnp.where(odd, flat[:, channels : 2 * channels], flat[:, 0:channels])


def edges_kernel(
    row_count,
    hidden,
    cell,
    grad_cell,
    pre,
    hidden_strip,
    cell_strip,
    grad_cell_strip,
    pre_strip,
    hidden_hbm,
    cell_hbm,
    grad_cell_hbm,
    pre_out,
    inner_out,
    outer_out,
    hidden_low,
    hidden_here,
    cell_here,
    grad_cell_here,
    left,
):
    hid, _, width = hidden_low.shape
    leaving = []
    for source, strip, here, ready, target in (
        (cell, cell_strip, cell_here, cell_here, cell_hbm),
        (grad_cell, grad_cell_strip, grad_cell_here, grad_cell_here, grad_cell_hbm),
        (hidden, hidden_strip, hidden_here, hidden_low, hidden_hbm),
    ):
        columns = strip[...]
        for index in range(row_count):
            strided = pl.ds(index, hid, stride=row_count)
            here[strided, :] = at_edges(source[strided, :], index + 1, columns)
        if ready is hidden_low:
            hidden_low[...] = here[...].reshape(hidden_low.shape).astype(BF16)
        leaving.append(pltpu.make_async_copy(ready, target, left.at[len(leaving)]))
        leaving[-1].start()
    first, last = None, None
    columns = pre_strip[...].astype(F32)
    for index in range(row_count):
        at = pl.ds(index * width, width)
        row = at_edges(pre[:, at].astype(F32), index + 1, columns)
        pre_out[:, at] = row.astype(BF16)
        first = row if index == 0 else first
        last = row
    row_sends(first, last, inner_out, outer_out)
    for copy in leaving:
        copy.wait()


def pair_kernel(place, keep, bias, received, *outs):
    sends, keep_out, scratch = outs[:-2], outs[-2], outs[-1]
    chunk = place.chunk
    rank = place.plane_rank()
    scratch[...] = keep[...] + received[...].astype(F32)
    block = encode(bias[...]).astype(BF16)
    for step, send in zip(range(place.plane - 1, 0, -1), sends):
        send[0:BIAS_ROWS, :] = block
        at = pl.ds(pl.multiple_of((rank ^ step) * chunk, 8), chunk)
        send[BIAS_ROWS:, :] = scratch[at, :].astype(BF16)
    keep_out[...] = scratch[pl.ds(pl.multiple_of(rank * chunk, 8), chunk), :]


def plane_kernel(keep, bias, *refs):
    received, out = refs[:-2], refs[-1]
    total, bias_total = keep[...], bias[...]
    for ref in received:
        total += ref[BIAS_ROWS:, :].astype(F32)
        bias_total += decode(ref[0:BIAS_ROWS, :].astype(F32))
    out[0:BIAS_ROWS, :] = encode(bias_total).astype(BF16)
    out[BIAS_ROWS:, :] = total.astype(BF16)


def join_kernel(*refs):
    blocks, out = refs[:-2], refs[-1]
    for index, block in enumerate(blocks):
        out[index] = block[...]


def add_kernel(scale, own, received, out):
    here, there = own[...].astype(F32), received[...].astype(F32)
    bias = (decode(here[0:BIAS_ROWS]) + decode(there[0:BIAS_ROWS])) * scale
    out[0:BIAS_ROWS, :] = encode(bias).astype(BF16)
    out[BIAS_ROWS:, :] = ((here[BIAS_ROWS:] + there[BIAS_ROWS:]) * scale).astype(BF16)


def store_half(place, half, blocks, out, wide, left):
    chunk, half_gates = place.chunk, place.half_gates
    gates = pl.ds(pl.multiple_of(half * half_gates, half_gates), half_gates)
    rank = place.plane_rank()
    for step, block in enumerate(blocks):
        at = pl.ds(pl.multiple_of((rank ^ step) * chunk, 8), chunk)
        wide[at, :] = block[BIAS_ROWS:, :].astype(F32)
    copies = []
    for tap in range(place.taps):
        source = wide.at[tap * half_gates : (tap + 1) * half_gates, :]
        copies.append(pltpu.make_async_copy(source, out.at[tap, gates, :], left.at[tap]))
        copies[-1].start()
    return copies


def in_steps(place, early, late):
    return [early.at[0], late] + [early.at[index] for index in range(1, place.plane - 1)]


def own_half_kernel(place, late, early, out, bias_out, wide, left):
    blocks = in_steps(place, early, late)
    copies = store_half(place, place.rank(0), blocks, out, wide, left)
    rank = place.plane_rank()
    bias = decode(blocks[0][0:BIAS_ROWS, :].astype(F32))
    for step in range(1, place.plane):
        bias = pick(rank == step, decode(blocks[step][0:BIAS_ROWS, :].astype(F32)), bias)
    bias_out[...] = bias
    for copy in copies:
        copy.wait()


def other_half_kernel(
    place, bias_own, early, late, after, out_before, out, bias_out, wide, bias_here, left
):
    del after, out_before
    blocks = in_steps(place, early, late)
    copies = store_half(place, 1 - place.rank(0), blocks, out, wide, left)
    rank = place.plane_rank()
    bias = decode(blocks[0][0:BIAS_ROWS, :].astype(F32))
    for step in range(1, place.plane):
        bias = pick(rank == step, decode(blocks[step][0:BIAS_ROWS, :].astype(F32)), bias)
    bias += bias_own[...]
    width = bias.shape[1]
    for index in range(bias_here.shape[0] // width):
        bias_here[pl.ds(index * width, width)] = bias[index]
    bias_copy = pltpu.make_async_copy(bias_here, bias_out, left.at[place.taps])
    bias_copy.start()
    bias_copy.wait()
    for copy in copies:
        copy.wait()


def field_kernel(pre, weights, wide_out, turned_out, done_out, shifted):
    done_out[...] = jnp.zeros(done_out.shape, F32)
    gate_count, cells = pre.shape
    width = wide_out.shape[1]
    channels = weights.shape[1] // 9
    row_count = cells // width
    lane = lanes((gate_count, width))
    for index in range(row_count):
        at = pl.ds(index * width, width)
        row = pre[:, at].astype(F32)
        left = jnp.where(lane == 0, 0.0, rolled(row, 1))
        right = jnp.where(lane == width - 1, 0.0, rolled(row, -1))
        shifted[0:gate_count, at] = right.astype(BF16)
        shifted[gate_count : 2 * gate_count, at] = pre[:, at]
        shifted[2 * gate_count : 3 * gate_count, at] = left.astype(BF16)
    for a in range(3):
        for b in range(3):
            turned_out[a, :, b * gate_count : (b + 1) * gate_count] = (
                weights[:, pl.ds((3 * a + b) * channels, channels)].T
            )

    def product(a, index, count):
        return jnp.dot(
            turned_out[a],
            shifted[:, pl.ds(index * width, count * width)],
            preferred_element_type=F32,
        )

    pair = 2 if row_count % 2 == 0 else 1
    for base in range(0, row_count, pair):
        total = product(1, base, pair)
        for a, first in ((2, base - 1), (0, base + 1)):
            low, high = max(first, 0), min(first + pair, row_count)
            if low >= high:
                continue
            part = product(a, low, high - low)
            blank = jnp.zeros((channels, width), F32)
            parts = [blank] * (low - first) + [part] + [blank] * (first + pair - high)
            total += jnp.concatenate(parts, axis=1)
        for offset in range(pair):
            value = total[:, offset * width : (offset + 1) * width]
            wide_out[pl.ds(base + offset, channels, stride=row_count), :] = value


def field_halo_kernel(
    place,
    wide,
    turned,
    outer_row,
    inner_row,
    outer_column,
    inner_column,
    inputs_out,
    hidden_out,
    done_out,
    total,
):
    done_out[...] = jnp.zeros(done_out.shape, F32)
    hid, row_count, width = hidden_out.shape
    channels = turned.shape[1]
    gate_count = turned.shape[2] // 3
    north, south = row_halo(inner_row, outer_row)
    west, east = column_halo(inner_column, outer_column, PRE_GROUPS)
    lane = lanes((gate_count, width))
    lat = place.position()[0]

    def row_part(taps, row, position):
        left = jnp.where(lane == 0, rolled(west, -LAST - position), rolled(row, 1))
        right = rolled(east, width - 1 - position)
        right = jnp.where(lane == width - 1, right, rolled(row, -1))
        stack = jnp.concatenate([right, row, left], axis=0).astype(BF16)
        return jnp.dot(taps, stack, preferred_element_type=F32)

    above = row_part(turned[jnp.where(lat == 0, 0, 2)], north, 0)
    below = row_part(turned[jnp.where(lat == place.lat - 1, 2, 0)], south, row_count + 1)

    inside = (lane >= 1) & (lane <= row_count)
    west = jnp.where(inside, rolled(west, -LAST), 0.0)
    east = jnp.where(inside, east, 0.0)
    sides = [rolled(west, a - 1) for a in range(3)] + [rolled(east, LAST + a - 1) for a in range(3)]
    taps = [turned[a, :, 2 * gate_count : 3 * gate_count] for a in range(3)]
    taps += [turned[a, :, 0:gate_count] for a in range(3)]
    columns = jnp.dot(
        jnp.concatenate(taps, axis=1),
        jnp.concatenate(sides, axis=0).astype(BF16),
        preferred_element_type=F32,
    )
    blank = jnp.zeros((channels, width), F32)
    for index in range(row_count):
        strided = pl.ds(index, channels, stride=row_count)
        value = wide[strided, :] + at_edges(blank, index + 1, columns)
        if index == 0:
            value += above
        if index == row_count - 1:
            value += below
        total[strided, :] = value
    size = (channels - hid) * row_count
    inputs_out[...] = total[0:size, :].reshape(inputs_out.shape).astype(BF16)
    hidden_out[...] = total[size:, :].reshape(hidden_out.shape).astype(BF16)


def body(
    place,
    inputs_below,
    hidden_prev,
    cell_prev,
    kernel_weights,
    gate_bias,
    readout,
    target_field,
    land_mask,
    fire_mask,
    hidden_grad,
):
    hid, row_count, width = hidden_prev.shape
    gate_count, channels = kernel_weights.shape[1:]
    cells = row_count * width
    halo_cells = (row_count + 2) * width
    scaling = 1.0 / math.sqrt(cells * place.lat * place.lon)
    bind = functools.partial
    inner_rows, outer_rows = place.pairs(place.inner_rows), place.pairs(place.outer_rows)
    inner_columns = place.pairs(place.inner_columns)
    outer_columns = place.pairs(place.outer_columns)
    flat = sds((hid * row_count, width), F32)
    strip = sds((hid, width), F32)

    inner, outer, wide = call(
        pack_kernel,
        (
            sds((channels, width), BF16),
            sds((channels, width), BF16),
            sds((channels * row_count, width), F32),
        ),
        [
            pltpu.VMEM(inputs_below.shape, BF16),
            pltpu.VMEM(hidden_prev.shape, BF16),
            pltpu.SemaphoreType.DMA((4,)),
        ],
        remote=2,
        moved=4 * channels * cells,
    )(inputs_below, hidden_prev)
    inner, outer = permuted(inner, inner_rows), permuted(outer, outer_rows)
    (
        rows,
        columns,
        second,
        cell_strip,
        hidden_grad_strip,
        fields_strip,
        cell_here,
        weights_here,
        hidden_grad_here,
        target_here,
        land_here,
        fire_here,
        bias_wide,
        readout_wide,
    ) = call(
        prepare_kernel,
        (
            sds((row_count, channels, width), BF16),
            sds((channels, width), F32),
            sds((channels, width), F32),
            strip,
            strip,
            sds((8, width), F32),
            flat,
            sds((gate_count, place.taps * channels), BF16),
            flat,
            sds(target_field.shape, F32),
            sds(land_mask.shape, jnp.int32),
            sds(fire_mask.shape, jnp.int32),
            sds((gate_count, width), F32),
            sds((hid, width), F32),
        ),
        [
            pltpu.VMEM(hidden_grad.shape, BF16),
            pltpu.VMEM(gate_bias.shape, F32),
            pltpu.VMEM(readout.shape, F32),
            pltpu.SemaphoreType.DMA((7 + place.taps,)),
        ],
        remote=8,
        moved=6_000_000,
    )(
        wide,
        cell_prev.reshape(hid * row_count, width),
        kernel_weights,
        hidden_grad,
        target_field,
        land_mask,
        fire_mask,
        gate_bias,
        readout,
    )
    columns, edge = call(
        bind(columns_kernel, row_count, GROUPS),
        (sds((channels // GROUPS, width), BF16), sds((channels, width), BF16)),
    )(columns, outer, inner)
    inner_column = permuted(columns, inner_columns)
    outer_column = permuted(columns, outer_columns)
    hidden_rows, cell_rows, grad_cell_rows, pre, second, sums, bias = call(
        bind(gates_kernel, place),
        (
            flat,
            flat,
            flat,
            sds((gate_count, cells), BF16),
            sds((channels, width), BF16),
            sds((2 * place.half_rows, channels), F32),
            sds((gate_count, width), F32),
        ),
        [pltpu.VMEM((3 * channels, halo_cells), BF16)],
        flops=4 * 9 * gate_count * channels * cells,
        moved=6_000_000,
        transcendentals=5 * hid * cells,
    )(
        rows,
        inner,
        outer,
        second,
        cell_here,
        weights_here,
        hidden_grad_here,
        target_here,
        land_here,
        fire_here,
        bias_wide,
        readout_wide,
    )
    send, pre_strip, pre_wide, patches, *strips = call(
        bind(strip_kernel, place, row_count),
        (
            sds((place.half_rows, channels), BF16),
            sds((gate_count, width), BF16),
            sds((gate_count, width), F32),
            sds((place.taps * channels, width), BF16),
            strip,
            strip,
            strip,
        ),
    )(
        edge,
        second,
        outer_column,
        inner_column,
        weights_here,
        bias_wide,
        readout_wide,
        cell_strip,
        hidden_grad_strip,
        fields_strip,
        sums,
    )
    keep, bias = call(
        bind(keep_kernel, place),
        (sds((place.half_rows, channels), F32), sds((8, channels), F32)),
    )(sums, pre_strip, patches, bias, pre_wide)
    hidden_next, cell_next, grad_cell, pre, pre_inner, pre_outer = call(
        bind(edges_kernel, row_count),
        (
            sds((hid, row_count, width), BF16),
            flat,
            flat,
            sds((gate_count, cells), BF16),
            sds((gate_count, width), BF16),
            sds((gate_count, width), BF16),
        ),
        [
            pltpu.VMEM((hid, row_count, width), BF16),
            pltpu.VMEM(flat.shape, F32),
            pltpu.VMEM(flat.shape, F32),
            pltpu.VMEM(flat.shape, F32),
            pltpu.SemaphoreType.DMA((3,)),
        ],
        leaving=3,
        moved=4_000_000,
    )(hidden_rows, cell_rows, grad_cell_rows, pre, *strips, pre_strip)
    pre_inner, pre_outer = permuted(pre_inner, inner_rows), permuted(pre_outer, outer_rows)
    pre_columns = call(
        bind(columns_kernel, row_count, PRE_GROUPS),
        (sds((gate_count // PRE_GROUPS, width), BF16),),
    )(pre_strip, pre_outer, pre_inner)[0]

    block = sds((BIAS_ROWS + place.chunk, channels), BF16)
    token = sds((8, width), F32)
    steps = range(place.plane - 1, 0, -1)
    *sends, keep = call(
        bind(pair_kernel, place),
        (*[block for _ in steps], sds((place.chunk, channels), F32)),
        [pltpu.VMEM((place.half_rows, channels), F32)],
    )(keep, bias, permuted(send, place.phase_pairs(0)))
    received = [permuted(send, place.plane_pairs(step)) for step, send in zip(steps, sends)]
    field, turned, field_done = call(
        field_kernel,
        (
            sds((channels * row_count, width), F32),
            sds((3, channels, 3 * gate_count), BF16),
            token,
        ),
        [pltpu.VMEM((3 * gate_count, cells), BF16)],
        flops=2 * 9 * gate_count * channels * cells,
        moved=3_000_000,
    )(pre, weights_here)
    part = call(plane_kernel, block)(keep, bias, *received, field_done)
    pre_inner_columns = permuted(pre_columns, inner_columns)
    pre_outer_columns = permuted(pre_columns, outer_columns)
    phases = len(place.orders[0])
    for phase in range(1, phases):
        is_last = phase == phases - 1
        part = call(bind(add_kernel, scaling if is_last else 1.0), block)(
            part, permuted(part, place.phase_pairs(phase))
        )
    received = [permuted(part, place.plane_pairs(step)) for step in steps[::-1]]
    grad_inputs, grad_hidden, field_done = call(
        bind(field_halo_kernel, place),
        (
            sds((channels - hid, row_count, width), BF16),
            sds((hid, row_count, width), BF16),
            token,
        ),
        [pltpu.VMEM((channels * row_count, width), F32)],
        flops=40 * gate_count * channels * cells * 9,
        moved=2_000_000,
    )(field, turned, pre_outer, pre_inner, pre_outer_columns, pre_inner_columns)
    early = call(join_kernel, sds((place.plane - 1, *block.shape), BF16))(
        part, *received[1:], field_done
    )
    late = received[0]
    early_other = permuted(early, place.phase_pairs(0))
    late_other = permuted(late, place.phase_pairs(0))
    half = [pltpu.VMEM((place.half_rows, channels), F32)]
    grad_kernel, bias = call(
        bind(own_half_kernel, place),
        (sds(kernel_weights.shape, F32), sds((8, channels), F32)),
        half + [pltpu.SemaphoreType.DMA((place.taps,))],
        leaving=1,
        flops=40 * gate_count * channels * cells * 9,
        moved=6 * place.half_rows * channels,
    )(late, early)
    grad_kernel, grad_bias = call(
        bind(other_half_kernel, place),
        (sds(kernel_weights.shape, F32), sds((gate_count,), F32)),
        half + [pltpu.VMEM((gate_count,), F32), pltpu.SemaphoreType.DMA((place.taps + 1,))],
        remote=1,
        leaving=2,
        aliases={4: 0},
        moved=6 * place.half_rows * channels,
    )(bias, early_other, late_other, target_here, grad_kernel)
    shape = hidden_prev.shape
    return (
        hidden_next,
        cell_next.reshape(shape),
        grad_inputs,
        grad_hidden,
        grad_cell.reshape(shape),
        grad_kernel,
        grad_bias,
    )


def solution(mesh):
    lat_count, lon_count = mesh.shape["lat"], mesh.shape["lon"]
    split = Mesh(mesh.devices.reshape(lat_count // 2, 2, lon_count // 2, 2), AXES)
    field = P(None, ("band", "core"), ("reach", "near"))
    flat = P(("band", "core"), ("reach", "near"))

    def run(*args):
        place = Layout(lat_count, lon_count, *args[3].shape[:2])
        return jax.shard_map(
            functools.partial(body, place),
            mesh=split,
            in_specs=(field, field, field, P(), P(), P(), flat, flat, flat, field),
            out_specs=(field, field, field, field, field, P(), P()),
            check_vma=False,
        )(*args)

    return run
```

```python
import functools
import math

import jax
import jax.numpy as jnp
from jax import lax
from jax.experimental import pallas as pl
from jax.experimental.pallas import tpu as pltpu
from jax.sharding import Mesh, PartitionSpec as P

F32 = jnp.float32
BF16 = jnp.bfloat16
AXES = ("band", "core", "reach", "near")
BIAS_ROWS = 16
GROUPS = 4
PRE_GROUPS = 4
LAST = 16
VMEM = pl.BlockSpec(memory_space=pltpu.VMEM)
HBM = pl.BlockSpec(memory_space=pltpu.HBM)
ACROSS = (((1,), (1,)), ((), ()))


def sds(shape, dtype):
    return jax.ShapeDtypeStruct(shape, dtype)


def call(
    kernel,
    out_shape,
    scratch=(),
    remote=0,
    leaving=0,
    aliases=None,
    flops=0,
    moved=0,
    transcendentals=0,
):
    several = isinstance(out_shape, tuple)
    shapes = out_shape if several else (out_shape,)
    out_specs = tuple([HBM] * leaving + [VMEM] * (len(shapes) - leaving))

    def run(*args):
        near = len(args) - remote
        far = [pltpu.with_memory_space_constraint(arg, pltpu.HBM) for arg in args[near:]]
        return pl.pallas_call(
            kernel,
            out_shape=out_shape,
            in_specs=[VMEM] * near + [HBM] * remote,
            out_specs=out_specs if several else out_specs[0],
            input_output_aliases=aliases or {},
            scratch_shapes=list(scratch),
            cost_estimate=pl.CostEstimate(
                flops=flops, bytes_accessed=moved, transcendentals=transcendentals
            ),
            compiler_params=pltpu.CompilerParams(vmem_limit_bytes=24 * 1024 * 1024),
        )(*args[:near], *far)

    return run


class Layout:
    def __init__(self, lat_count, lon_count, taps, gate_count):
        self.lat, self.lon = lat_count, lon_count
        self.half = lon_count // 2
        self.taps, self.half_gates = taps, gate_count // 2
        self.plane = lat_count
        whole = [("lon", 1 << k) for k in range(1, lon_count.bit_length() - 1)]
        self.orders = ([("lat", 1)] + whole, [("lat", 1)] + whole[::-1])
        self.half_rows = taps * self.half_gates
        self.chunk = self.half_rows // self.plane
        self.chunk_gates = self.half_gates // self.plane

    def position(self):
        lat = 2 * lax.axis_index("band") + lax.axis_index("core")
        return lat, 2 * lax.axis_index("reach") + lax.axis_index("near")

    def rank(self, phase):
        lat, lon = self.position()

        def digit(order):
            axis, bit = order[phase]
            return ((lat if axis == "lat" else lon) // bit) % 2

        return jnp.where(lat % 2 == 0, digit(self.orders[0]), digit(self.orders[1]))

    def pairs(self, partner):
        result = []
        for lat in range(self.lat):
            for lon in range(self.lon):
                there = partner(lat, lon)
                result.append((lat * self.lon + lon, there[0] * self.lon + there[1]))
        return result

    def phase_pairs(self, phase):
        def partner(lat, lon):
            axis, bit = self.orders[lat % 2][phase]
            return (lat ^ bit, lon) if axis == "lat" else (lat, lon ^ bit)

        return self.pairs(partner)

    def plane_rank(self):
        return 2 * lax.axis_index("band") + lax.axis_index("near")

    def plane_pairs(self, step):
        def partner(lat, lon):
            there = (lat // 2 * 2 + lon % 2) ^ step
            return there // 2 * 2 + lat % 2, lon // 2 * 2 + there % 2

        return self.pairs(partner)

    def inner_rows(self, lat, lon):
        return lat ^ 1, lon

    def outer_rows(self, lat, lon):
        there = lat + 1 if lat % 2 else lat - 1
        if 0 <= there < self.lat:
            return there, lon
        return lat, (lon + self.half) % self.lon

    def inner_columns(self, lat, lon):
        return lat, lon ^ 1

    def outer_columns(self, lat, lon):
        return lat, (lon + (1 if lon % 2 else -1)) % self.lon


def permuted(value, pairs):
    return lax.ppermute(value, AXES, pairs)


def lanes(shape):
    return lax.broadcasted_iota(jnp.int32, shape, len(shape) - 1)


def rolled(value, shift):
    shift %= value.shape[1]
    return pltpu.roll(value, shift, 1) if shift else value


def edge_columns(row, position, columns):
    lane = lanes(row.shape)
    columns = jnp.where(lane == position, rolled(row, position), columns)
    return jnp.where(lane == LAST + position, rolled(row, LAST + position + 1), columns)


def second_columns(row, position, columns):
    lane = lanes(row.shape)
    columns = jnp.where(lane == position, rolled(row, position - 1), columns)
    return jnp.where(lane == LAST + position, rolled(row, LAST + position + 2), columns)


def at_edges(row, position, columns):
    lane = lanes(row.shape)
    width = row.shape[1]
    row = jnp.where(lane == 0, rolled(columns, -position), row)
    return jnp.where(lane == width - 1, rolled(columns, width - 1 - LAST - position), row)


def pick(flag, yes, no):
    return jnp.where(flag, yes, no)


def is_odd(axis):
    return lax.axis_index(axis) % 2 == 1


def row_sends(first, last, inner_out, outer_out):
    odd = is_odd("core")
    inner_out[...] = pick(odd, first, last).astype(BF16)
    outer_out[...] = pick(odd, last, first).astype(BF16)


def row_halo(inner, outer):
    odd = is_odd("core")
    inner, outer = inner[...].astype(F32), outer[...].astype(F32)
    return pick(odd, inner, outer), pick(odd, outer, inner)


def packed(columns, groups):
    count, width = columns.shape[0] // groups, columns.shape[1] // groups
    lane = lanes((count, columns.shape[1]))
    value = columns[0:count]
    for group in range(1, groups):
        part = rolled(columns[group * count : (group + 1) * count], group * width)
        value = jnp.where(lane >= group * width, part, value)
    return value


def unpacked(value, groups):
    width = value.shape[1] // groups
    return jnp.concatenate([rolled(value, -group * width) for group in range(groups)], axis=0)


def column_halo(inner, outer, groups):
    odd = is_odd("near")
    inner, outer = inner[...].astype(F32), outer[...].astype(F32)
    return unpacked(pick(odd, inner, outer), groups), unpacked(pick(odd, outer, inner), groups)


def pack_kernel(below, hidden, inner_out, outer_out, wide_out, below_here, hidden_here, arrived):
    channels, row_count, width = below.shape
    size = channels * row_count
    part = channels // 2
    copies = []
    for source, here in ((below, below_here), (hidden, hidden_here)):
        for at in (pl.ds(0, part), pl.ds(part, part)):
            copies.append(
                pltpu.make_async_copy(source.at[at], here.at[at], arrived.at[len(copies)])
            )
            copies[-1].start()
    for index, copy in enumerate(copies):
        here = (below_here, hidden_here)[index // 2]
        copy.wait()
        value = here[pl.ds(index % 2 * part, part)].astype(F32)
        at = pl.ds(index * part * row_count, part * row_count)
        wide_out[at, :] = value.reshape(part * row_count, width)
    edges = [
        wide_out[pl.ds(index, 2 * channels, stride=row_count), :] for index in (0, row_count - 1)
    ]
    row_sends(edges[0], edges[1], inner_out, outer_out)


def down_rows(values, width):
    count = values.shape[0]
    return jnp.broadcast_to(values[None, :], (width, count)).T


def prepare_kernel(
    wide,
    cell_hbm,
    weights_hbm,
    hidden_grad_hbm,
    target_hbm,
    land_hbm,
    fire_hbm,
    gate_bias_hbm,
    readout_hbm,
    rows_out,
    columns_out,
    second_out,
    cell_strip_out,
    hidden_grad_strip_out,
    fields_strip_out,
    cell_out,
    weights_out,
    hidden_grad_out,
    target_out,
    land_out,
    fire_out,
    bias_wide_out,
    readout_wide_out,
    hidden_grad_here,
    gate_bias_here,
    readout_here,
    arrived,
):
    row_count, channels, width = rows_out.shape
    copies = [
        pltpu.make_async_copy(source, target, arrived.at[index])
        for index, (source, target) in enumerate(
            (
                (cell_hbm, cell_out),
                *(
                    (weights_hbm.at[tap], weights_out.at[:, pl.ds(tap * channels, channels)])
                    for tap in range(weights_hbm.shape[0])
                ),
                (hidden_grad_hbm, hidden_grad_here),
                (target_hbm, target_out),
                (land_hbm, land_out),
                (fire_hbm, fire_out),
                (gate_bias_hbm, gate_bias_here),
                (readout_hbm, readout_here),
            )
        )
    ]
    for copy in copies:
        copy.start()
    columns = jnp.zeros((channels, width), F32)
    second = jnp.zeros((channels, width), F32)
    for index in range(row_count):
        row = wide[pl.ds(index, channels, stride=row_count), :]
        rows_out[index] = row.astype(BF16)
        columns = edge_columns(row, index + 1, columns)
        second = second_columns(row, index + 1, second)
    columns_out[...] = columns
    second_out[...] = second
    for copy in copies:
        copy.wait()
    hidden_grad_out[...] = hidden_grad_here[...].astype(F32).reshape(hidden_grad_out.shape)
    bias_wide_out[...] = down_rows(gate_bias_here[...], width)
    readout_wide_out[...] = down_rows(readout_here[...], width)
    hid = hidden_grad_here.shape[0]
    cell_strip = jnp.zeros((hid, width), F32)
    hidden_grad_strip = jnp.zeros((hid, width), F32)
    fields_strip = jnp.zeros((8, width), F32)
    for index in range(row_count):
        strided = pl.ds(index, hid, stride=row_count)
        cell_strip = edge_columns(cell_out[strided, :], index + 1, cell_strip)
        hidden_grad_strip = edge_columns(hidden_grad_out[strided, :], index + 1, hidden_grad_strip)
        at = slice(index, index + 1)
        fields = [target_out[at, :], land_out[at, :].astype(F32), fire_out[at, :].astype(F32)]
        fields = jnp.concatenate(fields + [jnp.zeros((5, width), F32)], axis=0)
        fields_strip = edge_columns(fields, index + 1, fields_strip)
    cell_strip_out[...] = cell_strip
    hidden_grad_strip_out[...] = hidden_grad_strip
    fields_strip_out[...] = fields_strip


def columns_kernel(row_count, groups, columns, outer, inner, packed_out, *whole_out):
    north, south = row_halo(inner, outer)
    value = edge_columns(north, 0, columns[...].astype(F32))
    value = edge_columns(south, row_count + 1, value)
    packed_out[...] = packed(value, groups).astype(BF16)
    for out in whole_out:
        out[...] = value.astype(BF16)


def encode(bias):
    high = bias.astype(BF16).astype(F32)
    return jnp.concatenate([high, bias - high], axis=0)


def decode(block):
    return block[0:8] + block[8:16]


def cell_step(part, cell_before, hidden_grad, target, land, fire, readout):
    hid = part.shape[0] // 4
    input_gate = 0.5 + 0.5 * jnp.tanh(0.5 * part[0:hid])
    forget_gate = 0.5 + 0.5 * jnp.tanh(0.5 * part[hid : 2 * hid])
    output_gate = 0.5 + 0.5 * jnp.tanh(0.5 * part[2 * hid : 3 * hid])
    candidate = jnp.tanh(part[3 * hid : 4 * hid])
    cell_next = land * (forget_gate * cell_before + input_gate * candidate)
    squashed = jnp.tanh(cell_next)
    hidden_next = (output_gate * squashed).astype(BF16).astype(F32)
    predicted = jnp.sum(readout * hidden_next, axis=0, keepdims=True)
    total_grad = hidden_grad + 2.0 * (fire * (predicted - target)) * readout
    cell_grad = land * total_grad * output_gate * (1.0 - squashed * squashed)
    pre_grad = jnp.concatenate(
        [
            cell_grad * candidate * input_gate * (1.0 - input_gate),
            cell_grad * cell_before * forget_gate * (1.0 - forget_gate),
            total_grad * squashed * output_gate * (1.0 - output_gate),
            cell_grad * input_gate * (1.0 - candidate * candidate),
        ],
        axis=0,
    )
    return hidden_next, cell_next, cell_grad * forget_gate, pre_grad


def gates_kernel(
    place,
    rows_in,
    inner_row,
    outer_row,
    second,
    cell_prev,
    weights,
    hidden_grad,
    target,
    land,
    fire,
    bias_wide,
    readout_wide,
    hidden_out,
    cell_out,
    grad_cell_out,
    pre_out,
    second_out,
    sums,
    bias_out,
    shifted,
):
    row_count, channels, width = rows_in.shape
    gate_count = weights.shape[0]
    hid = gate_count // 4
    half_gates = place.half_gates
    north, south = row_halo(inner_row, outer_row)
    columns = second_columns(north, 0, second[...])
    second_out[...] = second_columns(south, row_count + 1, columns).astype(BF16)
    for position in range(row_count + 2):
        if position == 0:
            row = north
        elif position == row_count + 1:
            row = south
        else:
            row = rows_in[position - 1].astype(F32)
        at = pl.ds(position * width, width)
        shifted[0:channels, at] = rolled(row, 1).astype(BF16)
        shifted[channels : 2 * channels, at] = row.astype(BF16)
        shifted[2 * channels : 3 * channels, at] = rolled(row, -1).astype(BF16)

    bias_total = jnp.zeros((gate_count, width), F32)
    lane = lanes((gate_count, width))
    inside = (lane > 0) & (lane < width - 1)
    readout = readout_wide[...]
    pair = 2 if row_count % 2 == 0 else 1
    for base in range(0, row_count, pair):
        preact = jnp.zeros((gate_count, pair * width), F32)
        for a in range(3):
            preact += jnp.dot(
                weights[:, pl.ds(3 * a * channels, 3 * channels)],
                shifted[:, pl.ds((base + a) * width, pair * width)],
                preferred_element_type=F32,
            )
        for offset in range(pair):
            index = base + offset
            strided = pl.ds(index, hid, stride=row_count)
            at = slice(index, index + 1)
            hidden_next, cell_next, grad_cell, pre_grad = cell_step(
                preact[:, offset * width : (offset + 1) * width] + bias_wide[...],
                cell_prev[strided, :],
                hidden_grad[strided, :],
                target[at, :],
                land[at, :].astype(F32),
                fire[at, :].astype(F32),
                readout,
            )
            hidden_out[strided, :] = hidden_next
            cell_out[strided, :] = cell_next
            grad_cell_out[strided, :] = grad_cell
            pre_grad = jnp.where(inside, pre_grad, 0.0)
            bias_total += pre_grad
            pre_out[:, pl.ds(index * width, width)] = pre_grad.astype(BF16)
    bias_out[...] = bias_total

    for a in range(3):
        product = lax.dot_general(
            pre_out[...],
            shifted[:, pl.ds(a * width, row_count * width)],
            ACROSS,
            preferred_element_type=F32,
        )
        for b in range(3):
            for half in range(2):
                at = half * place.half_rows + (3 * a + b) * half_gates
                sums[at : at + half_gates, :] = product[
                    half * half_gates : (half + 1) * half_gates, b * channels : (b + 1) * channels
                ]


def add_strip(place, half, sums, pre_strip, patches, out):
    half_gates, channels = place.half_gates, sums.shape[1]
    gates = pre_strip[pl.ds(pl.multiple_of(half * half_gates, half_gates), half_gates), :]
    product = lax.dot_general(gates, patches[...], ACROSS, preferred_element_type=F32)
    base = half * place.half_rows
    size = place.chunk_gates
    for tap in range(place.taps):
        at = pl.ds(pl.multiple_of(base + tap * half_gates, 8), half_gates)
        value = sums[at, :] + product[:, tap * channels : (tap + 1) * channels]
        value = value.astype(out.dtype)
        for index in range(place.plane):
            to = (index * place.taps + tap) * size
            out[to : to + size, :] = value[index * size : (index + 1) * size]


def strip_kernel(
    place,
    row_count,
    edge,
    second,
    outer_column,
    inner_column,
    weights,
    bias_wide,
    readout_wide,
    cell_strip,
    hidden_grad_strip,
    fields_strip,
    sums,
    send_out,
    pre_out,
    pre_wide_out,
    patches,
    hidden_out,
    cell_out,
    grad_cell_out,
):
    channels, width = edge.shape
    west, east = column_halo(inner_column, outer_column, GROUPS)
    near_first = lanes((channels, width)) < LAST
    inner = second[...].astype(F32)
    columns = (
        jnp.where(near_first, rolled(west, -LAST), inner),
        edge[...].astype(F32),
        jnp.where(near_first, inner, rolled(east, LAST)),
    )
    for a in range(3):
        for b in range(3):
            at = (3 * a + b) * channels
            patches[at : at + channels, :] = rolled(columns[b], 1 - a).astype(BF16)
    preact = jnp.dot(weights[...], patches[...], preferred_element_type=F32) + bias_wide[...]
    hidden_next, cell_next, grad_cell, pre_grad = cell_step(
        preact,
        cell_strip[...],
        hidden_grad_strip[...],
        fields_strip[0:1, :],
        fields_strip[1:2, :],
        fields_strip[2:3, :],
        readout_wide[...],
    )
    hidden_out[...] = hidden_next
    cell_out[...] = cell_next
    grad_cell_out[...] = grad_cell
    lane = lanes(pre_grad.shape)
    lane = jnp.where(lane >= LAST, lane - LAST, lane)
    pre_grad = jnp.where((lane >= 1) & (lane <= row_count), pre_grad, 0.0)
    pre_out[...] = pre_grad.astype(BF16)
    pre_wide_out[...] = pre_grad
    add_strip(place, 1 - place.rank(0), sums, pre_out, patches, send_out)


def keep_kernel(place, sums, pre_strip, patches, bias_partial, pre_wide, out, bias_out):
    add_strip(place, place.rank(0), sums, pre_strip, patches, out)
    channels = sums.shape[1]
    bias_total = bias_partial[...] + pre_wide[...]
    ones = jnp.ones((8, bias_total.shape[1]), BF16)
    high = bias_total.astype(BF16)
    low = (bias_total - high.astype(F32)).astype(BF16)
    flat = lax.dot_general(ones, high, ACROSS, preferred_element_type=F32)
    flat += lax.dot_general(ones, low, ACROSS, preferred_element_type=F32)
    odd = lax.broadcasted_iota(jnp.int32, (8, channels), 0) % 2 == 1
    bias_out[...] = jnp.where(odd, flat[:, channels : 2 * channels], flat[:, 0:channels])


def edges_kernel(
    row_count,
    hidden,
    cell,
    grad_cell,
    pre,
    hidden_strip,
    cell_strip,
    grad_cell_strip,
    pre_strip,
    hidden_hbm,
    cell_hbm,
    grad_cell_hbm,
    pre_out,
    inner_out,
    outer_out,
    hidden_low,
    hidden_here,
    cell_here,
    grad_cell_here,
    left,
):
    hid, _, width = hidden_low.shape
    leaving = []
    for source, strip, here, ready, target in (
        (cell, cell_strip, cell_here, cell_here, cell_hbm),
        (grad_cell, grad_cell_strip, grad_cell_here, grad_cell_here, grad_cell_hbm),
        (hidden, hidden_strip, hidden_here, hidden_low, hidden_hbm),
    ):
        columns = strip[...]
        for index in range(row_count):
            strided = pl.ds(index, hid, stride=row_count)
            here[strided, :] = at_edges(source[strided, :], index + 1, columns)
        if ready is hidden_low:
            hidden_low[...] = here[...].reshape(hidden_low.shape).astype(BF16)
        leaving.append(pltpu.make_async_copy(ready, target, left.at[len(leaving)]))
        leaving[-1].start()
    first, last = None, None
    columns = pre_strip[...].astype(F32)
    for index in range(row_count):
        at = pl.ds(index * width, width)
        row = at_edges(pre[:, at].astype(F32), index + 1, columns)
        pre_out[:, at] = row.astype(BF16)
        first = row if index == 0 else first
        last = row
    row_sends(first, last, inner_out, outer_out)
    for copy in leaving:
        copy.wait()


def pair_kernel(place, keep, bias, received, *outs):
    sends, keep_out, scratch = outs[:-2], outs[-2], outs[-1]
    chunk = place.chunk
    rank = place.plane_rank()
    scratch[...] = keep[...] + received[...].astype(F32)
    block = encode(bias[...]).astype(BF16)
    for step, send in zip(range(place.plane - 1, 0, -1), sends):
        send[0:BIAS_ROWS, :] = block
        at = pl.ds(pl.multiple_of((rank ^ step) * chunk, 8), chunk)
        send[BIAS_ROWS:, :] = scratch[at, :].astype(BF16)
    keep_out[...] = scratch[pl.ds(pl.multiple_of(rank * chunk, 8), chunk), :]


def plane_kernel(keep, bias, *refs):
    received, out = refs[:-2], refs[-1]
    total, bias_total = keep[...], bias[...]
    for ref in received:
        total += ref[BIAS_ROWS:, :].astype(F32)
        bias_total += decode(ref[0:BIAS_ROWS, :].astype(F32))
    out[0:BIAS_ROWS, :] = encode(bias_total).astype(BF16)
    out[BIAS_ROWS:, :] = total.astype(BF16)


def join_kernel(*refs):
    blocks, out = refs[:-3], refs[-1]
    for index, block in enumerate(blocks):
        out[index] = block[...]


def add_kernel(scale, own, received, out):
    here, there = own[...].astype(F32), received[...].astype(F32)
    bias = (decode(here[0:BIAS_ROWS]) + decode(there[0:BIAS_ROWS])) * scale
    out[0:BIAS_ROWS, :] = encode(bias).astype(BF16)
    out[BIAS_ROWS:, :] = ((here[BIAS_ROWS:] + there[BIAS_ROWS:]) * scale).astype(BF16)


def store_blocks(place, half, blocks, out, wide, left):
    size = place.chunk_gates
    rank = place.plane_rank()
    copies = []
    for step, block in blocks:
        index = len(copies)
        value = block[BIAS_ROWS:, :].astype(F32)
        wide[index] = value.reshape(place.taps, size, value.shape[1])
        first = pl.multiple_of(half * place.half_gates + (rank ^ step) * size, 8)
        target = out.at[:, pl.ds(first, size), :]
        copies.append(pltpu.make_async_copy(wide.at[index], target, left.at[index]))
        copies[-1].start()
    return copies


def plane_bias(place, blocks):
    rank = place.plane_rank()
    bias = jnp.zeros((8, blocks[0][1].shape[1]), F32)
    for step, block in blocks:
        bias = pick(rank == step, decode(block[0:BIAS_ROWS, :].astype(F32)), bias)
    return bias


def first_store_kernel(place, part, last, out, done_out, wide, left):
    done_out[...] = jnp.zeros(done_out.shape, F32)
    blocks = [(0, part), (place.plane - 1, last)]
    for copy in store_blocks(place, place.rank(0), blocks, out, wide, left):
        copy.wait()


def second_store_kernel(place, *refs):
    count = place.plane
    own, early, out, bias_out, wide, left = refs[:count], refs[count], *refs[-4:]
    rank = place.rank(0)
    own = list(enumerate(own))
    other = [(0, early.at[0]), (count - 1, early.at[1])]
    copies = store_blocks(place, rank, own[1:-1], out, wide.at[0], left.at[0])
    copies += store_blocks(place, 1 - rank, other, out, wide.at[1], left.at[1])
    bias_out[...] = plane_bias(place, own) + plane_bias(place, other)
    for copy in copies:
        copy.wait()


def third_store_kernel(place, bias_before, late, out_before, out, bias_out, wide, bias_here, left):
    del out_before
    rank = place.rank(0)
    blocks = [(step, late.at[step - 1]) for step in range(1, place.plane - 1)]
    copies = store_blocks(place, 1 - rank, blocks, out, wide, left)
    bias = bias_before[...] + plane_bias(place, blocks)
    width = bias.shape[1]
    for index in range(bias_here.shape[0] // width):
        bias_here[pl.ds(index * width, width)] = bias[index]
    copies.append(pltpu.make_async_copy(bias_here, bias_out, left.at[len(copies)]))
    copies[-1].start()
    for copy in copies:
        copy.wait()


def field_kernel(pre, weights, wide_out, turned_out, done_out, shifted):
    done_out[...] = jnp.zeros(done_out.shape, F32)
    gate_count, cells = pre.shape
    width = wide_out.shape[1]
    channels = weights.shape[1] // 9
    row_count = cells // width
    lane = lanes((gate_count, width))
    for index in range(row_count):
        at = pl.ds(index * width, width)
        row = pre[:, at].astype(F32)
        left = jnp.where(lane == 0, 0.0, rolled(row, 1))
        right = jnp.where(lane == width - 1, 0.0, rolled(row, -1))
        shifted[0:gate_count, at] = right.astype(BF16)
        shifted[gate_count : 2 * gate_count, at] = pre[:, at]
        shifted[2 * gate_count : 3 * gate_count, at] = left.astype(BF16)
    for a in range(3):
        for b in range(3):
            turned_out[a, :, b * gate_count : (b + 1) * gate_count] = (
                weights[:, pl.ds((3 * a + b) * channels, channels)].T
            )

    def product(a, index, count):
        return jnp.dot(
            turned_out[a],
            shifted[:, pl.ds(index * width, count * width)],
            preferred_element_type=F32,
        )

    pair = 2 if row_count % 2 == 0 else 1
    for base in range(0, row_count, pair):
        total = product(1, base, pair)
        for a, first in ((2, base - 1), (0, base + 1)):
            low, high = max(first, 0), min(first + pair, row_count)
            if low >= high:
                continue
            part = product(a, low, high - low)
            blank = jnp.zeros((channels, width), F32)
            parts = [blank] * (low - first) + [part] + [blank] * (first + pair - high)
            total += jnp.concatenate(parts, axis=1)
        for offset in range(pair):
            value = total[:, offset * width : (offset + 1) * width]
            wide_out[pl.ds(base + offset, channels, stride=row_count), :] = value


def field_halo_kernel(
    place,
    wide,
    turned,
    outer_row,
    inner_row,
    outer_column,
    inner_column,
    inputs_out,
    hidden_out,
    done_out,
    total,
):
    done_out[...] = jnp.zeros(done_out.shape, F32)
    hid, row_count, width = hidden_out.shape
    channels = turned.shape[1]
    gate_count = turned.shape[2] // 3
    north, south = row_halo(inner_row, outer_row)
    west, east = column_halo(inner_column, outer_column, PRE_GROUPS)
    lane = lanes((gate_count, width))
    lat = place.position()[0]

    def row_part(taps, row, position):
        left = jnp.where(lane == 0, rolled(west, -LAST - position), rolled(row, 1))
        right = rolled(east, width - 1 - position)
        right = jnp.where(lane == width - 1, right, rolled(row, -1))
        stack = jnp.concatenate([right, row, left], axis=0).astype(BF16)
        return jnp.dot(taps, stack, preferred_element_type=F32)

    above = row_part(turned[jnp.where(lat == 0, 0, 2)], north, 0)
    below = row_part(turned[jnp.where(lat == place.lat - 1, 2, 0)], south, row_count + 1)

    inside = (lane >= 1) & (lane <= row_count)
    west = jnp.where(inside, rolled(west, -LAST), 0.0)
    east = jnp.where(inside, east, 0.0)
    sides = [rolled(west, a - 1) for a in range(3)] + [rolled(east, LAST + a - 1) for a in range(3)]
    taps = [turned[a, :, 2 * gate_count : 3 * gate_count] for a in range(3)]
    taps += [turned[a, :, 0:gate_count] for a in range(3)]
    columns = jnp.dot(
        jnp.concatenate(taps, axis=1),
        jnp.concatenate(sides, axis=0).astype(BF16),
        preferred_element_type=F32,
    )
    blank = jnp.zeros((channels, width), F32)
    for index in range(row_count):
        strided = pl.ds(index, channels, stride=row_count)
        value = wide[strided, :] + at_edges(blank, index + 1, columns)
        if index == 0:
            value += above
        if index == row_count - 1:
            value += below
        total[strided, :] = value
    size = (channels - hid) * row_count
    inputs_out[...] = total[0:size, :].reshape(inputs_out.shape).astype(BF16)
    hidden_out[...] = total[size:, :].reshape(hidden_out.shape).astype(BF16)


def body(
    place,
    inputs_below,
    hidden_prev,
    cell_prev,
    kernel_weights,
    gate_bias,
    readout,
    target_field,
    land_mask,
    fire_mask,
    hidden_grad,
):
    hid, row_count, width = hidden_prev.shape
    gate_count, channels = kernel_weights.shape[1:]
    cells = row_count * width
    halo_cells = (row_count + 2) * width
    scaling = 1.0 / math.sqrt(cells * place.lat * place.lon)
    bind = functools.partial
    inner_rows, outer_rows = place.pairs(place.inner_rows), place.pairs(place.outer_rows)
    inner_columns = place.pairs(place.inner_columns)
    outer_columns = place.pairs(place.outer_columns)
    flat = sds((hid * row_count, width), F32)
    strip = sds((hid, width), F32)

    inner, outer, wide = call(
        pack_kernel,
        (
            sds((channels, width), BF16),
            sds((channels, width), BF16),
            sds((channels * row_count, width), F32),
        ),
        [
            pltpu.VMEM(inputs_below.shape, BF16),
            pltpu.VMEM(hidden_prev.shape, BF16),
            pltpu.SemaphoreType.DMA((4,)),
        ],
        remote=2,
        moved=4 * channels * cells,
    )(inputs_below, hidden_prev)
    inner, outer = permuted(inner, inner_rows), permuted(outer, outer_rows)
    (
        rows,
        columns,
        second,
        cell_strip,
        hidden_grad_strip,
        fields_strip,
        cell_here,
        weights_here,
        hidden_grad_here,
        target_here,
        land_here,
        fire_here,
        bias_wide,
        readout_wide,
    ) = call(
        prepare_kernel,
        (
            sds((row_count, channels, width), BF16),
            sds((channels, width), F32),
            sds((channels, width), F32),
            strip,
            strip,
            sds((8, width), F32),
            flat,
            sds((gate_count, place.taps * channels), BF16),
            flat,
            sds(target_field.shape, F32),
            sds(land_mask.shape, jnp.int32),
            sds(fire_mask.shape, jnp.int32),
            sds((gate_count, width), F32),
            sds((hid, width), F32),
        ),
        [
            pltpu.VMEM(hidden_grad.shape, BF16),
            pltpu.VMEM(gate_bias.shape, F32),
            pltpu.VMEM(readout.shape, F32),
            pltpu.SemaphoreType.DMA((7 + place.taps,)),
        ],
        remote=8,
        moved=6_000_000,
    )(
        wide,
        cell_prev.reshape(hid * row_count, width),
        kernel_weights,
        hidden_grad,
        target_field,
        land_mask,
        fire_mask,
        gate_bias,
        readout,
    )
    columns, edge = call(
        bind(columns_kernel, row_count, GROUPS),
        (sds((channels // GROUPS, width), BF16), sds((channels, width), BF16)),
    )(columns, outer, inner)
    inner_column = permuted(columns, inner_columns)
    outer_column = permuted(columns, outer_columns)
    hidden_rows, cell_rows, grad_cell_rows, pre, second, sums, bias = call(
        bind(gates_kernel, place),
        (
            flat,
            flat,
            flat,
            sds((gate_count, cells), BF16),
            sds((channels, width), BF16),
            sds((2 * place.half_rows, channels), F32),
            sds((gate_count, width), F32),
        ),
        [pltpu.VMEM((3 * channels, halo_cells), BF16)],
        flops=4 * 9 * gate_count * channels * cells,
        moved=6_000_000,
        transcendentals=5 * hid * cells,
    )(
        rows,
        inner,
        outer,
        second,
        cell_here,
        weights_here,
        hidden_grad_here,
        target_here,
        land_here,
        fire_here,
        bias_wide,
        readout_wide,
    )
    send, pre_strip, pre_wide, patches, *strips = call(
        bind(strip_kernel, place, row_count),
        (
            sds((place.half_rows, channels), BF16),
            sds((gate_count, width), BF16),
            sds((gate_count, width), F32),
            sds((place.taps * channels, width), BF16),
            strip,
            strip,
            strip,
        ),
    )(
        edge,
        second,
        outer_column,
        inner_column,
        weights_here,
        bias_wide,
        readout_wide,
        cell_strip,
        hidden_grad_strip,
        fields_strip,
        sums,
    )
    keep, bias = call(
        bind(keep_kernel, place),
        (sds((place.half_rows, channels), F32), sds((8, channels), F32)),
    )(sums, pre_strip, patches, bias, pre_wide)
    hidden_next, cell_next, grad_cell, pre, pre_inner, pre_outer = call(
        bind(edges_kernel, row_count),
        (
            sds((hid, row_count, width), BF16),
            flat,
            flat,
            sds((gate_count, cells), BF16),
            sds((gate_count, width), BF16),
            sds((gate_count, width), BF16),
        ),
        [
            pltpu.VMEM((hid, row_count, width), BF16),
            pltpu.VMEM(flat.shape, F32),
            pltpu.VMEM(flat.shape, F32),
            pltpu.VMEM(flat.shape, F32),
            pltpu.SemaphoreType.DMA((3,)),
        ],
        leaving=3,
        moved=4_000_000,
    )(hidden_rows, cell_rows, grad_cell_rows, pre, *strips, pre_strip)
    pre_inner, pre_outer = permuted(pre_inner, inner_rows), permuted(pre_outer, outer_rows)
    pre_columns = call(
        bind(columns_kernel, row_count, PRE_GROUPS),
        (sds((gate_count // PRE_GROUPS, width), BF16),),
    )(pre_strip, pre_outer, pre_inner)[0]

    block = sds((BIAS_ROWS + place.chunk, channels), BF16)
    token = sds((8, width), F32)
    steps = range(place.plane - 1, 0, -1)
    *sends, keep = call(
        bind(pair_kernel, place),
        (*[block for _ in steps], sds((place.chunk, channels), F32)),
        [pltpu.VMEM((place.half_rows, channels), F32)],
    )(keep, bias, permuted(send, place.phase_pairs(0)))
    received = [permuted(send, place.plane_pairs(step)) for step, send in zip(steps, sends)]
    field, turned, field_done = call(
        field_kernel,
        (
            sds((channels * row_count, width), F32),
            sds((3, channels, 3 * gate_count), BF16),
            token,
        ),
        [pltpu.VMEM((3 * gate_count, cells), BF16)],
        flops=2 * 9 * gate_count * channels * cells,
        moved=3_000_000,
    )(pre, weights_here)
    part = call(plane_kernel, block)(keep, bias, *received, field_done)
    pre_inner_columns = permuted(pre_columns, inner_columns)
    pre_outer_columns = permuted(pre_columns, outer_columns)
    phases = len(place.orders[0])
    for phase in range(1, phases):
        is_last = phase == phases - 1
        part = call(bind(add_kernel, scaling if is_last else 1.0), block)(
            part, permuted(part, place.phase_pairs(phase))
        )
    received = [permuted(part, place.plane_pairs(step)) for step in steps[::-1]]
    grad_inputs, grad_hidden, field_done = call(
        bind(field_halo_kernel, place),
        (
            sds((channels - hid, row_count, width), BF16),
            sds((hid, row_count, width), BF16),
            token,
        ),
        [pltpu.VMEM((channels * row_count, width), F32)],
        flops=40 * gate_count * channels * cells * 9,
        moved=2_000_000,
    )(field, turned, pre_outer, pre_inner, pre_outer_columns, pre_inner_columns)
    last = received[-1]
    early = call(join_kernel, sds((2, *block.shape), BF16))(part, last, target_here, target_here)
    early_other = permuted(early, place.phase_pairs(0))
    wide_block = (place.taps, place.chunk_gates, channels)
    grad_kernel, stored = call(
        bind(first_store_kernel, place),
        (sds(kernel_weights.shape, F32), token),
        [pltpu.VMEM((2, *wide_block), F32), pltpu.SemaphoreType.DMA((2,))],
        leaving=1,
    )(part, last)
    late = call(join_kernel, sds((place.plane - 2, *block.shape), BF16))(
        *received[:-1], field_done, stored
    )
    late_other = permuted(late, place.phase_pairs(0))
    grad_kernel, bias = call(
        bind(second_store_kernel, place),
        (sds(kernel_weights.shape, F32), sds((8, channels), F32)),
        [
            pltpu.VMEM((2, place.plane, *wide_block), F32),
            pltpu.SemaphoreType.DMA((2, place.plane)),
        ],
        remote=1,
        leaving=1,
        aliases={place.plane + 1: 0},
    )(part, *received, early_other, grad_kernel)
    grad_kernel, grad_bias = call(
        bind(third_store_kernel, place),
        (sds(kernel_weights.shape, F32), sds((gate_count,), F32)),
        [
            pltpu.VMEM((place.plane - 2, *wide_block), F32),
            pltpu.VMEM((gate_count,), F32),
            pltpu.SemaphoreType.DMA((place.plane - 1,)),
        ],
        remote=1,
        leaving=2,
        aliases={2: 0},
    )(bias, late_other, grad_kernel)
    shape = hidden_prev.shape
    return (
        hidden_next,
        cell_next.reshape(shape),
        grad_inputs,
        grad_hidden,
        grad_cell.reshape(shape),
        grad_kernel,
        grad_bias,
    )


def solution(mesh):
    lat_count, lon_count = mesh.shape["lat"], mesh.shape["lon"]
    split = Mesh(mesh.devices.reshape(lat_count // 2, 2, lon_count // 2, 2), AXES)
    field = P(None, ("band", "core"), ("reach", "near"))
    flat = P(("band", "core"), ("reach", "near"))

    def run(*args):
        place = Layout(lat_count, lon_count, *args[3].shape[:2])
        return jax.shard_map(
            functools.partial(body, place),
            mesh=split,
            in_specs=(field, field, field, P(), P(), P(), flat, flat, flat, field),
            out_specs=(field, field, field, field, field, P(), P()),
            check_vma=False,
        )(*args)

    return run
```

```python
import functools
import math

import jax
import jax.numpy as jnp
from jax import lax
from jax.experimental import pallas as pl
from jax.experimental.pallas import tpu as pltpu
from jax.sharding import Mesh, PartitionSpec as P

F32 = jnp.float32
BF16 = jnp.bfloat16
AXES = ("band", "core", "reach", "near")
BIAS_ROWS = 16
GROUPS = 4
PRE_GROUPS = 4
LAST = 16
VMEM = pl.BlockSpec(memory_space=pltpu.VMEM)
HBM = pl.BlockSpec(memory_space=pltpu.HBM)
ACROSS = (((1,), (1,)), ((), ()))


def sds(shape, dtype):
    return jax.ShapeDtypeStruct(shape, dtype)


def call(
    kernel,
    out_shape,
    scratch=(),
    remote=0,
    leaving=0,
    aliases=None,
    flops=0,
    moved=0,
    transcendentals=0,
):
    several = isinstance(out_shape, tuple)
    shapes = out_shape if several else (out_shape,)
    out_specs = tuple([HBM] * leaving + [VMEM] * (len(shapes) - leaving))

    def run(*args):
        near = len(args) - remote
        far = [pltpu.with_memory_space_constraint(arg, pltpu.HBM) for arg in args[near:]]
        return pl.pallas_call(
            kernel,
            out_shape=out_shape,
            in_specs=[VMEM] * near + [HBM] * remote,
            out_specs=out_specs if several else out_specs[0],
            input_output_aliases=aliases or {},
            scratch_shapes=list(scratch),
            cost_estimate=pl.CostEstimate(
                flops=flops, bytes_accessed=moved, transcendentals=transcendentals
            ),
            compiler_params=pltpu.CompilerParams(vmem_limit_bytes=24 * 1024 * 1024),
        )(*args[:near], *far)

    return run


class Layout:
    def __init__(self, lat_count, lon_count, taps, gate_count):
        self.lat, self.lon = lat_count, lon_count
        self.half = lon_count // 2
        self.taps, self.half_gates = taps, gate_count // 2
        self.plane = lat_count
        self.scatter_steps = [self.plane - 1, *range(1, self.plane - 1)]
        whole = [("lon", 1 << k) for k in range(1, lon_count.bit_length() - 1)]
        self.orders = ([("lat", 1)] + whole, [("lat", 1)] + whole[::-1])
        step = 8 * self.plane
        self.half_rows = -(-taps * self.half_gates // step) * step
        self.chunk = self.half_rows // self.plane

    def position(self):
        lat = 2 * lax.axis_index("band") + lax.axis_index("core")
        return lat, 2 * lax.axis_index("reach") + lax.axis_index("near")

    def rank(self, phase):
        lat, lon = self.position()

        def digit(order):
            axis, bit = order[phase]
            return ((lat if axis == "lat" else lon) // bit) % 2

        return jnp.where(lat % 2 == 0, digit(self.orders[0]), digit(self.orders[1]))

    def pairs(self, partner):
        result = []
        for lat in range(self.lat):
            for lon in range(self.lon):
                there = partner(lat, lon)
                result.append((lat * self.lon + lon, there[0] * self.lon + there[1]))
        return result

    def phase_pairs(self, phase):
        def partner(lat, lon):
            axis, bit = self.orders[lat % 2][phase]
            return (lat ^ bit, lon) if axis == "lat" else (lat, lon ^ bit)

        return self.pairs(partner)

    def plane_rank(self):
        return 2 * lax.axis_index("band") + lax.axis_index("near")

    def plane_pairs(self, step):
        def partner(lat, lon):
            there = (lat // 2 * 2 + lon % 2) ^ step
            return there // 2 * 2 + lat % 2, lon // 2 * 2 + there % 2

        return self.pairs(partner)

    def inner_rows(self, lat, lon):
        return lat ^ 1, lon

    def outer_rows(self, lat, lon):
        there = lat + 1 if lat % 2 else lat - 1
        if 0 <= there < self.lat:
            return there, lon
        return lat, (lon + self.half) % self.lon

    def inner_columns(self, lat, lon):
        return lat, lon ^ 1

    def outer_columns(self, lat, lon):
        return lat, (lon + (1 if lon % 2 else -1)) % self.lon


def permuted(value, pairs):
    return lax.ppermute(value, AXES, pairs)


def lanes(shape):
    return lax.broadcasted_iota(jnp.int32, shape, len(shape) - 1)


def rolled(value, shift):
    shift %= value.shape[1]
    return pltpu.roll(value, shift, 1) if shift else value


def edge_columns(row, position, columns):
    lane = lanes(row.shape)
    columns = jnp.where(lane == position, rolled(row, position), columns)
    return jnp.where(lane == LAST + position, rolled(row, LAST + position + 1), columns)


def second_columns(row, position, columns):
    lane = lanes(row.shape)
    columns = jnp.where(lane == position, rolled(row, position - 1), columns)
    return jnp.where(lane == LAST + position, rolled(row, LAST + position + 2), columns)


def at_edges(row, position, columns):
    lane = lanes(row.shape)
    width = row.shape[1]
    row = jnp.where(lane == 0, rolled(columns, -position), row)
    return jnp.where(lane == width - 1, rolled(columns, width - 1 - LAST - position), row)


def pick(flag, yes, no):
    return jnp.where(flag, yes, no)


def is_odd(axis):
    return lax.axis_index(axis) % 2 == 1


def row_sends(first, last, inner_out, outer_out):
    odd = is_odd("core")
    inner_out[...] = pick(odd, first, last).astype(BF16)
    outer_out[...] = pick(odd, last, first).astype(BF16)


def row_halo(inner, outer):
    odd = is_odd("core")
    inner, outer = inner[...].astype(F32), outer[...].astype(F32)
    return pick(odd, inner, outer), pick(odd, outer, inner)


def packed(columns, groups):
    count, width = columns.shape[0] // groups, columns.shape[1] // groups
    lane = lanes((count, columns.shape[1]))
    value = columns[0:count]
    for group in range(1, groups):
        part = rolled(columns[group * count : (group + 1) * count], group * width)
        value = jnp.where(lane >= group * width, part, value)
    return value


def unpacked(value, groups):
    width = value.shape[1] // groups
    return jnp.concatenate([rolled(value, -group * width) for group in range(groups)], axis=0)


def column_halo(inner, outer, groups):
    odd = is_odd("near")
    inner, outer = inner[...].astype(F32), outer[...].astype(F32)
    return unpacked(pick(odd, inner, outer), groups), unpacked(pick(odd, outer, inner), groups)


def pack_kernel(below, hidden, inner_out, outer_out, wide_out, below_here, hidden_here, arrived):
    channels, row_count, width = below.shape
    size = channels * row_count
    part = channels // 2
    copies = []
    for source, here in ((below, below_here), (hidden, hidden_here)):
        for at in (pl.ds(0, part), pl.ds(part, part)):
            copies.append(
                pltpu.make_async_copy(source.at[at], here.at[at], arrived.at[len(copies)])
            )
            copies[-1].start()
    for index, copy in enumerate(copies):
        here = (below_here, hidden_here)[index // 2]
        copy.wait()
        value = here[pl.ds(index % 2 * part, part)].astype(F32)
        at = pl.ds(index * part * row_count, part * row_count)
        wide_out[at, :] = value.reshape(part * row_count, width)
    edges = [
        wide_out[pl.ds(index, 2 * channels, stride=row_count), :] for index in (0, row_count - 1)
    ]
    row_sends(edges[0], edges[1], inner_out, outer_out)


def down_rows(values, width):
    count = values.shape[0]
    return jnp.broadcast_to(values[None, :], (width, count)).T


def prepare_kernel(
    wide,
    cell_hbm,
    weights_hbm,
    hidden_grad_hbm,
    target_hbm,
    land_hbm,
    fire_hbm,
    gate_bias_hbm,
    readout_hbm,
    rows_out,
    columns_out,
    second_out,
    cell_strip_out,
    hidden_grad_strip_out,
    fields_strip_out,
    cell_out,
    weights_out,
    hidden_grad_out,
    target_out,
    land_out,
    fire_out,
    bias_wide_out,
    readout_wide_out,
    hidden_grad_here,
    gate_bias_here,
    readout_here,
    arrived,
):
    row_count, channels, width = rows_out.shape
    copies = [
        pltpu.make_async_copy(source, target, arrived.at[index])
        for index, (source, target) in enumerate(
            (
                (cell_hbm, cell_out),
                *(
                    (weights_hbm.at[tap], weights_out.at[:, pl.ds(tap * channels, channels)])
                    for tap in range(weights_hbm.shape[0])
                ),
                (hidden_grad_hbm, hidden_grad_here),
                (target_hbm, target_out),
                (land_hbm, land_out),
                (fire_hbm, fire_out),
                (gate_bias_hbm, gate_bias_here),
                (readout_hbm, readout_here),
            )
        )
    ]
    for copy in copies:
        copy.start()
    columns = jnp.zeros((channels, width), F32)
    second = jnp.zeros((channels, width), F32)
    for index in range(row_count):
        row = wide[pl.ds(index, channels, stride=row_count), :]
        rows_out[index] = row.astype(BF16)
        columns = edge_columns(row, index + 1, columns)
        second = second_columns(row, index + 1, second)
    columns_out[...] = columns
    second_out[...] = second
    for copy in copies:
        copy.wait()
    hidden_grad_out[...] = hidden_grad_here[...].astype(F32).reshape(hidden_grad_out.shape)
    bias_wide_out[...] = down_rows(gate_bias_here[...], width)
    readout_wide_out[...] = down_rows(readout_here[...], width)
    hid = hidden_grad_here.shape[0]
    cell_strip = jnp.zeros((hid, width), F32)
    hidden_grad_strip = jnp.zeros((hid, width), F32)
    fields_strip = jnp.zeros((8, width), F32)
    for index in range(row_count):
        strided = pl.ds(index, hid, stride=row_count)
        cell_strip = edge_columns(cell_out[strided, :], index + 1, cell_strip)
        hidden_grad_strip = edge_columns(hidden_grad_out[strided, :], index + 1, hidden_grad_strip)
        at = slice(index, index + 1)
        fields = [target_out[at, :], land_out[at, :].astype(F32), fire_out[at, :].astype(F32)]
        fields = jnp.concatenate(fields + [jnp.zeros((5, width), F32)], axis=0)
        fields_strip = edge_columns(fields, index + 1, fields_strip)
    cell_strip_out[...] = cell_strip
    hidden_grad_strip_out[...] = hidden_grad_strip
    fields_strip_out[...] = fields_strip


def columns_kernel(row_count, groups, columns, outer, inner, packed_out, *whole_out):
    north, south = row_halo(inner, outer)
    value = edge_columns(north, 0, columns[...].astype(F32))
    value = edge_columns(south, row_count + 1, value)
    packed_out[...] = packed(value, groups).astype(BF16)
    for out in whole_out:
        out[...] = value.astype(BF16)


def encode(bias):
    high = bias.astype(BF16).astype(F32)
    return jnp.concatenate([high, bias - high], axis=0)


def decode(block):
    return block[0:8] + block[8:16]


def cell_step(part, cell_before, hidden_grad, target, land, fire, readout):
    hid = part.shape[0] // 4
    input_gate = 0.5 + 0.5 * jnp.tanh(0.5 * part[0:hid])
    forget_gate = 0.5 + 0.5 * jnp.tanh(0.5 * part[hid : 2 * hid])
    output_gate = 0.5 + 0.5 * jnp.tanh(0.5 * part[2 * hid : 3 * hid])
    candidate = jnp.tanh(part[3 * hid : 4 * hid])
    cell_next = land * (forget_gate * cell_before + input_gate * candidate)
    squashed = jnp.tanh(cell_next)
    hidden_next = (output_gate * squashed).astype(BF16).astype(F32)
    predicted = jnp.sum(readout * hidden_next, axis=0, keepdims=True)
    total_grad = hidden_grad + 2.0 * (fire * (predicted - target)) * readout
    cell_grad = land * total_grad * output_gate * (1.0 - squashed * squashed)
    pre_grad = jnp.concatenate(
        [
            cell_grad * candidate * input_gate * (1.0 - input_gate),
            cell_grad * cell_before * forget_gate * (1.0 - forget_gate),
            total_grad * squashed * output_gate * (1.0 - output_gate),
            cell_grad * input_gate * (1.0 - candidate * candidate),
        ],
        axis=0,
    )
    return hidden_next, cell_next, cell_grad * forget_gate, pre_grad


def gates_kernel(
    place,
    rows_in,
    inner_row,
    outer_row,
    second,
    cell_prev,
    weights,
    hidden_grad,
    target,
    land,
    fire,
    bias_wide,
    readout_wide,
    hidden_out,
    cell_out,
    grad_cell_out,
    pre_out,
    second_out,
    sums,
    bias_out,
    shifted,
):
    row_count, channels, width = rows_in.shape
    gate_count = weights.shape[0]
    hid = gate_count // 4
    half_gates = place.half_gates
    north, south = row_halo(inner_row, outer_row)
    columns = second_columns(north, 0, second[...])
    second_out[...] = second_columns(south, row_count + 1, columns).astype(BF16)
    for position in range(row_count + 2):
        if position == 0:
            row = north
        elif position == row_count + 1:
            row = south
        else:
            row = rows_in[position - 1].astype(F32)
        at = pl.ds(position * width, width)
        shifted[0:channels, at] = rolled(row, 1).astype(BF16)
        shifted[channels : 2 * channels, at] = row.astype(BF16)
        shifted[2 * channels : 3 * channels, at] = rolled(row, -1).astype(BF16)

    bias_total = jnp.zeros((gate_count, width), F32)
    lane = lanes((gate_count, width))
    inside = (lane > 0) & (lane < width - 1)
    readout = readout_wide[...]
    pair = 2 if row_count % 2 == 0 else 1
    for base in range(0, row_count, pair):
        preact = jnp.zeros((gate_count, pair * width), F32)
        for a in range(3):
            preact += jnp.dot(
                weights[:, pl.ds(3 * a * channels, 3 * channels)],
                shifted[:, pl.ds((base + a) * width, pair * width)],
                preferred_element_type=F32,
            )
        for offset in range(pair):
            index = base + offset
            strided = pl.ds(index, hid, stride=row_count)
            at = slice(index, index + 1)
            hidden_next, cell_next, grad_cell, pre_grad = cell_step(
                preact[:, offset * width : (offset + 1) * width] + bias_wide[...],
                cell_prev[strided, :],
                hidden_grad[strided, :],
                target[at, :],
                land[at, :].astype(F32),
                fire[at, :].astype(F32),
                readout,
            )
            hidden_out[strided, :] = hidden_next
            cell_out[strided, :] = cell_next
            grad_cell_out[strided, :] = grad_cell
            pre_grad = jnp.where(inside, pre_grad, 0.0)
            bias_total += pre_grad
            pre_out[:, pl.ds(index * width, width)] = pre_grad.astype(BF16)
    bias_out[...] = bias_total

    for a in range(3):
        product = lax.dot_general(
            pre_out[...],
            shifted[:, pl.ds(a * width, row_count * width)],
            ACROSS,
            preferred_element_type=F32,
        )
        for b in range(3):
            for half in range(2):
                at = half * place.half_rows + (3 * a + b) * half_gates
                sums[at : at + half_gates, :] = product[
                    half * half_gates : (half + 1) * half_gates, b * channels : (b + 1) * channels
                ]
    used = place.taps * half_gates
    if place.half_rows > used:
        for half in range(2):
            at = half * place.half_rows
            sums[at + used : at + place.half_rows, :] = jnp.zeros(
                (place.half_rows - used, channels), F32
            )


def add_strip(place, half, sums, pre_strip, patches, out):
    half_gates, channels = place.half_gates, sums.shape[1]
    gates = pre_strip[pl.ds(pl.multiple_of(half * half_gates, half_gates), half_gates), :]
    product = lax.dot_general(gates, patches[...], ACROSS, preferred_element_type=F32)
    base = half * place.half_rows
    for tap in range(place.taps):
        at = pl.ds(pl.multiple_of(base + tap * half_gates, 8), half_gates)
        value = sums[at, :] + product[:, tap * channels : (tap + 1) * channels]
        out[tap * half_gates : (tap + 1) * half_gates, :] = value.astype(out.dtype)
    used = place.taps * half_gates
    if place.half_rows > used:
        rest = jnp.zeros((place.half_rows - used, channels), out.dtype)
        out[used:, :] = rest


def strip_kernel(
    place,
    row_count,
    edge,
    second,
    outer_column,
    inner_column,
    weights,
    bias_wide,
    readout_wide,
    cell_strip,
    hidden_grad_strip,
    fields_strip,
    sums,
    send_out,
    pre_out,
    pre_wide_out,
    patches,
    hidden_out,
    cell_out,
    grad_cell_out,
):
    channels, width = edge.shape
    west, east = column_halo(inner_column, outer_column, GROUPS)
    near_first = lanes((channels, width)) < LAST
    inner = second[...].astype(F32)
    columns = (
        jnp.where(near_first, rolled(west, -LAST), inner),
        edge[...].astype(F32),
        jnp.where(near_first, inner, rolled(east, LAST)),
    )
    for a in range(3):
        for b in range(3):
            at = (3 * a + b) * channels
            patches[at : at + channels, :] = rolled(columns[b], 1 - a).astype(BF16)
    preact = jnp.dot(weights[...], patches[...], preferred_element_type=F32) + bias_wide[...]
    hidden_next, cell_next, grad_cell, pre_grad = cell_step(
        preact,
        cell_strip[...],
        hidden_grad_strip[...],
        fields_strip[0:1, :],
        fields_strip[1:2, :],
        fields_strip[2:3, :],
        readout_wide[...],
    )
    hidden_out[...] = hidden_next
    cell_out[...] = cell_next
    grad_cell_out[...] = grad_cell
    lane = lanes(pre_grad.shape)
    lane = jnp.where(lane >= LAST, lane - LAST, lane)
    pre_grad = jnp.where((lane >= 1) & (lane <= row_count), pre_grad, 0.0)
    pre_out[...] = pre_grad.astype(BF16)
    pre_wide_out[...] = pre_grad
    add_strip(place, 1 - place.rank(0), sums, pre_out, patches, send_out)


def keep_kernel(place, sums, pre_strip, patches, bias_partial, pre_wide, out, bias_out):
    add_strip(place, place.rank(0), sums, pre_strip, patches, out)
    channels = sums.shape[1]
    bias_total = bias_partial[...] + pre_wide[...]
    ones = jnp.ones((8, bias_total.shape[1]), BF16)
    high = bias_total.astype(BF16)
    low = (bias_total - high.astype(F32)).astype(BF16)
    flat = lax.dot_general(ones, high, ACROSS, preferred_element_type=F32)
    flat += lax.dot_general(ones, low, ACROSS, preferred_element_type=F32)
    odd = lax.broadcasted_iota(jnp.int32, (8, channels), 0) % 2 == 1
    bias_out[...] = jnp.where(odd, flat[:, channels : 2 * channels], flat[:, 0:channels])


def edges_kernel(
    row_count,
    hidden,
    cell,
    grad_cell,
    pre,
    hidden_strip,
    cell_strip,
    grad_cell_strip,
    pre_strip,
    hidden_hbm,
    cell_hbm,
    grad_cell_hbm,
    pre_out,
    inner_out,
    outer_out,
    hidden_low,
    hidden_here,
    cell_here,
    grad_cell_here,
    left,
):
    hid, _, width = hidden_low.shape
    leaving = []
    for source, strip, here, ready, target in (
        (cell, cell_strip, cell_here, cell_here, cell_hbm),
        (grad_cell, grad_cell_strip, grad_cell_here, grad_cell_here, grad_cell_hbm),
        (hidden, hidden_strip, hidden_here, hidden_low, hidden_hbm),
    ):
        columns = strip[...]
        for index in range(row_count):
            strided = pl.ds(index, hid, stride=row_count)
            here[strided, :] = at_edges(source[strided, :], index + 1, columns)
        if ready is hidden_low:
            hidden_low[...] = here[...].reshape(hidden_low.shape).astype(BF16)
        leaving.append(pltpu.make_async_copy(ready, target, left.at[len(leaving)]))
        leaving[-1].start()
    first, last = None, None
    columns = pre_strip[...].astype(F32)
    for index in range(row_count):
        at = pl.ds(index * width, width)
        row = at_edges(pre[:, at].astype(F32), index + 1, columns)
        pre_out[:, at] = row.astype(BF16)
        first = row if index == 0 else first
        last = row
    row_sends(first, last, inner_out, outer_out)
    for copy in leaving:
        copy.wait()


def pair_kernel(place, keep, bias, received, *outs):
    sends, keep_out, scratch = outs[:-2], outs[-2], outs[-1]
    chunk = place.chunk
    rank = place.plane_rank()
    scratch[...] = keep[...] + received[...].astype(F32)
    block = encode(bias[...]).astype(BF16)
    for step, send in zip(place.scatter_steps, sends):
        send[0:BIAS_ROWS, :] = block
        at = pl.ds(pl.multiple_of((rank ^ step) * chunk, 8), chunk)
        send[BIAS_ROWS:, :] = scratch[at, :].astype(BF16)
    keep_out[...] = scratch[pl.ds(pl.multiple_of(rank * chunk, 8), chunk), :]


def plane_kernel(keep, bias, *refs):
    received, out = refs[:-2], refs[-1]
    total, bias_total = keep[...], bias[...]
    for ref in received:
        total += ref[BIAS_ROWS:, :].astype(F32)
        bias_total += decode(ref[0:BIAS_ROWS, :].astype(F32))
    out[0:BIAS_ROWS, :] = encode(bias_total).astype(BF16)
    out[BIAS_ROWS:, :] = total.astype(BF16)


def join_kernel(*refs):
    blocks, out = refs[:-2], refs[-1]
    for index, block in enumerate(blocks):
        out[index] = block[...]


def add_kernel(scale, own, received, out):
    here, there = own[...].astype(F32), received[...].astype(F32)
    bias = (decode(here[0:BIAS_ROWS]) + decode(there[0:BIAS_ROWS])) * scale
    out[0:BIAS_ROWS, :] = encode(bias).astype(BF16)
    out[BIAS_ROWS:, :] = ((here[BIAS_ROWS:] + there[BIAS_ROWS:]) * scale).astype(BF16)


def store_half(place, half, blocks, out, wide, left):
    chunk, half_gates = place.chunk, place.half_gates
    gates = pl.ds(pl.multiple_of(half * half_gates, half_gates), half_gates)
    rank = place.plane_rank()
    for step, block in enumerate(blocks):
        at = pl.ds(pl.multiple_of((rank ^ step) * chunk, 8), chunk)
        wide[at, :] = block[BIAS_ROWS:, :].astype(F32)
    copies = []
    for tap in range(place.taps):
        source = wide.at[tap * half_gates : (tap + 1) * half_gates, :]
        copies.append(pltpu.make_async_copy(source, out.at[tap, gates, :], left.at[tap]))
        copies[-1].start()
    return copies


def in_steps(place, early, late):
    return [early.at[0], late] + [early.at[index] for index in range(1, place.plane - 1)]


def own_half_kernel(place, late, early, out, bias_out, wide, left):
    blocks = in_steps(place, early, late)
    copies = store_half(place, place.rank(0), blocks, out, wide, left)
    rank = place.plane_rank()
    bias = decode(blocks[0][0:BIAS_ROWS, :].astype(F32))
    for step in range(1, place.plane):
        bias = pick(rank == step, decode(blocks[step][0:BIAS_ROWS, :].astype(F32)), bias)
    bias_out[...] = bias
    for copy in copies:
        copy.wait()


def other_half_kernel(
    place, bias_own, early, late, after, out_before, out, bias_out, wide, bias_here, left
):
    del after, out_before
    blocks = in_steps(place, early, late)
    copies = store_half(place, 1 - place.rank(0), blocks, out, wide, left)
    rank = place.plane_rank()
    bias = decode(blocks[0][0:BIAS_ROWS, :].astype(F32))
    for step in range(1, place.plane):
        bias = pick(rank == step, decode(blocks[step][0:BIAS_ROWS, :].astype(F32)), bias)
    bias += bias_own[...]
    width = bias.shape[1]
    for index in range(bias_here.shape[0] // width):
        bias_here[pl.ds(index * width, width)] = bias[index]
    bias_copy = pltpu.make_async_copy(bias_here, bias_out, left.at[place.taps])
    bias_copy.start()
    bias_copy.wait()
    for copy in copies:
        copy.wait()


def field_kernel(pre, weights, wide_out, turned_out, done_out, shifted):
    done_out[...] = jnp.zeros(done_out.shape, F32)
    gate_count, cells = pre.shape
    width = wide_out.shape[1]
    channels = weights.shape[1] // 9
    row_count = cells // width
    lane = lanes((gate_count, width))
    for index in range(row_count):
        at = pl.ds(index * width, width)
        row = pre[:, at].astype(F32)
        left = jnp.where(lane == 0, 0.0, rolled(row, 1))
        right = jnp.where(lane == width - 1, 0.0, rolled(row, -1))
        shifted[0:gate_count, at] = right.astype(BF16)
        shifted[gate_count : 2 * gate_count, at] = pre[:, at]
        shifted[2 * gate_count : 3 * gate_count, at] = left.astype(BF16)
    for a in range(3):
        for b in range(3):
            turned_out[a, :, b * gate_count : (b + 1) * gate_count] = (
                weights[:, pl.ds((3 * a + b) * channels, channels)].T
            )

    def product(a, index, count):
        return jnp.dot(
            turned_out[a],
            shifted[:, pl.ds(index * width, count * width)],
            preferred_element_type=F32,
        )

    pair = 2 if row_count % 2 == 0 else 1
    for base in range(0, row_count, pair):
        total = product(1, base, pair)
        for a, first in ((2, base - 1), (0, base + 1)):
            low, high = max(first, 0), min(first + pair, row_count)
            if low >= high:
                continue
            part = product(a, low, high - low)
            blank = jnp.zeros((channels, width), F32)
            parts = [blank] * (low - first) + [part] + [blank] * (first + pair - high)
            total += jnp.concatenate(parts, axis=1)
        for offset in range(pair):
            value = total[:, offset * width : (offset + 1) * width]
            wide_out[pl.ds(base + offset, channels, stride=row_count), :] = value


def field_halo_kernel(
    place,
    wide,
    turned,
    outer_row,
    inner_row,
    outer_column,
    inner_column,
    inputs_out,
    hidden_out,
    done_out,
    total,
):
    done_out[...] = jnp.zeros(done_out.shape, F32)
    hid, row_count, width = hidden_out.shape
    channels = turned.shape[1]
    gate_count = turned.shape[2] // 3
    north, south = row_halo(inner_row, outer_row)
    west, east = column_halo(inner_column, outer_column, PRE_GROUPS)
    lane = lanes((gate_count, width))
    lat = place.position()[0]

    def row_part(taps, row, position):
        left = jnp.where(lane == 0, rolled(west, -LAST - position), rolled(row, 1))
        right = rolled(east, width - 1 - position)
        right = jnp.where(lane == width - 1, right, rolled(row, -1))
        stack = jnp.concatenate([right, row, left], axis=0).astype(BF16)
        return jnp.dot(taps, stack, preferred_element_type=F32)

    above = row_part(turned[jnp.where(lat == 0, 0, 2)], north, 0)
    below = row_part(turned[jnp.where(lat == place.lat - 1, 2, 0)], south, row_count + 1)

    inside = (lane >= 1) & (lane <= row_count)
    west = jnp.where(inside, rolled(west, -LAST), 0.0)
    east = jnp.where(inside, east, 0.0)
    sides = [rolled(west, a - 1) for a in range(3)] + [rolled(east, LAST + a - 1) for a in range(3)]
    taps = [turned[a, :, 2 * gate_count : 3 * gate_count] for a in range(3)]
    taps += [turned[a, :, 0:gate_count] for a in range(3)]
    columns = jnp.dot(
        jnp.concatenate(taps, axis=1),
        jnp.concatenate(sides, axis=0).astype(BF16),
        preferred_element_type=F32,
    )
    blank = jnp.zeros((channels, width), F32)
    for index in range(row_count):
        strided = pl.ds(index, channels, stride=row_count)
        value = wide[strided, :] + at_edges(blank, index + 1, columns)
        if index == 0:
            value += above
        if index == row_count - 1:
            value += below
        total[strided, :] = value
    size = (channels - hid) * row_count
    inputs_out[...] = total[0:size, :].reshape(inputs_out.shape).astype(BF16)
    hidden_out[...] = total[size:, :].reshape(hidden_out.shape).astype(BF16)


def body(
    place,
    inputs_below,
    hidden_prev,
    cell_prev,
    kernel_weights,
    gate_bias,
    readout,
    target_field,
    land_mask,
    fire_mask,
    hidden_grad,
):
    hid, row_count, width = hidden_prev.shape
    gate_count, channels = kernel_weights.shape[1:]
    cells = row_count * width
    halo_cells = (row_count + 2) * width
    scaling = 1.0 / math.sqrt(cells * place.lat * place.lon)
    bind = functools.partial
    inner_rows, outer_rows = place.pairs(place.inner_rows), place.pairs(place.outer_rows)
    inner_columns = place.pairs(place.inner_columns)
    outer_columns = place.pairs(place.outer_columns)
    flat = sds((hid * row_count, width), F32)
    strip = sds((hid, width), F32)

    inner, outer, wide = call(
        pack_kernel,
        (
            sds((channels, width), BF16),
            sds((channels, width), BF16),
            sds((channels * row_count, width), F32),
        ),
        [
            pltpu.VMEM(inputs_below.shape, BF16),
            pltpu.VMEM(hidden_prev.shape, BF16),
            pltpu.SemaphoreType.DMA((4,)),
        ],
        remote=2,
        moved=4 * channels * cells,
    )(inputs_below, hidden_prev)
    inner, outer = permuted(inner, inner_rows), permuted(outer, outer_rows)
    (
        rows,
        columns,
        second,
        cell_strip,
        hidden_grad_strip,
        fields_strip,
        cell_here,
        weights_here,
        hidden_grad_here,
        target_here,
        land_here,
        fire_here,
        bias_wide,
        readout_wide,
    ) = call(
        prepare_kernel,
        (
            sds((row_count, channels, width), BF16),
            sds((channels, width), F32),
            sds((channels, width), F32),
            strip,
            strip,
            sds((8, width), F32),
            flat,
            sds((gate_count, place.taps * channels), BF16),
            flat,
            sds(target_field.shape, F32),
            sds(land_mask.shape, jnp.int32),
            sds(fire_mask.shape, jnp.int32),
            sds((gate_count, width), F32),
            sds((hid, width), F32),
        ),
        [
            pltpu.VMEM(hidden_grad.shape, BF16),
            pltpu.VMEM(gate_bias.shape, F32),
            pltpu.VMEM(readout.shape, F32),
            pltpu.SemaphoreType.DMA((7 + place.taps,)),
        ],
        remote=8,
        moved=6_000_000,
    )(
        wide,
        cell_prev.reshape(hid * row_count, width),
        kernel_weights,
        hidden_grad,
        target_field,
        land_mask,
        fire_mask,
        gate_bias,
        readout,
    )
    columns, edge = call(
        bind(columns_kernel, row_count, GROUPS),
        (sds((channels // GROUPS, width), BF16), sds((channels, width), BF16)),
    )(columns, outer, inner)
    inner_column = permuted(columns, inner_columns)
    outer_column = permuted(columns, outer_columns)
    hidden_rows, cell_rows, grad_cell_rows, pre, second, sums, bias = call(
        bind(gates_kernel, place),
        (
            flat,
            flat,
            flat,
            sds((gate_count, cells), BF16),
            sds((channels, width), BF16),
            sds((2 * place.half_rows, channels), F32),
            sds((gate_count, width), F32),
        ),
        [pltpu.VMEM((3 * channels, halo_cells), BF16)],
        flops=4 * 9 * gate_count * channels * cells,
        moved=6_000_000,
        transcendentals=5 * hid * cells,
    )(
        rows,
        inner,
        outer,
        second,
        cell_here,
        weights_here,
        hidden_grad_here,
        target_here,
        land_here,
        fire_here,
        bias_wide,
        readout_wide,
    )
    send, pre_strip, pre_wide, patches, *strips = call(
        bind(strip_kernel, place, row_count),
        (
            sds((place.half_rows, channels), BF16),
            sds((gate_count, width), BF16),
            sds((gate_count, width), F32),
            sds((place.taps * channels, width), BF16),
            strip,
            strip,
            strip,
        ),
    )(
        edge,
        second,
        outer_column,
        inner_column,
        weights_here,
        bias_wide,
        readout_wide,
        cell_strip,
        hidden_grad_strip,
        fields_strip,
        sums,
    )
    keep, bias = call(
        bind(keep_kernel, place),
        (sds((place.half_rows, channels), F32), sds((8, channels), F32)),
    )(sums, pre_strip, patches, bias, pre_wide)
    hidden_next, cell_next, grad_cell, pre, pre_inner, pre_outer = call(
        bind(edges_kernel, row_count),
        (
            sds((hid, row_count, width), BF16),
            flat,
            flat,
            sds((gate_count, cells), BF16),
            sds((gate_count, width), BF16),
            sds((gate_count, width), BF16),
        ),
        [
            pltpu.VMEM((hid, row_count, width), BF16),
            pltpu.VMEM(flat.shape, F32),
            pltpu.VMEM(flat.shape, F32),
            pltpu.VMEM(flat.shape, F32),
            pltpu.SemaphoreType.DMA((3,)),
        ],
        leaving=3,
        moved=4_000_000,
    )(hidden_rows, cell_rows, grad_cell_rows, pre, *strips, pre_strip)
    pre_inner, pre_outer = permuted(pre_inner, inner_rows), permuted(pre_outer, outer_rows)
    pre_columns = call(
        bind(columns_kernel, row_count, PRE_GROUPS),
        (sds((gate_count // PRE_GROUPS, width), BF16),),
    )(pre_strip, pre_outer, pre_inner)[0]

    block = sds((BIAS_ROWS + place.chunk, channels), BF16)
    token = sds((8, width), F32)
    steps = range(place.plane - 1, 0, -1)
    *sends, keep = call(
        bind(pair_kernel, place),
        (*[block for _ in steps], sds((place.chunk, channels), F32)),
        [pltpu.VMEM((place.half_rows, channels), F32)],
    )(keep, bias, permuted(send, place.phase_pairs(0)))
    received = [
        permuted(send, place.plane_pairs(step)) for step, send in zip(place.scatter_steps, sends)
    ]
    field, turned, field_done = call(
        field_kernel,
        (
            sds((channels * row_count, width), F32),
            sds((3, channels, 3 * gate_count), BF16),
            token,
        ),
        [pltpu.VMEM((3 * gate_count, cells), BF16)],
        flops=2 * 9 * gate_count * channels * cells,
        moved=3_000_000,
    )(pre, weights_here)
    part = call(plane_kernel, block)(keep, bias, *received, field_done)
    pre_inner_columns = permuted(pre_columns, inner_columns)
    pre_outer_columns = permuted(pre_columns, outer_columns)
    phases = len(place.orders[0])
    for phase in range(1, phases):
        is_last = phase == phases - 1
        part = call(bind(add_kernel, scaling if is_last else 1.0), block)(
            part, permuted(part, place.phase_pairs(phase))
        )
    received = [permuted(part, place.plane_pairs(step)) for step in steps[::-1]]
    grad_inputs, grad_hidden, field_done = call(
        bind(field_halo_kernel, place),
        (
            sds((channels - hid, row_count, width), BF16),
            sds((hid, row_count, width), BF16),
            token,
        ),
        [pltpu.VMEM((channels * row_count, width), F32)],
        flops=40 * gate_count * channels * cells * 9,
        moved=2_000_000,
    )(field, turned, pre_outer, pre_inner, pre_outer_columns, pre_inner_columns)
    early = call(join_kernel, sds((place.plane - 1, *block.shape), BF16))(
        part, *received[1:], field_done
    )
    late = received[0]
    early_other = permuted(early, place.phase_pairs(0))
    late_other = permuted(late, place.phase_pairs(0))
    half = [pltpu.VMEM((place.half_rows, channels), F32)]
    grad_kernel, bias = call(
        bind(own_half_kernel, place),
        (sds(kernel_weights.shape, F32), sds((8, channels), F32)),
        half + [pltpu.SemaphoreType.DMA((place.taps,))],
        leaving=1,
        flops=40 * gate_count * channels * cells * 9,
        moved=6 * place.half_rows * channels,
    )(late, early)
    grad_kernel, grad_bias = call(
        bind(other_half_kernel, place),
        (sds(kernel_weights.shape, F32), sds((gate_count,), F32)),
        half + [pltpu.VMEM((gate_count,), F32), pltpu.SemaphoreType.DMA((place.taps + 1,))],
        remote=1,
        leaving=2,
        aliases={4: 0},
        moved=6 * place.half_rows * channels,
    )(bias, early_other, late_other, target_here, grad_kernel)
    shape = hidden_prev.shape
    return (
        hidden_next,
        cell_next.reshape(shape),
        grad_inputs,
        grad_hidden,
        grad_cell.reshape(shape),
        grad_kernel,
        grad_bias,
    )


def solution(mesh):
    lat_count, lon_count = mesh.shape["lat"], mesh.shape["lon"]
    split = Mesh(mesh.devices.reshape(lat_count // 2, 2, lon_count // 2, 2), AXES)
    field = P(None, ("band", "core"), ("reach", "near"))
    flat = P(("band", "core"), ("reach", "near"))

    def run(*args):
        place = Layout(lat_count, lon_count, *args[3].shape[:2])
        return jax.shard_map(
            functools.partial(body, place),
            mesh=split,
            in_specs=(field, field, field, P(), P(), P(), flat, flat, flat, field),
            out_specs=(field, field, field, field, field, P(), P()),
            check_vma=False,
        )(*args)

    return run
```

```python
import functools
import math

import jax
import jax.numpy as jnp
from jax import lax
from jax.experimental import pallas as pl
from jax.experimental.pallas import tpu as pltpu
from jax.sharding import Mesh, PartitionSpec as P

F32 = jnp.float32
BF16 = jnp.bfloat16
AXES = ("band", "core", "reach", "near")
BIAS_ROWS = 16
GROUPS = 4
PRE_GROUPS = 4
LAST = 16
VMEM = pl.BlockSpec(memory_space=pltpu.VMEM)
HBM = pl.BlockSpec(memory_space=pltpu.HBM)
ACROSS = (((1,), (1,)), ((), ()))


def sds(shape, dtype):
    return jax.ShapeDtypeStruct(shape, dtype)


def call(
    kernel,
    out_shape,
    scratch=(),
    remote=0,
    leaving=0,
    aliases=None,
    flops=0,
    moved=0,
    transcendentals=0,
):
    several = isinstance(out_shape, tuple)
    shapes = out_shape if several else (out_shape,)
    out_specs = tuple([HBM] * leaving + [VMEM] * (len(shapes) - leaving))

    def run(*args):
        near = len(args) - remote
        far = [pltpu.with_memory_space_constraint(arg, pltpu.HBM) for arg in args[near:]]
        return pl.pallas_call(
            kernel,
            out_shape=out_shape,
            in_specs=[VMEM] * near + [HBM] * remote,
            out_specs=out_specs if several else out_specs[0],
            input_output_aliases=aliases or {},
            scratch_shapes=list(scratch),
            cost_estimate=pl.CostEstimate(
                flops=flops, bytes_accessed=moved, transcendentals=transcendentals
            ),
            compiler_params=pltpu.CompilerParams(vmem_limit_bytes=24 * 1024 * 1024),
        )(*args[:near], *far)

    return run


class Layout:
    def __init__(self, lat_count, lon_count, taps, gate_count):
        self.lat, self.lon = lat_count, lon_count
        self.half = lon_count // 2
        self.taps, self.half_gates = taps, gate_count // 2
        self.plane = lat_count
        self.scatter_steps = [self.plane - 1, *range(1, self.plane - 1)]
        whole = [("lon", 1 << k) for k in range(1, lon_count.bit_length() - 1)]
        self.orders = ([("lat", 1)] + whole, [("lat", 1)] + whole[::-1])
        step = 8 * self.plane
        self.half_rows = -(-taps * self.half_gates // step) * step
        self.chunk = self.half_rows // self.plane

    def position(self):
        lat = 2 * lax.axis_index("band") + lax.axis_index("core")
        return lat, 2 * lax.axis_index("reach") + lax.axis_index("near")

    def rank(self, phase):
        lat, lon = self.position()

        def digit(order):
            axis, bit = order[phase]
            return ((lat if axis == "lat" else lon) // bit) % 2

        return jnp.where(lat % 2 == 0, digit(self.orders[0]), digit(self.orders[1]))

    def pairs(self, partner):
        result = []
        for lat in range(self.lat):
            for lon in range(self.lon):
                there = partner(lat, lon)
                result.append((lat * self.lon + lon, there[0] * self.lon + there[1]))
        return result

    def phase_pairs(self, phase):
        def partner(lat, lon):
            axis, bit = self.orders[lat % 2][phase]
            return (lat ^ bit, lon) if axis == "lat" else (lat, lon ^ bit)

        return self.pairs(partner)

    def plane_rank(self):
        return 2 * lax.axis_index("band") + lax.axis_index("near")

    def plane_pairs(self, step):
        def partner(lat, lon):
            there = (lat // 2 * 2 + lon % 2) ^ step
            return there // 2 * 2 + lat % 2, lon // 2 * 2 + there % 2

        return self.pairs(partner)

    def inner_rows(self, lat, lon):
        return lat ^ 1, lon

    def outer_rows(self, lat, lon):
        there = lat + 1 if lat % 2 else lat - 1
        if 0 <= there < self.lat:
            return there, lon
        return lat, (lon + self.half) % self.lon

    def inner_columns(self, lat, lon):
        return lat, lon ^ 1

    def outer_columns(self, lat, lon):
        return lat, (lon + (1 if lon % 2 else -1)) % self.lon


def permuted(value, pairs):
    return lax.ppermute(value, AXES, pairs)


def lanes(shape):
    return lax.broadcasted_iota(jnp.int32, shape, len(shape) - 1)


def rolled(value, shift):
    shift %= value.shape[1]
    return pltpu.roll(value, shift, 1) if shift else value


def edge_columns(row, position, columns):
    lane = lanes(row.shape)
    columns = jnp.where(lane == position, rolled(row, position), columns)
    return jnp.where(lane == LAST + position, rolled(row, LAST + position + 1), columns)


def second_columns(row, position, columns):
    lane = lanes(row.shape)
    columns = jnp.where(lane == position, rolled(row, position - 1), columns)
    return jnp.where(lane == LAST + position, rolled(row, LAST + position + 2), columns)


def at_edges(row, position, columns):
    lane = lanes(row.shape)
    width = row.shape[1]
    row = jnp.where(lane == 0, rolled(columns, -position), row)
    return jnp.where(lane == width - 1, rolled(columns, width - 1 - LAST - position), row)


def pick(flag, yes, no):
    return jnp.where(flag, yes, no)


def is_odd(axis):
    return lax.axis_index(axis) % 2 == 1


def row_sends(first, last, inner_out, outer_out):
    odd = is_odd("core")
    inner_out[...] = pick(odd, first, last).astype(BF16)
    outer_out[...] = pick(odd, last, first).astype(BF16)


def row_halo(inner, outer):
    odd = is_odd("core")
    inner, outer = inner[...].astype(F32), outer[...].astype(F32)
    return pick(odd, inner, outer), pick(odd, outer, inner)


def packed(columns, groups):
    count, width = columns.shape[0] // groups, columns.shape[1] // groups
    lane = lanes((count, columns.shape[1]))
    value = columns[0:count]
    for group in range(1, groups):
        part = rolled(columns[group * count : (group + 1) * count], group * width)
        value = jnp.where(lane >= group * width, part, value)
    return value


def unpacked(value, groups):
    width = value.shape[1] // groups
    return jnp.concatenate([rolled(value, -group * width) for group in range(groups)], axis=0)


def column_halo(inner, outer, groups):
    odd = is_odd("near")
    inner, outer = inner[...].astype(F32), outer[...].astype(F32)
    return unpacked(pick(odd, inner, outer), groups), unpacked(pick(odd, outer, inner), groups)


def pack_kernel(below, hidden, inner_out, outer_out, wide_out, below_here, hidden_here, arrived):
    channels, row_count, width = below.shape
    size = channels * row_count
    part = channels // 2
    copies = []
    for source, here in ((below, below_here), (hidden, hidden_here)):
        for at in (pl.ds(0, part), pl.ds(part, part)):
            copies.append(
                pltpu.make_async_copy(source.at[at], here.at[at], arrived.at[len(copies)])
            )
            copies[-1].start()
    for index, copy in enumerate(copies):
        here = (below_here, hidden_here)[index // 2]
        copy.wait()
        value = here[pl.ds(index % 2 * part, part)].astype(F32)
        at = pl.ds(index * part * row_count, part * row_count)
        wide_out[at, :] = value.reshape(part * row_count, width)
    edges = [
        wide_out[pl.ds(index, 2 * channels, stride=row_count), :] for index in (0, row_count - 1)
    ]
    row_sends(edges[0], edges[1], inner_out, outer_out)


def down_rows(values, width):
    count = values.shape[0]
    return jnp.broadcast_to(values[None, :], (width, count)).T


def prepare_kernel(
    wide,
    cell_hbm,
    weights_hbm,
    hidden_grad_hbm,
    target_hbm,
    land_hbm,
    fire_hbm,
    gate_bias_hbm,
    readout_hbm,
    rows_out,
    columns_out,
    second_out,
    cell_strip_out,
    hidden_grad_strip_out,
    fields_strip_out,
    cell_out,
    weights_out,
    hidden_grad_out,
    target_out,
    land_out,
    fire_out,
    bias_wide_out,
    readout_wide_out,
    hidden_grad_here,
    gate_bias_here,
    readout_here,
    arrived,
):
    row_count, channels, width = rows_out.shape
    copies = [
        pltpu.make_async_copy(source, target, arrived.at[index])
        for index, (source, target) in enumerate(
            (
                (cell_hbm, cell_out),
                *(
                    (weights_hbm.at[tap], weights_out.at[:, pl.ds(tap * channels, channels)])
                    for tap in range(weights_hbm.shape[0])
                ),
                (hidden_grad_hbm, hidden_grad_here),
                (target_hbm, target_out),
                (land_hbm, land_out),
                (fire_hbm, fire_out),
                (gate_bias_hbm, gate_bias_here),
                (readout_hbm, readout_here),
            )
        )
    ]
    for copy in copies:
        copy.start()
    columns = jnp.zeros((channels, width), F32)
    second = jnp.zeros((channels, width), F32)
    for index in range(row_count):
        row = wide[pl.ds(index, channels, stride=row_count), :]
        rows_out[index] = row.astype(BF16)
        columns = edge_columns(row, index + 1, columns)
        second = second_columns(row, index + 1, second)
    columns_out[...] = columns
    second_out[...] = second
    for copy in copies:
        copy.wait()
    hidden_grad_out[...] = hidden_grad_here[...].astype(F32).reshape(hidden_grad_out.shape)
    bias_wide_out[...] = down_rows(gate_bias_here[...], width)
    readout_wide_out[...] = down_rows(readout_here[...], width)
    hid = hidden_grad_here.shape[0]
    cell_strip = jnp.zeros((hid, width), F32)
    hidden_grad_strip = jnp.zeros((hid, width), F32)
    fields_strip = jnp.zeros((8, width), F32)
    for index in range(row_count):
        strided = pl.ds(index, hid, stride=row_count)
        cell_strip = edge_columns(cell_out[strided, :], index + 1, cell_strip)
        hidden_grad_strip = edge_columns(hidden_grad_out[strided, :], index + 1, hidden_grad_strip)
        at = slice(index, index + 1)
        fields = [target_out[at, :], land_out[at, :].astype(F32), fire_out[at, :].astype(F32)]
        fields = jnp.concatenate(fields + [jnp.zeros((5, width), F32)], axis=0)
        fields_strip = edge_columns(fields, index + 1, fields_strip)
    cell_strip_out[...] = cell_strip
    hidden_grad_strip_out[...] = hidden_grad_strip
    fields_strip_out[...] = fields_strip


def columns_kernel(row_count, groups, columns, outer, inner, packed_out, *whole_out):
    north, south = row_halo(inner, outer)
    value = edge_columns(north, 0, columns[...].astype(F32))
    value = edge_columns(south, row_count + 1, value)
    packed_out[...] = packed(value, groups).astype(BF16)
    for out in whole_out:
        out[...] = value.astype(BF16)


def encode(bias):
    high = bias.astype(BF16).astype(F32)
    return jnp.concatenate([high, bias - high], axis=0)


def decode(block):
    return block[0:8] + block[8:16]


def cell_step(part, cell_before, hidden_grad, target, land, fire, readout):
    hid = part.shape[0] // 4
    input_gate = 0.5 + 0.5 * jnp.tanh(0.5 * part[0:hid])
    forget_gate = 0.5 + 0.5 * jnp.tanh(0.5 * part[hid : 2 * hid])
    output_gate = 0.5 + 0.5 * jnp.tanh(0.5 * part[2 * hid : 3 * hid])
    candidate = jnp.tanh(part[3 * hid : 4 * hid])
    cell_next = land * (forget_gate * cell_before + input_gate * candidate)
    squashed = jnp.tanh(cell_next)
    hidden_next = (output_gate * squashed).astype(BF16).astype(F32)
    predicted = jnp.sum(readout * hidden_next, axis=0, keepdims=True)
    total_grad = hidden_grad + 2.0 * (fire * (predicted - target)) * readout
    cell_grad = land * total_grad * output_gate * (1.0 - squashed * squashed)
    pre_grad = jnp.concatenate(
        [
            cell_grad * candidate * input_gate * (1.0 - input_gate),
            cell_grad * cell_before * forget_gate * (1.0 - forget_gate),
            total_grad * squashed * output_gate * (1.0 - output_gate),
            cell_grad * input_gate * (1.0 - candidate * candidate),
        ],
        axis=0,
    )
    return hidden_next, cell_next, cell_grad * forget_gate, pre_grad


def gates_kernel(
    place,
    rows_in,
    inner_row,
    outer_row,
    second,
    cell_prev,
    weights,
    hidden_grad,
    target,
    land,
    fire,
    bias_wide,
    readout_wide,
    hidden_out,
    cell_out,
    grad_cell_out,
    pre_out,
    second_out,
    sums,
    bias_out,
    shifted,
):
    row_count, channels, width = rows_in.shape
    gate_count = weights.shape[0]
    hid = gate_count // 4
    half_gates = place.half_gates
    north, south = row_halo(inner_row, outer_row)
    columns = second_columns(north, 0, second[...])
    second_out[...] = second_columns(south, row_count + 1, columns).astype(BF16)
    for position in range(row_count + 2):
        if position == 0:
            row = north
        elif position == row_count + 1:
            row = south
        else:
            row = rows_in[position - 1].astype(F32)
        at = pl.ds(position * width, width)
        shifted[0:channels, at] = rolled(row, 1).astype(BF16)
        shifted[channels : 2 * channels, at] = row.astype(BF16)
        shifted[2 * channels : 3 * channels, at] = rolled(row, -1).astype(BF16)

    bias_total = jnp.zeros((gate_count, width), F32)
    lane = lanes((gate_count, width))
    inside = (lane > 0) & (lane < width - 1)
    readout = readout_wide[...]
    pair = 2 if row_count % 2 == 0 else 1
    for base in range(0, row_count, pair):
        preact = jnp.zeros((gate_count, pair * width), F32)
        for a in range(3):
            preact += jnp.dot(
                weights[:, pl.ds(3 * a * channels, 3 * channels)],
                shifted[:, pl.ds((base + a) * width, pair * width)],
                preferred_element_type=F32,
            )
        for offset in range(pair):
            index = base + offset
            strided = pl.ds(index, hid, stride=row_count)
            at = slice(index, index + 1)
            hidden_next, cell_next, grad_cell, pre_grad = cell_step(
                preact[:, offset * width : (offset + 1) * width] + bias_wide[...],
                cell_prev[strided, :],
                hidden_grad[strided, :],
                target[at, :],
                land[at, :].astype(F32),
                fire[at, :].astype(F32),
                readout,
            )
            hidden_out[strided, :] = hidden_next
            cell_out[strided, :] = cell_next
            grad_cell_out[strided, :] = grad_cell
            pre_grad = jnp.where(inside, pre_grad, 0.0)
            bias_total += pre_grad
            pre_out[:, pl.ds(index * width, width)] = pre_grad.astype(BF16)
    bias_out[...] = bias_total

    for a in range(3):
        product = lax.dot_general(
            pre_out[...],
            shifted[:, pl.ds(a * width, row_count * width)],
            ACROSS,
            preferred_element_type=F32,
        )
        for b in range(3):
            for half in range(2):
                at = half * place.half_rows + (3 * a + b) * half_gates
                sums[at : at + half_gates, :] = product[
                    half * half_gates : (half + 1) * half_gates, b * channels : (b + 1) * channels
                ]
    used = place.taps * half_gates
    if place.half_rows > used:
        for half in range(2):
            at = half * place.half_rows
            sums[at + used : at + place.half_rows, :] = jnp.zeros(
                (place.half_rows - used, channels), F32
            )


def add_strip(place, half, sums, pre_strip, patches, out):
    half_gates, channels = place.half_gates, sums.shape[1]
    gates = pre_strip[pl.ds(pl.multiple_of(half * half_gates, half_gates), half_gates), :]
    product = lax.dot_general(gates, patches[...], ACROSS, preferred_element_type=F32)
    base = half * place.half_rows
    for tap in range(place.taps):
        at = pl.ds(pl.multiple_of(base + tap * half_gates, 8), half_gates)
        value = sums[at, :] + product[:, tap * channels : (tap + 1) * channels]
        out[tap * half_gates : (tap + 1) * half_gates, :] = value.astype(out.dtype)
    used = place.taps * half_gates
    if place.half_rows > used:
        rest = jnp.zeros((place.half_rows - used, channels), out.dtype)
        out[used:, :] = rest


def strip_kernel(
    place,
    row_count,
    edge,
    second,
    outer_column,
    inner_column,
    weights,
    bias_wide,
    readout_wide,
    cell_strip,
    hidden_grad_strip,
    fields_strip,
    sums,
    send_out,
    pre_out,
    pre_wide_out,
    patches,
    hidden_out,
    cell_out,
    grad_cell_out,
):
    channels, width = edge.shape
    west, east = column_halo(inner_column, outer_column, GROUPS)
    near_first = lanes((channels, width)) < LAST
    inner = second[...].astype(F32)
    columns = (
        jnp.where(near_first, rolled(west, -LAST), inner),
        edge[...].astype(F32),
        jnp.where(near_first, inner, rolled(east, LAST)),
    )
    for a in range(3):
        for b in range(3):
            at = (3 * a + b) * channels
            patches[at : at + channels, :] = rolled(columns[b], 1 - a).astype(BF16)
    preact = jnp.dot(weights[...], patches[...], preferred_element_type=F32) + bias_wide[...]
    hidden_next, cell_next, grad_cell, pre_grad = cell_step(
        preact,
        cell_strip[...],
        hidden_grad_strip[...],
        fields_strip[0:1, :],
        fields_strip[1:2, :],
        fields_strip[2:3, :],
        readout_wide[...],
    )
    hidden_out[...] = hidden_next
    cell_out[...] = cell_next
    grad_cell_out[...] = grad_cell
    lane = lanes(pre_grad.shape)
    lane = jnp.where(lane >= LAST, lane - LAST, lane)
    pre_grad = jnp.where((lane >= 1) & (lane <= row_count), pre_grad, 0.0)
    pre_out[...] = pre_grad.astype(BF16)
    pre_wide_out[...] = pre_grad
    add_strip(place, 1 - place.rank(0), sums, pre_out, patches, send_out)


def keep_kernel(place, sums, pre_strip, patches, bias_partial, pre_wide, out, bias_out):
    add_strip(place, place.rank(0), sums, pre_strip, patches, out)
    channels = sums.shape[1]
    bias_total = bias_partial[...] + pre_wide[...]
    ones = jnp.ones((8, bias_total.shape[1]), BF16)
    high = bias_total.astype(BF16)
    low = (bias_total - high.astype(F32)).astype(BF16)
    flat = lax.dot_general(ones, high, ACROSS, preferred_element_type=F32)
    flat += lax.dot_general(ones, low, ACROSS, preferred_element_type=F32)
    odd = lax.broadcasted_iota(jnp.int32, (8, channels), 0) % 2 == 1
    bias_out[...] = jnp.where(odd, flat[:, channels : 2 * channels], flat[:, 0:channels])


def edges_kernel(
    row_count,
    hidden,
    cell,
    grad_cell,
    pre,
    hidden_strip,
    cell_strip,
    grad_cell_strip,
    pre_strip,
    hidden_hbm,
    cell_hbm,
    grad_cell_hbm,
    pre_out,
    inner_out,
    outer_out,
    hidden_low,
    hidden_here,
    cell_here,
    grad_cell_here,
    left,
):
    hid, _, width = hidden_low.shape
    leaving = []
    for source, strip, here, ready, target in (
        (cell, cell_strip, cell_here, cell_here, cell_hbm),
        (grad_cell, grad_cell_strip, grad_cell_here, grad_cell_here, grad_cell_hbm),
        (hidden, hidden_strip, hidden_here, hidden_low, hidden_hbm),
    ):
        columns = strip[...]
        for index in range(row_count):
            strided = pl.ds(index, hid, stride=row_count)
            here[strided, :] = at_edges(source[strided, :], index + 1, columns)
        if ready is hidden_low:
            hidden_low[...] = here[...].reshape(hidden_low.shape).astype(BF16)
        leaving.append(pltpu.make_async_copy(ready, target, left.at[len(leaving)]))
        leaving[-1].start()
    first, last = None, None
    columns = pre_strip[...].astype(F32)
    for index in range(row_count):
        at = pl.ds(index * width, width)
        row = at_edges(pre[:, at].astype(F32), index + 1, columns)
        pre_out[:, at] = row.astype(BF16)
        first = row if index == 0 else first
        last = row
    row_sends(first, last, inner_out, outer_out)
    for copy in leaving:
        copy.wait()


def pair_kernel(place, keep, bias, received, *outs):
    sends, keep_out, scratch = outs[:-2], outs[-2], outs[-1]
    chunk = place.chunk
    rank = place.plane_rank()
    scratch[...] = keep[...] + received[...].astype(F32)
    block = encode(bias[...]).astype(BF16)
    for step, send in zip(place.scatter_steps, sends):
        send[0:BIAS_ROWS, :] = block
        at = pl.ds(pl.multiple_of((rank ^ step) * chunk, 8), chunk)
        send[BIAS_ROWS:, :] = scratch[at, :].astype(BF16)
    keep_out[...] = scratch[pl.ds(pl.multiple_of(rank * chunk, 8), chunk), :]


def plane_kernel(keep, bias, *refs):
    received, out = refs[:-2], refs[-1]
    total, bias_total = keep[...], bias[...]
    for ref in received:
        total += ref[BIAS_ROWS:, :].astype(F32)
        bias_total += decode(ref[0:BIAS_ROWS, :].astype(F32))
    out[0:BIAS_ROWS, :] = encode(bias_total).astype(BF16)
    out[BIAS_ROWS:, :] = total.astype(BF16)


def join_kernel(*refs):
    blocks, out = refs[:-2], refs[-1]
    for index, block in enumerate(blocks):
        out[index] = block[...]


def add_kernel(scale, own, received, out):
    here, there = own[...].astype(F32), received[...].astype(F32)
    bias = (decode(here[0:BIAS_ROWS]) + decode(there[0:BIAS_ROWS])) * scale
    out[0:BIAS_ROWS, :] = encode(bias).astype(BF16)
    out[BIAS_ROWS:, :] = ((here[BIAS_ROWS:] + there[BIAS_ROWS:]) * scale).astype(BF16)


def store_half(place, half, blocks, out, wide, left):
    chunk, half_gates = place.chunk, place.half_gates
    gates = pl.ds(pl.multiple_of(half * half_gates, half_gates), half_gates)
    rank = place.plane_rank()
    for step, block in enumerate(blocks):
        at = pl.ds(pl.multiple_of((rank ^ step) * chunk, 8), chunk)
        wide[at, :] = block[BIAS_ROWS:, :].astype(F32)
    copies = []
    for tap in range(place.taps):
        source = wide.at[tap * half_gates : (tap + 1) * half_gates, :]
        copies.append(pltpu.make_async_copy(source, out.at[tap, gates, :], left.at[tap]))
        copies[-1].start()
    return copies


def in_steps(place, early, late):
    blocks = [early.at[index] for index in range(place.plane - 1)]
    return blocks[:-1] + [late] + blocks[-1:]


def own_half_kernel(place, late, early, out, bias_out, wide, left):
    blocks = in_steps(place, early, late)
    copies = store_half(place, place.rank(0), blocks, out, wide, left)
    rank = place.plane_rank()
    bias = decode(blocks[0][0:BIAS_ROWS, :].astype(F32))
    for step in range(1, place.plane):
        bias = pick(rank == step, decode(blocks[step][0:BIAS_ROWS, :].astype(F32)), bias)
    bias_out[...] = bias
    for copy in copies:
        copy.wait()


def other_half_kernel(
    place, bias_own, early, late, after, out_before, out, bias_out, wide, bias_here, left
):
    del after, out_before
    blocks = in_steps(place, early, late)
    copies = store_half(place, 1 - place.rank(0), blocks, out, wide, left)
    rank = place.plane_rank()
    bias = decode(blocks[0][0:BIAS_ROWS, :].astype(F32))
    for step in range(1, place.plane):
        bias = pick(rank == step, decode(blocks[step][0:BIAS_ROWS, :].astype(F32)), bias)
    bias += bias_own[...]
    width = bias.shape[1]
    for index in range(bias_here.shape[0] // width):
        bias_here[pl.ds(index * width, width)] = bias[index]
    bias_copy = pltpu.make_async_copy(bias_here, bias_out, left.at[place.taps])
    bias_copy.start()
    bias_copy.wait()
    for copy in copies:
        copy.wait()


def field_kernel(pre, weights, wide_out, turned_out, done_out, shifted):
    done_out[...] = jnp.zeros(done_out.shape, F32)
    gate_count, cells = pre.shape
    width = wide_out.shape[1]
    channels = weights.shape[1] // 9
    row_count = cells // width
    lane = lanes((gate_count, width))
    for index in range(row_count):
        at = pl.ds(index * width, width)
        row = pre[:, at].astype(F32)
        left = jnp.where(lane == 0, 0.0, rolled(row, 1))
        right = jnp.where(lane == width - 1, 0.0, rolled(row, -1))
        shifted[0:gate_count, at] = right.astype(BF16)
        shifted[gate_count : 2 * gate_count, at] = pre[:, at]
        shifted[2 * gate_count : 3 * gate_count, at] = left.astype(BF16)
    for a in range(3):
        for b in range(3):
            turned_out[a, :, b * gate_count : (b + 1) * gate_count] = (
                weights[:, pl.ds((3 * a + b) * channels, channels)].T
            )

    def product(a, index, count):
        return jnp.dot(
            turned_out[a],
            shifted[:, pl.ds(index * width, count * width)],
            preferred_element_type=F32,
        )

    pair = 2 if row_count % 2 == 0 else 1
    for base in range(0, row_count, pair):
        total = product(1, base, pair)
        for a, first in ((2, base - 1), (0, base + 1)):
            low, high = max(first, 0), min(first + pair, row_count)
            if low >= high:
                continue
            part = product(a, low, high - low)
            blank = jnp.zeros((channels, width), F32)
            parts = [blank] * (low - first) + [part] + [blank] * (first + pair - high)
            total += jnp.concatenate(parts, axis=1)
        for offset in range(pair):
            value = total[:, offset * width : (offset + 1) * width]
            wide_out[pl.ds(base + offset, channels, stride=row_count), :] = value


def field_halo_kernel(
    place,
    wide,
    turned,
    outer_row,
    inner_row,
    outer_column,
    inner_column,
    inputs_out,
    hidden_out,
    done_out,
    total,
):
    done_out[...] = jnp.zeros(done_out.shape, F32)
    hid, row_count, width = hidden_out.shape
    channels = turned.shape[1]
    gate_count = turned.shape[2] // 3
    north, south = row_halo(inner_row, outer_row)
    west, east = column_halo(inner_column, outer_column, PRE_GROUPS)
    lane = lanes((gate_count, width))
    lat = place.position()[0]

    def row_part(taps, row, position):
        left = jnp.where(lane == 0, rolled(west, -LAST - position), rolled(row, 1))
        right = rolled(east, width - 1 - position)
        right = jnp.where(lane == width - 1, right, rolled(row, -1))
        stack = jnp.concatenate([right, row, left], axis=0).astype(BF16)
        return jnp.dot(taps, stack, preferred_element_type=F32)

    above = row_part(turned[jnp.where(lat == 0, 0, 2)], north, 0)
    below = row_part(turned[jnp.where(lat == place.lat - 1, 2, 0)], south, row_count + 1)

    inside = (lane >= 1) & (lane <= row_count)
    west = jnp.where(inside, rolled(west, -LAST), 0.0)
    east = jnp.where(inside, east, 0.0)
    sides = [rolled(west, a - 1) for a in range(3)] + [rolled(east, LAST + a - 1) for a in range(3)]
    taps = [turned[a, :, 2 * gate_count : 3 * gate_count] for a in range(3)]
    taps += [turned[a, :, 0:gate_count] for a in range(3)]
    columns = jnp.dot(
        jnp.concatenate(taps, axis=1),
        jnp.concatenate(sides, axis=0).astype(BF16),
        preferred_element_type=F32,
    )
    blank = jnp.zeros((channels, width), F32)
    for index in range(row_count):
        strided = pl.ds(index, channels, stride=row_count)
        value = wide[strided, :] + at_edges(blank, index + 1, columns)
        if index == 0:
            value += above
        if index == row_count - 1:
            value += below
        total[strided, :] = value
    size = (channels - hid) * row_count
    inputs_out[...] = total[0:size, :].reshape(inputs_out.shape).astype(BF16)
    hidden_out[...] = total[size:, :].reshape(hidden_out.shape).astype(BF16)


def body(
    place,
    inputs_below,
    hidden_prev,
    cell_prev,
    kernel_weights,
    gate_bias,
    readout,
    target_field,
    land_mask,
    fire_mask,
    hidden_grad,
):
    hid, row_count, width = hidden_prev.shape
    gate_count, channels = kernel_weights.shape[1:]
    cells = row_count * width
    halo_cells = (row_count + 2) * width
    scaling = 1.0 / math.sqrt(cells * place.lat * place.lon)
    bind = functools.partial
    inner_rows, outer_rows = place.pairs(place.inner_rows), place.pairs(place.outer_rows)
    inner_columns = place.pairs(place.inner_columns)
    outer_columns = place.pairs(place.outer_columns)
    flat = sds((hid * row_count, width), F32)
    strip = sds((hid, width), F32)

    inner, outer, wide = call(
        pack_kernel,
        (
            sds((channels, width), BF16),
            sds((channels, width), BF16),
            sds((channels * row_count, width), F32),
        ),
        [
            pltpu.VMEM(inputs_below.shape, BF16),
            pltpu.VMEM(hidden_prev.shape, BF16),
            pltpu.SemaphoreType.DMA((4,)),
        ],
        remote=2,
        moved=4 * channels * cells,
    )(inputs_below, hidden_prev)
    inner, outer = permuted(inner, inner_rows), permuted(outer, outer_rows)
    (
        rows,
        columns,
        second,
        cell_strip,
        hidden_grad_strip,
        fields_strip,
        cell_here,
        weights_here,
        hidden_grad_here,
        target_here,
        land_here,
        fire_here,
        bias_wide,
        readout_wide,
    ) = call(
        prepare_kernel,
        (
            sds((row_count, channels, width), BF16),
            sds((channels, width), F32),
            sds((channels, width), F32),
            strip,
            strip,
            sds((8, width), F32),
            flat,
            sds((gate_count, place.taps * channels), BF16),
            flat,
            sds(target_field.shape, F32),
            sds(land_mask.shape, jnp.int32),
            sds(fire_mask.shape, jnp.int32),
            sds((gate_count, width), F32),
            sds((hid, width), F32),
        ),
        [
            pltpu.VMEM(hidden_grad.shape, BF16),
            pltpu.VMEM(gate_bias.shape, F32),
            pltpu.VMEM(readout.shape, F32),
            pltpu.SemaphoreType.DMA((7 + place.taps,)),
        ],
        remote=8,
        moved=6_000_000,
    )(
        wide,
        cell_prev.reshape(hid * row_count, width),
        kernel_weights,
        hidden_grad,
        target_field,
        land_mask,
        fire_mask,
        gate_bias,
        readout,
    )
    columns, edge = call(
        bind(columns_kernel, row_count, GROUPS),
        (sds((channels // GROUPS, width), BF16), sds((channels, width), BF16)),
    )(columns, outer, inner)
    inner_column = permuted(columns, inner_columns)
    outer_column = permuted(columns, outer_columns)
    hidden_rows, cell_rows, grad_cell_rows, pre, second, sums, bias = call(
        bind(gates_kernel, place),
        (
            flat,
            flat,
            flat,
            sds((gate_count, cells), BF16),
            sds((channels, width), BF16),
            sds((2 * place.half_rows, channels), F32),
            sds((gate_count, width), F32),
        ),
        [pltpu.VMEM((3 * channels, halo_cells), BF16)],
        flops=4 * 9 * gate_count * channels * cells,
        moved=6_000_000,
        transcendentals=5 * hid * cells,
    )(
        rows,
        inner,
        outer,
        second,
        cell_here,
        weights_here,
        hidden_grad_here,
        target_here,
        land_here,
        fire_here,
        bias_wide,
        readout_wide,
    )
    send, pre_strip, pre_wide, patches, *strips = call(
        bind(strip_kernel, place, row_count),
        (
            sds((place.half_rows, channels), BF16),
            sds((gate_count, width), BF16),
            sds((gate_count, width), F32),
            sds((place.taps * channels, width), BF16),
            strip,
            strip,
            strip,
        ),
    )(
        edge,
        second,
        outer_column,
        inner_column,
        weights_here,
        bias_wide,
        readout_wide,
        cell_strip,
        hidden_grad_strip,
        fields_strip,
        sums,
    )
    keep, bias = call(
        bind(keep_kernel, place),
        (sds((place.half_rows, channels), F32), sds((8, channels), F32)),
    )(sums, pre_strip, patches, bias, pre_wide)
    hidden_next, cell_next, grad_cell, pre, pre_inner, pre_outer = call(
        bind(edges_kernel, row_count),
        (
            sds((hid, row_count, width), BF16),
            flat,
            flat,
            sds((gate_count, cells), BF16),
            sds((gate_count, width), BF16),
            sds((gate_count, width), BF16),
        ),
        [
            pltpu.VMEM((hid, row_count, width), BF16),
            pltpu.VMEM(flat.shape, F32),
            pltpu.VMEM(flat.shape, F32),
            pltpu.VMEM(flat.shape, F32),
            pltpu.SemaphoreType.DMA((3,)),
        ],
        leaving=3,
        moved=4_000_000,
    )(hidden_rows, cell_rows, grad_cell_rows, pre, *strips, pre_strip)
    pre_inner, pre_outer = permuted(pre_inner, inner_rows), permuted(pre_outer, outer_rows)
    pre_columns = call(
        bind(columns_kernel, row_count, PRE_GROUPS),
        (sds((gate_count // PRE_GROUPS, width), BF16),),
    )(pre_strip, pre_outer, pre_inner)[0]

    block = sds((BIAS_ROWS + place.chunk, channels), BF16)
    token = sds((8, width), F32)
    steps = range(place.plane - 1, 0, -1)
    *sends, keep = call(
        bind(pair_kernel, place),
        (*[block for _ in steps], sds((place.chunk, channels), F32)),
        [pltpu.VMEM((place.half_rows, channels), F32)],
    )(keep, bias, permuted(send, place.phase_pairs(0)))
    received = [
        permuted(send, place.plane_pairs(step)) for step, send in zip(place.scatter_steps, sends)
    ]
    field, turned, field_done = call(
        field_kernel,
        (
            sds((channels * row_count, width), F32),
            sds((3, channels, 3 * gate_count), BF16),
            token,
        ),
        [pltpu.VMEM((3 * gate_count, cells), BF16)],
        flops=2 * 9 * gate_count * channels * cells,
        moved=3_000_000,
    )(pre, weights_here)
    part = call(plane_kernel, block)(keep, bias, *received, field_done)
    pre_inner_columns = permuted(pre_columns, inner_columns)
    pre_outer_columns = permuted(pre_columns, outer_columns)
    phases = len(place.orders[0])
    for phase in range(1, phases):
        is_last = phase == phases - 1
        part = call(bind(add_kernel, scaling if is_last else 1.0), block)(
            part, permuted(part, place.phase_pairs(phase))
        )
    received = [permuted(part, place.plane_pairs(step)) for step in steps[::-1]]
    grad_inputs, grad_hidden, field_done = call(
        bind(field_halo_kernel, place),
        (
            sds((channels - hid, row_count, width), BF16),
            sds((hid, row_count, width), BF16),
            token,
        ),
        [pltpu.VMEM((channels * row_count, width), F32)],
        flops=40 * gate_count * channels * cells * 9,
        moved=2_000_000,
    )(field, turned, pre_outer, pre_inner, pre_outer_columns, pre_inner_columns)
    early = call(join_kernel, sds((place.plane - 1, *block.shape), BF16))(
        part, *received[:-2], received[-1], field_done
    )
    late = received[-2]
    early_other = permuted(early, place.phase_pairs(0))
    late_other = permuted(late, place.phase_pairs(0))
    half = [pltpu.VMEM((place.half_rows, channels), F32)]
    grad_kernel, bias = call(
        bind(own_half_kernel, place),
        (sds(kernel_weights.shape, F32), sds((8, channels), F32)),
        half + [pltpu.SemaphoreType.DMA((place.taps,))],
        leaving=1,
        flops=40 * gate_count * channels * cells * 9,
        moved=6 * place.half_rows * channels,
    )(late, early)
    grad_kernel, grad_bias = call(
        bind(other_half_kernel, place),
        (sds(kernel_weights.shape, F32), sds((gate_count,), F32)),
        half + [pltpu.VMEM((gate_count,), F32), pltpu.SemaphoreType.DMA((place.taps + 1,))],
        remote=1,
        leaving=2,
        aliases={4: 0},
        moved=6 * place.half_rows * channels,
    )(bias, early_other, late_other, target_here, grad_kernel)
    shape = hidden_prev.shape
    return (
        hidden_next,
        cell_next.reshape(shape),
        grad_inputs,
        grad_hidden,
        grad_cell.reshape(shape),
        grad_kernel,
        grad_bias,
    )


def solution(mesh):
    lat_count, lon_count = mesh.shape["lat"], mesh.shape["lon"]
    split = Mesh(mesh.devices.reshape(lat_count // 2, 2, lon_count // 2, 2), AXES)
    field = P(None, ("band", "core"), ("reach", "near"))
    flat = P(("band", "core"), ("reach", "near"))

    def run(*args):
        place = Layout(lat_count, lon_count, *args[3].shape[:2])
        return jax.shard_map(
            functools.partial(body, place),
            mesh=split,
            in_specs=(field, field, field, P(), P(), P(), flat, flat, flat, field),
            out_specs=(field, field, field, field, field, P(), P()),
            check_vma=False,
        )(*args)

    return run
```

```python
import functools
import math

import jax
import jax.numpy as jnp
from jax import lax
from jax.experimental import pallas as pl
from jax.experimental.pallas import tpu as pltpu
from jax.sharding import Mesh, PartitionSpec as P

F32 = jnp.float32
BF16 = jnp.bfloat16
AXES = ("band", "core", "reach", "near")
BIAS_ROWS = 16
GROUPS = 4
PRE_GROUPS = 4
LAST = 16
VMEM = pl.BlockSpec(memory_space=pltpu.VMEM)
HBM = pl.BlockSpec(memory_space=pltpu.HBM)
ACROSS = (((1,), (1,)), ((), ()))


def sds(shape, dtype):
    return jax.ShapeDtypeStruct(shape, dtype)


def call(
    kernel,
    out_shape,
    scratch=(),
    remote=0,
    leaving=0,
    aliases=None,
    flops=0,
    moved=0,
    transcendentals=0,
):
    several = isinstance(out_shape, tuple)
    shapes = out_shape if several else (out_shape,)
    out_specs = tuple([HBM] * leaving + [VMEM] * (len(shapes) - leaving))

    def run(*args):
        near = len(args) - remote
        far = [pltpu.with_memory_space_constraint(arg, pltpu.HBM) for arg in args[near:]]
        return pl.pallas_call(
            kernel,
            out_shape=out_shape,
            in_specs=[VMEM] * near + [HBM] * remote,
            out_specs=out_specs if several else out_specs[0],
            input_output_aliases=aliases or {},
            scratch_shapes=list(scratch),
            cost_estimate=pl.CostEstimate(
                flops=flops, bytes_accessed=moved, transcendentals=transcendentals
            ),
            compiler_params=pltpu.CompilerParams(vmem_limit_bytes=24 * 1024 * 1024),
        )(*args[:near], *far)

    return run


class Layout:
    def __init__(self, lat_count, lon_count, taps, gate_count):
        self.lat, self.lon = lat_count, lon_count
        self.half = lon_count // 2
        self.taps, self.half_gates = taps, gate_count // 2
        self.plane = lat_count
        self.scatter_steps = [1, self.plane - 1, *range(2, self.plane - 1)]
        whole = [("lon", 1 << k) for k in range(1, lon_count.bit_length() - 1)]
        self.orders = ([("lat", 1)] + whole, [("lat", 1)] + whole[::-1])
        step = 8 * self.plane
        self.half_rows = -(-taps * self.half_gates // step) * step
        self.chunk = self.half_rows // self.plane

    def position(self):
        lat = 2 * lax.axis_index("band") + lax.axis_index("core")
        return lat, 2 * lax.axis_index("reach") + lax.axis_index("near")

    def rank(self, phase):
        lat, lon = self.position()

        def digit(order):
            axis, bit = order[phase]
            return ((lat if axis == "lat" else lon) // bit) % 2

        return jnp.where(lat % 2 == 0, digit(self.orders[0]), digit(self.orders[1]))

    def pairs(self, partner):
        result = []
        for lat in range(self.lat):
            for lon in range(self.lon):
                there = partner(lat, lon)
                result.append((lat * self.lon + lon, there[0] * self.lon + there[1]))
        return result

    def phase_pairs(self, phase):
        def partner(lat, lon):
            axis, bit = self.orders[lat % 2][phase]
            return (lat ^ bit, lon) if axis == "lat" else (lat, lon ^ bit)

        return self.pairs(partner)

    def plane_rank(self):
        return 2 * lax.axis_index("band") + lax.axis_index("near")

    def plane_pairs(self, step):
        def partner(lat, lon):
            there = (lat // 2 * 2 + lon % 2) ^ step
            return there // 2 * 2 + lat % 2, lon // 2 * 2 + there % 2

        return self.pairs(partner)

    def inner_rows(self, lat, lon):
        return lat ^ 1, lon

    def outer_rows(self, lat, lon):
        there = lat + 1 if lat % 2 else lat - 1
        if 0 <= there < self.lat:
            return there, lon
        return lat, (lon + self.half) % self.lon

    def inner_columns(self, lat, lon):
        return lat, lon ^ 1

    def outer_columns(self, lat, lon):
        return lat, (lon + (1 if lon % 2 else -1)) % self.lon


def permuted(value, pairs):
    return lax.ppermute(value, AXES, pairs)


def lanes(shape):
    return lax.broadcasted_iota(jnp.int32, shape, len(shape) - 1)


def rolled(value, shift):
    shift %= value.shape[1]
    return pltpu.roll(value, shift, 1) if shift else value


def edge_columns(row, position, columns):
    lane = lanes(row.shape)
    columns = jnp.where(lane == position, rolled(row, position), columns)
    return jnp.where(lane == LAST + position, rolled(row, LAST + position + 1), columns)


def second_columns(row, position, columns):
    lane = lanes(row.shape)
    columns = jnp.where(lane == position, rolled(row, position - 1), columns)
    return jnp.where(lane == LAST + position, rolled(row, LAST + position + 2), columns)


def at_edges(row, position, columns):
    lane = lanes(row.shape)
    width = row.shape[1]
    row = jnp.where(lane == 0, rolled(columns, -position), row)
    return jnp.where(lane == width - 1, rolled(columns, width - 1 - LAST - position), row)


def pick(flag, yes, no):
    return jnp.where(flag, yes, no)


def is_odd(axis):
    return lax.axis_index(axis) % 2 == 1


def row_sends(first, last, inner_out, outer_out):
    odd = is_odd("core")
    inner_out[...] = pick(odd, first, last).astype(BF16)
    outer_out[...] = pick(odd, last, first).astype(BF16)


def row_halo(inner, outer):
    odd = is_odd("core")
    inner, outer = inner[...].astype(F32), outer[...].astype(F32)
    return pick(odd, inner, outer), pick(odd, outer, inner)


def packed(columns, groups):
    count, width = columns.shape[0] // groups, columns.shape[1] // groups
    lane = lanes((count, columns.shape[1]))
    value = columns[0:count]
    for group in range(1, groups):
        part = rolled(columns[group * count : (group + 1) * count], group * width)
        value = jnp.where(lane >= group * width, part, value)
    return value


def unpacked(value, groups):
    width = value.shape[1] // groups
    return jnp.concatenate([rolled(value, -group * width) for group in range(groups)], axis=0)


def column_halo(inner, outer, groups):
    odd = is_odd("near")
    inner, outer = inner[...].astype(F32), outer[...].astype(F32)
    return unpacked(pick(odd, inner, outer), groups), unpacked(pick(odd, outer, inner), groups)


def pack_kernel(below, hidden, inner_out, outer_out, wide_out, below_here, hidden_here, arrived):
    channels, row_count, width = below.shape
    size = channels * row_count
    part = channels // 2
    copies = []
    for source, here in ((below, below_here), (hidden, hidden_here)):
        for at in (pl.ds(0, part), pl.ds(part, part)):
            copies.append(
                pltpu.make_async_copy(source.at[at], here.at[at], arrived.at[len(copies)])
            )
            copies[-1].start()
    for index, copy in enumerate(copies):
        here = (below_here, hidden_here)[index // 2]
        copy.wait()
        value = here[pl.ds(index % 2 * part, part)].astype(F32)
        at = pl.ds(index * part * row_count, part * row_count)
        wide_out[at, :] = value.reshape(part * row_count, width)
    edges = [
        wide_out[pl.ds(index, 2 * channels, stride=row_count), :] for index in (0, row_count - 1)
    ]
    row_sends(edges[0], edges[1], inner_out, outer_out)


def down_rows(values, width):
    count = values.shape[0]
    return jnp.broadcast_to(values[None, :], (width, count)).T


def prepare_kernel(
    wide,
    cell_hbm,
    weights_hbm,
    hidden_grad_hbm,
    target_hbm,
    land_hbm,
    fire_hbm,
    gate_bias_hbm,
    readout_hbm,
    rows_out,
    columns_out,
    second_out,
    cell_strip_out,
    hidden_grad_strip_out,
    fields_strip_out,
    cell_out,
    weights_out,
    hidden_grad_out,
    target_out,
    land_out,
    fire_out,
    bias_wide_out,
    readout_wide_out,
    hidden_grad_here,
    gate_bias_here,
    readout_here,
    arrived,
):
    row_count, channels, width = rows_out.shape
    copies = [
        pltpu.make_async_copy(source, target, arrived.at[index])
        for index, (source, target) in enumerate(
            (
                (cell_hbm, cell_out),
                *(
                    (weights_hbm.at[tap], weights_out.at[:, pl.ds(tap * channels, channels)])
                    for tap in range(weights_hbm.shape[0])
                ),
                (hidden_grad_hbm, hidden_grad_here),
                (target_hbm, target_out),
                (land_hbm, land_out),
                (fire_hbm, fire_out),
                (gate_bias_hbm, gate_bias_here),
                (readout_hbm, readout_here),
            )
        )
    ]
    for copy in copies:
        copy.start()
    columns = jnp.zeros((channels, width), F32)
    second = jnp.zeros((channels, width), F32)
    for index in range(row_count):
        row = wide[pl.ds(index, channels, stride=row_count), :]
        rows_out[index] = row.astype(BF16)
        columns = edge_columns(row, index + 1, columns)
        second = second_columns(row, index + 1, second)
    columns_out[...] = columns
    second_out[...] = second
    for copy in copies:
        copy.wait()
    hidden_grad_out[...] = hidden_grad_here[...].astype(F32).reshape(hidden_grad_out.shape)
    bias_wide_out[...] = down_rows(gate_bias_here[...], width)
    readout_wide_out[...] = down_rows(readout_here[...], width)
    hid = hidden_grad_here.shape[0]
    cell_strip = jnp.zeros((hid, width), F32)
    hidden_grad_strip = jnp.zeros((hid, width), F32)
    fields_strip = jnp.zeros((8, width), F32)
    for index in range(row_count):
        strided = pl.ds(index, hid, stride=row_count)
        cell_strip = edge_columns(cell_out[strided, :], index + 1, cell_strip)
        hidden_grad_strip = edge_columns(hidden_grad_out[strided, :], index + 1, hidden_grad_strip)
        at = slice(index, index + 1)
        fields = [target_out[at, :], land_out[at, :].astype(F32), fire_out[at, :].astype(F32)]
        fields = jnp.concatenate(fields + [jnp.zeros((5, width), F32)], axis=0)
        fields_strip = edge_columns(fields, index + 1, fields_strip)
    cell_strip_out[...] = cell_strip
    hidden_grad_strip_out[...] = hidden_grad_strip
    fields_strip_out[...] = fields_strip


def columns_kernel(row_count, groups, columns, outer, inner, packed_out, *whole_out):
    north, south = row_halo(inner, outer)
    value = edge_columns(north, 0, columns[...].astype(F32))
    value = edge_columns(south, row_count + 1, value)
    packed_out[...] = packed(value, groups).astype(BF16)
    for out in whole_out:
        out[...] = value.astype(BF16)


def encode(bias):
    high = bias.astype(BF16).astype(F32)
    return jnp.concatenate([high, bias - high], axis=0)


def decode(block):
    return block[0:8] + block[8:16]


def cell_step(part, cell_before, hidden_grad, target, land, fire, readout):
    hid = part.shape[0] // 4
    input_gate = 0.5 + 0.5 * jnp.tanh(0.5 * part[0:hid])
    forget_gate = 0.5 + 0.5 * jnp.tanh(0.5 * part[hid : 2 * hid])
    output_gate = 0.5 + 0.5 * jnp.tanh(0.5 * part[2 * hid : 3 * hid])
    candidate = jnp.tanh(part[3 * hid : 4 * hid])
    cell_next = land * (forget_gate * cell_before + input_gate * candidate)
    squashed = jnp.tanh(cell_next)
    hidden_next = (output_gate * squashed).astype(BF16).astype(F32)
    predicted = jnp.sum(readout * hidden_next, axis=0, keepdims=True)
    total_grad = hidden_grad + 2.0 * (fire * (predicted - target)) * readout
    cell_grad = land * total_grad * output_gate * (1.0 - squashed * squashed)
    pre_grad = jnp.concatenate(
        [
            cell_grad * candidate * input_gate * (1.0 - input_gate),
            cell_grad * cell_before * forget_gate * (1.0 - forget_gate),
            total_grad * squashed * output_gate * (1.0 - output_gate),
            cell_grad * input_gate * (1.0 - candidate * candidate),
        ],
        axis=0,
    )
    return hidden_next, cell_next, cell_grad * forget_gate, pre_grad


def gates_kernel(
    place,
    rows_in,
    inner_row,
    outer_row,
    second,
    cell_prev,
    weights,
    hidden_grad,
    target,
    land,
    fire,
    bias_wide,
    readout_wide,
    hidden_out,
    cell_out,
    grad_cell_out,
    pre_out,
    second_out,
    sums,
    bias_out,
    shifted,
):
    row_count, channels, width = rows_in.shape
    gate_count = weights.shape[0]
    hid = gate_count // 4
    half_gates = place.half_gates
    north, south = row_halo(inner_row, outer_row)
    columns = second_columns(north, 0, second[...])
    second_out[...] = second_columns(south, row_count + 1, columns).astype(BF16)
    for position in range(row_count + 2):
        if position == 0:
            row = north
        elif position == row_count + 1:
            row = south
        else:
            row = rows_in[position - 1].astype(F32)
        at = pl.ds(position * width, width)
        shifted[0:channels, at] = rolled(row, 1).astype(BF16)
        shifted[channels : 2 * channels, at] = row.astype(BF16)
        shifted[2 * channels : 3 * channels, at] = rolled(row, -1).astype(BF16)

    bias_total = jnp.zeros((gate_count, width), F32)
    lane = lanes((gate_count, width))
    inside = (lane > 0) & (lane < width - 1)
    readout = readout_wide[...]
    pair = 2 if row_count % 2 == 0 else 1
    for base in range(0, row_count, pair):
        preact = jnp.zeros((gate_count, pair * width), F32)
        for a in range(3):
            preact += jnp.dot(
                weights[:, pl.ds(3 * a * channels, 3 * channels)],
                shifted[:, pl.ds((base + a) * width, pair * width)],
                preferred_element_type=F32,
            )
        for offset in range(pair):
            index = base + offset
            strided = pl.ds(index, hid, stride=row_count)
            at = slice(index, index + 1)
            hidden_next, cell_next, grad_cell, pre_grad = cell_step(
                preact[:, offset * width : (offset + 1) * width] + bias_wide[...],
                cell_prev[strided, :],
                hidden_grad[strided, :],
                target[at, :],
                land[at, :].astype(F32),
                fire[at, :].astype(F32),
                readout,
            )
            hidden_out[strided, :] = hidden_next
            cell_out[strided, :] = cell_next
            grad_cell_out[strided, :] = grad_cell
            pre_grad = jnp.where(inside, pre_grad, 0.0)
            bias_total += pre_grad
            pre_out[:, pl.ds(index * width, width)] = pre_grad.astype(BF16)
    bias_out[...] = bias_total

    for a in range(3):
        product = lax.dot_general(
            pre_out[...],
            shifted[:, pl.ds(a * width, row_count * width)],
            ACROSS,
            preferred_element_type=F32,
        )
        for b in range(3):
            for half in range(2):
                at = half * place.half_rows + (3 * a + b) * half_gates
                sums[at : at + half_gates, :] = product[
                    half * half_gates : (half + 1) * half_gates, b * channels : (b + 1) * channels
                ]
    used = place.taps * half_gates
    if place.half_rows > used:
        for half in range(2):
            at = half * place.half_rows
            sums[at + used : at + place.half_rows, :] = jnp.zeros(
                (place.half_rows - used, channels), F32
            )


def add_strip(place, half, sums, pre_strip, patches, out):
    half_gates, channels = place.half_gates, sums.shape[1]
    gates = pre_strip[pl.ds(pl.multiple_of(half * half_gates, half_gates), half_gates), :]
    product = lax.dot_general(gates, patches[...], ACROSS, preferred_element_type=F32)
    base = half * place.half_rows
    for tap in range(place.taps):
        at = pl.ds(pl.multiple_of(base + tap * half_gates, 8), half_gates)
        value = sums[at, :] + product[:, tap * channels : (tap + 1) * channels]
        out[tap * half_gates : (tap + 1) * half_gates, :] = value.astype(out.dtype)
    used = place.taps * half_gates
    if place.half_rows > used:
        rest = jnp.zeros((place.half_rows - used, channels), out.dtype)
        out[used:, :] = rest


def strip_kernel(
    place,
    row_count,
    edge,
    second,
    outer_column,
    inner_column,
    weights,
    bias_wide,
    readout_wide,
    cell_strip,
    hidden_grad_strip,
    fields_strip,
    sums,
    send_out,
    pre_out,
    pre_wide_out,
    patches,
    hidden_out,
    cell_out,
    grad_cell_out,
):
    channels, width = edge.shape
    west, east = column_halo(inner_column, outer_column, GROUPS)
    near_first = lanes((channels, width)) < LAST
    inner = second[...].astype(F32)
    columns = (
        jnp.where(near_first, rolled(west, -LAST), inner),
        edge[...].astype(F32),
        jnp.where(near_first, inner, rolled(east, LAST)),
    )
    for a in range(3):
        for b in range(3):
            at = (3 * a + b) * channels
            patches[at : at + channels, :] = rolled(columns[b], 1 - a).astype(BF16)
    preact = jnp.dot(weights[...], patches[...], preferred_element_type=F32) + bias_wide[...]
    hidden_next, cell_next, grad_cell, pre_grad = cell_step(
        preact,
        cell_strip[...],
        hidden_grad_strip[...],
        fields_strip[0:1, :],
        fields_strip[1:2, :],
        fields_strip[2:3, :],
        readout_wide[...],
    )
    hidden_out[...] = hidden_next
    cell_out[...] = cell_next
    grad_cell_out[...] = grad_cell
    lane = lanes(pre_grad.shape)
    lane = jnp.where(lane >= LAST, lane - LAST, lane)
    pre_grad = jnp.where((lane >= 1) & (lane <= row_count), pre_grad, 0.0)
    pre_out[...] = pre_grad.astype(BF16)
    pre_wide_out[...] = pre_grad
    add_strip(place, 1 - place.rank(0), sums, pre_out, patches, send_out)


def keep_kernel(place, sums, pre_strip, patches, bias_partial, pre_wide, out, bias_out):
    add_strip(place, place.rank(0), sums, pre_strip, patches, out)
    channels = sums.shape[1]
    bias_total = bias_partial[...] + pre_wide[...]
    ones = jnp.ones((8, bias_total.shape[1]), BF16)
    high = bias_total.astype(BF16)
    low = (bias_total - high.astype(F32)).astype(BF16)
    flat = lax.dot_general(ones, high, ACROSS, preferred_element_type=F32)
    flat += lax.dot_general(ones, low, ACROSS, preferred_element_type=F32)
    odd = lax.broadcasted_iota(jnp.int32, (8, channels), 0) % 2 == 1
    bias_out[...] = jnp.where(odd, flat[:, channels : 2 * channels], flat[:, 0:channels])


def edges_kernel(
    row_count,
    hidden,
    cell,
    grad_cell,
    pre,
    hidden_strip,
    cell_strip,
    grad_cell_strip,
    pre_strip,
    hidden_hbm,
    cell_hbm,
    grad_cell_hbm,
    pre_out,
    inner_out,
    outer_out,
    hidden_low,
    hidden_here,
    cell_here,
    grad_cell_here,
    left,
):
    hid, _, width = hidden_low.shape
    leaving = []
    for source, strip, here, ready, target in (
        (cell, cell_strip, cell_here, cell_here, cell_hbm),
        (grad_cell, grad_cell_strip, grad_cell_here, grad_cell_here, grad_cell_hbm),
        (hidden, hidden_strip, hidden_here, hidden_low, hidden_hbm),
    ):
        columns = strip[...]
        for index in range(row_count):
            strided = pl.ds(index, hid, stride=row_count)
            here[strided, :] = at_edges(source[strided, :], index + 1, columns)
        if ready is hidden_low:
            hidden_low[...] = here[...].reshape(hidden_low.shape).astype(BF16)
        leaving.append(pltpu.make_async_copy(ready, target, left.at[len(leaving)]))
        leaving[-1].start()
    first, last = None, None
    columns = pre_strip[...].astype(F32)
    for index in range(row_count):
        at = pl.ds(index * width, width)
        row = at_edges(pre[:, at].astype(F32), index + 1, columns)
        pre_out[:, at] = row.astype(BF16)
        first = row if index == 0 else first
        last = row
    row_sends(first, last, inner_out, outer_out)
    for copy in leaving:
        copy.wait()


def pair_kernel(place, keep, bias, received, *outs):
    sends, keep_out, scratch = outs[:-2], outs[-2], outs[-1]
    chunk = place.chunk
    rank = place.plane_rank()
    scratch[...] = keep[...] + received[...].astype(F32)
    block = encode(bias[...]).astype(BF16)
    for step, send in zip(place.scatter_steps, sends):
        send[0:BIAS_ROWS, :] = block
        at = pl.ds(pl.multiple_of((rank ^ step) * chunk, 8), chunk)
        send[BIAS_ROWS:, :] = scratch[at, :].astype(BF16)
    keep_out[...] = scratch[pl.ds(pl.multiple_of(rank * chunk, 8), chunk), :]


def plane_kernel(keep, bias, *refs):
    received, out = refs[:-2], refs[-1]
    total, bias_total = keep[...], bias[...]
    for ref in received:
        total += ref[BIAS_ROWS:, :].astype(F32)
        bias_total += decode(ref[0:BIAS_ROWS, :].astype(F32))
    out[0:BIAS_ROWS, :] = encode(bias_total).astype(BF16)
    out[BIAS_ROWS:, :] = total.astype(BF16)


def join_kernel(*refs):
    blocks, out = refs[:-2], refs[-1]
    for index, block in enumerate(blocks):
        out[index] = block[...]


def add_kernel(scale, own, received, out):
    here, there = own[...].astype(F32), received[...].astype(F32)
    bias = (decode(here[0:BIAS_ROWS]) + decode(there[0:BIAS_ROWS])) * scale
    out[0:BIAS_ROWS, :] = encode(bias).astype(BF16)
    out[BIAS_ROWS:, :] = ((here[BIAS_ROWS:] + there[BIAS_ROWS:]) * scale).astype(BF16)


def store_half(place, half, blocks, out, wide, left):
    chunk, half_gates = place.chunk, place.half_gates
    gates = pl.ds(pl.multiple_of(half * half_gates, half_gates), half_gates)
    rank = place.plane_rank()
    for step, block in enumerate(blocks):
        at = pl.ds(pl.multiple_of((rank ^ step) * chunk, 8), chunk)
        wide[at, :] = block[BIAS_ROWS:, :].astype(F32)
    copies = []
    for tap in range(place.taps):
        source = wide.at[tap * half_gates : (tap + 1) * half_gates, :]
        copies.append(pltpu.make_async_copy(source, out.at[tap, gates, :], left.at[tap]))
        copies[-1].start()
    return copies


def in_steps(place, early, late):
    blocks = [early.at[index] for index in range(place.plane - 1)]
    return blocks[:-1] + [late] + blocks[-1:]


def own_half_kernel(place, late, early, out, bias_out, wide, left):
    blocks = in_steps(place, early, late)
    copies = store_half(place, place.rank(0), blocks, out, wide, left)
    rank = place.plane_rank()
    bias = decode(blocks[0][0:BIAS_ROWS, :].astype(F32))
    for step in range(1, place.plane):
        bias = pick(rank == step, decode(blocks[step][0:BIAS_ROWS, :].astype(F32)), bias)
    bias_out[...] = bias
    for copy in copies:
        copy.wait()


def other_half_kernel(
    place, bias_own, early, late, after, out_before, out, bias_out, wide, bias_here, left
):
    del after, out_before
    blocks = in_steps(place, early, late)
    copies = store_half(place, 1 - place.rank(0), blocks, out, wide, left)
    rank = place.plane_rank()
    bias = decode(blocks[0][0:BIAS_ROWS, :].astype(F32))
    for step in range(1, place.plane):
        bias = pick(rank == step, decode(blocks[step][0:BIAS_ROWS, :].astype(F32)), bias)
    bias += bias_own[...]
    width = bias.shape[1]
    for index in range(bias_here.shape[0] // width):
        bias_here[pl.ds(index * width, width)] = bias[index]
    bias_copy = pltpu.make_async_copy(bias_here, bias_out, left.at[place.taps])
    bias_copy.start()
    bias_copy.wait()
    for copy in copies:
        copy.wait()


def field_kernel(pre, weights, wide_out, turned_out, done_out, shifted):
    done_out[...] = jnp.zeros(done_out.shape, F32)
    gate_count, cells = pre.shape
    width = wide_out.shape[1]
    channels = weights.shape[1] // 9
    row_count = cells // width
    lane = lanes((gate_count, width))
    for index in range(row_count):
        at = pl.ds(index * width, width)
        row = pre[:, at].astype(F32)
        left = jnp.where(lane == 0, 0.0, rolled(row, 1))
        right = jnp.where(lane == width - 1, 0.0, rolled(row, -1))
        shifted[0:gate_count, at] = right.astype(BF16)
        shifted[gate_count : 2 * gate_count, at] = pre[:, at]
        shifted[2 * gate_count : 3 * gate_count, at] = left.astype(BF16)
    for a in range(3):
        for b in range(3):
            turned_out[a, :, b * gate_count : (b + 1) * gate_count] = (
                weights[:, pl.ds((3 * a + b) * channels, channels)].T
            )

    def product(a, index, count):
        return jnp.dot(
            turned_out[a],
            shifted[:, pl.ds(index * width, count * width)],
            preferred_element_type=F32,
        )

    pair = 2 if row_count % 2 == 0 else 1
    for base in range(0, row_count, pair):
        total = product(1, base, pair)
        for a, first in ((2, base - 1), (0, base + 1)):
            low, high = max(first, 0), min(first + pair, row_count)
            if low >= high:
                continue
            part = product(a, low, high - low)
            blank = jnp.zeros((channels, width), F32)
            parts = [blank] * (low - first) + [part] + [blank] * (first + pair - high)
            total += jnp.concatenate(parts, axis=1)
        for offset in range(pair):
            value = total[:, offset * width : (offset + 1) * width]
            wide_out[pl.ds(base + offset, channels, stride=row_count), :] = value


def field_halo_kernel(
    place,
    wide,
    turned,
    outer_row,
    inner_row,
    outer_column,
    inner_column,
    inputs_out,
    hidden_out,
    done_out,
    total,
):
    done_out[...] = jnp.zeros(done_out.shape, F32)
    hid, row_count, width = hidden_out.shape
    channels = turned.shape[1]
    gate_count = turned.shape[2] // 3
    north, south = row_halo(inner_row, outer_row)
    west, east = column_halo(inner_column, outer_column, PRE_GROUPS)
    lane = lanes((gate_count, width))
    lat = place.position()[0]

    def row_part(taps, row, position):
        left = jnp.where(lane == 0, rolled(west, -LAST - position), rolled(row, 1))
        right = rolled(east, width - 1 - position)
        right = jnp.where(lane == width - 1, right, rolled(row, -1))
        stack = jnp.concatenate([right, row, left], axis=0).astype(BF16)
        return jnp.dot(taps, stack, preferred_element_type=F32)

    above = row_part(turned[jnp.where(lat == 0, 0, 2)], north, 0)
    below = row_part(turned[jnp.where(lat == place.lat - 1, 2, 0)], south, row_count + 1)

    inside = (lane >= 1) & (lane <= row_count)
    west = jnp.where(inside, rolled(west, -LAST), 0.0)
    east = jnp.where(inside, east, 0.0)
    sides = [rolled(west, a - 1) for a in range(3)] + [rolled(east, LAST + a - 1) for a in range(3)]
    taps = [turned[a, :, 2 * gate_count : 3 * gate_count] for a in range(3)]
    taps += [turned[a, :, 0:gate_count] for a in range(3)]
    columns = jnp.dot(
        jnp.concatenate(taps, axis=1),
        jnp.concatenate(sides, axis=0).astype(BF16),
        preferred_element_type=F32,
    )
    blank = jnp.zeros((channels, width), F32)
    for index in range(row_count):
        strided = pl.ds(index, channels, stride=row_count)
        value = wide[strided, :] + at_edges(blank, index + 1, columns)
        if index == 0:
            value += above
        if index == row_count - 1:
            value += below
        total[strided, :] = value
    size = (channels - hid) * row_count
    inputs_out[...] = total[0:size, :].reshape(inputs_out.shape).astype(BF16)
    hidden_out[...] = total[size:, :].reshape(hidden_out.shape).astype(BF16)


def body(
    place,
    inputs_below,
    hidden_prev,
    cell_prev,
    kernel_weights,
    gate_bias,
    readout,
    target_field,
    land_mask,
    fire_mask,
    hidden_grad,
):
    hid, row_count, width = hidden_prev.shape
    gate_count, channels = kernel_weights.shape[1:]
    cells = row_count * width
    halo_cells = (row_count + 2) * width
    scaling = 1.0 / math.sqrt(cells * place.lat * place.lon)
    bind = functools.partial
    inner_rows, outer_rows = place.pairs(place.inner_rows), place.pairs(place.outer_rows)
    inner_columns = place.pairs(place.inner_columns)
    outer_columns = place.pairs(place.outer_columns)
    flat = sds((hid * row_count, width), F32)
    strip = sds((hid, width), F32)

    inner, outer, wide = call(
        pack_kernel,
        (
            sds((channels, width), BF16),
            sds((channels, width), BF16),
            sds((channels * row_count, width), F32),
        ),
        [
            pltpu.VMEM(inputs_below.shape, BF16),
            pltpu.VMEM(hidden_prev.shape, BF16),
            pltpu.SemaphoreType.DMA((4,)),
        ],
        remote=2,
        moved=4 * channels * cells,
    )(inputs_below, hidden_prev)
    inner, outer = permuted(inner, inner_rows), permuted(outer, outer_rows)
    (
        rows,
        columns,
        second,
        cell_strip,
        hidden_grad_strip,
        fields_strip,
        cell_here,
        weights_here,
        hidden_grad_here,
        target_here,
        land_here,
        fire_here,
        bias_wide,
        readout_wide,
    ) = call(
        prepare_kernel,
        (
            sds((row_count, channels, width), BF16),
            sds((channels, width), F32),
            sds((channels, width), F32),
            strip,
            strip,
            sds((8, width), F32),
            flat,
            sds((gate_count, place.taps * channels), BF16),
            flat,
            sds(target_field.shape, F32),
            sds(land_mask.shape, jnp.int32),
            sds(fire_mask.shape, jnp.int32),
            sds((gate_count, width), F32),
            sds((hid, width), F32),
        ),
        [
            pltpu.VMEM(hidden_grad.shape, BF16),
            pltpu.VMEM(gate_bias.shape, F32),
            pltpu.VMEM(readout.shape, F32),
            pltpu.SemaphoreType.DMA((7 + place.taps,)),
        ],
        remote=8,
        moved=6_000_000,
    )(
        wide,
        cell_prev.reshape(hid * row_count, width),
        kernel_weights,
        hidden_grad,
        target_field,
        land_mask,
        fire_mask,
        gate_bias,
        readout,
    )
    columns, edge = call(
        bind(columns_kernel, row_count, GROUPS),
        (sds((channels // GROUPS, width), BF16), sds((channels, width), BF16)),
    )(columns, outer, inner)
    inner_column = permuted(columns, inner_columns)
    outer_column = permuted(columns, outer_columns)
    hidden_rows, cell_rows, grad_cell_rows, pre, second, sums, bias = call(
        bind(gates_kernel, place),
        (
            flat,
            flat,
            flat,
            sds((gate_count, cells), BF16),
            sds((channels, width), BF16),
            sds((2 * place.half_rows, channels), F32),
            sds((gate_count, width), F32),
        ),
        [pltpu.VMEM((3 * channels, halo_cells), BF16)],
        flops=4 * 9 * gate_count * channels * cells,
        moved=6_000_000,
        transcendentals=5 * hid * cells,
    )(
        rows,
        inner,
        outer,
        second,
        cell_here,
        weights_here,
        hidden_grad_here,
        target_here,
        land_here,
        fire_here,
        bias_wide,
        readout_wide,
    )
    send, pre_strip, pre_wide, patches, *strips = call(
        bind(strip_kernel, place, row_count),
        (
            sds((place.half_rows, channels), BF16),
            sds((gate_count, width), BF16),
            sds((gate_count, width), F32),
            sds((place.taps * channels, width), BF16),
            strip,
            strip,
            strip,
        ),
    )(
        edge,
        second,
        outer_column,
        inner_column,
        weights_here,
        bias_wide,
        readout_wide,
        cell_strip,
        hidden_grad_strip,
        fields_strip,
        sums,
    )
    keep, bias = call(
        bind(keep_kernel, place),
        (sds((place.half_rows, channels), F32), sds((8, channels), F32)),
    )(sums, pre_strip, patches, bias, pre_wide)
    hidden_next, cell_next, grad_cell, pre, pre_inner, pre_outer = call(
        bind(edges_kernel, row_count),
        (
            sds((hid, row_count, width), BF16),
            flat,
            flat,
            sds((gate_count, cells), BF16),
            sds((gate_count, width), BF16),
            sds((gate_count, width), BF16),
        ),
        [
            pltpu.VMEM((hid, row_count, width), BF16),
            pltpu.VMEM(flat.shape, F32),
            pltpu.VMEM(flat.shape, F32),
            pltpu.VMEM(flat.shape, F32),
            pltpu.SemaphoreType.DMA((3,)),
        ],
        leaving=3,
        moved=4_000_000,
    )(hidden_rows, cell_rows, grad_cell_rows, pre, *strips, pre_strip)
    pre_inner, pre_outer = permuted(pre_inner, inner_rows), permuted(pre_outer, outer_rows)
    pre_columns = call(
        bind(columns_kernel, row_count, PRE_GROUPS),
        (sds((gate_count // PRE_GROUPS, width), BF16),),
    )(pre_strip, pre_outer, pre_inner)[0]

    block = sds((BIAS_ROWS + place.chunk, channels), BF16)
    token = sds((8, width), F32)
    steps = range(place.plane - 1, 0, -1)
    *sends, keep = call(
        bind(pair_kernel, place),
        (*[block for _ in steps], sds((place.chunk, channels), F32)),
        [pltpu.VMEM((place.half_rows, channels), F32)],
    )(keep, bias, permuted(send, place.phase_pairs(0)))
    received = [
        permuted(send, place.plane_pairs(step)) for step, send in zip(place.scatter_steps, sends)
    ]
    field, turned, field_done = call(
        field_kernel,
        (
            sds((channels * row_count, width), F32),
            sds((3, channels, 3 * gate_count), BF16),
            token,
        ),
        [pltpu.VMEM((3 * gate_count, cells), BF16)],
        flops=2 * 9 * gate_count * channels * cells,
        moved=3_000_000,
    )(pre, weights_here)
    part = call(plane_kernel, block)(keep, bias, *received, field_done)
    pre_inner_columns = permuted(pre_columns, inner_columns)
    pre_outer_columns = permuted(pre_columns, outer_columns)
    phases = len(place.orders[0])
    for phase in range(1, phases):
        is_last = phase == phases - 1
        part = call(bind(add_kernel, scaling if is_last else 1.0), block)(
            part, permuted(part, place.phase_pairs(phase))
        )
    received = [permuted(part, place.plane_pairs(step)) for step in steps[::-1]]
    grad_inputs, grad_hidden, field_done = call(
        bind(field_halo_kernel, place),
        (
            sds((channels - hid, row_count, width), BF16),
            sds((hid, row_count, width), BF16),
            token,
        ),
        [pltpu.VMEM((channels * row_count, width), F32)],
        flops=40 * gate_count * channels * cells * 9,
        moved=2_000_000,
    )(field, turned, pre_outer, pre_inner, pre_outer_columns, pre_inner_columns)
    early = call(join_kernel, sds((place.plane - 1, *block.shape), BF16))(
        part, *received[:-2], received[-1], field_done
    )
    late = received[-2]
    early_other = permuted(early, place.phase_pairs(0))
    late_other = permuted(late, place.phase_pairs(0))
    half = [pltpu.VMEM((place.half_rows, channels), F32)]
    grad_kernel, bias = call(
        bind(own_half_kernel, place),
        (sds(kernel_weights.shape, F32), sds((8, channels), F32)),
        half + [pltpu.SemaphoreType.DMA((place.taps,))],
        leaving=1,
        flops=40 * gate_count * channels * cells * 9,
        moved=6 * place.half_rows * channels,
    )(late, early)
    grad_kernel, grad_bias = call(
        bind(other_half_kernel, place),
        (sds(kernel_weights.shape, F32), sds((gate_count,), F32)),
        half + [pltpu.VMEM((gate_count,), F32), pltpu.SemaphoreType.DMA((place.taps + 1,))],
        remote=1,
        leaving=2,
        aliases={4: 0},
        moved=6 * place.half_rows * channels,
    )(bias, early_other, late_other, target_here, grad_kernel)
    shape = hidden_prev.shape
    return (
        hidden_next,
        cell_next.reshape(shape),
        grad_inputs,
        grad_hidden,
        grad_cell.reshape(shape),
        grad_kernel,
        grad_bias,
    )


def solution(mesh):
    lat_count, lon_count = mesh.shape["lat"], mesh.shape["lon"]
    split = Mesh(mesh.devices.reshape(lat_count // 2, 2, lon_count // 2, 2), AXES)
    field = P(None, ("band", "core"), ("reach", "near"))
    flat = P(("band", "core"), ("reach", "near"))

    def run(*args):
        place = Layout(lat_count, lon_count, *args[3].shape[:2])
        return jax.shard_map(
            functools.partial(body, place),
            mesh=split,
            in_specs=(field, field, field, P(), P(), P(), flat, flat, flat, field),
            out_specs=(field, field, field, field, field, P(), P()),
            check_vma=False,
        )(*args)

    return run
```
